32 devices in a mesh: tm: 2 (over y), net: 4 (over z), cols: 4 (over x, core).
Axes of the slice: x: 2, y: 2, z: 4, core: 2. Of those that a mesh axis runs over, the one named last changes fastest.
Arguments:
- jac: bfloat16 [4, 16, 3, 128, 128], P('tm', 'net'), may hold values from -0.5 to 1.5
- block_cols: int32 [16, 2], P('net'), may hold values from 0 to 3
- iface_jac: bfloat16 [4, 4, 4, 128, 128], P('tm', 'net'), may hold values from -0.1796875 to 0.1796875
- iface_send: int32 [4, 4], P('net'), may hold values from 0 to 3
- iface_recv: int32 [4, 4], P('net'), may hold values from 0 to 3
- iface_live: int32 [4, 4], P('net'), may hold values from 0 to 128
- ctrl_node: int32 [768], P('cols'), may hold values from 0 to 2047
- ctrl_gain: float32 [4, 768], P('tm', 'cols'), may hold values from -6 to 6
Outputs:
- sens: bfloat16 [4, 768, 2048], P('tm', 'cols', 'net')
The draws below stay inside these ranges and needn't reach their ends.
All inputs are finite; a program needn't handle non-finite values.
Results may differ from the reference program's by a relative error of at most 0.013.
Values may be sent and summed in bfloat16 or wider, within the bound.
No kernel may reach another device: no remote copies, remote signals or barrier semaphores. Data moves between devices by JAX's collectives and lax.ppermute only.
A program may use at most 64 MiB of HBM per device.

```python
import math
import jax
import jax.numpy as jnp
from jax import lax

BLK = 128
NB = 4
K = 3
CTRL = 768
BLOCKS = 16
NSTATES = 2048
HORIZON = 4
N_NET = 4


def draw_jac(key, part):
    shape = (HORIZON, BLOCKS, K, BLK, BLK)
    spread = 0.2 / math.sqrt(BLK * K)
    noise = jax.random.normal(key, shape, jnp.float32) * spread
    keeping = jnp.exp(jax.random.uniform(jax.random.fold_in(key, 11), (BLOCKS, BLK), jnp.float32, math.log(0.55), math.log(0.995)))
    unit = jnp.eye(BLK, dtype=jnp.float32)
    leading = (jnp.arange(K) == 0).astype(jnp.float32)
    diagonal = keeping[None, :, None, :, None] * unit[None, None, None] * leading[None, None, :, None, None]
    return (noise + diagonal).astype(jnp.bfloat16)


def place_ends(values, stream_key, low, top_value):
    spot = [jax.random.randint(jax.random.fold_in(stream_key, axis), (), 0, length) for axis, length in enumerate(values.shape)]
    main_axis = values.shape.index(max(values.shape))
    neighbour = spot[:main_axis] + [(spot[main_axis] + 1) % values.shape[main_axis]] + spot[main_axis + 1:]
    return values.at[tuple(spot)].set(low).at[tuple(neighbour)].set(top_value)


def shard_levels(rng, dims, shards, low, top_value):
    loudness = 1.0
    for dim, parts in shards:
        draws = jax.random.uniform(jax.random.fold_in(jax.random.fold_in(rng, 6), dim), (parts,), jnp.float32, low / len(shards), top_value / len(shards))
        loudness = loudness * jnp.repeat(jnp.exp(draws), dims[dim] // parts).reshape((-1,) + (1,) * (len(dims) - 1 - dim))
    return loudness


def centred(own_key, shape, deviation, bound, cuts=(), kind=jnp.bfloat16):
    drawn = jax.random.normal(own_key, shape, jnp.float32) * deviation
    if len(cuts) > 0:
        drawn = shard_levels(own_key, shape, cuts, -0.22, 0.18) * drawn
    return jnp.clip(drawn, min=-bound, max=bound).astype(kind)


def setup_inputs(seed: int = 0) -> dict:
    seeds = jax.random.split(jax.random.key(seed), 9)
    jac = draw_jac(jax.random.fold_in(seeds[8], 71), 0)
    block_cols = place_ends(jax.random.randint(seeds[1], (BLOCKS, K - 1), 0, NB), jax.random.fold_in(seeds[1], 1), 0, NB - 1).astype(jnp.int32)
    iface_jac = centred(seeds[2], (HORIZON, N_NET, N_NET, BLK, BLK), 0.03, 0.1796875, ((0, 2), (1, 4)))
    iface_send = place_ends(jax.random.randint(seeds[3], (N_NET, N_NET), 0, NB), jax.random.fold_in(seeds[3], 1), 0, NB - 1).astype(jnp.int32)
    iface_recv = place_ends(jax.random.randint(seeds[4], (N_NET, N_NET), 0, NB), jax.random.fold_in(seeds[4], 1), 0, NB - 1).astype(jnp.int32)
    iface_live = place_ends(jax.random.randint(seeds[5], (N_NET, N_NET), 0, BLK + 1), jax.random.fold_in(seeds[5], 1), 0, BLK).astype(jnp.int32)
    ctrl_node = place_ends(jax.random.randint(seeds[6], (CTRL,), 0, NSTATES), jax.random.fold_in(seeds[6], 1), 0, NSTATES - 1).astype(jnp.int32)
    ctrl_gain = centred(seeds[7], (HORIZON, CTRL), 1.0, 6.0, ((0, 2), (1, 4)), jnp.float32)
    return dict(jac=jac, block_cols=block_cols, iface_jac=iface_jac, iface_send=iface_send, iface_recv=iface_recv, iface_live=iface_live, ctrl_node=ctrl_node, ctrl_gain=ctrl_gain)


def reference(jac, block_cols, iface_jac, iface_send, iface_recv, iface_live, ctrl_node, ctrl_gain):
    block_count = N_NET * NB
    state_count = block_count * BLK
    partition = jnp.arange(block_count, dtype=jnp.int32) // NB
    near_blocks = (partition[:, None] * NB + block_cols).astype(jnp.int32)
    senders = jnp.arange(N_NET, dtype=jnp.int32)
    send_blocks = (senders[None, :] * NB + iface_send.T).astype(jnp.int32)
    recv_blocks = (senders[:, None] * NB + iface_recv).astype(jnp.int32)
    live_mask = (jnp.arange(BLK, dtype=jnp.int32)[None, None, :] < iface_live[:, :, None]).astype(jnp.float32)
    receive_map = (recv_blocks[:, :, None] == jnp.arange(block_count, dtype=jnp.int32)[None, None, :]).astype(jnp.float32)
    placed = (ctrl_node[:, None] == jnp.arange(state_count, dtype=jnp.int32)[None, :]).astype(jnp.float32)
    highest = lax.Precision.HIGHEST

    def advance(state, inputs):
        step_jac, step_iface, gain_row = inputs
        state_tiles = state.astype(jnp.float32).reshape(CTRL, block_count, BLK)
        dense = step_jac.astype(jnp.float32)
        summed = jnp.einsum('iab,cib->cia', dense[:, 0], state_tiles, precision=highest)
        near_tiles = state_tiles[:, near_blocks, :]
        summed = summed + jnp.einsum('ikab,cikb->cia', dense[:, 1:], near_tiles, precision=highest)
        sources = state_tiles[:, send_blocks, :]
        coupled = jnp.einsum('pqab,cpqb->cpqa', step_iface.astype(jnp.float32), sources, precision=highest)
        coupled = coupled * live_mask[None]
        summed = summed + jnp.einsum('cpqa,pqi->cia', coupled, receive_map, precision=highest)
        total = summed.reshape(CTRL, state_count) + gain_row[:, None] * placed
        new_state = total.astype(jnp.bfloat16)
        return new_state, new_state

    initial = jnp.zeros((CTRL, state_count), jnp.bfloat16)
    final_state, produced = lax.scan(advance, initial, (jac, iface_jac, ctrl_gain))
    return produced
```

```python
import functools

import jax
import jax.numpy as jnp
from jax import lax
from jax.experimental import pallas as pl
from jax.experimental.pallas import tpu as pltpu
from jax.sharding import PartitionSpec as P

VMEM = pl.BlockSpec(memory_space=pltpu.VMEM)
SMEM = pl.BlockSpec(memory_space=pltpu.SMEM)
ANY = pl.BlockSpec(memory_space=pl.ANY)
LIMIT = pltpu.CompilerParams(vmem_limit_bytes=16 * 1024 * 1024)


def times_transposed(rows, block):
    return lax.dot_general(rows, block, (((1,), (1,)), ((), ())), preferred_element_type=jnp.float32)


def columns_of(node_ref, gain_ref):
    steps, cols = gain_ref.shape
    rows = jnp.concatenate(
        [node_ref[...].astype(jnp.float32), gain_ref[...], jnp.zeros((7 - steps, cols), jnp.float32)], axis=0
    )
    return rows.T


def injected(table, step, first_state, width):
    lane = lax.broadcasted_iota(jnp.int32, (table.shape[0], width), 1).astype(jnp.float32)
    hit = table[:, 0:1] == lane + first_state.astype(jnp.float32)
    return jnp.where(hit, table[:, step + 1 : step + 2], 0.0)


def add_own(state_ref, jac_ref, step, cols_ref, table, z_ref):
    blocks, _, width = state_ref.shape
    first = lax.axis_index("net") * blocks * width
    for i in range(blocks):
        total = injected(table, step, first + i * width, width)
        total += times_transposed(state_ref[i], jac_ref[step, i, 0])
        for k in range(1, jac_ref.shape[2]):
            total += times_transposed(state_ref[cols_ref[i, k - 1]], jac_ref[step, i, k])
        z_ref[i] = total


def add_coupled(incoming, iface_ref, step, source, recv_ref, live_ref, z_ref):
    width = z_ref.shape[2]
    lane = lax.broadcasted_iota(jnp.int32, z_ref.shape[1:], 1)
    term = times_transposed(incoming, iface_ref[step, 0, source])
    z_ref[recv_ref[0, source]] += jnp.where(lane < live_ref[0, source], term, 0.0)


def begin_kernel(jac_ref, iface_ref, cols_ref, recv_ref, live_ref, node_ref, gain_ref, state_ref, z_ref):
    table = columns_of(node_ref, gain_ref)
    state_ref[...] = jnp.zeros_like(state_ref)
    add_own(state_ref, jac_ref, 0, cols_ref, table, z_ref)
    for q in range(iface_ref.shape[2]):
        add_coupled(state_ref[0], iface_ref, 0, q, recv_ref, live_ref, z_ref)
    state_ref[...] = z_ref[...].astype(state_ref.dtype)
    add_own(state_ref, jac_ref, 1, cols_ref, table, z_ref)


def own_kernel(step, state_ref, jac_ref, cols_ref, node_ref, gain_ref, z_ref):
    add_own(state_ref, jac_ref, step, cols_ref, columns_of(node_ref, gain_ref), z_ref)


def join_kernel(step, known, *refs):
    n = lax.axis_size("net")
    me = lax.axis_index("net")
    if known:
        z_ref, iface_ref, send_ref, recv_ref, live_ref, node_ref, gain_ref, from_ref = refs[:8]
        refs = refs[8:]
    else:
        z_ref, iface_ref, send_ref, recv_ref, live_ref, state_in_ref = refs[:6]
        arrived = refs[6 : 6 + n - 1]
        refs = refs[6 + n - 1 :]
    state_ref, *outgoing = refs[:-1]
    acc_ref = refs[-1]
    blocks, _, width = z_ref.shape
    acc_ref[...] = z_ref[...]
    if known:
        table = columns_of(node_ref, gain_ref)
        for q in range(n):
            first = (q * blocks + from_ref[q]) * width
            block = injected(table, 0, first, width).astype(jnp.bfloat16)
            add_coupled(block, iface_ref, step, q, recv_ref, live_ref, acc_ref)
    else:
        add_coupled(state_in_ref[send_ref[0, me]], iface_ref, step, me, recv_ref, live_ref, acc_ref)
        for d in range(1, n):
            source = lax.rem(me - d + n, n)
            add_coupled(arrived[d - 1][...], iface_ref, step, source, recv_ref, live_ref, acc_ref)
    state_ref[...] = acc_ref[...].astype(state_ref.dtype)
    for d in range(1, n):
        if outgoing:
            outgoing[d - 1][...] = state_ref[send_ref[0, lax.rem(me + d, n)]]


def store_kernel(section, *refs):
    *states, _, out_ref, sems = refs

    @pl.when(lax.axis_index("tm") == section)
    def _():
        copies = []
        for s, state_ref in enumerate(states):
            width = state_ref.shape[2]
            for i in range(state_ref.shape[0]):
                copies.append(
                    pltpu.make_async_copy(
                        state_ref.at[i], out_ref.at[s, :, pl.ds(i * width, width)], sems.at[s, i]
                    )
                )
        for copy in copies:
            copy.start()
        for copy in copies:
            copy.wait()


def local(jac, block_cols, iface_jac, iface_send, iface_recv, iface_live, ctrl_node, ctrl_gain):
    steps, blocks, _, width, _ = jac.shape
    cols = ctrl_node.shape[0]
    tm = lax.axis_size("tm")
    n = lax.axis_size("net")
    node = ctrl_node[None]
    bf16 = functools.partial(jax.ShapeDtypeStruct, dtype=jnp.bfloat16)
    whole = bf16((blocks, cols, width))
    one = bf16((cols, width))
    sums = jax.ShapeDtypeStruct((blocks, cols, width), jnp.float32)

    def own(state, step):
        return pl.pallas_call(
            functools.partial(own_kernel, step),
            out_shape=sums,
            in_specs=[VMEM, VMEM, SMEM, VMEM, VMEM],
            out_specs=VMEM,
            compiler_params=LIMIT,
        )(state, jac, block_cols, node, ctrl_gain)

    def join(z, step, last, state=None, arrived=None, from_blocks=None):
        known = from_blocks is not None
        outs = [whole] + ([] if last else [one] * (n - 1))
        if known:
            extra = (node, ctrl_gain, from_blocks)
            extra_specs = [VMEM, VMEM, SMEM]
        else:
            extra = (state, *arrived)
            extra_specs = [VMEM] * n
        return pl.pallas_call(
            functools.partial(join_kernel, step, known),
            out_shape=outs,
            in_specs=[VMEM, VMEM, SMEM, SMEM, SMEM] + extra_specs,
            out_specs=[VMEM] * len(outs),
            scratch_shapes=[pltpu.VMEM(sums.shape, jnp.float32)],
            compiler_params=LIMIT,
        )(z, iface_jac, iface_send, iface_recv, iface_live, *extra)

    def store(section, states, out):
        return pl.pallas_call(
            functools.partial(store_kernel, section),
            out_shape=bf16((steps, cols, blocks * width)),
            in_specs=[VMEM] * len(states) + [ANY],
            out_specs=ANY,
            input_output_aliases={len(states): 0},
            scratch_shapes=[pltpu.SemaphoreType.DMA((steps, blocks))],
            compiler_params=LIMIT,
        )(*states, out)

    def exchange(outgoing, from_section, to_section):
        return [
            lax.ppermute(
                block,
                ("tm", "net"),
                [(from_section * n + q, to_section * n + (q + d) % n) for q in range(n)],
            )
            for d, block in enumerate(outgoing, 1)
        ]

    out = jnp.zeros((steps, cols, blocks * width), jnp.bfloat16)
    from_blocks = lax.all_to_all(iface_send[0], "net", split_axis=0, concat_axis=0, tiled=True)
    state, z = pl.pallas_call(
        begin_kernel,
        out_shape=[whole, sums],
        in_specs=[VMEM, VMEM, SMEM, SMEM, SMEM, VMEM, VMEM],
        out_specs=[VMEM, VMEM],
        compiler_params=LIMIT,
    )(jac, iface_jac, block_cols, iface_recv, iface_live, node, ctrl_gain)
    states = [state]
    for r in range(tm):
        if r > 0:
            pairs = [((r - 1) * n + q, r * n + q) for q in range(n)]
            before = states
            state = lax.ppermute(state, ("tm", "net"), pairs)
            arrived = exchange(outgoing, r - 1, r)
            out = store(r - 1, before, out)
            states = []
        for s in range(1 if r == 0 else 0, steps):
            last = r == tm - 1 and s == steps - 1
            if s > 0 and not (r == 0 and s == 1):
                arrived = exchange(outgoing, r, r)
            if r == 0 and s == 1:
                state, *outgoing = join(z, s, last, from_blocks=from_blocks)
            else:
                z = own(state, s)
                state, *outgoing = join(z, s, last, state=state, arrived=arrived)
            states.append(state)
    return store(tm - 1, states, out)


def solution(mesh):
    return jax.shard_map(
        local,
        mesh=mesh,
        in_specs=(
            P("tm", "net", None, None, None),
            P("net", None),
            P("tm", "net", None, None, None),
            P("net", None),
            P("net", None),
            P("net", None),
            P("cols"),
            P("tm", "cols"),
        ),
        out_specs=P("tm", "cols", "net"),
        check_vma=False,
    )
```

```python
import functools

import jax
import jax.numpy as jnp
from jax import lax
from jax.experimental import pallas as pl
from jax.experimental.pallas import tpu as pltpu
from jax.sharding import PartitionSpec as P

VMEM = pl.BlockSpec(memory_space=pltpu.VMEM)
SMEM = pl.BlockSpec(memory_space=pltpu.SMEM)
HBM = pl.BlockSpec(memory_space=pltpu.HBM)
ANY = pl.BlockSpec(memory_space=pl.ANY)
LIMIT = pltpu.CompilerParams(vmem_limit_bytes=16 * 1024 * 1024)
DMA = pltpu.SemaphoreType.DMA

STATE, LANE, BLOCK, PART, GAIN = 0, 1, 2, 3, 4


def times_transposed(rows, block):
    return lax.dot_general(rows, block, (((1,), (1,)), ((), ())), preferred_element_type=jnp.float32)


def injected(table, step, first_state, width):
    lane = lax.broadcasted_iota(jnp.int32, (table.shape[0], width), 1)
    hit = table[:, STATE : STATE + 1] == (lane + first_state).astype(jnp.float32)
    return jnp.where(hit, table[:, GAIN + step : GAIN + step + 1], 0.0)


def own_sum(i, state_ref, jac_ref, cols_ref, table, step):
    blocks, _, width = state_ref.shape
    first = (lax.axis_index("net") * blocks + i) * width
    total = injected(table, step, first, width)
    total += times_transposed(state_ref[i], jac_ref[i, 0])
    for k in range(1, jac_ref.shape[1]):
        total += times_transposed(state_ref[cols_ref[k - 1, i]], jac_ref[i, k])
    return total


def add_coupled(incoming, block, live, recv, z_ref):
    lane = lax.broadcasted_iota(jnp.int32, z_ref.shape[1:], 1)
    term = times_transposed(incoming, block)
    z_ref[recv] += jnp.where(lane < live, term, 0.0)


def kept(table, partition, send_ref, n):
    part, block = table[:, PART : PART + 1], table[:, BLOCK : BLOCK + 1]
    keep = part == partition.astype(jnp.float32)
    for q in range(n):
        same = block == send_ref[q, partition].astype(jnp.float32)
        keep = jnp.logical_or(keep, jnp.logical_and(part == float(q), same))
    return keep


def second_kernel(
    jac_hbm, iface_hbm, cols_ref, send_ref, recv_ref, live_ref, node_ref, gain_ref, table_ref, state_ref, *refs
):
    *outgoing, jac_ref, iface_ref, first_ref, z_ref, sems = refs
    n = lax.axis_size("net")
    me = lax.axis_index("net")
    blocks, cols, width = state_ref.shape
    loads = [
        pltpu.make_async_copy(jac_hbm.at[1], jac_ref, sems.at[0]),
        pltpu.make_async_copy(iface_hbm.at[1, 0], iface_ref, sems.at[1]),
    ]
    for load in loads:
        load.start()
    node = node_ref[...]
    block_of = node // width
    rows = [
        node,
        node - block_of * width,
        block_of % blocks,
        block_of // blocks,
    ]
    steps = gain_ref.shape[0]
    fill = -(GAIN + steps) % 8
    rows = [row.astype(jnp.float32) for row in rows] + [gain_ref[...], jnp.zeros((fill, cols), jnp.float32)]
    table_ref[...] = jnp.concatenate(rows, axis=0).T
    table = table_ref[...]
    for i in range(blocks):
        first_ref[i] = injected(table, 0, (me * blocks + i) * width, width).astype(first_ref.dtype)
    lane = lax.broadcasted_iota(jnp.int32, (cols, width), 1).astype(jnp.float32)
    shot = jnp.where(lane == table[:, LANE : LANE + 1], table[:, GAIN : GAIN + 1], 0.0)
    loads[0].wait()
    for i in range(blocks):
        z_ref[i] = own_sum(i, first_ref, jac_ref, cols_ref, table, 1)
    loads[1].wait()
    part, block = table[:, PART : PART + 1], table[:, BLOCK : BLOCK + 1]
    mine = jnp.logical_or(part != me.astype(jnp.float32), block == send_ref[0, me].astype(jnp.float32))
    shot = jnp.where(mine, shot, 0.0)
    for q in range(n):
        sent = jnp.where(part == float(q), shot, 0.0).astype(first_ref.dtype)
        add_coupled(sent, iface_ref[q], live_ref[0, q], recv_ref[0, q], z_ref)
    state_ref[...] = z_ref[...].astype(state_ref.dtype)
    for d in range(1, n):
        outgoing[d - 1][...] = state_ref[send_ref[0, lax.rem(me + d, n)]]


def first_store_kernel(
    steps, jac_ref, iface_ref, cols_ref, recv_ref, live_ref, every_ref, table_ref, *refs
):
    *states, out_ref, zero_ref, z_ref, made_ref, sems = refs
    n = lax.axis_size("net")

    @pl.when(lax.axis_index("tm") == 0)
    def _():
        table = table_ref[...]
        zero_ref[...] = jnp.zeros_like(zero_ref)
        for i in range(z_ref.shape[0]):
            z_ref[i] = own_sum(i, zero_ref, jac_ref.at[0], cols_ref, table, 0)
        for q in range(n):
            add_coupled(zero_ref[0], iface_ref[0, 0, q], live_ref[0, q], recv_ref[0, q], z_ref)
        made_ref[0] = z_ref[...].astype(made_ref.dtype)
        keep = kept(table, lax.axis_index("net"), every_ref, n)
        for i in range(z_ref.shape[0]):
            made_ref[1, i] = jnp.where(keep, states[0][i], jnp.zeros_like(states[0][i]))
        write([made_ref.at[0], made_ref.at[1], *states[1:]], out_ref, sems)


def write(states, out_ref, sems):
    copies = write_start(states, 0, out_ref, sems)
    for copy in copies:
        copy.wait()


def write_start(states, first, out_ref, sems):
    copies = []
    for s, state_ref in enumerate(states, first):
        width = state_ref.shape[2]
        for i in range(state_ref.shape[0]):
            copies.append(
                pltpu.make_async_copy(state_ref.at[i], out_ref.at[s, :, pl.ds(i * width, width)], sems.at[s, i])
            )
    for copy in copies:
        copy.start()
    return copies


def own_kernel(step, fix, state_ref, jac_ref, cols_ref, table_ref, every_ref, z_ref, *fixed):
    table = table_ref[...]
    if fix:
        keep = kept(table, lax.axis_index("net"), every_ref, lax.axis_size("net"))
        for i in range(state_ref.shape[0]):
            fixed[0][i] = jnp.where(keep, state_ref[i], jnp.zeros_like(state_ref[i]))
        state_ref = fixed[0]
    for i in range(state_ref.shape[0]):
        z_ref[i] = own_sum(i, state_ref, jac_ref.at[step], cols_ref, table, step)


def join_kernel(step, fix, stacked, send_out, section, store, *refs):
    n = lax.axis_size("net")
    me = lax.axis_index("net")
    z_ref, iface_ref, send_ref, recv_ref, live_ref, every_ref, table_ref, state_in_ref, *refs = refs
    if stacked:
        arrived, *refs = refs
    else:
        arrived, refs = refs[: n - 1], refs[n - 1 :]
    acc_ref = refs.pop()
    if store:
        before, refs = refs[:store], refs[store:]
        _, out_ref, sems = refs.pop(0), refs.pop(0), refs.pop()
        here = lax.axis_index("tm") == section

        @pl.when(here)
        def _():
            write_start(before, 0, out_ref, sems)

    state_ref, *outgoing = refs
    acc_ref[...] = z_ref[...]
    add_coupled(state_in_ref[send_ref[0, me]], iface_ref[step, 0, me], live_ref[0, me], recv_ref[0, me], acc_ref)
    for d in range(1, n):
        q = lax.rem(me - d + n, n)
        block = arrived[q] if stacked else arrived[d - 1][...]
        if fix:
            block = jnp.where(kept(table_ref[...], q, every_ref, n), block, jnp.zeros_like(block))
        add_coupled(block, iface_ref[step, 0, q], live_ref[0, q], recv_ref[0, q], acc_ref)
    state_ref[...] = acc_ref[...].astype(state_ref.dtype)
    if send_out == "stack":
        for q in range(n):
            outgoing[0][q] = state_ref[send_ref[0, q]]
    if send_out == "each":
        for d in range(1, n):
            outgoing[d - 1][...] = state_ref[send_ref[0, lax.rem(me + d, n)]]
    if store:

        @pl.when(here)
        def _():
            last = write_start([state_ref], store, out_ref, sems)
            for s, ref in enumerate(before):
                for i in range(ref.shape[0]):
                    width = ref.shape[2]
                    pltpu.make_async_copy(
                        ref.at[i], out_ref.at[s, :, pl.ds(i * width, width)], sems.at[s, i]
                    ).wait()
            for copy in last:
                copy.wait()


def local(jac, block_cols, iface_jac, iface_send, iface_recv, iface_live, ctrl_node, ctrl_gain):
    steps, blocks, kinds, width, _ = jac.shape
    cols = ctrl_node.shape[0]
    tm = lax.axis_size("tm")
    n = lax.axis_size("net")
    node = ctrl_node[None]
    near = block_cols.T
    bf16 = functools.partial(jax.ShapeDtypeStruct, dtype=jnp.bfloat16)
    f32 = functools.partial(jax.ShapeDtypeStruct, dtype=jnp.float32)
    whole, one, stack = bf16((blocks, cols, width)), bf16((cols, width)), bf16((n, cols, width))
    table_rows = GAIN + steps + -(GAIN + steps) % 8
    written = bf16((steps, cols, blocks * width))

    every = lax.all_gather(iface_send, "net", axis=0, tiled=True)

    table, state, *outgoing = pl.pallas_call(
        second_kernel,
        out_shape=[f32((cols, table_rows)), whole] + [one] * (n - 1),
        in_specs=[HBM, HBM, SMEM, SMEM, SMEM, SMEM, VMEM, VMEM],
        out_specs=[VMEM] * (n + 1),
        scratch_shapes=[
            pltpu.VMEM((blocks, kinds, width, width), jnp.bfloat16),
            pltpu.VMEM((n, width, width), jnp.bfloat16),
            pltpu.VMEM(whole.shape, jnp.bfloat16),
            pltpu.VMEM(whole.shape, jnp.float32),
            DMA((2,)),
        ],
        compiler_params=LIMIT,
    )(jac, iface_jac, near, iface_send, iface_recv, iface_live, node, ctrl_gain)

    def own(state, step, fix):
        result = pl.pallas_call(
            functools.partial(own_kernel, step, fix),
            out_shape=[f32(whole.shape)] + ([whole] if fix else []),
            in_specs=[VMEM, VMEM, SMEM, VMEM, SMEM],
            out_specs=[VMEM] * (2 if fix else 1),
            compiler_params=LIMIT,
        )(state, jac, near, table_here, every)
        return result if fix else (result[0], state)

    def join(z, step, fix, state, arrived, send_out, section, before=(), out=None):
        stacked = not isinstance(arrived, list)
        arrays = [z, iface_jac, iface_send, iface_recv, iface_live, every, table_here, state]
        specs = [VMEM, VMEM, SMEM, SMEM, SMEM, SMEM, VMEM, VMEM]
        arrays += [arrived] if stacked else arrived
        specs += [VMEM] * (1 if stacked else n - 1)
        shapes = []
        scratch = [pltpu.VMEM(whole.shape, jnp.float32)]
        aliases = {}
        out_specs = []
        if out is not None:
            arrays += [*before, out]
            specs += [VMEM] * len(before) + [ANY]
            aliases = {len(arrays) - 1: 0}
            shapes.append(written)
            out_specs.append(ANY)
            scratch.insert(0, DMA((steps, blocks)))
        if send_out == "none":
            scratch.insert(0, pltpu.VMEM(whole.shape, jnp.bfloat16))
        else:
            shapes.append(whole)
        shapes += {"stack": [stack], "each": [one] * (n - 1), "none": []}[send_out]
        out_specs += [VMEM] * (len(shapes) - len(out_specs))
        return pl.pallas_call(
            functools.partial(join_kernel, step, fix, stacked, send_out, section, len(before)),
            out_shape=shapes,
            in_specs=specs,
            out_specs=out_specs,
            input_output_aliases=aliases,
            scratch_shapes=scratch,
            compiler_params=LIMIT,
        )(*arrays)

    def hand_over(blocks_to_send, section):
        return [
            lax.ppermute(
                block,
                ("tm", "net"),
                [((section - 1) * n + q, section * n + (q + d) % n) for q in range(n)],
            )
            for d, block in enumerate(blocks_to_send)
        ]

    fix = True
    table_here = table
    states = [state]
    out = None
    for r in range(tm):
        if r > 0:
            state, *arrived = hand_over([state, *outgoing], r)
            if out is None:
                out = pl.pallas_call(
                    functools.partial(first_store_kernel, steps),
                    out_shape=written,
                    in_specs=[VMEM, VMEM, SMEM, SMEM, SMEM, SMEM, VMEM] + [VMEM] * len(states),
                    out_specs=ANY,
                    scratch_shapes=[
                        pltpu.VMEM(whole.shape, jnp.bfloat16),
                        pltpu.VMEM(whole.shape, jnp.float32),
                        pltpu.VMEM((2, *whole.shape), jnp.bfloat16),
                        DMA((steps, blocks)),
                    ],
                    compiler_params=LIMIT,
                )(jac, iface_jac, near, iface_recv, iface_live, every, table, *states)
            states = []
        for s in range(2 if r == 0 else 0, steps):
            if s > 0:
                arrived = lax.all_to_all(outgoing, "net", split_axis=0, concat_axis=0, tiled=True)
            z, state = own(state, s, fix)
            end = s == steps - 1
            send_out = "stack" if not end else "each" if r < tm - 1 else "none"
            if end and r > 0:
                out, *rest = join(z, s, fix, state, arrived, send_out, r, states, out)
                state, *outgoing = rest or [None]
            else:
                state, *outgoing = join(z, s, fix, state, arrived, send_out, r)
            if send_out == "stack":
                outgoing = outgoing[0]
            fix = False
            states.append(state)
    return out


def solution(mesh):
    return jax.shard_map(
        local,
        mesh=mesh,
        in_specs=(
            P("tm", "net", None, None, None),
            P("net", None),
            P("tm", "net", None, None, None),
            P("net", None),
            P("net", None),
            P("net", None),
            P("cols"),
            P("tm", "cols"),
        ),
        out_specs=P("tm", "cols", "net"),
        check_vma=False,
    )
```

```python
import functools

import jax
import jax.numpy as jnp
from jax import lax
from jax.experimental import pallas as pl
from jax.experimental.pallas import tpu as pltpu
from jax.sharding import PartitionSpec as P

VMEM = pl.BlockSpec(memory_space=pltpu.VMEM)
SMEM = pl.BlockSpec(memory_space=pltpu.SMEM)
HBM = pl.BlockSpec(memory_space=pltpu.HBM)
ANY = pl.BlockSpec(memory_space=pl.ANY)
LIMIT = pltpu.CompilerParams(vmem_limit_bytes=16 * 1024 * 1024)
LARGE = pltpu.CompilerParams(vmem_limit_bytes=60 * 1024 * 1024)
DMA = pltpu.SemaphoreType.DMA

STATE, LANE, BLOCK, PART, GAIN = 0, 1, 2, 3, 4
ROWS = 16


def times_transposed(rows, block):
    return lax.dot_general(rows, block, (((1,), (1,)), ((), ())), preferred_element_type=jnp.float32)


def injected(table, step, first_state, width):
    lane = lax.broadcasted_iota(jnp.int32, (table.shape[0], width), 1)
    hit = table[:, STATE : STATE + 1] == (lane + first_state).astype(jnp.float32)
    return jnp.where(hit, table[:, GAIN + step : GAIN + step + 1], 0.0)


def own_sum(i, state_ref, jac_ref, cols_ref, table, step):
    blocks, _, width = state_ref.shape
    first = (lax.axis_index("net") * blocks + i) * width
    total = injected(table, step, first, width)
    total += times_transposed(state_ref[i], jac_ref[i, 0])
    for k in range(1, jac_ref.shape[1]):
        total += times_transposed(state_ref[cols_ref[k - 1, i]], jac_ref[i, k])
    return total


def add_coupled(incoming, block, live, recv, z_ref):
    lane = lax.broadcasted_iota(jnp.int32, z_ref.shape[1:], 1)
    term = times_transposed(incoming, block)
    z_ref[recv] += jnp.where(lane < live, term, 0.0)


def table_row(send_ref, partition, width):
    n = lax.axis_size("net")
    lane = lax.broadcasted_iota(jnp.int32, (1, width), 1)
    row = jnp.zeros((1, width), jnp.float32)
    for e in range(n):
        row = jnp.where(lane == e, send_ref[0, lax.rem(partition - e + n, n)].astype(jnp.float32), row)
    return row


def kept(table, rows):
    n = lax.axis_size("net")
    me = lax.axis_index("net")
    part, block = table[:, PART : PART + 1], table[:, BLOCK : BLOCK + 1]
    back = me.astype(jnp.float32) - part
    back = jnp.where(back < 0.0, back + float(n), back)
    sent = jnp.broadcast_to(rows[0], (table.shape[0], rows[0].shape[1]))
    for d in range(1, n):
        sent = jnp.where(back == float(d), rows[d], sent)
    lane = lax.broadcasted_iota(jnp.int32, sent.shape, 1).astype(jnp.float32)
    return jnp.where(jnp.logical_or(back == lane, block == sent), 1.0, 0.0)


def second_kernel(
    jac_hbm, iface_hbm, cols_ref, send_ref, recv_ref, live_ref, node_ref, gain_ref, table_ref, state_ref, *refs
):
    *outgoing, jac_ref, iface_ref, first_ref, z_ref, sems = refs
    n = lax.axis_size("net")
    me = lax.axis_index("net")
    blocks, cols, width = state_ref.shape
    loads = [
        pltpu.make_async_copy(jac_hbm.at[1], jac_ref, sems.at[0]),
        pltpu.make_async_copy(iface_hbm.at[1, 0], iface_ref, sems.at[1]),
    ]
    for load in loads:
        load.start()
    node = node_ref[...]
    block_of = node // width
    rows = [
        node,
        node - block_of * width,
        block_of % blocks,
        block_of // blocks,
    ]
    steps = gain_ref.shape[0]
    fill = -(GAIN + steps) % 8
    rows = [row.astype(jnp.float32) for row in rows] + [gain_ref[...], jnp.zeros((fill, cols), jnp.float32)]
    table_ref[...] = jnp.concatenate(rows, axis=0).T
    table = table_ref[...]
    for i in range(blocks):
        first_ref[i] = injected(table, 0, (me * blocks + i) * width, width).astype(first_ref.dtype)
    lane = lax.broadcasted_iota(jnp.int32, (cols, width), 1).astype(jnp.float32)
    shot = jnp.where(lane == table[:, LANE : LANE + 1], table[:, GAIN : GAIN + 1], 0.0)
    loads[0].wait()
    for i in range(blocks):
        z_ref[i] = own_sum(i, first_ref, jac_ref, cols_ref, table, 1)
    loads[1].wait()
    part, block = table[:, PART : PART + 1], table[:, BLOCK : BLOCK + 1]
    mine = jnp.logical_or(part != me.astype(jnp.float32), block == send_ref[0, me].astype(jnp.float32))
    shot = jnp.where(mine, shot, 0.0)
    for q in range(n):
        sent = jnp.where(part == float(q), shot, 0.0).astype(first_ref.dtype)
        add_coupled(sent, iface_ref[q], live_ref[0, q], recv_ref[0, q], z_ref)
    state_ref[...] = z_ref[...].astype(state_ref.dtype)
    for d in range(1, n):
        target = lax.rem(me + d, n)
        outgoing[d - 1][pl.ds(0, cols)] = state_ref[send_ref[0, target]]
        row = table_row(send_ref, target, width).astype(state_ref.dtype)
        outgoing[d - 1][pl.ds(cols, ROWS)] = jnp.broadcast_to(row, (ROWS, width))


def write_start(states, first, out_ref, sems):
    copies = []
    for s, state_ref in enumerate(states, first):
        width = state_ref.shape[2]
        for i in range(state_ref.shape[0]):
            copies.append(
                pltpu.make_async_copy(state_ref.at[i], out_ref.at[s, :, pl.ds(i * width, width)], sems.at[s, i])
            )
    for copy in copies:
        copy.start()
    return copies


def own_kernel(step, state_ref, jac_ref, cols_ref, table_ref, z_ref):
    table = table_ref[...]
    for i in range(state_ref.shape[0]):
        z_ref[i] = own_sum(i, state_ref, jac_ref.at[step], cols_ref, table, step)


def first_states(states, jac_ref, iface_ref, cols_ref, send_ref, recv_ref, live_ref, table_ref, arrived, made_ref, z_ref):
    n = lax.axis_size("net")
    blocks, cols, width = z_ref.shape
    table = table_ref[...]
    made_ref[0] = jnp.zeros_like(made_ref[0])
    for i in range(blocks):
        z_ref[i] = own_sum(i, made_ref.at[0], jac_ref.at[0], cols_ref, table, 0)
    for q in range(n):
        add_coupled(made_ref[0, 0], iface_ref[0, 0, q], live_ref[0, q], recv_ref[0, q], z_ref)
    made_ref[0] = z_ref[...].astype(made_ref.dtype)
    me = lax.axis_index("net")
    rows = [table_row(send_ref, me, width)]
    for d in range(1, n):
        rows.append(arrived[lax.rem(me - d + n, n)][0:1].astype(jnp.float32))
    keep = kept(table, rows)[:, 0:1]
    for i in range(blocks):
        made_ref[1, i] = jnp.where(keep > 0.0, states[0][i], jnp.zeros_like(states[0][i]))
    return [made_ref.at[0], made_ref.at[1], *states[1:]]


def join_kernel(step, fix, stacked, send_out, section, firsts, store, *refs):
    n = lax.axis_size("net")
    me = lax.axis_index("net")
    tm = lax.axis_index("tm")
    z_ref, iface_ref, send_ref, recv_ref, live_ref, table_ref, state_in_ref, *refs = refs
    if stacked:
        arrived, *refs = refs
    else:
        arrived, refs = refs[: n - 1], refs[n - 1 :]
    acc_ref = refs.pop()
    blocks, cols, width = z_ref.shape
    before = []
    if store:
        sems = refs.pop()
        if firsts:
            made_ref = refs.pop()
            opening, refs = refs[:firsts], refs[firsts:]
            jac_ref, cols_ref = refs.pop(0), refs.pop(0)
        before, refs = refs[: store - 1], refs[store - 1 :]
        if not firsts:
            refs.pop(0)
        out_ref = refs.pop(0)
    state_ref, *outgoing = refs

    def join():
        if store:
            copies = write_start(before, 0, out_ref, sems)
        if fix:
            table = table_ref[...]
            rows = [table_row(send_ref, me, width)]
            rows += [arrived[d - 1][cols : cols + 1].astype(jnp.float32) for d in range(1, n)]
            keep = kept(table, rows)
            for i in range(blocks):
                acc_ref[i] = jnp.where(keep[:, 0:1] > 0.0, z_ref[i], 0.0)
        else:
            acc_ref[...] = z_ref[...]
        for d in range(n):
            q = lax.rem(me - d + n, n)
            if d == 0:
                block = state_in_ref[send_ref[0, me]]
            elif stacked:
                block = arrived[q]
            else:
                block = arrived[d - 1][pl.ds(0, cols)]
            if fix:
                block = jnp.where(keep[:, d : d + 1] > 0.0, block, jnp.zeros_like(block))
            add_coupled(block, iface_ref[step, 0, q], live_ref[0, q], recv_ref[0, q], acc_ref)
        state_ref[...] = acc_ref[...].astype(state_ref.dtype)
        if send_out == "stack":
            for q in range(n):
                outgoing[0][q] = state_ref[send_ref[0, q]]
        if send_out == "each":
            for d in range(1, n):
                outgoing[d - 1][...] = state_ref[send_ref[0, lax.rem(me + d, n)]]
        if store:
            copies += write_start([state_ref], store - 1, out_ref, sems)
            for copy in copies:
                copy.wait()

    if store:
        pl.when(tm == section)(join)
    else:
        join()
    if fix and send_out == "stack":

        @pl.when(tm == 0)
        def _():
            for q in range(n):
                row = table_row(send_ref, jnp.int32(q), width).astype(state_ref.dtype)
                outgoing[0][q, pl.ds(0, ROWS)] = jnp.broadcast_to(row, (ROWS, width))

    if firsts:

        @pl.when(tm == 0)
        def _():
            made = first_states(
                opening, jac_ref, iface_ref, cols_ref, send_ref, recv_ref, live_ref, table_ref, arrived, made_ref, acc_ref
            )
            for copy in write_start(made, 0, out_ref, sems):
                copy.wait()


def local(jac, block_cols, iface_jac, iface_send, iface_recv, iface_live, ctrl_node, ctrl_gain):
    steps, blocks, kinds, width, _ = jac.shape
    cols = ctrl_node.shape[0]
    tm = lax.axis_size("tm")
    n = lax.axis_size("net")
    node = ctrl_node[None]
    near = block_cols.T
    bf16 = functools.partial(jax.ShapeDtypeStruct, dtype=jnp.bfloat16)
    f32 = functools.partial(jax.ShapeDtypeStruct, dtype=jnp.float32)
    whole, one, stack = bf16((blocks, cols, width)), bf16((cols, width)), bf16((n, cols, width))
    table_rows = GAIN + steps + -(GAIN + steps) % 8
    written = bf16((steps, cols, blocks * width))

    table, state, *outgoing = pl.pallas_call(
        second_kernel,
        out_shape=[f32((cols, table_rows)), whole] + [bf16((cols + ROWS, width))] * (n - 1),
        in_specs=[ANY, ANY, SMEM, SMEM, SMEM, SMEM, VMEM, VMEM],
        out_specs=[VMEM] * (n + 1),
        scratch_shapes=[
            pltpu.VMEM((blocks, kinds, width, width), jnp.bfloat16),
            pltpu.VMEM((n, width, width), jnp.bfloat16),
            pltpu.VMEM(whole.shape, jnp.bfloat16),
            pltpu.VMEM(whole.shape, jnp.float32),
            DMA((2,)),
        ],
        compiler_params=LARGE,
    )(jac, iface_jac, near, iface_send, iface_recv, iface_live, node, ctrl_gain)

    def own(state, step):
        return pl.pallas_call(
            functools.partial(own_kernel, step),
            out_shape=f32(whole.shape),
            in_specs=[VMEM, VMEM, SMEM, VMEM],
            out_specs=VMEM,
            compiler_params=LIMIT,
        )(state, jac, near, table)

    def join(z, step, fix, state, arrived, send_out, section, opening=(), before=(), out=None, store=0):
        stacked = not isinstance(arrived, list)
        arrays = [z, iface_jac, iface_send, iface_recv, iface_live, table, state]
        specs = [VMEM, VMEM, SMEM, SMEM, SMEM, VMEM, VMEM]
        arrays += [arrived] if stacked else arrived
        specs += [VMEM] * (1 if stacked else n - 1)
        shapes = []
        scratch = [pltpu.VMEM(whole.shape, jnp.float32)]
        aliases = {}
        out_specs = []
        if store:
            if out is None:
                arrays += [*opening, jac, near]
                specs += [VMEM] * len(opening) + [VMEM, SMEM]
            arrays += before
            specs += [VMEM] * len(before)
            if out is not None:
                aliases = {len(arrays): 0}
                arrays.append(out)
                specs.append(ANY)
            shapes.append(written)
            out_specs.append(ANY)
            scratch.insert(0, DMA((steps, blocks)))
            if out is None:
                scratch.insert(0, pltpu.VMEM((2, *whole.shape), jnp.bfloat16))
        if send_out == "none":
            scratch.insert(0, pltpu.VMEM(whole.shape, jnp.bfloat16))
        else:
            shapes.append(whole)
        shapes += {"stack": [stack], "each": [one] * (n - 1), "none": []}[send_out]
        out_specs += [VMEM] * (len(shapes) - len(out_specs))
        firsts = len(opening) if store and out is None else 0
        return pl.pallas_call(
            functools.partial(join_kernel, step, fix, stacked, send_out, section, firsts, store),
            out_shape=shapes,
            in_specs=specs,
            out_specs=out_specs,
            input_output_aliases=aliases,
            scratch_shapes=scratch,
            compiler_params=LIMIT,
        )(*arrays)

    def hand_over(blocks_to_send, section):
        return [
            lax.ppermute(
                block,
                ("tm", "net"),
                [((section - 1) * n + q, section * n + (q + d) % n) for q in range(n)],
            )
            for d, block in enumerate(blocks_to_send)
        ]

    opening = [state]
    out = None
    for r in range(1, tm):
        state, *arrived = hand_over([state, *outgoing], r)
        before = []
        for s in range(steps):
            fix = r == 1 and s == 0
            if s > 0:
                arrived = lax.all_to_all(outgoing, "net", split_axis=0, concat_axis=0, tiled=True)
            z = own(state, s)
            if s < steps - 1:
                state, outgoing = join(z, s, fix, state, arrived, "stack", r)
                before.append(state)
            elif r < tm - 1:
                out, state, *outgoing = join(z, s, fix, state, arrived, "each", r, opening, before, out, steps)
            else:
                (out,) = join(z, s, fix, state, arrived, "none", r, opening, before, out, steps)
    return out


def solution(mesh):
    return jax.shard_map(
        local,
        mesh=mesh,
        in_specs=(
            P("tm", "net", None, None, None),
            P("net", None),
            P("tm", "net", None, None, None),
            P("net", None),
            P("net", None),
            P("net", None),
            P("cols"),
            P("tm", "cols"),
        ),
        out_specs=P("tm", "cols", "net"),
        check_vma=False,
    )
```

```python
import functools

import jax
import jax.numpy as jnp
from jax import lax
from jax.experimental import pallas as pl
from jax.experimental.pallas import tpu as pltpu
from jax.sharding import PartitionSpec as P

VMEM = pl.BlockSpec(memory_space=pltpu.VMEM)
SMEM = pl.BlockSpec(memory_space=pltpu.SMEM)
HBM = pl.BlockSpec(memory_space=pltpu.HBM)
ANY = pl.BlockSpec(memory_space=pl.ANY)
LIMIT = pltpu.CompilerParams(vmem_limit_bytes=16 * 1024 * 1024)
DMA = pltpu.SemaphoreType.DMA

STATE, LANE, BLOCK, PART, GAIN = 0, 1, 2, 3, 4
ROWS = 16


def times_transposed(rows, block):
    return lax.dot_general(rows, block, (((1,), (1,)), ((), ())), preferred_element_type=jnp.float32)


def injected(table, step, first_state, width):
    lane = lax.broadcasted_iota(jnp.int32, (table.shape[0], width), 1)
    hit = table[:, STATE : STATE + 1] == (lane + first_state).astype(jnp.float32)
    return jnp.where(hit, table[:, GAIN + step : GAIN + step + 1], 0.0)


def own_sum(i, state_ref, jac_ref, cols_ref, table, step):
    blocks, _, width = state_ref.shape
    first = (lax.axis_index("net") * blocks + i) * width
    kinds = jac_ref.shape[1]
    rows = [state_ref[i]] + [state_ref[cols_ref[k - 1, i]] for k in range(1, kinds)]
    row_blocks = [jac_ref[i, k] for k in range(kinds)]
    total = times_transposed(jnp.concatenate(rows, axis=1), jnp.concatenate(row_blocks, axis=1))
    return total + injected(table, step, first, width)


def add_coupled(incoming, block, live, recv, z_ref, keep=None):
    mask = lax.broadcasted_iota(jnp.int32, z_ref.shape[1:], 1) < live
    if keep is not None:
        mask = jnp.logical_and(mask, keep > 0.0)
    z_ref[recv] += jnp.where(mask, times_transposed(incoming, block), 0.0)


def table_row(send_ref, partition, width):
    n = lax.axis_size("net")
    lane = lax.broadcasted_iota(jnp.int32, (1, width), 1)
    row = jnp.zeros((1, width), jnp.float32)
    for e in range(n):
        row = jnp.where(lane == e, send_ref[0, lax.rem(partition - e + n, n)].astype(jnp.float32), row)
    return row


def kept(table, rows):
    n = lax.axis_size("net")
    me = lax.axis_index("net")
    part, block = table[:, PART : PART + 1], table[:, BLOCK : BLOCK + 1]
    back = me.astype(jnp.float32) - part
    back = jnp.where(back < 0.0, back + float(n), back)
    sent = jnp.broadcast_to(rows[0], (table.shape[0], rows[0].shape[1]))
    for d in range(1, n):
        sent = jnp.where(back == float(d), rows[d], sent)
    lane = lax.broadcasted_iota(jnp.int32, sent.shape, 1).astype(jnp.float32)
    return jnp.where(jnp.logical_or(back == lane, block == sent), 1.0, 0.0)


def second_kernel(*refs):
    jac_hbm, iface_hbm, *small, table_ref, state_ref = refs[:10]
    n = lax.axis_size("net")
    me = lax.axis_index("net")
    outgoing, refs = refs[10 : 9 + n], refs[9 + n :]
    jac_ref, iface_ref, *loaded, first_ref, z_ref, sems = refs
    cols_ref, send_ref, recv_ref, live_ref, node_ref, gain_ref = loaded
    blocks, cols, width = state_ref.shape
    loads = [
        pltpu.make_async_copy(source, target, sems.at[i])
        for i, (source, target) in enumerate(
            zip([jac_hbm.at[1], iface_hbm.at[1, 0], *small], [jac_ref, iface_ref, *loaded])
        )
    ]
    for load in loads:
        load.start()
    for load in loads[2:]:
        load.wait()
    node = node_ref[...]
    block_of = node // width
    rows = [
        node,
        node - block_of * width,
        block_of % blocks,
        block_of // blocks,
    ]
    steps = gain_ref.shape[0]
    fill = -(GAIN + steps) % 8
    rows = [row.astype(jnp.float32) for row in rows] + [gain_ref[...], jnp.zeros((fill, cols), jnp.float32)]
    table_ref[...] = jnp.concatenate(rows, axis=0).T
    table = table_ref[...]
    for i in range(blocks):
        first_ref[i] = injected(table, 0, (me * blocks + i) * width, width).astype(first_ref.dtype)
    lane = lax.broadcasted_iota(jnp.int32, (cols, width), 1).astype(jnp.float32)
    shot = jnp.where(lane == table[:, LANE : LANE + 1], table[:, GAIN : GAIN + 1], 0.0)
    loads[0].wait()
    for i in range(blocks):
        z_ref[i] = own_sum(i, first_ref, jac_ref, cols_ref, table, 1)
    loads[1].wait()
    part, block = table[:, PART : PART + 1], table[:, BLOCK : BLOCK + 1]
    mine = jnp.logical_or(part != me.astype(jnp.float32), block == send_ref[0, me].astype(jnp.float32))
    shot = jnp.where(mine, shot, 0.0)
    for q in range(n):
        sent = jnp.where(part == float(q), shot, 0.0).astype(first_ref.dtype)
        add_coupled(sent, iface_ref[q], live_ref[0, q], recv_ref[0, q], z_ref)
    state_ref[...] = z_ref[...].astype(state_ref.dtype)
    for d in range(1, n):
        target = lax.rem(me + d, n)
        outgoing[d - 1][pl.ds(0, cols)] = state_ref[send_ref[0, target]]
        row = table_row(send_ref, target, width).astype(state_ref.dtype)
        outgoing[d - 1][pl.ds(cols, ROWS)] = jnp.broadcast_to(row, (ROWS, width))


def write_start(states, first, out_ref, sems):
    copies = []
    for s, state_ref in enumerate(states, first):
        width = state_ref.shape[2]
        for i in range(state_ref.shape[0]):
            copies.append(
                pltpu.make_async_copy(state_ref.at[i], out_ref.at[s, :, pl.ds(i * width, width)], sems.at[s, i])
            )
    for copy in copies:
        copy.start()
    return copies


def own_kernel(step, state_ref, jac_ref, cols_ref, table_ref, z_ref):
    table = table_ref[...]
    for i in range(state_ref.shape[0]):
        z_ref[i] = own_sum(i, state_ref, jac_ref.at[step], cols_ref, table, step)


def first_states(states, jac_ref, iface_ref, cols_ref, send_ref, recv_ref, live_ref, table_ref, arrived, made_ref, z_ref):
    n = lax.axis_size("net")
    blocks, cols, width = z_ref.shape
    table = table_ref[...]
    made_ref[0] = jnp.zeros_like(made_ref[0])
    for i in range(blocks):
        z_ref[i] = own_sum(i, made_ref.at[0], jac_ref.at[0], cols_ref, table, 0)
    for q in range(n):
        add_coupled(made_ref[0, 0], iface_ref[0, 0, q], live_ref[0, q], recv_ref[0, q], z_ref)
    made_ref[0] = z_ref[...].astype(made_ref.dtype)
    me = lax.axis_index("net")
    rows = [table_row(send_ref, me, width)]
    for d in range(1, n):
        rows.append(arrived[lax.rem(me - d + n, n)][0:1].astype(jnp.float32))
    keep = kept(table, rows)[:, 0:1]
    for i in range(blocks):
        made_ref[1, i] = jnp.where(keep > 0.0, states[0][i], jnp.zeros_like(states[0][i]))
    return [made_ref.at[0], made_ref.at[1], *states[1:]]


def join_kernel(step, fix, stacked, send_out, section, firsts, store, *refs):
    n = lax.axis_size("net")
    me = lax.axis_index("net")
    tm = lax.axis_index("tm")
    z_ref, iface_ref, send_ref, recv_ref, live_ref, table_ref, state_in_ref, *refs = refs
    if stacked:
        arrived, *refs = refs
    else:
        arrived, refs = refs[: n - 1], refs[n - 1 :]
    acc_ref = refs.pop()
    blocks, cols, width = z_ref.shape
    before = []
    if store:
        sems = refs.pop()
        if firsts:
            made_ref = refs.pop()
            opening, refs = refs[:firsts], refs[firsts:]
            jac_ref, cols_ref = refs.pop(0), refs.pop(0)
        before, refs = refs[: store - 1], refs[store - 1 :]
        if not firsts:
            refs.pop(0)
        out_ref = refs.pop(0)
    state_ref, *outgoing = refs

    def join():
        if store:
            copies = write_start(before, 0, out_ref, sems)
        if fix:
            table = table_ref[...]
            rows = [table_row(send_ref, me, width)]
            rows += [arrived[d - 1][cols : cols + 1].astype(jnp.float32) for d in range(1, n)]
            keep = kept(table, rows)
            for i in range(blocks):
                acc_ref[i] = jnp.where(keep[:, 0:1] > 0.0, z_ref[i], 0.0)
        else:
            acc_ref[...] = z_ref[...]
        for d in range(n):
            q = lax.rem(me - d + n, n)
            if d == 0:
                block = state_in_ref[send_ref[0, me]]
            elif stacked:
                block = arrived[q]
            else:
                block = arrived[d - 1][pl.ds(0, cols)]
            stands = keep[:, d : d + 1] if fix else None
            add_coupled(block, iface_ref[step, 0, q], live_ref[0, q], recv_ref[0, q], acc_ref, stands)
        state_ref[...] = acc_ref[...].astype(state_ref.dtype)
        if send_out == "stack":
            for q in range(n):
                outgoing[0][q] = state_ref[send_ref[0, q]]
        if send_out == "each":
            for d in range(1, n):
                outgoing[d - 1][...] = state_ref[send_ref[0, lax.rem(me + d, n)]]
        if store:
            copies += write_start([state_ref], store - 1, out_ref, sems)
            for copy in copies:
                copy.wait()

    if store:
        pl.when(tm == section)(join)
    else:
        join()
    if fix and send_out == "stack":

        @pl.when(tm == 0)
        def _():
            for q in range(n):
                row = table_row(send_ref, jnp.int32(q), width).astype(state_ref.dtype)
                outgoing[0][q, pl.ds(0, ROWS)] = jnp.broadcast_to(row, (ROWS, width))

    if firsts:

        @pl.when(tm == 0)
        def _():
            made = first_states(
                opening, jac_ref, iface_ref, cols_ref, send_ref, recv_ref, live_ref, table_ref, arrived, made_ref, acc_ref
            )
            for copy in write_start(made, 0, out_ref, sems):
                copy.wait()


def local(jac, block_cols, iface_jac, iface_send, iface_recv, iface_live, ctrl_node, ctrl_gain):
    steps, blocks, kinds, width, _ = jac.shape
    cols = ctrl_node.shape[0]
    tm = lax.axis_size("tm")
    n = lax.axis_size("net")
    node = ctrl_node[None]
    near = block_cols.T
    bf16 = functools.partial(jax.ShapeDtypeStruct, dtype=jnp.bfloat16)
    f32 = functools.partial(jax.ShapeDtypeStruct, dtype=jnp.float32)
    whole, one, stack = bf16((blocks, cols, width)), bf16((cols, width)), bf16((n, cols, width))
    table_rows = GAIN + steps + -(GAIN + steps) % 8
    written = bf16((steps, cols, blocks * width))

    pinned = [
        pltpu.with_memory_space_constraint(x, pltpu.HBM)
        for x in (jac, iface_jac, near, iface_send, iface_recv, iface_live, node, ctrl_gain)
    ]
    table, state, *outgoing = pl.pallas_call(
        second_kernel,
        out_shape=[f32((cols, table_rows)), whole] + [bf16((cols + ROWS, width))] * (n - 1),
        in_specs=[HBM] * len(pinned),
        out_specs=[VMEM] * (n + 1),
        scratch_shapes=[
            pltpu.VMEM((blocks, kinds, width, width), jnp.bfloat16),
            pltpu.VMEM((n, width, width), jnp.bfloat16),
            *[pltpu.SMEM(x.shape, x.dtype) for x in (near, iface_send, iface_recv, iface_live)],
            *[pltpu.VMEM(x.shape, x.dtype) for x in (node, ctrl_gain)],
            pltpu.VMEM(whole.shape, jnp.bfloat16),
            pltpu.VMEM(whole.shape, jnp.float32),
            DMA((len(pinned),)),
        ],
        compiler_params=LIMIT,
    )(*pinned)

    def own(state, step):
        return pl.pallas_call(
            functools.partial(own_kernel, step),
            out_shape=f32(whole.shape),
            in_specs=[VMEM, VMEM, SMEM, VMEM],
            out_specs=VMEM,
            compiler_params=LIMIT,
        )(state, jac, near, table)

    def join(z, step, fix, state, arrived, send_out, section, opening=(), before=(), out=None, store=0):
        stacked = not isinstance(arrived, list)
        arrays = [z, iface_jac, iface_send, iface_recv, iface_live, table, state]
        specs = [VMEM, VMEM, SMEM, SMEM, SMEM, VMEM, VMEM]
        arrays += [arrived] if stacked else arrived
        specs += [VMEM] * (1 if stacked else n - 1)
        shapes = []
        scratch = [pltpu.VMEM(whole.shape, jnp.float32)]
        aliases = {}
        out_specs = []
        if store:
            if out is None:
                arrays += [*opening, jac, near]
                specs += [VMEM] * len(opening) + [VMEM, SMEM]
            arrays += before
            specs += [VMEM] * len(before)
            if out is not None:
                aliases = {len(arrays): 0}
                arrays.append(out)
                specs.append(ANY)
            shapes.append(written)
            out_specs.append(ANY)
            scratch.insert(0, DMA((steps, blocks)))
            if out is None:
                scratch.insert(0, pltpu.VMEM((2, *whole.shape), jnp.bfloat16))
        if send_out == "none":
            scratch.insert(0, pltpu.VMEM(whole.shape, jnp.bfloat16))
        else:
            shapes.append(whole)
        shapes += {"stack": [stack], "each": [one] * (n - 1), "none": []}[send_out]
        out_specs += [VMEM] * (len(shapes) - len(out_specs))
        firsts = len(opening) if store and out is None else 0
        return pl.pallas_call(
            functools.partial(join_kernel, step, fix, stacked, send_out, section, firsts, store),
            out_shape=shapes,
            in_specs=specs,
            out_specs=out_specs,
            input_output_aliases=aliases,
            scratch_shapes=scratch,
            compiler_params=LIMIT,
        )(*arrays)

    def hand_over(blocks_to_send, section):
        return [
            lax.ppermute(
                block,
                ("tm", "net"),
                [((section - 1) * n + q, section * n + (q + d) % n) for q in range(n)],
            )
            for d, block in enumerate(blocks_to_send)
        ]

    opening = [state]
    out = None
    for r in range(1, tm):
        state, *arrived = hand_over([state, *outgoing], r)
        before = []
        for s in range(steps):
            fix = r == 1 and s == 0
            if s > 0:
                arrived = lax.all_to_all(outgoing, "net", split_axis=0, concat_axis=0, tiled=True)
            z = own(state, s)
            if s < steps - 1:
                state, outgoing = join(z, s, fix, state, arrived, "stack", r)
                before.append(state)
            elif r < tm - 1:
                out, state, *outgoing = join(z, s, fix, state, arrived, "each", r, opening, before, out, steps)
            else:
                (out,) = join(z, s, fix, state, arrived, "none", r, opening, before, out, steps)
    return out


def solution(mesh):
    return jax.shard_map(
        local,
        mesh=mesh,
        in_specs=(
            P("tm", "net", None, None, None),
            P("net", None),
            P("tm", "net", None, None, None),
            P("net", None),
            P("net", None),
            P("net", None),
            P("cols"),
            P("tm", "cols"),
        ),
        out_specs=P("tm", "cols", "net"),
        check_vma=False,
    )
```

```python
import functools

import jax
import jax.numpy as jnp
from jax import lax
from jax.experimental import pallas as pl
from jax.experimental.pallas import tpu as pltpu
from jax.sharding import PartitionSpec as P

VMEM = pl.BlockSpec(memory_space=pltpu.VMEM)
SMEM = pl.BlockSpec(memory_space=pltpu.SMEM)
HBM = pl.BlockSpec(memory_space=pltpu.HBM)
ANY = pl.BlockSpec(memory_space=pl.ANY)
LIMIT = pltpu.CompilerParams(vmem_limit_bytes=16 * 1024 * 1024)
DMA = pltpu.SemaphoreType.DMA

STATE, LANE, BLOCK, PART, GAIN = 0, 1, 2, 3, 4
ROWS = 16


def times_transposed(rows, block):
    return lax.dot_general(rows, block, (((1,), (1,)), ((), ())), preferred_element_type=jnp.float32)


def injected(table, step, first_state, width):
    lane = lax.broadcasted_iota(jnp.int32, (table.shape[0], width), 1)
    hit = table[:, STATE : STATE + 1] == (lane + first_state).astype(jnp.float32)
    return jnp.where(hit, table[:, GAIN + step : GAIN + step + 1], 0.0)


def own_sum(i, state_ref, jac_ref, cols_ref, table, step):
    blocks, _, width = state_ref.shape
    first = (lax.axis_index("net") * blocks + i) * width
    kinds = jac_ref.shape[1]
    rows = [state_ref[i]] + [state_ref[cols_ref[k - 1, i]] for k in range(1, kinds)]
    row_blocks = [jac_ref[i, k] for k in range(kinds)]
    total = times_transposed(jnp.concatenate(rows, axis=1), jnp.concatenate(row_blocks, axis=1))
    return total + injected(table, step, first, width)


def add_coupled(incoming, block, live, recv, z_ref, keep=None):
    mask = lax.broadcasted_iota(jnp.int32, z_ref.shape[1:], 1) < live
    if keep is not None:
        mask = jnp.logical_and(mask, keep > 0.0)
    z_ref[recv] += jnp.where(mask, times_transposed(incoming, block), 0.0)


def table_row(send_ref, partition, width):
    n = lax.axis_size("net")
    lane = lax.broadcasted_iota(jnp.int32, (1, width), 1)
    row = jnp.zeros((1, width), jnp.float32)
    for e in range(n):
        row = jnp.where(lane == e, send_ref[0, lax.rem(partition - e + n, n)].astype(jnp.float32), row)
    return row


def kept(table, rows):
    n = lax.axis_size("net")
    me = lax.axis_index("net")
    part, block = table[:, PART : PART + 1], table[:, BLOCK : BLOCK + 1]
    back = me.astype(jnp.float32) - part
    back = jnp.where(back < 0.0, back + float(n), back)
    sent = jnp.broadcast_to(rows[0], (table.shape[0], rows[0].shape[1]))
    for d in range(1, n):
        sent = jnp.where(back == float(d), rows[d], sent)
    lane = lax.broadcasted_iota(jnp.int32, sent.shape, 1).astype(jnp.float32)
    return jnp.where(jnp.logical_or(back == lane, block == sent), 1.0, 0.0)


def second_kernel(*refs):
    jac_hbm, iface_hbm, *small, table_ref, state_ref = refs[:10]
    n = lax.axis_size("net")
    me = lax.axis_index("net")
    outgoing, refs = refs[10 : 9 + n], refs[9 + n :]
    jac_ref, iface_ref, *loaded, first_ref, z_ref, sems = refs
    cols_ref, send_ref, recv_ref, live_ref, node_ref, gain_ref = loaded
    blocks, cols, width = state_ref.shape
    loads = [
        pltpu.make_async_copy(source, target, sems.at[i])
        for i, (source, target) in enumerate(
            zip([jac_hbm.at[1], iface_hbm.at[1, 0], *small], [jac_ref, iface_ref, *loaded])
        )
    ]
    for load in loads:
        load.start()
    for load in loads[2:]:
        load.wait()
    node = node_ref[...]
    block_of = node // width
    rows = [
        node,
        node - block_of * width,
        block_of % blocks,
        block_of // blocks,
    ]
    steps = gain_ref.shape[0]
    fill = -(GAIN + steps) % 8
    rows = [row.astype(jnp.float32) for row in rows] + [gain_ref[...], jnp.zeros((fill, cols), jnp.float32)]
    table_ref[...] = jnp.concatenate(rows, axis=0).T
    table = table_ref[...]
    for i in range(blocks):
        first_ref[i] = injected(table, 0, (me * blocks + i) * width, width).astype(first_ref.dtype)
    lane = lax.broadcasted_iota(jnp.int32, (cols, width), 1).astype(jnp.float32)
    shot = jnp.where(lane == table[:, LANE : LANE + 1], table[:, GAIN : GAIN + 1], 0.0)
    loads[0].wait()
    for i in range(blocks):
        z_ref[i] = own_sum(i, first_ref, jac_ref, cols_ref, table, 1)
    loads[1].wait()
    part, block = table[:, PART : PART + 1], table[:, BLOCK : BLOCK + 1]
    mine = jnp.logical_or(part != me.astype(jnp.float32), block == send_ref[0, me].astype(jnp.float32))
    shot = jnp.where(mine, shot, 0.0)
    for q in range(n):
        sent = jnp.where(part == float(q), shot, 0.0).astype(first_ref.dtype)
        add_coupled(sent, iface_ref[q], live_ref[0, q], recv_ref[0, q], z_ref)
    state_ref[...] = z_ref[...].astype(state_ref.dtype)
    for d in range(1, n):
        target = lax.rem(me + d, n)
        outgoing[d - 1][pl.ds(0, cols)] = state_ref[send_ref[0, target]]
        row = table_row(send_ref, target, width).astype(state_ref.dtype)
        outgoing[d - 1][pl.ds(cols, ROWS)] = jnp.broadcast_to(row, (ROWS, width))


def write_start(states, first, out_ref, sems):
    copies = []
    for s, state_ref in enumerate(states, first):
        width = state_ref.shape[2]
        for i in range(state_ref.shape[0]):
            copies.append(
                pltpu.make_async_copy(state_ref.at[i], out_ref.at[s, :, pl.ds(i * width, width)], sems.at[s, i])
            )
    for copy in copies:
        copy.start()
    return copies


def own_kernel(step, state_ref, jac_ref, cols_ref, table_ref, z_ref):
    table = table_ref[...]
    for i in range(state_ref.shape[0]):
        z_ref[i] = own_sum(i, state_ref, jac_ref.at[step], cols_ref, table, step)


def first_states(states, jac_ref, iface_ref, cols_ref, send_ref, recv_ref, live_ref, table_ref, arrived, made_ref, z_ref):
    n = lax.axis_size("net")
    blocks, cols, width = z_ref.shape
    table = table_ref[...]
    made_ref[0] = jnp.zeros_like(made_ref[0])
    for i in range(blocks):
        z_ref[i] = own_sum(i, made_ref.at[0], jac_ref.at[0], cols_ref, table, 0)
    for q in range(n):
        add_coupled(made_ref[0, 0], iface_ref[0, 0, q], live_ref[0, q], recv_ref[0, q], z_ref)
    made_ref[0] = z_ref[...].astype(made_ref.dtype)
    me = lax.axis_index("net")
    rows = [table_row(send_ref, me, width)]
    for d in range(1, n):
        rows.append(arrived[lax.rem(me - d + n, n)][0:1].astype(jnp.float32))
    keep = kept(table, rows)[:, 0:1]
    for i in range(blocks):
        made_ref[1, i] = jnp.where(keep > 0.0, states[0][i], jnp.zeros_like(states[0][i]))
    return [made_ref.at[0], made_ref.at[1], *states[1:]]


def join_kernel(step, fix, stacked, send_out, section, firsts, store, *refs):
    n = lax.axis_size("net")
    me = lax.axis_index("net")
    tm = lax.axis_index("tm")
    z_ref, iface_ref, send_ref, recv_ref, live_ref, table_ref, state_in_ref, *refs = refs
    if stacked:
        arrived, *refs = refs
    else:
        arrived, refs = refs[: n - 1], refs[n - 1 :]
    acc_ref = refs.pop()
    blocks, cols, width = z_ref.shape
    before = []
    if store:
        sems = refs.pop()
        if firsts:
            made_ref = refs.pop()
            opening, refs = refs[:firsts], refs[firsts:]
            jac_ref, cols_ref = refs.pop(0), refs.pop(0)
        before, refs = refs[: store - 1], refs[store - 1 :]
        if not firsts:
            refs.pop(0)
        out_ref = refs.pop(0)
    state_ref, *outgoing = refs

    def join():
        if store:
            copies = write_start(before, 0, out_ref, sems)
        if fix:
            table = table_ref[...]
            rows = [table_row(send_ref, me, width)]
            rows += [arrived[d - 1][cols : cols + 1].astype(jnp.float32) for d in range(1, n)]
            keep = kept(table, rows)
            for i in range(blocks):
                acc_ref[i] = jnp.where(keep[:, 0:1] > 0.0, z_ref[i], 0.0)
        else:
            acc_ref[...] = z_ref[...]
        for d in range(n):
            q = lax.rem(me - d + n, n)
            if d == 0:
                block = state_in_ref[send_ref[0, me]]
            elif stacked:
                block = arrived[q]
            else:
                block = arrived[d - 1][pl.ds(0, cols)]
            stands = keep[:, d : d + 1] if fix else None
            add_coupled(block, iface_ref[step, 0, q], live_ref[0, q], recv_ref[0, q], acc_ref, stands)
        state_ref[...] = acc_ref[...].astype(state_ref.dtype)
        if send_out == "stack":
            for q in range(n):
                outgoing[0][q] = state_ref[send_ref[0, q]]
        if send_out == "each":
            for d in range(1, n):
                outgoing[d - 1][...] = state_ref[send_ref[0, lax.rem(me + d, n)]]
        if store:
            copies += write_start([state_ref], store - 1, out_ref, sems)
            for copy in copies:
                copy.wait()

    if store:
        pl.when(tm == section)(join)
    else:
        join()
    if fix and send_out == "stack":

        @pl.when(tm == 0)
        def _():
            for q in range(n):
                row = table_row(send_ref, jnp.int32(q), width).astype(state_ref.dtype)
                outgoing[0][q, pl.ds(0, ROWS)] = jnp.broadcast_to(row, (ROWS, width))

    if firsts:

        @pl.when(tm == 0)
        def _():
            made = first_states(
                opening, jac_ref, iface_ref, cols_ref, send_ref, recv_ref, live_ref, table_ref, arrived, made_ref, acc_ref
            )
            for copy in write_start(made, 0, out_ref, sems):
                copy.wait()


def local(jac, block_cols, iface_jac, iface_send, iface_recv, iface_live, ctrl_node, ctrl_gain):
    steps, blocks, kinds, width, _ = jac.shape
    cols = ctrl_node.shape[0]
    tm = lax.axis_size("tm")
    n = lax.axis_size("net")
    node = ctrl_node[None]
    near = block_cols.T
    bf16 = functools.partial(jax.ShapeDtypeStruct, dtype=jnp.bfloat16)
    f32 = functools.partial(jax.ShapeDtypeStruct, dtype=jnp.float32)
    whole, one, stack = bf16((blocks, cols, width)), bf16((cols, width)), bf16((n, cols, width))
    table_rows = GAIN + steps + -(GAIN + steps) % 8
    written = bf16((steps, cols, blocks * width))

    pinned = [
        pltpu.with_memory_space_constraint(x, pltpu.HBM)
        for x in (jac, iface_jac, near, iface_send, iface_recv, iface_live, node, ctrl_gain)
    ]
    table, state, *outgoing = pl.pallas_call(
        second_kernel,
        out_shape=[f32((cols, table_rows)), whole] + [bf16((cols + ROWS, width))] * (n - 1),
        in_specs=[HBM] * len(pinned),
        out_specs=[VMEM] * (n + 1),
        scratch_shapes=[
            pltpu.VMEM((blocks, kinds, width, width), jnp.bfloat16),
            pltpu.VMEM((n, width, width), jnp.bfloat16),
            *[pltpu.SMEM(x.shape, x.dtype) for x in (near, iface_send, iface_recv, iface_live)],
            *[pltpu.VMEM(x.shape, x.dtype) for x in (node, ctrl_gain)],
            pltpu.VMEM(whole.shape, jnp.bfloat16),
            pltpu.VMEM(whole.shape, jnp.float32),
            DMA((len(pinned),)),
        ],
        compiler_params=LIMIT,
    )(*pinned)

    def own(state, step):
        return pl.pallas_call(
            functools.partial(own_kernel, step),
            out_shape=f32(whole.shape),
            in_specs=[VMEM, VMEM, SMEM, VMEM],
            out_specs=VMEM,
            compiler_params=LIMIT,
        )(state, jac, near, table)

    def join(z, step, fix, state, arrived, send_out, section, opening=(), before=(), out=None, store=0):
        stacked = not isinstance(arrived, list)
        arrays = [z, iface_jac, iface_send, iface_recv, iface_live, table, state]
        specs = [VMEM, VMEM, SMEM, SMEM, SMEM, VMEM, VMEM]
        arrays += [arrived] if stacked else arrived
        specs += [VMEM] * (1 if stacked else n - 1)
        shapes = []
        scratch = [pltpu.VMEM(whole.shape, jnp.float32)]
        aliases = {}
        out_specs = []
        if store:
            if out is None:
                arrays += [*opening, jac, near]
                specs += [VMEM] * len(opening) + [VMEM, SMEM]
            arrays += before
            specs += [VMEM] * len(before)
            if out is not None:
                aliases = {len(arrays): 0}
                arrays.append(out)
                specs.append(ANY)
            shapes.append(written)
            out_specs.append(ANY)
            scratch.insert(0, DMA((steps, blocks)))
            if out is None:
                scratch.insert(0, pltpu.VMEM((2, *whole.shape), jnp.bfloat16))
        if send_out == "none":
            scratch.insert(0, pltpu.VMEM(whole.shape, jnp.bfloat16))
        else:
            shapes.append(whole)
        shapes += {"stack": [stack], "each": [one] * (n - 1), "none": []}[send_out]
        out_specs += [VMEM] * (len(shapes) - len(out_specs))
        firsts = len(opening) if store and out is None else 0
        return pl.pallas_call(
            functools.partial(join_kernel, step, fix, stacked, send_out, section, firsts, store),
            out_shape=shapes,
            in_specs=specs,
            out_specs=out_specs,
            input_output_aliases=aliases,
            scratch_shapes=scratch,
            compiler_params=LIMIT,
        )(*arrays)

    def hand_over(blocks_to_send, section):
        return [
            lax.ppermute(
                block,
                ("tm", "net"),
                [((section - 1) * n + q, section * n + (q + d) % n) for q in range(n)],
            )
            for d, block in enumerate(blocks_to_send, 1)
        ]

    opening = [state]
    out = None
    for r in range(1, tm):
        arrived = hand_over(outgoing, r)
        state = lax.all_gather(state, "tm")[r - 1]
        before = []
        for s in range(steps):
            fix = r == 1 and s == 0
            if s > 0:
                arrived = lax.all_to_all(outgoing, "net", split_axis=0, concat_axis=0, tiled=True)
            z = own(state, s)
            if s < steps - 1:
                state, outgoing = join(z, s, fix, state, arrived, "stack", r)
                before.append(state)
            elif r < tm - 1:
                out, state, *outgoing = join(z, s, fix, state, arrived, "each", r, opening, before, out, steps)
            else:
                (out,) = join(z, s, fix, state, arrived, "none", r, opening, before, out, steps)
    return out


def solution(mesh):
    return jax.shard_map(
        local,
        mesh=mesh,
        in_specs=(
            P("tm", "net", None, None, None),
            P("net", None),
            P("tm", "net", None, None, None),
            P("net", None),
            P("net", None),
            P("net", None),
            P("cols"),
            P("tm", "cols"),
        ),
        out_specs=P("tm", "cols", "net"),
        check_vma=False,
    )
```

```python
import functools

import jax
import jax.numpy as jnp
from jax import lax
from jax.experimental import pallas as pl
from jax.experimental.pallas import tpu as pltpu
from jax.sharding import PartitionSpec as P

VMEM = pl.BlockSpec(memory_space=pltpu.VMEM)
SMEM = pl.BlockSpec(memory_space=pltpu.SMEM)
HBM = pl.BlockSpec(memory_space=pltpu.HBM)
ANY = pl.BlockSpec(memory_space=pl.ANY)
LIMIT = pltpu.CompilerParams(vmem_limit_bytes=16 * 1024 * 1024)
DMA = pltpu.SemaphoreType.DMA

STATE, LANE, BLOCK, AWAY, GAIN = 0, 1, 2, 3, 4
ROWS = 16


def times_transposed(rows, block):
    return lax.dot_general(rows, block, (((1,), (1,)), ((), ())), preferred_element_type=jnp.float32)


def injected(table, step, first_state, width):
    lane = lax.broadcasted_iota(jnp.int32, (table.shape[0], width), 1)
    hit = table[:, STATE : STATE + 1] == (lane + first_state).astype(jnp.float32)
    return jnp.where(hit, table[:, GAIN + step : GAIN + step + 1], 0.0)


def own_sum(i, state_ref, jac_ref, cols_ref, table, step):
    blocks, _, width = state_ref.shape
    first = (lax.axis_index("net") * blocks + i) * width
    kinds = jac_ref.shape[1]
    rows = [state_ref[i]] + [state_ref[cols_ref[k - 1, i]] for k in range(1, kinds)]
    row_blocks = [jac_ref[i, k] for k in range(kinds)]
    total = times_transposed(jnp.concatenate(rows, axis=1), jnp.concatenate(row_blocks, axis=1))
    return total + injected(table, step, first, width)


def add_coupled(incoming, block, live, recv, z_ref, keep=None):
    mask = lax.broadcasted_iota(jnp.int32, z_ref.shape[1:], 1) < live
    if keep is not None:
        mask = jnp.logical_and(mask, keep > 0.0)
    z_ref[recv] += jnp.where(mask, times_transposed(incoming, block), 0.0)


def table_row(send_ref, partition, width):
    lane = lax.broadcasted_iota(jnp.int32, (1, width), 1)
    row = jnp.zeros((1, width), jnp.float32)
    for e in range(lax.axis_size("net")):
        row = jnp.where(lane == e, send_ref[0, partition ^ e].astype(jnp.float32), row)
    return row


def kept(table, rows):
    away, block = table[:, AWAY : AWAY + 1], table[:, BLOCK : BLOCK + 1]
    sent = jnp.broadcast_to(rows[0], (table.shape[0], rows[0].shape[1]))
    for d in range(1, len(rows)):
        sent = jnp.where(away == float(d), rows[d], sent)
    lane = lax.broadcasted_iota(jnp.int32, sent.shape, 1).astype(jnp.float32)
    return jnp.where(jnp.logical_or(away == lane, block == sent), 1.0, 0.0)


def second_kernel(*refs):
    jac_hbm, iface_hbm, *small, table_ref, state_ref = refs[:10]
    n = lax.axis_size("net")
    me = lax.axis_index("net")
    outgoing, refs = refs[10 : 9 + n], refs[9 + n :]
    jac_ref, iface_ref, *loaded, first_ref, z_ref, sems = refs
    cols_ref, send_ref, recv_ref, live_ref, node_ref, gain_ref = loaded
    blocks, cols, width = state_ref.shape
    loads = [
        pltpu.make_async_copy(source, target, sems.at[i])
        for i, (source, target) in enumerate(
            zip([jac_hbm.at[1], iface_hbm.at[1, 0], *small], [jac_ref, iface_ref, *loaded])
        )
    ]
    here = lax.axis_index("tm") == 0

    @pl.when(here)
    def _():
        for load in loads[:2]:
            load.start()

    for load in loads[2:]:
        load.start()
    for load in loads[2:]:
        load.wait()
    node = node_ref[...]
    block_of = node // width
    rows = [
        node,
        node - block_of * width,
        block_of % blocks,
        (block_of // blocks) ^ me,
    ]
    steps = gain_ref.shape[0]
    fill = -(GAIN + steps) % 8
    rows = [row.astype(jnp.float32) for row in rows] + [gain_ref[...], jnp.zeros((fill, cols), jnp.float32)]
    table_ref[...] = jnp.concatenate(rows, axis=0).T

    @pl.when(here)
    def _():
        table = table_ref[...]
        for i in range(blocks):
            first_ref[i] = injected(table, 0, (me * blocks + i) * width, width).astype(first_ref.dtype)
        lane = lax.broadcasted_iota(jnp.int32, (cols, width), 1).astype(jnp.float32)
        shot = jnp.where(lane == table[:, LANE : LANE + 1], table[:, GAIN : GAIN + 1], 0.0)
        loads[0].wait()
        for i in range(blocks):
            z_ref[i] = own_sum(i, first_ref, jac_ref, cols_ref, table, 1)
        loads[1].wait()
        away, block = table[:, AWAY : AWAY + 1], table[:, BLOCK : BLOCK + 1]
        mine = jnp.logical_or(away != 0.0, block == send_ref[0, me].astype(jnp.float32))
        shot = jnp.where(mine, shot, 0.0)
        for d in range(n):
            q = me ^ d
            sent = jnp.where(away == float(d), shot, 0.0).astype(first_ref.dtype)
            add_coupled(sent, iface_ref[q], live_ref[0, q], recv_ref[0, q], z_ref)
        state_ref[...] = z_ref[...].astype(state_ref.dtype)
        for d in range(1, n):
            outgoing[d - 1][pl.ds(0, cols)] = state_ref[send_ref[0, me ^ d]]
            row = table_row(send_ref, me ^ d, width).astype(state_ref.dtype)
            outgoing[d - 1][pl.ds(cols, ROWS)] = jnp.broadcast_to(row, (ROWS, width))


def write_start(states, first, out_ref, sems):
    copies = []
    for s, state_ref in enumerate(states, first):
        width = state_ref.shape[2]
        for i in range(state_ref.shape[0]):
            copies.append(
                pltpu.make_async_copy(state_ref.at[i], out_ref.at[s, :, pl.ds(i * width, width)], sems.at[s, i])
            )
    for copy in copies:
        copy.start()
    return copies


def own_kernel(step, state_ref, jac_ref, cols_ref, table_ref, z_ref):
    table = table_ref[...]
    for i in range(state_ref.shape[0]):
        z_ref[i] = own_sum(i, state_ref, jac_ref.at[step], cols_ref, table, step)


def first_states(states, jac_ref, iface_ref, cols_ref, send_ref, recv_ref, live_ref, table_ref, arrived, made_ref, z_ref):
    n = lax.axis_size("net")
    blocks, cols, width = z_ref.shape
    table = table_ref[...]
    made_ref[0] = jnp.zeros_like(made_ref[0])
    for i in range(blocks):
        z_ref[i] = own_sum(i, made_ref.at[0], jac_ref.at[0], cols_ref, table, 0)
    for q in range(n):
        add_coupled(made_ref[0, 0], iface_ref[0, 0, q], live_ref[0, q], recv_ref[0, q], z_ref)
    made_ref[0] = z_ref[...].astype(made_ref.dtype)
    me = lax.axis_index("net")
    rows = [table_row(send_ref, me, width)]
    rows += [block[0:1].astype(jnp.float32) for block in arrived]
    keep = kept(table, rows)[:, 0:1]
    for i in range(blocks):
        made_ref[1, i] = jnp.where(keep > 0.0, states[0][i], jnp.zeros_like(states[0][i]))
    return [made_ref.at[0], made_ref.at[1], *states[1:]]


def join_kernel(step, fix, send, section, firsts, store, *refs):
    n = lax.axis_size("net")
    me = lax.axis_index("net")
    tm = lax.axis_index("tm")
    z_ref, iface_ref, send_ref, recv_ref, live_ref, table_ref, state_in_ref, *refs = refs
    arrived, refs = refs[: n - 1], refs[n - 1 :]
    acc_ref = refs.pop()
    blocks, cols, width = z_ref.shape
    before = []
    if store:
        sems = refs.pop()
        if firsts:
            made_ref = refs.pop()
            opening, refs = refs[:firsts], refs[firsts:]
            jac_ref, cols_ref = refs.pop(0), refs.pop(0)
        before, refs = refs[: store - 1], refs[store - 1 :]
        if not firsts:
            refs.pop(0)
        out_ref = refs.pop(0)
    state_ref, *outgoing = refs

    def join():
        if store:
            copies = write_start(before, 0, out_ref, sems)
        if fix:
            table = table_ref[...]
            rows = [table_row(send_ref, me, width)]
            rows += [arrived[d - 1][cols : cols + 1].astype(jnp.float32) for d in range(1, n)]
            keep = kept(table, rows)
            for i in range(blocks):
                acc_ref[i] = jnp.where(keep[:, 0:1] > 0.0, z_ref[i], 0.0)
        else:
            acc_ref[...] = z_ref[...]
        for d in range(n):
            q = me ^ d
            block = arrived[d - 1][pl.ds(0, cols)] if d else state_in_ref[send_ref[0, me]]
            stands = keep[:, d : d + 1] if fix else None
            add_coupled(block, iface_ref[step, 0, q], live_ref[0, q], recv_ref[0, q], acc_ref, stands)
        state_ref[...] = acc_ref[...].astype(state_ref.dtype)
        if send:
            for d in range(1, n):
                outgoing[d - 1][...] = state_ref[send_ref[0, me ^ d]]
        if store:
            copies += write_start([state_ref], store - 1, out_ref, sems)
            for copy in copies:
                copy.wait()

    if store:
        pl.when(tm == section)(join)
    else:
        join()
    if fix:

        @pl.when(tm == 0)
        def _():
            for d in range(1, n):
                row = table_row(send_ref, me ^ d, width).astype(state_ref.dtype)
                outgoing[d - 1][pl.ds(0, ROWS)] = jnp.broadcast_to(row, (ROWS, width))

    if firsts:

        @pl.when(tm == 0)
        def _():
            made = first_states(
                opening, jac_ref, iface_ref, cols_ref, send_ref, recv_ref, live_ref, table_ref, arrived, made_ref, acc_ref
            )
            for copy in write_start(made, 0, out_ref, sems):
                copy.wait()


def local(jac, block_cols, iface_jac, iface_send, iface_recv, iface_live, ctrl_node, ctrl_gain):
    steps, blocks, kinds, width, _ = jac.shape
    cols = ctrl_node.shape[0]
    tm = lax.axis_size("tm")
    n = lax.axis_size("net")
    node = ctrl_node[None]
    near = block_cols.T
    bf16 = functools.partial(jax.ShapeDtypeStruct, dtype=jnp.bfloat16)
    f32 = functools.partial(jax.ShapeDtypeStruct, dtype=jnp.float32)
    whole, one = bf16((blocks, cols, width)), bf16((cols, width))
    table_rows = GAIN + steps + -(GAIN + steps) % 8
    written = bf16((steps, cols, blocks * width))

    pinned = [
        pltpu.with_memory_space_constraint(x, pltpu.HBM)
        for x in (jac, iface_jac, near, iface_send, iface_recv, iface_live, node, ctrl_gain)
    ]
    table, state, *outgoing = pl.pallas_call(
        second_kernel,
        out_shape=[f32((cols, table_rows)), whole] + [bf16((cols + ROWS, width))] * (n - 1),
        in_specs=[HBM] * len(pinned),
        out_specs=[VMEM] * (n + 1),
        scratch_shapes=[
            pltpu.VMEM((blocks, kinds, width, width), jnp.bfloat16),
            pltpu.VMEM((n, width, width), jnp.bfloat16),
            *[pltpu.SMEM(x.shape, x.dtype) for x in (near, iface_send, iface_recv, iface_live)],
            *[pltpu.VMEM(x.shape, x.dtype) for x in (node, ctrl_gain)],
            pltpu.VMEM(whole.shape, jnp.bfloat16),
            pltpu.VMEM(whole.shape, jnp.float32),
            DMA((len(pinned),)),
        ],
        compiler_params=LIMIT,
    )(*pinned)

    def own(state, step):
        return pl.pallas_call(
            functools.partial(own_kernel, step),
            out_shape=f32(whole.shape),
            in_specs=[VMEM, VMEM, SMEM, VMEM],
            out_specs=VMEM,
            compiler_params=LIMIT,
        )(state, jac, near, table)

    def join(z, step, fix, state, arrived, send, section, opening=(), before=(), out=None, store=0):
        arrays = [z, iface_jac, iface_send, iface_recv, iface_live, table, state]
        specs = [VMEM, VMEM, SMEM, SMEM, SMEM, VMEM, VMEM]
        arrays += arrived
        specs += [VMEM] * (n - 1)
        shapes = []
        scratch = [pltpu.VMEM(whole.shape, jnp.float32)]
        aliases = {}
        out_specs = []
        if store:
            if out is None:
                arrays += [*opening, jac, near]
                specs += [VMEM] * len(opening) + [VMEM, SMEM]
            arrays += before
            specs += [VMEM] * len(before)
            if out is not None:
                aliases = {len(arrays): 0}
                arrays.append(out)
                specs.append(ANY)
            shapes.append(written)
            out_specs.append(ANY)
            scratch.insert(0, DMA((steps, blocks)))
            if out is None:
                scratch.insert(0, pltpu.VMEM((2, *whole.shape), jnp.bfloat16))
        if send:
            shapes += [whole] + [one] * (n - 1)
        else:
            scratch.insert(0, pltpu.VMEM(whole.shape, jnp.bfloat16))
        out_specs += [VMEM] * (len(shapes) - len(out_specs))
        firsts = len(opening) if store and out is None else 0
        return pl.pallas_call(
            functools.partial(join_kernel, step, fix, send, section, firsts, store),
            out_shape=shapes,
            in_specs=specs,
            out_specs=out_specs,
            input_output_aliases=aliases,
            scratch_shapes=scratch,
            compiler_params=LIMIT,
        )(*arrays)

    def swap(outgoing, sections):
        return [
            lax.ppermute(
                block, ("tm", "net"), [(a * n + q, b * n + (q ^ d)) for a, b in sections for q in range(n)]
            )
            for d, block in enumerate(outgoing, 1)
        ]

    opening = [state]
    out = None
    for r in range(1, tm):
        state = lax.ppermute(state, "tm", [(r - 1, r)])
        arrived = swap(outgoing, [(r - 1, r)])
        before = []
        for s in range(steps):
            fix = r == 1 and s == 0
            if s > 0:
                arrived = swap(outgoing, [(0, 0), (r, r)] if r == 1 else [(r, r)])
            z = own(state, s)
            if s < steps - 1:
                state, *outgoing = join(z, s, fix, state, arrived, True, r)
                before.append(state)
            elif r < tm - 1:
                out, state, *outgoing = join(z, s, fix, state, arrived, True, r, opening, before, out, steps)
            else:
                (out,) = join(z, s, fix, state, arrived, False, r, opening, before, out, steps)
    return out


def solution(mesh):
    return jax.shard_map(
        local,
        mesh=mesh,
        in_specs=(
            P("tm", "net", None, None, None),
            P("net", None),
            P("tm", "net", None, None, None),
            P("net", None),
            P("net", None),
            P("net", None),
            P("cols"),
            P("tm", "cols"),
        ),
        out_specs=P("tm", "cols", "net"),
        check_vma=False,
    )
```

```python
import functools

import jax
import jax.numpy as jnp
from jax import lax
from jax.experimental import pallas as pl
from jax.experimental.pallas import tpu as pltpu
from jax.sharding import PartitionSpec as P

VMEM = pl.BlockSpec(memory_space=pltpu.VMEM)
SMEM = pl.BlockSpec(memory_space=pltpu.SMEM)
HBM = pl.BlockSpec(memory_space=pltpu.HBM)
ANY = pl.BlockSpec(memory_space=pl.ANY)
LIMIT = pltpu.CompilerParams(vmem_limit_bytes=16 * 1024 * 1024)
DMA = pltpu.SemaphoreType.DMA

STATE, LANE, BLOCK, AWAY, GAIN = 0, 1, 2, 3, 4
ROWS = 16


def times_transposed(rows, block):
    return lax.dot_general(rows, block, (((1,), (1,)), ((), ())), preferred_element_type=jnp.float32)


def injected(table, step, first_state, width):
    lane = lax.broadcasted_iota(jnp.int32, (table.shape[0], width), 1)
    hit = table[:, STATE : STATE + 1] == (lane + first_state).astype(jnp.float32)
    return jnp.where(hit, table[:, GAIN + step : GAIN + step + 1], 0.0)


def own_sum(i, state_ref, jac_ref, cols_ref, table, step):
    blocks, _, width = state_ref.shape
    first = (lax.axis_index("net") * blocks + i) * width
    kinds = jac_ref.shape[1]
    rows = [state_ref[i]] + [state_ref[cols_ref[k - 1, i]] for k in range(1, kinds)]
    row_blocks = [jac_ref[i, k] for k in range(kinds)]
    total = times_transposed(jnp.concatenate(rows, axis=1), jnp.concatenate(row_blocks, axis=1))
    return total + injected(table, step, first, width)


def add_coupled(incoming, block, live, recv, z_ref, keep=None):
    mask = lax.broadcasted_iota(jnp.int32, z_ref.shape[1:], 1) < live
    if keep is not None:
        mask = jnp.logical_and(mask, keep > 0.0)
    z_ref[recv] += jnp.where(mask, times_transposed(incoming, block), 0.0)


def table_row(send_ref, partition, width):
    lane = lax.broadcasted_iota(jnp.int32, (1, width), 1)
    row = jnp.zeros((1, width), jnp.float32)
    for e in range(lax.axis_size("net")):
        row = jnp.where(lane == e, send_ref[0, partition ^ e].astype(jnp.float32), row)
    return row


def kept(table, rows):
    away, block = table[:, AWAY : AWAY + 1], table[:, BLOCK : BLOCK + 1]
    sent = jnp.broadcast_to(rows[0], (table.shape[0], rows[0].shape[1]))
    for d in range(1, len(rows)):
        sent = jnp.where(away == float(d), rows[d], sent)
    lane = lax.broadcasted_iota(jnp.int32, sent.shape, 1).astype(jnp.float32)
    return jnp.where(jnp.logical_or(away == lane, block == sent), 1.0, 0.0)


def second_kernel(*refs):
    jac_hbm, iface_hbm, *small, table_ref, state_ref = refs[:10]
    n = lax.axis_size("net")
    me = lax.axis_index("net")
    outgoing, refs = refs[10 : 9 + n], refs[9 + n :]
    jac_ref, iface_ref, *loaded, first_ref, z_ref, sems = refs
    cols_ref, send_ref, recv_ref, live_ref, node_ref, gain_ref = loaded
    blocks, cols, width = state_ref.shape
    loads = [
        pltpu.make_async_copy(source, target, sems.at[i])
        for i, (source, target) in enumerate(
            zip([jac_hbm.at[1], iface_hbm.at[1, 0], *small], [jac_ref, iface_ref, *loaded])
        )
    ]
    here = lax.axis_index("tm") == 0

    @pl.when(here)
    def _():
        for load in loads[:2]:
            load.start()

    for load in loads[2:]:
        load.start()
    for load in loads[2:]:
        load.wait()
    node = node_ref[...]
    block_of = node // width
    rows = [
        node,
        node - block_of * width,
        block_of % blocks,
        (block_of // blocks) ^ me,
    ]
    steps = gain_ref.shape[0]
    fill = -(GAIN + steps) % 8
    rows = [row.astype(jnp.float32) for row in rows] + [gain_ref[...], jnp.zeros((fill, cols), jnp.float32)]
    table_ref[...] = jnp.concatenate(rows, axis=0).T

    @pl.when(here)
    def _():
        table = table_ref[...]
        for i in range(blocks):
            first_ref[i] = injected(table, 0, (me * blocks + i) * width, width).astype(first_ref.dtype)
        lane = lax.broadcasted_iota(jnp.int32, (cols, width), 1).astype(jnp.float32)
        shot = jnp.where(lane == table[:, LANE : LANE + 1], table[:, GAIN : GAIN + 1], 0.0)
        loads[0].wait()
        for i in range(blocks):
            z_ref[i] = own_sum(i, first_ref, jac_ref, cols_ref, table, 1)
        loads[1].wait()
        away, block = table[:, AWAY : AWAY + 1], table[:, BLOCK : BLOCK + 1]
        mine = jnp.logical_or(away != 0.0, block == send_ref[0, me].astype(jnp.float32))
        shot = jnp.where(mine, shot, 0.0)
        for d in range(n):
            q = me ^ d
            sent = jnp.where(away == float(d), shot, 0.0).astype(first_ref.dtype)
            add_coupled(sent, iface_ref[q], live_ref[0, q], recv_ref[0, q], z_ref)
        state_ref[...] = z_ref[...].astype(state_ref.dtype)
        for d in range(1, n):
            outgoing[d - 1][pl.ds(0, cols)] = state_ref[send_ref[0, me ^ d]]
            row = table_row(send_ref, me ^ d, width).astype(state_ref.dtype)
            outgoing[d - 1][pl.ds(cols, ROWS)] = jnp.broadcast_to(row, (ROWS, width))


def write_start(states, first, out_ref, sems):
    copies = []
    for s, state_ref in enumerate(states, first):
        width = state_ref.shape[2]
        for i in range(state_ref.shape[0]):
            copies.append(
                pltpu.make_async_copy(state_ref.at[i], out_ref.at[s, :, pl.ds(i * width, width)], sems.at[s, i])
            )
    for copy in copies:
        copy.start()
    return copies


def own_kernel(step, state_ref, jac_ref, cols_ref, table_ref, z_ref):
    table = table_ref[...]
    for i in range(state_ref.shape[0]):
        z_ref[i] = own_sum(i, state_ref, jac_ref.at[step], cols_ref, table, step)


def first_states(states, jac_ref, iface_ref, cols_ref, send_ref, recv_ref, live_ref, table_ref, arrived, made_ref, z_ref):
    n = lax.axis_size("net")
    blocks, cols, width = z_ref.shape
    table = table_ref[...]
    made_ref[0] = jnp.zeros_like(made_ref[0])
    for i in range(blocks):
        z_ref[i] = own_sum(i, made_ref.at[0], jac_ref.at[0], cols_ref, table, 0)
    for q in range(n):
        add_coupled(made_ref[0, 0], iface_ref[0, 0, q], live_ref[0, q], recv_ref[0, q], z_ref)
    made_ref[0] = z_ref[...].astype(made_ref.dtype)
    me = lax.axis_index("net")
    rows = [table_row(send_ref, me, width)]
    rows += [block[0:1].astype(jnp.float32) for block in arrived]
    keep = kept(table, rows)[:, 0:1]
    for i in range(blocks):
        made_ref[1, i] = jnp.where(keep > 0.0, states[0][i], jnp.zeros_like(states[0][i]))
    return [made_ref.at[0], made_ref.at[1], *states[1:]]


def join_kernel(step, fix, send, section, firsts, store, *refs):
    n = lax.axis_size("net")
    me = lax.axis_index("net")
    tm = lax.axis_index("tm")
    z_ref, iface_ref, send_ref, recv_ref, live_ref, table_ref, state_in_ref, *refs = refs
    arrived, refs = refs[: n - 1], refs[n - 1 :]
    acc_ref = refs.pop()
    blocks, cols, width = z_ref.shape
    before = []
    if store:
        sems = refs.pop()
        if firsts:
            made_ref = refs.pop()
            opening, refs = refs[:firsts], refs[firsts:]
            jac_ref, cols_ref = refs.pop(0), refs.pop(0)
        before, refs = refs[: store - 1], refs[store - 1 :]
        if not firsts:
            refs.pop(0)
        out_ref = refs.pop(0)
    state_ref, *outgoing = refs

    def join():
        if store:
            copies = write_start(before, 0, out_ref, sems)
        if fix:
            table = table_ref[...]
            rows = [table_row(send_ref, me, width)]
            rows += [arrived[d - 1][cols : cols + 1].astype(jnp.float32) for d in range(1, n)]
            keep = kept(table, rows)
            for i in range(blocks):
                acc_ref[i] = jnp.where(keep[:, 0:1] > 0.0, z_ref[i], 0.0)
        else:
            acc_ref[...] = z_ref[...]
        for d in range(n):
            q = me ^ d
            block = arrived[d - 1][pl.ds(0, cols)] if d else state_in_ref[send_ref[0, me]]
            stands = keep[:, d : d + 1] if fix else None
            add_coupled(block, iface_ref[step, 0, q], live_ref[0, q], recv_ref[0, q], acc_ref, stands)
        state_ref[...] = acc_ref[...].astype(state_ref.dtype)
        if send:
            for d in range(1, n):
                outgoing[d - 1][...] = state_ref[send_ref[0, me ^ d]]
        if store:
            copies += write_start([state_ref], store - 1, out_ref, sems)
            for copy in copies:
                copy.wait()

    if store:
        pl.when(tm == section)(join)
    else:
        join()
    if fix:

        @pl.when(tm == 0)
        def _():
            for d in range(1, n):
                row = table_row(send_ref, me ^ d, width).astype(state_ref.dtype)
                outgoing[d - 1][pl.ds(0, ROWS)] = jnp.broadcast_to(row, (ROWS, width))

    if firsts:

        @pl.when(tm == 0)
        def _():
            made = first_states(
                opening, jac_ref, iface_ref, cols_ref, send_ref, recv_ref, live_ref, table_ref, arrived, made_ref, acc_ref
            )
            for copy in write_start(made, 0, out_ref, sems):
                copy.wait()


def local(jac, block_cols, iface_jac, iface_send, iface_recv, iface_live, ctrl_node, ctrl_gain):
    steps, blocks, kinds, width, _ = jac.shape
    cols = ctrl_node.shape[0]
    tm = lax.axis_size("tm")
    n = lax.axis_size("net")
    node = ctrl_node[None]
    near = block_cols.T
    bf16 = functools.partial(jax.ShapeDtypeStruct, dtype=jnp.bfloat16)
    f32 = functools.partial(jax.ShapeDtypeStruct, dtype=jnp.float32)
    whole, one = bf16((blocks, cols, width)), bf16((cols, width))
    table_rows = GAIN + steps + -(GAIN + steps) % 8
    written = bf16((steps, cols, blocks * width))

    pinned = [
        pltpu.with_memory_space_constraint(x, pltpu.HBM)
        for x in (jac, iface_jac, near, iface_send, iface_recv, iface_live, node, ctrl_gain)
    ]
    table, state, *outgoing = pl.pallas_call(
        second_kernel,
        out_shape=[f32((cols, table_rows)), whole] + [bf16((cols + ROWS, width))] * (n - 1),
        in_specs=[HBM] * len(pinned),
        out_specs=[VMEM] * (n + 1),
        scratch_shapes=[
            pltpu.VMEM((blocks, kinds, width, width), jnp.bfloat16),
            pltpu.VMEM((n, width, width), jnp.bfloat16),
            *[pltpu.SMEM(x.shape, x.dtype) for x in (near, iface_send, iface_recv, iface_live)],
            *[pltpu.VMEM(x.shape, x.dtype) for x in (node, ctrl_gain)],
            pltpu.VMEM(whole.shape, jnp.bfloat16),
            pltpu.VMEM(whole.shape, jnp.float32),
            DMA((len(pinned),)),
        ],
        compiler_params=LIMIT,
    )(*pinned)

    def own(state, step):
        return pl.pallas_call(
            functools.partial(own_kernel, step),
            out_shape=f32(whole.shape),
            in_specs=[VMEM, VMEM, SMEM, VMEM],
            out_specs=VMEM,
            compiler_params=LIMIT,
        )(state, jac, near, table)

    def join(z, step, fix, state, arrived, send, section, opening=(), before=(), out=None, store=0):
        arrays = [z, iface_jac, iface_send, iface_recv, iface_live, table, state]
        specs = [VMEM, VMEM, SMEM, SMEM, SMEM, VMEM, VMEM]
        arrays += arrived
        specs += [VMEM] * (n - 1)
        shapes = []
        scratch = [pltpu.VMEM(whole.shape, jnp.float32)]
        aliases = {}
        out_specs = []
        if store:
            if out is None:
                arrays += [*opening, jac, near]
                specs += [VMEM] * len(opening) + [VMEM, SMEM]
            arrays += before
            specs += [VMEM] * len(before)
            if out is not None:
                aliases = {len(arrays): 0}
                arrays.append(out)
                specs.append(ANY)
            shapes.append(written)
            out_specs.append(ANY)
            scratch.insert(0, DMA((steps, blocks)))
            if out is None:
                scratch.insert(0, pltpu.VMEM((2, *whole.shape), jnp.bfloat16))
        if send:
            shapes += [whole] + [one] * (n - 1)
        else:
            scratch.insert(0, pltpu.VMEM(whole.shape, jnp.bfloat16))
        out_specs += [VMEM] * (len(shapes) - len(out_specs))
        firsts = len(opening) if store and out is None else 0
        return pl.pallas_call(
            functools.partial(join_kernel, step, fix, send, section, firsts, store),
            out_shape=shapes,
            in_specs=specs,
            out_specs=out_specs,
            input_output_aliases=aliases,
            scratch_shapes=scratch,
            compiler_params=LIMIT,
        )(*arrays)

    def swap(outgoing, sections):
        arrived = {}
        for d in reversed(range(1, n)):
            pairs = [(a * n + q, b * n + (q ^ d)) for a, b in sections for q in range(n)]
            arrived[d] = lax.ppermute(outgoing[d - 1], ("tm", "net"), pairs)
        return [arrived[d] for d in range(1, n)]

    opening = [state]
    out = None
    for r in range(1, tm):
        state = lax.ppermute(state, "tm", [(r - 1, r), (r, r - 1)])
        arrived = swap(outgoing, [(r - 1, r), (r, r - 1)])
        before = []
        for s in range(steps):
            fix = r == 1 and s == 0
            if s > 0:
                arrived = swap(outgoing, [(0, 0), (r, r)] if r == 1 else [(r, r)])
            z = own(state, s)
            if s < steps - 1:
                state, *outgoing = join(z, s, fix, state, arrived, True, r)
                before.append(state)
            elif r < tm - 1:
                out, state, *outgoing = join(z, s, fix, state, arrived, True, r, opening, before, out, steps)
            else:
                (out,) = join(z, s, fix, state, arrived, False, r, opening, before, out, steps)
    return out


def solution(mesh):
    return jax.shard_map(
        local,
        mesh=mesh,
        in_specs=(
            P("tm", "net", None, None, None),
            P("net", None),
            P("tm", "net", None, None, None),
            P("net", None),
            P("net", None),
            P("net", None),
            P("cols"),
            P("tm", "cols"),
        ),
        out_specs=P("tm", "cols", "net"),
        check_vma=False,
    )
```

```python
import functools

import jax
import jax.numpy as jnp
from jax import lax
from jax.experimental import pallas as pl
from jax.experimental.pallas import tpu as pltpu
from jax.sharding import PartitionSpec as P

VMEM = pl.BlockSpec(memory_space=pltpu.VMEM)
SMEM = pl.BlockSpec(memory_space=pltpu.SMEM)
HBM = pl.BlockSpec(memory_space=pltpu.HBM)
ANY = pl.BlockSpec(memory_space=pl.ANY)
LIMIT = pltpu.CompilerParams(vmem_limit_bytes=16 * 1024 * 1024)
DMA = pltpu.SemaphoreType.DMA

STATE, LANE, BLOCK, AWAY, GAIN = 0, 1, 2, 3, 4
ROWS = 16


def times_transposed(rows, block):
    return lax.dot_general(rows, block, (((1,), (1,)), ((), ())), preferred_element_type=jnp.float32)


def injected(table, step, first_state, width):
    lane = lax.broadcasted_iota(jnp.int32, (table.shape[0], width), 1)
    hit = table[:, STATE : STATE + 1] == (lane + first_state).astype(jnp.float32)
    return jnp.where(hit, table[:, GAIN + step : GAIN + step + 1], 0.0)


def own_sum(i, state_ref, jac_ref, cols_ref, table, step):
    blocks, _, width = state_ref.shape
    first = (lax.axis_index("net") * blocks + i) * width
    kinds = jac_ref.shape[1]
    rows = [state_ref[i]] + [state_ref[cols_ref[k - 1, i]] for k in range(1, kinds)]
    row_blocks = [jac_ref[i, k] for k in range(kinds)]
    total = times_transposed(jnp.concatenate(rows, axis=1), jnp.concatenate(row_blocks, axis=1))
    return total + injected(table, step, first, width)


def add_coupled(incoming, block, live, recv, z_ref, keep=None):
    mask = lax.broadcasted_iota(jnp.int32, z_ref.shape[1:], 1) < live
    if keep is not None:
        mask = jnp.logical_and(mask, keep > 0.0)
    z_ref[recv] += jnp.where(mask, times_transposed(incoming, block), 0.0)


def table_row(send_ref, partition, width):
    lane = lax.broadcasted_iota(jnp.int32, (1, width), 1)
    row = jnp.zeros((1, width), jnp.float32)
    for e in range(lax.axis_size("net")):
        row = jnp.where(lane == e, send_ref[0, partition ^ e].astype(jnp.float32), row)
    return row


def kept(table, rows):
    away, block = table[:, AWAY : AWAY + 1], table[:, BLOCK : BLOCK + 1]
    sent = jnp.broadcast_to(rows[0], (table.shape[0], rows[0].shape[1]))
    for d in range(1, len(rows)):
        sent = jnp.where(away == float(d), rows[d], sent)
    lane = lax.broadcasted_iota(jnp.int32, sent.shape, 1).astype(jnp.float32)
    return jnp.where(jnp.logical_or(away == lane, block == sent), 1.0, 0.0)


def second_kernel(*refs):
    jac_hbm, iface_hbm, *small, table_ref, state_ref = refs[:10]
    n = lax.axis_size("net")
    me = lax.axis_index("net")
    outgoing, refs = refs[10 : 9 + n], refs[9 + n :]
    jac_ref, iface_ref, *loaded, first_ref, z_ref, sems = refs
    cols_ref, send_ref, recv_ref, live_ref, node_ref, gain_ref = loaded
    blocks, cols, width = state_ref.shape
    loads = [
        pltpu.make_async_copy(source, target, sems.at[i])
        for i, (source, target) in enumerate(
            zip([jac_hbm.at[1], iface_hbm.at[1, 0], *small], [jac_ref, iface_ref, *loaded])
        )
    ]
    here = lax.axis_index("tm") == 0

    @pl.when(here)
    def _():
        for load in loads[:2]:
            load.start()

    for load in loads[2:]:
        load.start()
    for load in loads[2:]:
        load.wait()
    node = node_ref[...]
    block_of = node // width
    rows = [
        node,
        node - block_of * width,
        block_of % blocks,
        (block_of // blocks) ^ me,
    ]
    steps = gain_ref.shape[0]
    fill = -(GAIN + steps) % 8
    rows = [row.astype(jnp.float32) for row in rows] + [gain_ref[...], jnp.zeros((fill, cols), jnp.float32)]
    table_ref[...] = jnp.concatenate(rows, axis=0).T

    @pl.when(here)
    def _():
        table = table_ref[...]
        for i in range(blocks):
            first_ref[i] = injected(table, 0, (me * blocks + i) * width, width).astype(first_ref.dtype)
        lane = lax.broadcasted_iota(jnp.int32, (cols, width), 1).astype(jnp.float32)
        shot = jnp.where(lane == table[:, LANE : LANE + 1], table[:, GAIN : GAIN + 1], 0.0)
        loads[0].wait()
        for i in range(blocks):
            z_ref[i] = own_sum(i, first_ref, jac_ref, cols_ref, table, 1)
        loads[1].wait()
        away, block = table[:, AWAY : AWAY + 1], table[:, BLOCK : BLOCK + 1]
        mine = jnp.logical_or(away != 0.0, block == send_ref[0, me].astype(jnp.float32))
        shot = jnp.where(mine, shot, 0.0)
        for d in range(n):
            q = me ^ d
            sent = jnp.where(away == float(d), shot, 0.0).astype(first_ref.dtype)
            add_coupled(sent, iface_ref[q], live_ref[0, q], recv_ref[0, q], z_ref)
        state_ref[...] = z_ref[...].astype(state_ref.dtype)
        for d in range(1, n):
            outgoing[d - 1][pl.ds(0, cols)] = state_ref[send_ref[0, me ^ d]]

    for d in range(1, n):
        row = table_row(send_ref, me ^ d, width).astype(state_ref.dtype)
        outgoing[d - 1][pl.ds(cols, ROWS)] = jnp.broadcast_to(row, (ROWS, width))


def write_start(states, first, out_ref, sems):
    copies = []
    for s, state_ref in enumerate(states, first):
        width = state_ref.shape[2]
        for i in range(state_ref.shape[0]):
            copies.append(
                pltpu.make_async_copy(state_ref.at[i], out_ref.at[s, :, pl.ds(i * width, width)], sems.at[s, i])
            )
    for copy in copies:
        copy.start()
    return copies


def own_kernel(step, state_ref, jac_ref, cols_ref, table_ref, z_ref):
    table = table_ref[...]
    for i in range(state_ref.shape[0]):
        z_ref[i] = own_sum(i, state_ref, jac_ref.at[step], cols_ref, table, step)


def first_states(states, jac_ref, iface_ref, cols_ref, send_ref, recv_ref, live_ref, table_ref, handed, made_ref, z_ref):
    n = lax.axis_size("net")
    blocks, cols, width = z_ref.shape
    table = table_ref[...]
    made_ref[0] = jnp.zeros_like(made_ref[0])
    for i in range(blocks):
        z_ref[i] = own_sum(i, made_ref.at[0], jac_ref.at[0], cols_ref, table, 0)
    for q in range(n):
        add_coupled(made_ref[0, 0], iface_ref[0, 0, q], live_ref[0, q], recv_ref[0, q], z_ref)
    made_ref[0] = z_ref[...].astype(made_ref.dtype)
    me = lax.axis_index("net")
    rows = [table_row(send_ref, me, width)]
    rows += [block[cols : cols + 1].astype(jnp.float32) for block in handed]
    keep = kept(table, rows)[:, 0:1]
    for i in range(blocks):
        made_ref[1, i] = jnp.where(keep > 0.0, states[0][i], jnp.zeros_like(states[0][i]))
    return [made_ref.at[0], made_ref.at[1], *states[1:]]


def join_kernel(step, fix, send, section, firsts, store, *refs):
    n = lax.axis_size("net")
    me = lax.axis_index("net")
    tm = lax.axis_index("tm")
    z_ref, iface_ref, send_ref, recv_ref, live_ref, table_ref, state_in_ref, *refs = refs
    arrived, refs = refs[: n - 1], refs[n - 1 :]
    acc_ref = refs.pop()
    blocks, cols, width = z_ref.shape
    before = []
    if store:
        sems = refs.pop()
        if firsts:
            made_ref = refs.pop()
            opening, refs = refs[:firsts], refs[firsts:]
            handed, refs = refs[: n - 1], refs[n - 1 :]
            jac_ref, cols_ref = refs.pop(0), refs.pop(0)
        before, refs = refs[: store - 1], refs[store - 1 :]
        if not firsts:
            refs.pop(0)
        out_ref = refs.pop(0)
    state_ref, *outgoing = refs

    def join():
        if store:
            copies = write_start(before, 0, out_ref, sems)
        if fix:
            table = table_ref[...]
            rows = [table_row(send_ref, me, width)]
            rows += [arrived[d - 1][cols : cols + 1].astype(jnp.float32) for d in range(1, n)]
            keep = kept(table, rows)
            for i in range(blocks):
                acc_ref[i] = jnp.where(keep[:, 0:1] > 0.0, z_ref[i], 0.0)
        else:
            acc_ref[...] = z_ref[...]
        for d in range(n):
            q = me ^ d
            block = arrived[d - 1][pl.ds(0, cols)] if d else state_in_ref[send_ref[0, me]]
            stands = keep[:, d : d + 1] if fix else None
            add_coupled(block, iface_ref[step, 0, q], live_ref[0, q], recv_ref[0, q], acc_ref, stands)
        state_ref[...] = acc_ref[...].astype(state_ref.dtype)
        if send:
            for d in range(1, n):
                outgoing[d - 1][...] = state_ref[send_ref[0, me ^ d]]
        if store:
            copies += write_start([state_ref], store - 1, out_ref, sems)
            for copy in copies:
                copy.wait()

    if store:
        pl.when(tm == section)(join)
    else:
        join()
    if firsts:

        @pl.when(tm == 0)
        def _():
            made = first_states(
                opening, jac_ref, iface_ref, cols_ref, send_ref, recv_ref, live_ref, table_ref, handed, made_ref, acc_ref
            )
            for copy in write_start(made, 0, out_ref, sems):
                copy.wait()


def local(jac, block_cols, iface_jac, iface_send, iface_recv, iface_live, ctrl_node, ctrl_gain):
    steps, blocks, kinds, width, _ = jac.shape
    cols = ctrl_node.shape[0]
    tm = lax.axis_size("tm")
    n = lax.axis_size("net")
    node = ctrl_node[None]
    near = block_cols.T
    bf16 = functools.partial(jax.ShapeDtypeStruct, dtype=jnp.bfloat16)
    f32 = functools.partial(jax.ShapeDtypeStruct, dtype=jnp.float32)
    whole, one = bf16((blocks, cols, width)), bf16((cols, width))
    table_rows = GAIN + steps + -(GAIN + steps) % 8
    written = bf16((steps, cols, blocks * width))

    pinned = [
        pltpu.with_memory_space_constraint(x, pltpu.HBM)
        for x in (jac, iface_jac, near, iface_send, iface_recv, iface_live, node, ctrl_gain)
    ]
    table, state, *outgoing = pl.pallas_call(
        second_kernel,
        out_shape=[f32((cols, table_rows)), whole] + [bf16((cols + ROWS, width))] * (n - 1),
        in_specs=[HBM] * len(pinned),
        out_specs=[VMEM] * (n + 1),
        scratch_shapes=[
            pltpu.VMEM((blocks, kinds, width, width), jnp.bfloat16),
            pltpu.VMEM((n, width, width), jnp.bfloat16),
            *[pltpu.SMEM(x.shape, x.dtype) for x in (near, iface_send, iface_recv, iface_live)],
            *[pltpu.VMEM(x.shape, x.dtype) for x in (node, ctrl_gain)],
            pltpu.VMEM(whole.shape, jnp.bfloat16),
            pltpu.VMEM(whole.shape, jnp.float32),
            DMA((len(pinned),)),
        ],
        compiler_params=LIMIT,
    )(*pinned)

    def own(state, step):
        return pl.pallas_call(
            functools.partial(own_kernel, step),
            out_shape=f32(whole.shape),
            in_specs=[VMEM, VMEM, SMEM, VMEM],
            out_specs=VMEM,
            compiler_params=LIMIT,
        )(state, jac, near, table)

    def join(z, step, fix, state, arrived, send, section, opening=(), before=(), out=None, store=0):
        arrays = [z, iface_jac, iface_send, iface_recv, iface_live, table, state]
        specs = [VMEM, VMEM, SMEM, SMEM, SMEM, VMEM, VMEM]
        arrays += arrived
        specs += [VMEM] * (n - 1)
        shapes = []
        scratch = [pltpu.VMEM(whole.shape, jnp.float32)]
        aliases = {}
        out_specs = []
        if store:
            if out is None:
                arrays += [*opening, *handed, jac, near]
                specs += [VMEM] * (len(opening) + n - 1) + [VMEM, SMEM]
            arrays += before
            specs += [VMEM] * len(before)
            if out is not None:
                aliases = {len(arrays): 0}
                arrays.append(out)
                specs.append(ANY)
            shapes.append(written)
            out_specs.append(ANY)
            scratch.insert(0, DMA((steps, blocks)))
            if out is None:
                scratch.insert(0, pltpu.VMEM((2, *whole.shape), jnp.bfloat16))
        if send:
            shapes += [whole] + [one] * (n - 1)
        else:
            scratch.insert(0, pltpu.VMEM(whole.shape, jnp.bfloat16))
        out_specs += [VMEM] * (len(shapes) - len(out_specs))
        firsts = len(opening) if store and out is None else 0
        return pl.pallas_call(
            functools.partial(join_kernel, step, fix, send, section, firsts, store),
            out_shape=shapes,
            in_specs=specs,
            out_specs=out_specs,
            input_output_aliases=aliases,
            scratch_shapes=scratch,
            compiler_params=LIMIT,
        )(*arrays)

    def swap(outgoing, sections):
        arrived = {}
        for d in reversed(range(1, n)):
            pairs = [(a * n + q, b * n + (q ^ d)) for a, b in sections for q in range(n)]
            arrived[d] = lax.ppermute(outgoing[d - 1], ("tm", "net"), pairs)
        return [arrived[d] for d in range(1, n)]

    opening = [state]
    out = None
    for r in range(1, tm):
        state = lax.ppermute(state, "tm", [(r - 1, r), (r, r - 1)])
        arrived = swap(outgoing, [(r - 1, r), (r, r - 1)])
        if r == 1:
            handed = arrived
        before = []
        for s in range(steps):
            fix = r == 1 and s == 0
            if s > 0:
                arrived = swap(outgoing, [(r, r)])
            z = own(state, s)
            if s < steps - 1:
                state, *outgoing = join(z, s, fix, state, arrived, True, r)
                before.append(state)
            elif r < tm - 1:
                out, state, *outgoing = join(z, s, fix, state, arrived, True, r, opening, before, out, steps)
            else:
                (out,) = join(z, s, fix, state, arrived, False, r, opening, before, out, steps)
    return out


def solution(mesh):
    return jax.shard_map(
        local,
        mesh=mesh,
        in_specs=(
            P("tm", "net", None, None, None),
            P("net", None),
            P("tm", "net", None, None, None),
            P("net", None),
            P("net", None),
            P("net", None),
            P("cols"),
            P("tm", "cols"),
        ),
        out_specs=P("tm", "cols", "net"),
        check_vma=False,
    )
```

```python
import functools

import jax
import jax.numpy as jnp
from jax import lax
from jax.experimental import pallas as pl
from jax.experimental.pallas import tpu as pltpu
from jax.sharding import PartitionSpec as P

VMEM = pl.BlockSpec(memory_space=pltpu.VMEM)
SMEM = pl.BlockSpec(memory_space=pltpu.SMEM)
HBM = pl.BlockSpec(memory_space=pltpu.HBM)
ANY = pl.BlockSpec(memory_space=pl.ANY)
LIMIT = pltpu.CompilerParams(vmem_limit_bytes=16 * 1024 * 1024)
DMA = pltpu.SemaphoreType.DMA

STATE, LANE, BLOCK, AWAY, GAIN = 0, 1, 2, 3, 4
ROWS = 16


def times_transposed(rows, block):
    return lax.dot_general(rows, block, (((1,), (1,)), ((), ())), preferred_element_type=jnp.float32)


def injected(table, step, first_state, width):
    lane = lax.broadcasted_iota(jnp.int32, (table.shape[0], width), 1)
    hit = table[:, STATE : STATE + 1] == (lane + first_state).astype(jnp.float32)
    return jnp.where(hit, table[:, GAIN + step : GAIN + step + 1], 0.0)


def own_sum(i, state_ref, jac_ref, cols_ref, table, step):
    blocks, _, width = state_ref.shape
    first = (lax.axis_index("net") * blocks + i) * width
    kinds = jac_ref.shape[1]
    rows = [state_ref[i]] + [state_ref[cols_ref[k - 1, i]] for k in range(1, kinds)]
    row_blocks = [jac_ref[i, k] for k in range(kinds)]
    total = times_transposed(jnp.concatenate(rows, axis=1), jnp.concatenate(row_blocks, axis=1))
    return total + injected(table, step, first, width)


def add_coupled(incoming, block, live, recv, z_ref, keep=None):
    mask = lax.broadcasted_iota(jnp.int32, z_ref.shape[1:], 1) < live
    if keep is not None:
        mask = jnp.logical_and(mask, keep > 0.0)
    z_ref[recv] += jnp.where(mask, times_transposed(incoming, block), 0.0)


def table_row(send_ref, partition, width):
    lane = lax.broadcasted_iota(jnp.int32, (1, width), 1)
    row = jnp.zeros((1, width), jnp.float32)
    for e in range(lax.axis_size("net")):
        row = jnp.where(lane == e, send_ref[0, partition ^ e].astype(jnp.float32), row)
    return row


def kept(table, rows):
    away, block = table[:, AWAY : AWAY + 1], table[:, BLOCK : BLOCK + 1]
    sent = jnp.broadcast_to(rows[0], (table.shape[0], rows[0].shape[1]))
    for d in range(1, len(rows)):
        sent = jnp.where(away == float(d), rows[d], sent)
    lane = lax.broadcasted_iota(jnp.int32, sent.shape, 1).astype(jnp.float32)
    return jnp.where(jnp.logical_or(away == lane, block == sent), 1.0, 0.0)


def second_kernel(*refs):
    jac_hbm, iface_hbm, *small, table_ref, state_ref = refs[:10]
    n = lax.axis_size("net")
    me = lax.axis_index("net")
    outgoing, refs = refs[10 : 9 + n], refs[9 + n :]
    jac_ref, iface_ref, *loaded, first_ref, z_ref, sems = refs
    cols_ref, send_ref, recv_ref, live_ref, node_ref, gain_ref = loaded
    blocks, cols, width = state_ref.shape
    loads = [
        pltpu.make_async_copy(source, target, sems.at[i])
        for i, (source, target) in enumerate(
            zip([jac_hbm.at[1], iface_hbm.at[1, 0], *small], [jac_ref, iface_ref, *loaded])
        )
    ]
    here = lax.axis_index("tm") == 0

    @pl.when(here)
    def _():
        for load in loads[:2]:
            load.start()

    for load in loads[2:]:
        load.start()
    for load in loads[2:]:
        load.wait()
    node = node_ref[...]
    block_of = node // width
    rows = [
        node,
        node - block_of * width,
        block_of % blocks,
        (block_of // blocks) ^ me,
    ]
    steps = gain_ref.shape[0]
    fill = -(GAIN + steps) % 8
    rows = [row.astype(jnp.float32) for row in rows] + [gain_ref[...], jnp.zeros((fill, cols), jnp.float32)]
    table_ref[...] = jnp.concatenate(rows, axis=0).T

    @pl.when(here)
    def _():
        table = table_ref[...]
        for i in range(blocks):
            first_ref[i] = injected(table, 0, (me * blocks + i) * width, width).astype(first_ref.dtype)
        lane = lax.broadcasted_iota(jnp.int32, (cols, width), 1).astype(jnp.float32)
        shot = jnp.where(lane == table[:, LANE : LANE + 1], table[:, GAIN : GAIN + 1], 0.0)
        loads[0].wait()
        for i in range(blocks):
            z_ref[i] = own_sum(i, first_ref, jac_ref, cols_ref, table, 1)
        loads[1].wait()
        away, block = table[:, AWAY : AWAY + 1], table[:, BLOCK : BLOCK + 1]
        mine = jnp.logical_or(away != 0.0, block == send_ref[0, me].astype(jnp.float32))
        shot = jnp.where(mine, shot, 0.0)
        for d in range(n):
            q = me ^ d
            sent = jnp.where(away == float(d), shot, 0.0).astype(first_ref.dtype)
            add_coupled(sent, iface_ref[q], live_ref[0, q], recv_ref[0, q], z_ref)
        state_ref[...] = z_ref[...].astype(state_ref.dtype)
        for d in range(1, n):
            outgoing[d - 1][pl.ds(0, cols)] = state_ref[send_ref[0, me ^ d]]

    for d in range(1, n):
        row = table_row(send_ref, me ^ d, width).astype(state_ref.dtype)
        outgoing[d - 1][pl.ds(cols, ROWS)] = jnp.broadcast_to(row, (ROWS, width))


def write_start(states, first, out_ref, sems):
    copies = []
    for s, state_ref in enumerate(states, first):
        width = state_ref.shape[2]
        for i in range(state_ref.shape[0]):
            copies.append(
                pltpu.make_async_copy(state_ref.at[i], out_ref.at[s, :, pl.ds(i * width, width)], sems.at[s, i])
            )
    for copy in copies:
        copy.start()
    return copies


def own_kernel(step, state_ref, jac_ref, cols_ref, table_ref, z_ref):
    table = table_ref[...]
    for i in range(state_ref.shape[0]):
        z_ref[i] = own_sum(i, state_ref, jac_ref.at[step], cols_ref, table, step)


def first_states(states, jac_ref, iface_ref, cols_ref, send_ref, recv_ref, live_ref, table_ref, handed, made_ref, z_ref):
    n = lax.axis_size("net")
    blocks, cols, width = z_ref.shape
    table = table_ref[...]
    made_ref[0] = jnp.zeros_like(made_ref[0])
    for i in range(blocks):
        z_ref[i] = own_sum(i, made_ref.at[0], jac_ref.at[0], cols_ref, table, 0)
    for q in range(n):
        add_coupled(made_ref[0, 0], iface_ref[0, 0, q], live_ref[0, q], recv_ref[0, q], z_ref)
    made_ref[0] = z_ref[...].astype(made_ref.dtype)
    me = lax.axis_index("net")
    rows = [table_row(send_ref, me, width)]
    rows += [block[cols : cols + 1].astype(jnp.float32) for block in handed]
    keep = kept(table, rows)[:, 0:1]
    for i in range(blocks):
        made_ref[1, i] = jnp.where(keep > 0.0, states[0][i], jnp.zeros_like(states[0][i]))
    return [made_ref.at[0], made_ref.at[1], *states[1:]]


def join_kernel(step, fix, send, section, firsts, store, *refs):
    n = lax.axis_size("net")
    me = lax.axis_index("net")
    tm = lax.axis_index("tm")
    z_ref, iface_ref, send_ref, recv_ref, live_ref, table_ref, state_in_ref, *refs = refs
    arrived, refs = refs[: n - 1], refs[n - 1 :]
    acc_ref = refs.pop()
    blocks, cols, width = z_ref.shape
    before = []
    if store:
        sems = refs.pop()
        if firsts:
            made_ref = refs.pop()
            opening, refs = refs[:firsts], refs[firsts:]
            handed, refs = refs[: n - 1], refs[n - 1 :]
            jac_ref, cols_ref = refs.pop(0), refs.pop(0)
        before, refs = refs[: store - 1], refs[store - 1 :]
        if not firsts:
            refs.pop(0)
        out_ref = refs.pop(0)
    state_ref, *outgoing = refs

    def join():
        if store:
            copies = write_start(before, 0, out_ref, sems)
        if fix:
            table = table_ref[...]
            rows = [table_row(send_ref, me, width)]
            rows += [arrived[d - 1][cols : cols + 1].astype(jnp.float32) for d in range(1, n)]
            keep = kept(table, rows)
            for i in range(blocks):
                acc_ref[i] = jnp.where(keep[:, 0:1] > 0.0, z_ref[i], 0.0)
        else:
            acc_ref[...] = z_ref[...]
        for d in range(n):
            q = me ^ d
            block = arrived[d - 1][pl.ds(0, cols)] if d else state_in_ref[send_ref[0, me]]
            stands = keep[:, d : d + 1] if fix else None
            add_coupled(block, iface_ref[step, 0, q], live_ref[0, q], recv_ref[0, q], acc_ref, stands)
        state_ref[...] = acc_ref[...].astype(state_ref.dtype)
        if send:
            for d in range(1, n):
                outgoing[d - 1][...] = state_ref[send_ref[0, me ^ d]]
        if store:
            copies += write_start([state_ref], store - 1, out_ref, sems)
            for copy in copies:
                copy.wait()

    if store:
        pl.when(tm == section)(join)
    else:
        join()
    if firsts:

        @pl.when(tm == 0)
        def _():
            made = first_states(
                opening, jac_ref, iface_ref, cols_ref, send_ref, recv_ref, live_ref, table_ref, handed, made_ref, acc_ref
            )
            for copy in write_start(made, 0, out_ref, sems):
                copy.wait()


def local(jac, block_cols, iface_jac, iface_send, iface_recv, iface_live, ctrl_node, ctrl_gain):
    steps, blocks, kinds, width, _ = jac.shape
    cols = ctrl_node.shape[0]
    tm = lax.axis_size("tm")
    n = lax.axis_size("net")
    node = ctrl_node[None]
    near = block_cols.T
    bf16 = functools.partial(jax.ShapeDtypeStruct, dtype=jnp.bfloat16)
    f32 = functools.partial(jax.ShapeDtypeStruct, dtype=jnp.float32)
    whole, one = bf16((blocks, cols, width)), bf16((cols, width))
    table_rows = GAIN + steps + -(GAIN + steps) % 8
    written = bf16((steps, cols, blocks * width))

    pinned = [
        pltpu.with_memory_space_constraint(x, pltpu.HBM)
        for x in (jac, iface_jac, near, iface_send, iface_recv, iface_live, node, ctrl_gain)
    ]
    table, state, *outgoing = pl.pallas_call(
        second_kernel,
        out_shape=[f32((cols, table_rows)), whole] + [bf16((cols + ROWS, width))] * (n - 1),
        in_specs=[HBM] * len(pinned),
        out_specs=[VMEM] * (n + 1),
        scratch_shapes=[
            pltpu.VMEM((blocks, kinds, width, width), jnp.bfloat16),
            pltpu.VMEM((n, width, width), jnp.bfloat16),
            *[pltpu.SMEM(x.shape, x.dtype) for x in (near, iface_send, iface_recv, iface_live)],
            *[pltpu.VMEM(x.shape, x.dtype) for x in (node, ctrl_gain)],
            pltpu.VMEM(whole.shape, jnp.bfloat16),
            pltpu.VMEM(whole.shape, jnp.float32),
            DMA((len(pinned),)),
        ],
        compiler_params=LIMIT,
    )(*pinned)

    def own(state, step):
        return pl.pallas_call(
            functools.partial(own_kernel, step),
            out_shape=f32(whole.shape),
            in_specs=[VMEM, VMEM, SMEM, VMEM],
            out_specs=VMEM,
            compiler_params=LIMIT,
        )(state, jac, near, table)

    def join(z, step, fix, state, arrived, send, section, opening=(), before=(), out=None, store=0):
        arrays = [z, iface_jac, iface_send, iface_recv, iface_live, table, state]
        specs = [VMEM, VMEM, SMEM, SMEM, SMEM, VMEM, VMEM]
        arrays += arrived
        specs += [VMEM] * (n - 1)
        shapes = []
        scratch = [pltpu.VMEM(whole.shape, jnp.float32)]
        aliases = {}
        out_specs = []
        if store:
            if out is None:
                arrays += [*opening, *handed, jac, near]
                specs += [VMEM] * (len(opening) + n - 1) + [VMEM, SMEM]
            arrays += before
            specs += [VMEM] * len(before)
            if out is not None:
                aliases = {len(arrays): 0}
                arrays.append(out)
                specs.append(ANY)
            shapes.append(written)
            out_specs.append(ANY)
            scratch.insert(0, DMA((steps, blocks)))
            if out is None:
                scratch.insert(0, pltpu.VMEM((2, *whole.shape), jnp.bfloat16))
        if send:
            shapes += [whole] + [one] * (n - 1)
        else:
            scratch.insert(0, pltpu.VMEM(whole.shape, jnp.bfloat16))
        out_specs += [VMEM] * (len(shapes) - len(out_specs))
        firsts = len(opening) if store and out is None else 0
        return pl.pallas_call(
            functools.partial(join_kernel, step, fix, send, section, firsts, store),
            out_shape=shapes,
            in_specs=specs,
            out_specs=out_specs,
            input_output_aliases=aliases,
            scratch_shapes=scratch,
            compiler_params=LIMIT,
        )(*arrays)

    def swap(block, first, second, d):
        other = {first: second, second: first}
        pairs = [(a * n + q, other[a] * n + (q ^ d) if a in other else a * n + q) for a in range(tm) for q in range(n)]
        return lax.ppermute(block, ("tm", "net"), pairs)

    def exchange(outgoing, first, second):
        arrived = [swap(outgoing[d - 1], first, second, d) for d in reversed(range(1, n))]
        return arrived[::-1]

    opening = [state]
    out = None
    for r in range(1, tm):
        state = swap(state, r - 1, r, 0)
        arrived = exchange(outgoing, r - 1, r)
        if r == 1:
            handed = arrived
        before = []
        for s in range(steps):
            fix = r == 1 and s == 0
            if s > 0:
                arrived = exchange(outgoing, r, r)
            z = own(state, s)
            if s < steps - 1:
                state, *outgoing = join(z, s, fix, state, arrived, True, r)
                before.append(state)
            elif r < tm - 1:
                out, state, *outgoing = join(z, s, fix, state, arrived, True, r, opening, before, out, steps)
            else:
                (out,) = join(z, s, fix, state, arrived, False, r, opening, before, out, steps)
    return out


def solution(mesh):
    return jax.shard_map(
        local,
        mesh=mesh,
        in_specs=(
            P("tm", "net", None, None, None),
            P("net", None),
            P("tm", "net", None, None, None),
            P("net", None),
            P("net", None),
            P("net", None),
            P("cols"),
            P("tm", "cols"),
        ),
        out_specs=P("tm", "cols", "net"),
        check_vma=False,
    )
```

```python
import functools

import jax
import jax.numpy as jnp
from jax import lax
from jax.experimental import pallas as pl
from jax.experimental.pallas import tpu as pltpu
from jax.sharding import PartitionSpec as P

VMEM = pl.BlockSpec(memory_space=pltpu.VMEM)
SMEM = pl.BlockSpec(memory_space=pltpu.SMEM)
HBM = pl.BlockSpec(memory_space=pltpu.HBM)
ANY = pl.BlockSpec(memory_space=pl.ANY)
LIMIT = pltpu.CompilerParams(vmem_limit_bytes=16 * 1024 * 1024)
DMA = pltpu.SemaphoreType.DMA

STATE, LANE, BLOCK, AWAY, GAIN = 0, 1, 2, 3, 4
ROWS = 16


def times_transposed(rows, block):
    return lax.dot_general(rows, block, (((1,), (1,)), ((), ())), preferred_element_type=jnp.float32)


def injected(table, step, first_state, width):
    lane = lax.broadcasted_iota(jnp.int32, (table.shape[0], width), 1)
    hit = table[:, STATE : STATE + 1] == (lane + first_state).astype(jnp.float32)
    return jnp.where(hit, table[:, GAIN + step : GAIN + step + 1], 0.0)


def own_sum(i, state_ref, jac_ref, cols_ref, table, step):
    blocks, _, width = state_ref.shape
    first = (lax.axis_index("net") * blocks + i) * width
    kinds = jac_ref.shape[1]
    rows = [state_ref[i]] + [state_ref[cols_ref[k - 1, i]] for k in range(1, kinds)]
    row_blocks = [jac_ref[i, k] for k in range(kinds)]
    total = times_transposed(jnp.concatenate(rows, axis=1), jnp.concatenate(row_blocks, axis=1))
    return total + injected(table, step, first, width)


def add_coupled(incoming, block, live, recv, z_ref, keep=None):
    mask = lax.broadcasted_iota(jnp.int32, z_ref.shape[1:], 1) < live
    if keep is not None:
        mask = jnp.logical_and(mask, keep > 0.0)
    z_ref[recv] += jnp.where(mask, times_transposed(incoming, block), 0.0)


def table_row(send_ref, partition, width):
    lane = lax.broadcasted_iota(jnp.int32, (1, width), 1)
    row = jnp.zeros((1, width), jnp.float32)
    for e in range(lax.axis_size("net")):
        row = jnp.where(lane == e, send_ref[0, partition ^ e].astype(jnp.float32), row)
    return row


def kept(table, rows):
    away, block = table[:, AWAY : AWAY + 1], table[:, BLOCK : BLOCK + 1]
    sent = jnp.broadcast_to(rows[0], (table.shape[0], rows[0].shape[1]))
    for d in range(1, len(rows)):
        sent = jnp.where(away == float(d), rows[d], sent)
    lane = lax.broadcasted_iota(jnp.int32, sent.shape, 1).astype(jnp.float32)
    return jnp.where(jnp.logical_or(away == lane, block == sent), 1.0, 0.0)


def second_kernel(*refs):
    jac_hbm, iface_hbm, *small, table_ref, state_ref = refs[:10]
    n = lax.axis_size("net")
    me = lax.axis_index("net")
    outgoing, refs = refs[10 : 9 + n], refs[9 + n :]
    jac_ref, iface_ref, *loaded, first_ref, z_ref, sems = refs
    cols_ref, send_ref, recv_ref, live_ref, node_ref, gain_ref = loaded
    blocks, cols, width = state_ref.shape
    loads = [
        pltpu.make_async_copy(source, target, sems.at[i])
        for i, (source, target) in enumerate(
            zip([jac_hbm.at[1], iface_hbm.at[1, 0], *small], [jac_ref, iface_ref, *loaded])
        )
    ]
    here = lax.axis_index("tm") == 0

    @pl.when(here)
    def _():
        for load in loads[:2]:
            load.start()

    for load in loads[2:]:
        load.start()
    for load in loads[2:]:
        load.wait()
    node = node_ref[...]
    block_of = node // width
    rows = [
        node,
        node - block_of * width,
        block_of % blocks,
        (block_of // blocks) ^ me,
    ]
    steps = gain_ref.shape[0]
    fill = -(GAIN + steps) % 8
    rows = [row.astype(jnp.float32) for row in rows] + [gain_ref[...], jnp.zeros((fill, cols), jnp.float32)]
    table_ref[...] = jnp.concatenate(rows, axis=0).T

    @pl.when(here)
    def _():
        table = table_ref[...]
        for i in range(blocks):
            first_ref[i] = injected(table, 0, (me * blocks + i) * width, width).astype(first_ref.dtype)
        lane = lax.broadcasted_iota(jnp.int32, (cols, width), 1).astype(jnp.float32)
        shot = jnp.where(lane == table[:, LANE : LANE + 1], table[:, GAIN : GAIN + 1], 0.0)
        loads[0].wait()
        for i in range(blocks):
            z_ref[i] = own_sum(i, first_ref, jac_ref, cols_ref, table, 1)
        loads[1].wait()
        away, block = table[:, AWAY : AWAY + 1], table[:, BLOCK : BLOCK + 1]
        mine = jnp.logical_or(away != 0.0, block == send_ref[0, me].astype(jnp.float32))
        shot = jnp.where(mine, shot, 0.0)
        for d in range(n):
            q = me ^ d
            sent = jnp.where(away == float(d), shot, 0.0).astype(first_ref.dtype)
            add_coupled(sent, iface_ref[q], live_ref[0, q], recv_ref[0, q], z_ref)
        state_ref[...] = z_ref[...].astype(state_ref.dtype)
        for d in range(1, n):
            outgoing[d - 1][pl.ds(0, cols)] = state_ref[send_ref[0, me ^ d]]

    for d in range(1, n):
        row = table_row(send_ref, me ^ d, width).astype(state_ref.dtype)
        outgoing[d - 1][pl.ds(cols, ROWS)] = jnp.broadcast_to(row, (ROWS, width))


def write_start(states, first, out_ref, sems):
    copies = []
    for s, state_ref in enumerate(states, first):
        width = state_ref.shape[2]
        for i in range(state_ref.shape[0]):
            copies.append(
                pltpu.make_async_copy(state_ref.at[i], out_ref.at[s, :, pl.ds(i * width, width)], sems.at[s, i])
            )
    for copy in copies:
        copy.start()
    return copies


def own_kernel(step, state_ref, jac_ref, cols_ref, table_ref, z_ref):
    table = table_ref[...]
    for i in range(state_ref.shape[0]):
        z_ref[i] = own_sum(i, state_ref, jac_ref.at[step], cols_ref, table, step)


def first_states(states, jac_ref, iface_ref, cols_ref, send_ref, recv_ref, live_ref, table_ref, handed, made_ref, z_ref):
    n = lax.axis_size("net")
    blocks, cols, width = z_ref.shape
    table = table_ref[...]
    made_ref[0] = jnp.zeros_like(made_ref[0])
    for i in range(blocks):
        z_ref[i] = own_sum(i, made_ref.at[0], jac_ref.at[0], cols_ref, table, 0)
    for q in range(n):
        add_coupled(made_ref[0, 0], iface_ref[0, 0, q], live_ref[0, q], recv_ref[0, q], z_ref)
    made_ref[0] = z_ref[...].astype(made_ref.dtype)
    me = lax.axis_index("net")
    rows = [table_row(send_ref, me, width)]
    rows += [block[cols : cols + 1].astype(jnp.float32) for block in handed]
    keep = kept(table, rows)[:, 0:1]
    for i in range(blocks):
        made_ref[1, i] = jnp.where(keep > 0.0, states[0][i], jnp.zeros_like(states[0][i]))
    return [made_ref.at[0], made_ref.at[1], *states[1:]]


def join_kernel(step, fix, send, section, firsts, store, *refs):
    n = lax.axis_size("net")
    me = lax.axis_index("net")
    tm = lax.axis_index("tm")
    z_ref, iface_ref, send_ref, recv_ref, live_ref, table_ref, state_in_ref, *refs = refs
    arrived, refs = refs[: n - 1], refs[n - 1 :]
    acc_ref = refs.pop()
    blocks, cols, width = z_ref.shape
    before = []
    if store:
        sems = refs.pop()
        if firsts:
            made_ref = refs.pop()
            opening, refs = refs[:firsts], refs[firsts:]
            handed, refs = refs[: n - 1], refs[n - 1 :]
            jac_ref, cols_ref = refs.pop(0), refs.pop(0)
        before, refs = refs[: store - 1], refs[store - 1 :]
        if not firsts:
            refs.pop(0)
        out_ref = refs.pop(0)
    state_ref, *outgoing = refs

    def join():
        if store:
            copies = write_start(before, 0, out_ref, sems)
        if fix:
            table = table_ref[...]
            rows = [table_row(send_ref, me, width)]
            rows += [arrived[d - 1][cols : cols + 1].astype(jnp.float32) for d in range(1, n)]
            keep = kept(table, rows)
            for i in range(blocks):
                acc_ref[i] = jnp.where(keep[:, 0:1] > 0.0, z_ref[i], 0.0)
        else:
            acc_ref[...] = z_ref[...]
        for d in range(n):
            q = me ^ d
            block = arrived[d - 1][pl.ds(0, cols)] if d else state_in_ref[send_ref[0, me]]
            stands = keep[:, d : d + 1] if fix else None
            add_coupled(block, iface_ref[step, 0, q], live_ref[0, q], recv_ref[0, q], acc_ref, stands)
        state_ref[...] = acc_ref[...].astype(state_ref.dtype)
        if send:
            for d in range(1, n):
                outgoing[d - 1][...] = state_ref[send_ref[0, me ^ d]]
        if store:
            copies += write_start([state_ref], store - 1, out_ref, sems)
            for copy in copies:
                copy.wait()

    if store:
        pl.when(tm == section)(join)
    else:
        join()
    if firsts:

        @pl.when(tm == 0)
        def _():
            made = first_states(
                opening, jac_ref, iface_ref, cols_ref, send_ref, recv_ref, live_ref, table_ref, handed, made_ref, acc_ref
            )
            for copy in write_start(made, 0, out_ref, sems):
                copy.wait()


def local(jac, block_cols, iface_jac, iface_send, iface_recv, iface_live, ctrl_node, ctrl_gain):
    steps, blocks, kinds, width, _ = jac.shape
    cols = ctrl_node.shape[0]
    tm = lax.axis_size("tm")
    n = lax.axis_size("net")
    col_parts = lax.axis_size("cols")
    node = ctrl_node[None]
    near = block_cols.T
    bf16 = functools.partial(jax.ShapeDtypeStruct, dtype=jnp.bfloat16)
    f32 = functools.partial(jax.ShapeDtypeStruct, dtype=jnp.float32)
    whole, one = bf16((blocks, cols, width)), bf16((cols, width))
    table_rows = GAIN + steps + -(GAIN + steps) % 8
    written = bf16((steps, cols, blocks * width))

    pinned = [
        pltpu.with_memory_space_constraint(x, pltpu.HBM)
        for x in (jac, iface_jac, near, iface_send, iface_recv, iface_live, node, ctrl_gain)
    ]
    table, state, *outgoing = pl.pallas_call(
        second_kernel,
        out_shape=[f32((cols, table_rows)), whole] + [bf16((cols + ROWS, width))] * (n - 1),
        in_specs=[HBM] * len(pinned),
        out_specs=[VMEM] * (n + 1),
        scratch_shapes=[
            pltpu.VMEM((blocks, kinds, width, width), jnp.bfloat16),
            pltpu.VMEM((n, width, width), jnp.bfloat16),
            *[pltpu.SMEM(x.shape, x.dtype) for x in (near, iface_send, iface_recv, iface_live)],
            *[pltpu.VMEM(x.shape, x.dtype) for x in (node, ctrl_gain)],
            pltpu.VMEM(whole.shape, jnp.bfloat16),
            pltpu.VMEM(whole.shape, jnp.float32),
            DMA((len(pinned),)),
        ],
        compiler_params=LIMIT,
    )(*pinned)

    def own(state, step):
        return pl.pallas_call(
            functools.partial(own_kernel, step),
            out_shape=f32(whole.shape),
            in_specs=[VMEM, VMEM, SMEM, VMEM],
            out_specs=VMEM,
            compiler_params=LIMIT,
        )(state, jac, near, table)

    def join(z, step, fix, state, arrived, send, section, opening=(), before=(), out=None, store=0):
        arrays = [z, iface_jac, iface_send, iface_recv, iface_live, table, state]
        specs = [VMEM, VMEM, SMEM, SMEM, SMEM, VMEM, VMEM]
        arrays += arrived
        specs += [VMEM] * (n - 1)
        shapes = []
        scratch = [pltpu.VMEM(whole.shape, jnp.float32)]
        aliases = {}
        out_specs = []
        if store:
            if out is None:
                arrays += [*opening, *handed, jac, near]
                specs += [VMEM] * (len(opening) + n - 1) + [VMEM, SMEM]
            arrays += before
            specs += [VMEM] * len(before)
            if out is not None:
                aliases = {len(arrays): 0}
                arrays.append(out)
                specs.append(ANY)
            shapes.append(written)
            out_specs.append(ANY)
            scratch.insert(0, DMA((steps, blocks)))
            if out is None:
                scratch.insert(0, pltpu.VMEM((2, *whole.shape), jnp.bfloat16))
        if send:
            shapes += [whole] + [one] * (n - 1)
        else:
            scratch.insert(0, pltpu.VMEM(whole.shape, jnp.bfloat16))
        out_specs += [VMEM] * (len(shapes) - len(out_specs))
        firsts = len(opening) if store and out is None else 0
        return pl.pallas_call(
            functools.partial(join_kernel, step, fix, send, section, firsts, store),
            out_shape=shapes,
            in_specs=specs,
            out_specs=out_specs,
            input_output_aliases=aliases,
            scratch_shapes=scratch,
            compiler_params=LIMIT,
        )(*arrays)

    def swap(block, first, second, d):
        other = {first: second, second: first}
        pairs = []
        for a in range(tm):
            for q in range(n):
                for c in range(col_parts):
                    to = (other[a] * n + (q ^ d)) * col_parts + c if a in other else (a * n + q) * col_parts + (c ^ 1)
                    pairs.append(((a * n + q) * col_parts + c, to))
        return lax.ppermute(block, ("tm", "net", "cols"), pairs)

    def exchange(outgoing, first, second):
        arrived = [swap(outgoing[d - 1], first, second, d) for d in reversed(range(1, n))]
        return arrived[::-1]

    opening = [state]
    out = None
    for r in range(1, tm):
        state = swap(state, r - 1, r, 0)
        arrived = exchange(outgoing, r - 1, r)
        if r == 1:
            handed = arrived
        before = []
        for s in range(steps):
            fix = r == 1 and s == 0
            if s > 0:
                arrived = exchange(outgoing, r, r)
            z = own(state, s)
            if s < steps - 1:
                state, *outgoing = join(z, s, fix, state, arrived, True, r)
                before.append(state)
            elif r < tm - 1:
                out, state, *outgoing = join(z, s, fix, state, arrived, True, r, opening, before, out, steps)
            else:
                (out,) = join(z, s, fix, state, arrived, False, r, opening, before, out, steps)
    return out


def solution(mesh):
    return jax.shard_map(
        local,
        mesh=mesh,
        in_specs=(
            P("tm", "net", None, None, None),
            P("net", None),
            P("tm", "net", None, None, None),
            P("net", None),
            P("net", None),
            P("net", None),
            P("cols"),
            P("tm", "cols"),
        ),
        out_specs=P("tm", "cols", "net"),
        check_vma=False,
    )
```

```python
import functools

import jax
import jax.numpy as jnp
from jax import lax
from jax.experimental import pallas as pl
from jax.experimental.pallas import tpu as pltpu
from jax.sharding import PartitionSpec as P

VMEM = pl.BlockSpec(memory_space=pltpu.VMEM)
SMEM = pl.BlockSpec(memory_space=pltpu.SMEM)
HBM = pl.BlockSpec(memory_space=pltpu.HBM)
ANY = pl.BlockSpec(memory_space=pl.ANY)
LIMIT = pltpu.CompilerParams(vmem_limit_bytes=16 * 1024 * 1024)
DMA = pltpu.SemaphoreType.DMA

STATE, LANE, BLOCK, AWAY, GAIN = 0, 1, 2, 3, 4
ROWS = 16


def times_transposed(rows, block):
    return lax.dot_general(rows, block, (((1,), (1,)), ((), ())), preferred_element_type=jnp.float32)


def injected(table, step, first_state, width):
    lane = lax.broadcasted_iota(jnp.int32, (table.shape[0], width), 1)
    hit = table[:, STATE : STATE + 1] == (lane + first_state).astype(jnp.float32)
    return jnp.where(hit, table[:, GAIN + step : GAIN + step + 1], 0.0)


def own_sum(i, state_ref, jac_ref, cols_ref, table, step):
    blocks, _, width = state_ref.shape
    first = (lax.axis_index("net") * blocks + i) * width
    kinds = jac_ref.shape[1]
    rows = [state_ref[i]] + [state_ref[cols_ref[k - 1, i]] for k in range(1, kinds)]
    row_blocks = [jac_ref[i, k] for k in range(kinds)]
    total = times_transposed(jnp.concatenate(rows, axis=1), jnp.concatenate(row_blocks, axis=1))
    return total + injected(table, step, first, width)


def add_coupled(incoming, block, live, recv, z_ref, keep=None):
    mask = lax.broadcasted_iota(jnp.int32, z_ref.shape[1:], 1) < live
    if keep is not None:
        mask = jnp.logical_and(mask, keep > 0.0)
    z_ref[recv] += jnp.where(mask, times_transposed(incoming, block), 0.0)


def table_row(send_ref, partition, width):
    lane = lax.broadcasted_iota(jnp.int32, (1, width), 1)
    row = jnp.zeros((1, width), jnp.float32)
    for e in range(lax.axis_size("net")):
        row = jnp.where(lane == e, send_ref[0, partition ^ e].astype(jnp.float32), row)
    return row


def kept(table, rows):
    away, block = table[:, AWAY : AWAY + 1], table[:, BLOCK : BLOCK + 1]
    sent = jnp.broadcast_to(rows[0], (table.shape[0], rows[0].shape[1]))
    for d in range(1, len(rows)):
        sent = jnp.where(away == float(d), rows[d], sent)
    lane = lax.broadcasted_iota(jnp.int32, sent.shape, 1).astype(jnp.float32)
    return jnp.where(jnp.logical_or(away == lane, block == sent), 1.0, 0.0)


def second_kernel(*refs):
    jac_hbm, iface_hbm, *small, table_ref, state_ref = refs[:10]
    n = lax.axis_size("net")
    me = lax.axis_index("net")
    outgoing, refs = refs[10 : 9 + n], refs[9 + n :]
    jac_ref, iface_ref, *loaded, first_ref, z_ref, sems = refs
    cols_ref, send_ref, recv_ref, live_ref, node_ref, gain_ref = loaded
    blocks, cols, width = state_ref.shape
    loads = [
        pltpu.make_async_copy(source, target, sems.at[i])
        for i, (source, target) in enumerate(
            zip([jac_hbm.at[1], iface_hbm.at[1, 0], *small], [jac_ref, iface_ref, *loaded])
        )
    ]
    here = lax.axis_index("tm") == 0

    @pl.when(here)
    def _():
        for load in loads[:2]:
            load.start()

    for load in loads[2:]:
        load.start()
    for load in loads[2:]:
        load.wait()
    node = node_ref[...]
    block_of = node // width
    rows = [
        node,
        node - block_of * width,
        block_of % blocks,
        (block_of // blocks) ^ me,
    ]
    steps = gain_ref.shape[0]
    fill = -(GAIN + steps) % 8
    rows = [row.astype(jnp.float32) for row in rows] + [gain_ref[...], jnp.zeros((fill, cols), jnp.float32)]
    table_ref[...] = jnp.concatenate(rows, axis=0).T

    @pl.when(here)
    def _():
        table = table_ref[...]
        for i in range(blocks):
            first_ref[i] = injected(table, 0, (me * blocks + i) * width, width).astype(first_ref.dtype)
        lane = lax.broadcasted_iota(jnp.int32, (cols, width), 1).astype(jnp.float32)
        shot = jnp.where(lane == table[:, LANE : LANE + 1], table[:, GAIN : GAIN + 1], 0.0)
        loads[0].wait()
        for i in range(blocks):
            z_ref[i] = own_sum(i, first_ref, jac_ref, cols_ref, table, 1)
        loads[1].wait()
        away, block = table[:, AWAY : AWAY + 1], table[:, BLOCK : BLOCK + 1]
        mine = jnp.logical_or(away != 0.0, block == send_ref[0, me].astype(jnp.float32))
        shot = jnp.where(mine, shot, 0.0)
        for d in range(n):
            q = me ^ d
            sent = jnp.where(away == float(d), shot, 0.0).astype(first_ref.dtype)
            add_coupled(sent, iface_ref[q], live_ref[0, q], recv_ref[0, q], z_ref)
        state_ref[...] = z_ref[...].astype(state_ref.dtype)
        for d in range(1, n):
            outgoing[d - 1][pl.ds(0, cols)] = state_ref[send_ref[0, me ^ d]]

    for d in range(1, n):
        row = table_row(send_ref, me ^ d, width).astype(state_ref.dtype)
        outgoing[d - 1][pl.ds(cols, ROWS)] = jnp.broadcast_to(row, (ROWS, width))


def write_start(states, first, out_ref, sems):
    copies = []
    for s, state_ref in enumerate(states, first):
        width = state_ref.shape[2]
        for i in range(state_ref.shape[0]):
            copies.append(
                pltpu.make_async_copy(state_ref.at[i], out_ref.at[s, :, pl.ds(i * width, width)], sems.at[s, i])
            )
    for copy in copies:
        copy.start()
    return copies


def own_kernel(step, state_ref, jac_ref, cols_ref, table_ref, z_ref):
    table = table_ref[...]
    for i in range(state_ref.shape[0]):
        z_ref[i] = own_sum(i, state_ref, jac_ref.at[step], cols_ref, table, step)


def first_states(states, jac_ref, iface_ref, cols_ref, send_ref, recv_ref, live_ref, table_ref, handed, made_ref, z_ref):
    n = lax.axis_size("net")
    blocks, cols, width = z_ref.shape
    table = table_ref[...]
    made_ref[0] = jnp.zeros_like(made_ref[0])
    for i in range(blocks):
        z_ref[i] = own_sum(i, made_ref.at[0], jac_ref.at[0], cols_ref, table, 0)
    for q in range(n):
        add_coupled(made_ref[0, 0], iface_ref[0, 0, q], live_ref[0, q], recv_ref[0, q], z_ref)
    made_ref[0] = z_ref[...].astype(made_ref.dtype)
    me = lax.axis_index("net")
    rows = [table_row(send_ref, me, width)]
    rows += [block[cols : cols + 1].astype(jnp.float32) for block in handed]
    keep = kept(table, rows)[:, 0:1]
    for i in range(blocks):
        made_ref[1, i] = jnp.where(keep > 0.0, states[0][i], jnp.zeros_like(states[0][i]))
    return [made_ref.at[0], made_ref.at[1], *states[1:]]


def join_kernel(step, fix, send, section, firsts, store, *refs):
    n = lax.axis_size("net")
    me = lax.axis_index("net")
    tm = lax.axis_index("tm")
    if fix:
        jac_ref, cols_ref, *refs = refs
    else:
        z_ref, *refs = refs
    iface_ref, send_ref, recv_ref, live_ref, table_ref, state_in_ref, *refs = refs
    arrived, refs = refs[: n - 1], refs[n - 1 :]
    acc_ref = refs.pop()
    blocks, cols, width = acc_ref.shape
    before = []
    if store:
        sems = refs.pop()
        if firsts:
            made_ref = refs.pop()
            opening, refs = refs[:firsts], refs[firsts:]
            handed, refs = refs[: n - 1], refs[n - 1 :]
            jac_ref, cols_ref = refs.pop(0), refs.pop(0)
        before, refs = refs[: store - 1], refs[store - 1 :]
        if not firsts:
            refs.pop(0)
        out_ref = refs.pop(0)
    state_ref, *outgoing = refs

    def join():
        if store:
            copies = write_start(before, 0, out_ref, sems)
        if fix:
            table = table_ref[...]
            rows = [table_row(send_ref, me, width)]
            rows += [arrived[d - 1][cols : cols + 1].astype(jnp.float32) for d in range(1, n)]
            keep = kept(table, rows)
            for i in range(blocks):
                own = own_sum(i, state_in_ref, jac_ref.at[step], cols_ref, table, step)
                acc_ref[i] = jnp.where(keep[:, 0:1] > 0.0, own, 0.0)
        else:
            acc_ref[...] = z_ref[...]
        for d in range(n):
            q = me ^ d
            block = arrived[d - 1][pl.ds(0, cols)] if d else state_in_ref[send_ref[0, me]]
            stands = keep[:, d : d + 1] if fix else None
            add_coupled(block, iface_ref[step, 0, q], live_ref[0, q], recv_ref[0, q], acc_ref, stands)
        state_ref[...] = acc_ref[...].astype(state_ref.dtype)
        if send:
            for d in range(1, n):
                outgoing[d - 1][...] = state_ref[send_ref[0, me ^ d]]
        if store:
            copies += write_start([state_ref], store - 1, out_ref, sems)
            for copy in copies:
                copy.wait()

    if store:
        pl.when(tm == section)(join)
    else:
        join()
    if firsts:

        @pl.when(tm == 0)
        def _():
            made = first_states(
                opening, jac_ref, iface_ref, cols_ref, send_ref, recv_ref, live_ref, table_ref, handed, made_ref, acc_ref
            )
            for copy in write_start(made, 0, out_ref, sems):
                copy.wait()


def local(jac, block_cols, iface_jac, iface_send, iface_recv, iface_live, ctrl_node, ctrl_gain):
    steps, blocks, kinds, width, _ = jac.shape
    cols = ctrl_node.shape[0]
    tm = lax.axis_size("tm")
    n = lax.axis_size("net")
    col_parts = lax.axis_size("cols")
    node = ctrl_node[None]
    near = block_cols.T
    bf16 = functools.partial(jax.ShapeDtypeStruct, dtype=jnp.bfloat16)
    f32 = functools.partial(jax.ShapeDtypeStruct, dtype=jnp.float32)
    whole, one = bf16((blocks, cols, width)), bf16((cols, width))
    table_rows = GAIN + steps + -(GAIN + steps) % 8
    written = bf16((steps, cols, blocks * width))

    pinned = [
        pltpu.with_memory_space_constraint(x, pltpu.HBM)
        for x in (jac, iface_jac, near, iface_send, iface_recv, iface_live, node, ctrl_gain)
    ]
    table, state, *outgoing = pl.pallas_call(
        second_kernel,
        out_shape=[f32((cols, table_rows)), whole] + [bf16((cols + ROWS, width))] * (n - 1),
        in_specs=[HBM] * len(pinned),
        out_specs=[VMEM] * (n + 1),
        scratch_shapes=[
            pltpu.VMEM((blocks, kinds, width, width), jnp.bfloat16),
            pltpu.VMEM((n, width, width), jnp.bfloat16),
            *[pltpu.SMEM(x.shape, x.dtype) for x in (near, iface_send, iface_recv, iface_live)],
            *[pltpu.VMEM(x.shape, x.dtype) for x in (node, ctrl_gain)],
            pltpu.VMEM(whole.shape, jnp.bfloat16),
            pltpu.VMEM(whole.shape, jnp.float32),
            DMA((len(pinned),)),
        ],
        compiler_params=LIMIT,
    )(*pinned)

    def own(state, step):
        return pl.pallas_call(
            functools.partial(own_kernel, step),
            out_shape=f32(whole.shape),
            in_specs=[VMEM, VMEM, SMEM, VMEM],
            out_specs=VMEM,
            compiler_params=LIMIT,
        )(state, jac, near, table)

    def join(z, step, fix, state, arrived, send, section, opening=(), before=(), out=None, store=0):
        arrays = [*([jac, near] if fix else [z]), iface_jac, iface_send, iface_recv, iface_live, table, state]
        specs = [*([VMEM, SMEM] if fix else [VMEM]), VMEM, SMEM, SMEM, SMEM, VMEM, VMEM]
        arrays += arrived
        specs += [VMEM] * (n - 1)
        shapes = []
        scratch = [pltpu.VMEM(whole.shape, jnp.float32)]
        aliases = {}
        out_specs = []
        if store:
            if out is None:
                arrays += [*opening, *handed, jac, near]
                specs += [VMEM] * (len(opening) + n - 1) + [VMEM, SMEM]
            arrays += before
            specs += [VMEM] * len(before)
            if out is not None:
                aliases = {len(arrays): 0}
                arrays.append(out)
                specs.append(ANY)
            shapes.append(written)
            out_specs.append(ANY)
            scratch.insert(0, DMA((steps, blocks)))
            if out is None:
                scratch.insert(0, pltpu.VMEM((2, *whole.shape), jnp.bfloat16))
        if send:
            shapes += [whole] + [one] * (n - 1)
        else:
            scratch.insert(0, pltpu.VMEM(whole.shape, jnp.bfloat16))
        out_specs += [VMEM] * (len(shapes) - len(out_specs))
        firsts = len(opening) if store and out is None else 0
        return pl.pallas_call(
            functools.partial(join_kernel, step, fix, send, section, firsts, store),
            out_shape=shapes,
            in_specs=specs,
            out_specs=out_specs,
            input_output_aliases=aliases,
            scratch_shapes=scratch,
            compiler_params=LIMIT,
        )(*arrays)

    def swap(block, first, second, d):
        other = {first: second, second: first}
        pairs = []
        for a in range(tm):
            for q in range(n):
                for c in range(col_parts):
                    to = (other[a] * n + (q ^ d)) * col_parts + c if a in other else (a * n + q) * col_parts + (c ^ 1)
                    pairs.append(((a * n + q) * col_parts + c, to))
        return lax.ppermute(block, ("tm", "net", "cols"), pairs)

    def exchange(outgoing, first, second):
        arrived = [swap(outgoing[d - 1], first, second, d) for d in reversed(range(1, n))]
        return arrived[::-1]

    opening = [state]
    out = None
    for r in range(1, tm):
        arrived = exchange(outgoing, r - 1, r)
        state = swap(state, r - 1, r, 0)
        if r == 1:
            handed = arrived
        before = []
        for s in range(steps):
            fix = r == 1 and s == 0
            if s > 0:
                arrived = exchange(outgoing, r, r)
            z = None if fix else own(state, s)
            if s < steps - 1:
                state, *outgoing = join(z, s, fix, state, arrived, True, r)
                before.append(state)
            elif r < tm - 1:
                out, state, *outgoing = join(z, s, fix, state, arrived, True, r, opening, before, out, steps)
            else:
                (out,) = join(z, s, fix, state, arrived, False, r, opening, before, out, steps)
    return out


def solution(mesh):
    return jax.shard_map(
        local,
        mesh=mesh,
        in_specs=(
            P("tm", "net", None, None, None),
            P("net", None),
            P("tm", "net", None, None, None),
            P("net", None),
            P("net", None),
            P("net", None),
            P("cols"),
            P("tm", "cols"),
        ),
        out_specs=P("tm", "cols", "net"),
        check_vma=False,
    )
```

```python
import functools

import jax
import jax.numpy as jnp
from jax import lax
from jax.experimental import pallas as pl
from jax.experimental.pallas import tpu as pltpu
from jax.sharding import PartitionSpec as P

VMEM = pl.BlockSpec(memory_space=pltpu.VMEM)
SMEM = pl.BlockSpec(memory_space=pltpu.SMEM)
HBM = pl.BlockSpec(memory_space=pltpu.HBM)
ANY = pl.BlockSpec(memory_space=pl.ANY)
LIMIT = pltpu.CompilerParams(vmem_limit_bytes=16 * 1024 * 1024)
DMA = pltpu.SemaphoreType.DMA

STATE, LANE, BLOCK, AWAY, GAIN = 0, 1, 2, 3, 4
ROWS = 16


def times_transposed(rows, block):
    return lax.dot_general(rows, block, (((1,), (1,)), ((), ())), preferred_element_type=jnp.float32)


def injected(table, step, first_state, width):
    lane = lax.broadcasted_iota(jnp.int32, (table.shape[0], width), 1)
    hit = table[:, STATE : STATE + 1] == (lane + first_state).astype(jnp.float32)
    return jnp.where(hit, table[:, GAIN + step : GAIN + step + 1], 0.0)


def own_sum(i, state_ref, jac_ref, cols_ref, table, step):
    blocks, _, width = state_ref.shape
    first = (lax.axis_index("net") * blocks + i) * width
    kinds = jac_ref.shape[1]
    rows = [state_ref[i]] + [state_ref[cols_ref[k - 1, i]] for k in range(1, kinds)]
    row_blocks = [jac_ref[i, k] for k in range(kinds)]
    total = times_transposed(jnp.concatenate(rows, axis=1), jnp.concatenate(row_blocks, axis=1))
    return total + injected(table, step, first, width)


def add_coupled(incoming, block, live, recv, z_ref, keep=None):
    mask = lax.broadcasted_iota(jnp.int32, z_ref.shape[1:], 1) < live
    if keep is not None:
        mask = jnp.logical_and(mask, keep > 0.0)
    z_ref[recv] += jnp.where(mask, times_transposed(incoming, block), 0.0)


def table_row(send_ref, partition, width):
    lane = lax.broadcasted_iota(jnp.int32, (1, width), 1)
    row = jnp.zeros((1, width), jnp.float32)
    for e in range(lax.axis_size("net")):
        row = jnp.where(lane == e, send_ref[0, partition ^ e].astype(jnp.float32), row)
    return row


def kept(table, rows):
    away, block = table[:, AWAY : AWAY + 1], table[:, BLOCK : BLOCK + 1]
    sent = jnp.broadcast_to(rows[0], (table.shape[0], rows[0].shape[1]))
    for d in range(1, len(rows)):
        sent = jnp.where(away == float(d), rows[d], sent)
    lane = lax.broadcasted_iota(jnp.int32, sent.shape, 1).astype(jnp.float32)
    return jnp.where(jnp.logical_or(away == lane, block == sent), 1.0, 0.0)


def second_kernel(*refs):
    jac_hbm, iface_hbm, *small, table_ref = refs[:9]
    n = lax.axis_size("net")
    me = lax.axis_index("net")
    jac_ref, iface_ref, *loaded, first_ref, state_ref, z_ref, sems = refs[-12:]
    cols_ref, send_ref, recv_ref, live_ref, node_ref, gain_ref = loaded
    blocks, cols, width = state_ref.shape
    states, outgoing = refs[9 : 9 + blocks], refs[9 + blocks : -12]
    loads = [
        pltpu.make_async_copy(source, target, sems.at[i])
        for i, (source, target) in enumerate(
            zip([jac_hbm.at[1], iface_hbm.at[1, 0], *small], [jac_ref, iface_ref, *loaded])
        )
    ]
    here = lax.axis_index("tm") == 0

    @pl.when(here)
    def _():
        for load in loads[:2]:
            load.start()

    for load in loads[2:]:
        load.start()
    for load in loads[2:]:
        load.wait()
    node = node_ref[...]
    block_of = node // width
    rows = [
        node,
        node - block_of * width,
        block_of % blocks,
        (block_of // blocks) ^ me,
    ]
    steps = gain_ref.shape[0]
    fill = -(GAIN + steps) % 8
    rows = [row.astype(jnp.float32) for row in rows] + [gain_ref[...], jnp.zeros((fill, cols), jnp.float32)]
    table_ref[...] = jnp.concatenate(rows, axis=0).T

    @pl.when(here)
    def _():
        table = table_ref[...]
        for i in range(blocks):
            first_ref[i] = injected(table, 0, (me * blocks + i) * width, width).astype(first_ref.dtype)
        lane = lax.broadcasted_iota(jnp.int32, (cols, width), 1).astype(jnp.float32)
        shot = jnp.where(lane == table[:, LANE : LANE + 1], table[:, GAIN : GAIN + 1], 0.0)
        loads[0].wait()
        for i in range(blocks):
            z_ref[i] = own_sum(i, first_ref, jac_ref, cols_ref, table, 1)
        loads[1].wait()
        away, block = table[:, AWAY : AWAY + 1], table[:, BLOCK : BLOCK + 1]
        mine = jnp.logical_or(away != 0.0, block == send_ref[0, me].astype(jnp.float32))
        shot = jnp.where(mine, shot, 0.0)
        for d in range(n):
            q = me ^ d
            sent = jnp.where(away == float(d), shot, 0.0).astype(first_ref.dtype)
            add_coupled(sent, iface_ref[q], live_ref[0, q], recv_ref[0, q], z_ref)
        state_ref[...] = z_ref[...].astype(state_ref.dtype)
        for i in range(blocks):
            states[i][...] = state_ref[i]
        for d in range(1, n):
            outgoing[d - 1][pl.ds(0, cols)] = state_ref[send_ref[0, me ^ d]]

    for d in range(1, n):
        row = table_row(send_ref, me ^ d, width).astype(state_ref.dtype)
        outgoing[d - 1][pl.ds(cols, ROWS)] = jnp.broadcast_to(row, (ROWS, width))


def write_start(states, first, out_ref, sems):
    copies = []
    for s, state_ref in enumerate(states, first):
        width = state_ref.shape[2]
        for i in range(state_ref.shape[0]):
            copies.append(
                pltpu.make_async_copy(state_ref.at[i], out_ref.at[s, :, pl.ds(i * width, width)], sems.at[s, i])
            )
    for copy in copies:
        copy.start()
    return copies


def own_kernel(step, state_ref, jac_ref, cols_ref, table_ref, z_ref):
    table = table_ref[...]
    for i in range(state_ref.shape[0]):
        z_ref[i] = own_sum(i, state_ref, jac_ref.at[step], cols_ref, table, step)


def first_states(second, jac_ref, iface_ref, cols_ref, send_ref, recv_ref, live_ref, table_ref, handed, made_ref, z_ref):
    n = lax.axis_size("net")
    blocks, cols, width = z_ref.shape
    table = table_ref[...]
    made_ref[0] = jnp.zeros_like(made_ref[0])
    for i in range(blocks):
        z_ref[i] = own_sum(i, made_ref.at[0], jac_ref.at[0], cols_ref, table, 0)
    for q in range(n):
        add_coupled(made_ref[0, 0], iface_ref[0, 0, q], live_ref[0, q], recv_ref[0, q], z_ref)
    made_ref[0] = z_ref[...].astype(made_ref.dtype)
    me = lax.axis_index("net")
    rows = [table_row(send_ref, me, width)]
    rows += [block[cols : cols + 1].astype(jnp.float32) for block in handed]
    keep = kept(table, rows)[:, 0:1]
    for i in range(blocks):
        made_ref[1, i] = jnp.where(keep > 0.0, second[i][...], jnp.zeros_like(second[i]))
    return [made_ref.at[0], made_ref.at[1]]


def join_kernel(step, fix, send, section, firsts, store, *refs):
    n = lax.axis_size("net")
    me = lax.axis_index("net")
    tm = lax.axis_index("tm")
    if fix:
        jac_ref, cols_ref, *refs = refs
    else:
        z_ref, *refs = refs
    iface_ref, send_ref, recv_ref, live_ref, table_ref, *refs = refs
    acc_ref = refs.pop()
    blocks, cols, width = acc_ref.shape
    if fix:
        state_in_ref = refs.pop()
        for i in range(blocks):
            state_in_ref[i] = refs.pop(0)[...]
    else:
        state_in_ref = refs.pop(0)
    arrived, refs = refs[: n - 1], refs[n - 1 :]
    before = []
    if store:
        sems = refs.pop()
        if firsts:
            made_ref = refs.pop()
            opening, refs = refs[:firsts], refs[firsts:]
            handed, refs = refs[: n - 1], refs[n - 1 :]
            jac_ref, cols_ref = refs.pop(0), refs.pop(0)
        before, refs = refs[: store - 1], refs[store - 1 :]
        if not firsts:
            refs.pop(0)
        out_ref = refs.pop(0)
    state_ref, *outgoing = refs

    def join():
        if store:
            copies = write_start(before, 0, out_ref, sems)
        if fix:
            table = table_ref[...]
            rows = [table_row(send_ref, me, width)]
            rows += [arrived[d - 1][cols : cols + 1].astype(jnp.float32) for d in range(1, n)]
            keep = kept(table, rows)
            for i in range(blocks):
                own = own_sum(i, state_in_ref, jac_ref.at[step], cols_ref, table, step)
                acc_ref[i] = jnp.where(keep[:, 0:1] > 0.0, own, 0.0)
        else:
            acc_ref[...] = z_ref[...]
        for d in range(n):
            q = me ^ d
            block = arrived[d - 1][pl.ds(0, cols)] if d else state_in_ref[send_ref[0, me]]
            stands = keep[:, d : d + 1] if fix else None
            add_coupled(block, iface_ref[step, 0, q], live_ref[0, q], recv_ref[0, q], acc_ref, stands)
        state_ref[...] = acc_ref[...].astype(state_ref.dtype)
        if send:
            for d in range(1, n):
                outgoing[d - 1][...] = state_ref[send_ref[0, me ^ d]]
        if store:
            copies += write_start([state_ref], store - 1, out_ref, sems)
            for copy in copies:
                copy.wait()

    if store:
        pl.when(tm == section)(join)
    else:
        join()
    if firsts:

        @pl.when(tm == 0)
        def _():
            made = first_states(
                opening, jac_ref, iface_ref, cols_ref, send_ref, recv_ref, live_ref, table_ref, handed, made_ref, acc_ref
            )
            for copy in write_start(made, 0, out_ref, sems):
                copy.wait()


def local(jac, block_cols, iface_jac, iface_send, iface_recv, iface_live, ctrl_node, ctrl_gain):
    steps, blocks, kinds, width, _ = jac.shape
    cols = ctrl_node.shape[0]
    tm = lax.axis_size("tm")
    n = lax.axis_size("net")
    col_parts = lax.axis_size("cols")
    node = ctrl_node[None]
    near = block_cols.T
    bf16 = functools.partial(jax.ShapeDtypeStruct, dtype=jnp.bfloat16)
    f32 = functools.partial(jax.ShapeDtypeStruct, dtype=jnp.float32)
    whole, one = bf16((blocks, cols, width)), bf16((cols, width))
    table_rows = GAIN + steps + -(GAIN + steps) % 8
    written = bf16((steps, cols, blocks * width))

    pinned = [
        pltpu.with_memory_space_constraint(x, pltpu.HBM)
        for x in (jac, iface_jac, near, iface_send, iface_recv, iface_live, node, ctrl_gain)
    ]
    table, *outgoing = pl.pallas_call(
        second_kernel,
        out_shape=[f32((cols, table_rows))] + [one] * blocks + [bf16((cols + ROWS, width))] * (n - 1),
        in_specs=[HBM] * len(pinned),
        out_specs=[VMEM] * (blocks + n),
        scratch_shapes=[
            pltpu.VMEM((blocks, kinds, width, width), jnp.bfloat16),
            pltpu.VMEM((n, width, width), jnp.bfloat16),
            *[pltpu.SMEM(x.shape, x.dtype) for x in (near, iface_send, iface_recv, iface_live)],
            *[pltpu.VMEM(x.shape, x.dtype) for x in (node, ctrl_gain)],
            pltpu.VMEM(whole.shape, jnp.bfloat16),
            pltpu.VMEM(whole.shape, jnp.bfloat16),
            pltpu.VMEM(whole.shape, jnp.float32),
            DMA((len(pinned),)),
        ],
        compiler_params=LIMIT,
    )(*pinned)

    def own(state, step):
        return pl.pallas_call(
            functools.partial(own_kernel, step),
            out_shape=f32(whole.shape),
            in_specs=[VMEM, VMEM, SMEM, VMEM],
            out_specs=VMEM,
            compiler_params=LIMIT,
        )(state, jac, near, table)

    def join(z, step, fix, state, arrived, send, section, opening=(), before=(), out=None, store=0):
        arrays = [*([jac, near] if fix else [z]), iface_jac, iface_send, iface_recv, iface_live, table]
        specs = [*([VMEM, SMEM] if fix else [VMEM]), VMEM, SMEM, SMEM, SMEM, VMEM]
        states = state if fix else [state]
        arrays += states
        specs += [VMEM] * len(states)
        arrays += arrived
        specs += [VMEM] * (n - 1)
        shapes = []
        scratch = [pltpu.VMEM(whole.shape, jnp.bfloat16)] if fix else []
        scratch.append(pltpu.VMEM(whole.shape, jnp.float32))
        aliases = {}
        out_specs = []
        if store:
            if out is None:
                arrays += [*opening, *handed, jac, near]
                specs += [VMEM] * (len(opening) + n - 1) + [VMEM, SMEM]
            arrays += before
            specs += [VMEM] * len(before)
            if out is not None:
                aliases = {len(arrays): 0}
                arrays.append(out)
                specs.append(ANY)
            shapes.append(written)
            out_specs.append(ANY)
            scratch.insert(0, DMA((steps, blocks)))
            if out is None:
                scratch.insert(0, pltpu.VMEM((2, *whole.shape), jnp.bfloat16))
        if send:
            shapes += [whole] + [one] * (n - 1)
        else:
            scratch.insert(0, pltpu.VMEM(whole.shape, jnp.bfloat16))
        out_specs += [VMEM] * (len(shapes) - len(out_specs))
        firsts = len(opening) if store and out is None else 0
        return pl.pallas_call(
            functools.partial(join_kernel, step, fix, send, section, firsts, store),
            out_shape=shapes,
            in_specs=specs,
            out_specs=out_specs,
            input_output_aliases=aliases,
            scratch_shapes=scratch,
            compiler_params=LIMIT,
        )(*arrays)

    def swap(block, first, second, d):
        other = {first: second, second: first}
        pairs = []
        for a in range(tm):
            for q in range(n):
                for c in range(col_parts):
                    to = (other[a] * n + (q ^ d)) * col_parts + c if a in other else (a * n + q) * col_parts + (c ^ 1)
                    pairs.append(((a * n + q) * col_parts + c, to))
        return lax.ppermute(block, ("tm", "net", "cols"), pairs)

    def exchange(outgoing, first, second):
        arrived = [swap(outgoing[d - 1], first, second, d) for d in reversed(range(1, n))]
        return arrived[::-1]

    opening, outgoing = outgoing[:blocks], outgoing[blocks:]
    out = None
    for r in range(1, tm):
        arrived = exchange(outgoing, r - 1, r)
        if r == 1:
            handed = arrived
            state = [swap(block, 0, 1, 0) for block in opening]
        else:
            state = swap(state, r - 1, r, 0)
        before = []
        for s in range(steps):
            fix = r == 1 and s == 0
            if s > 0:
                arrived = exchange(outgoing, r, r)
            z = None if fix else own(state, s)
            if s < steps - 1:
                state, *outgoing = join(z, s, fix, state, arrived, True, r)
                before.append(state)
            elif r < tm - 1:
                out, state, *outgoing = join(z, s, fix, state, arrived, True, r, opening, before, out, steps)
            else:
                (out,) = join(z, s, fix, state, arrived, False, r, opening, before, out, steps)
    return out


def solution(mesh):
    return jax.shard_map(
        local,
        mesh=mesh,
        in_specs=(
            P("tm", "net", None, None, None),
            P("net", None),
            P("tm", "net", None, None, None),
            P("net", None),
            P("net", None),
            P("net", None),
            P("cols"),
            P("tm", "cols"),
        ),
        out_specs=P("tm", "cols", "net"),
        check_vma=False,
    )
```

```python
import functools

import jax
import jax.numpy as jnp
from jax import lax
from jax.experimental import pallas as pl
from jax.experimental.pallas import tpu as pltpu
from jax.sharding import PartitionSpec as P

VMEM = pl.BlockSpec(memory_space=pltpu.VMEM)
SMEM = pl.BlockSpec(memory_space=pltpu.SMEM)
HBM = pl.BlockSpec(memory_space=pltpu.HBM)
ANY = pl.BlockSpec(memory_space=pl.ANY)
LIMIT = pltpu.CompilerParams(vmem_limit_bytes=16 * 1024 * 1024)
DMA = pltpu.SemaphoreType.DMA

STATE, LANE, BLOCK, AWAY, GAIN = 0, 1, 2, 3, 4
ROWS = 16


def times_transposed(rows, block):
    return lax.dot_general(rows, block, (((1,), (1,)), ((), ())), preferred_element_type=jnp.float32)


def injected(table, step, first_state, width):
    lane = lax.broadcasted_iota(jnp.int32, (table.shape[0], width), 1)
    hit = table[:, STATE : STATE + 1] == (lane + first_state).astype(jnp.float32)
    return jnp.where(hit, table[:, GAIN + step : GAIN + step + 1], 0.0)


def own_sum(i, state_ref, jac_ref, cols_ref, table, step):
    blocks, _, width = state_ref.shape
    first = (lax.axis_index("net") * blocks + i) * width
    kinds = jac_ref.shape[1]
    rows = [state_ref[i]] + [state_ref[cols_ref[k - 1, i]] for k in range(1, kinds)]
    row_blocks = [jac_ref[i, k] for k in range(kinds)]
    total = times_transposed(jnp.concatenate(rows, axis=1), jnp.concatenate(row_blocks, axis=1))
    return total + injected(table, step, first, width)


def add_coupled(incoming, block, live, recv, z_ref, keep=None):
    mask = lax.broadcasted_iota(jnp.int32, z_ref.shape[1:], 1) < live
    if keep is not None:
        mask = jnp.logical_and(mask, keep > 0.0)
    z_ref[recv] += jnp.where(mask, times_transposed(incoming, block), 0.0)


def table_row(send_ref, partition, width):
    lane = lax.broadcasted_iota(jnp.int32, (1, width), 1)
    row = jnp.zeros((1, width), jnp.float32)
    for e in range(lax.axis_size("net")):
        row = jnp.where(lane == e, send_ref[0, partition ^ e].astype(jnp.float32), row)
    return row


def kept(table, rows):
    away, block = table[:, AWAY : AWAY + 1], table[:, BLOCK : BLOCK + 1]
    sent = jnp.broadcast_to(rows[0], (table.shape[0], rows[0].shape[1]))
    for d in range(1, len(rows)):
        sent = jnp.where(away == float(d), rows[d], sent)
    lane = lax.broadcasted_iota(jnp.int32, sent.shape, 1).astype(jnp.float32)
    return jnp.where(jnp.logical_or(away == lane, block == sent), 1.0, 0.0)


def second_kernel(*refs):
    jac_hbm, iface_hbm, *small, table_ref, state_ref = refs[:10]
    n = lax.axis_size("net")
    me = lax.axis_index("net")
    outgoing, refs = refs[10 : 9 + n], refs[9 + n :]
    jac_ref, iface_ref, *loaded, first_ref, z_ref, sems = refs
    cols_ref, send_ref, recv_ref, live_ref, node_ref, gain_ref = loaded
    blocks, cols, width = state_ref.shape
    loads = [
        pltpu.make_async_copy(source, target, sems.at[i])
        for i, (source, target) in enumerate(
            zip([jac_hbm.at[1], iface_hbm.at[1, 0], *small], [jac_ref, iface_ref, *loaded])
        )
    ]
    here = lax.axis_index("tm") == 0

    @pl.when(here)
    def _():
        for load in loads[:2]:
            load.start()

    for load in loads[2:]:
        load.start()
    for load in loads[2:]:
        load.wait()
    node = node_ref[...]
    block_of = node // width
    rows = [
        node,
        node - block_of * width,
        block_of % blocks,
        (block_of // blocks) ^ me,
    ]
    steps = gain_ref.shape[0]
    fill = -(GAIN + steps) % 8
    rows = [row.astype(jnp.float32) for row in rows] + [gain_ref[...], jnp.zeros((fill, cols), jnp.float32)]
    table_ref[...] = jnp.concatenate(rows, axis=0).T

    @pl.when(here)
    def _():
        table = table_ref[...]
        for i in range(blocks):
            first_ref[i] = injected(table, 0, (me * blocks + i) * width, width).astype(first_ref.dtype)
        lane = lax.broadcasted_iota(jnp.int32, (cols, width), 1).astype(jnp.float32)
        shot = jnp.where(lane == table[:, LANE : LANE + 1], table[:, GAIN : GAIN + 1], 0.0)
        loads[0].wait()
        for i in range(blocks):
            z_ref[i] = own_sum(i, first_ref, jac_ref, cols_ref, table, 1)
        loads[1].wait()
        away, block = table[:, AWAY : AWAY + 1], table[:, BLOCK : BLOCK + 1]
        mine = jnp.logical_or(away != 0.0, block == send_ref[0, me].astype(jnp.float32))
        shot = jnp.where(mine, shot, 0.0)
        for d in range(n):
            q = me ^ d
            sent = jnp.where(away == float(d), shot, 0.0).astype(first_ref.dtype)
            add_coupled(sent, iface_ref[q], live_ref[0, q], recv_ref[0, q], z_ref)
        state_ref[...] = z_ref[...].astype(state_ref.dtype)
        for d in range(1, n):
            outgoing[d - 1][pl.ds(0, cols)] = state_ref[send_ref[0, me ^ d]]

    for d in range(1, n):
        row = table_row(send_ref, me ^ d, width).astype(state_ref.dtype)
        outgoing[d - 1][pl.ds(cols, ROWS)] = jnp.broadcast_to(row, (ROWS, width))


def write_start(states, first, out_ref, sems):
    copies = []
    for s, state_ref in enumerate(states, first):
        width = state_ref.shape[2]
        for i in range(state_ref.shape[0]):
            copies.append(
                pltpu.make_async_copy(state_ref.at[i], out_ref.at[s, :, pl.ds(i * width, width)], sems.at[s, i])
            )
    for copy in copies:
        copy.start()
    return copies


def own_kernel(step, state_ref, jac_ref, cols_ref, table_ref, z_ref):
    table = table_ref[...]
    for i in range(state_ref.shape[0]):
        z_ref[i] = own_sum(i, state_ref, jac_ref.at[step], cols_ref, table, step)


def first_states(states, jac_ref, iface_ref, cols_ref, send_ref, recv_ref, live_ref, table_ref, handed, made_ref, z_ref):
    n = lax.axis_size("net")
    blocks, cols, width = z_ref.shape
    table = table_ref[...]
    made_ref[0] = jnp.zeros_like(made_ref[0])
    for i in range(blocks):
        z_ref[i] = own_sum(i, made_ref.at[0], jac_ref.at[0], cols_ref, table, 0)
    for q in range(n):
        add_coupled(made_ref[0, 0], iface_ref[0, 0, q], live_ref[0, q], recv_ref[0, q], z_ref)
    made_ref[0] = z_ref[...].astype(made_ref.dtype)
    me = lax.axis_index("net")
    rows = [table_row(send_ref, me, width)]
    rows += [block[cols : cols + 1].astype(jnp.float32) for block in handed]
    keep = kept(table, rows)[:, 0:1]
    for i in range(blocks):
        made_ref[1, i] = jnp.where(keep > 0.0, states[0][i], jnp.zeros_like(states[0][i]))
    return [made_ref.at[0], made_ref.at[1], *states[1:]]


def join_kernel(step, fix, send, section, firsts, store, *refs):
    n = lax.axis_size("net")
    me = lax.axis_index("net")
    tm = lax.axis_index("tm")
    if fix:
        jac_ref, cols_ref, *refs = refs
    else:
        z_ref, *refs = refs
    iface_ref, send_ref, recv_ref, live_ref, table_ref, state_in_ref, *refs = refs
    arrived, refs = refs[: n - 1], refs[n - 1 :]
    acc_ref = refs.pop()
    blocks, cols, width = acc_ref.shape
    before = []
    if store:
        sems = refs.pop()
        if firsts:
            made_ref = refs.pop()
            opening, refs = refs[:firsts], refs[firsts:]
            handed, refs = refs[: n - 1], refs[n - 1 :]
            jac_ref, cols_ref = refs.pop(0), refs.pop(0)
        before, refs = refs[: store - 1], refs[store - 1 :]
        if not firsts:
            refs.pop(0)
        out_ref = refs.pop(0)
    state_ref, *outgoing = refs

    def join():
        if store:
            copies = write_start(before, 0, out_ref, sems)
        if fix:
            table = table_ref[...]
            rows = [table_row(send_ref, me, width)]
            rows += [arrived[d - 1][cols : cols + 1].astype(jnp.float32) for d in range(1, n)]
            keep = kept(table, rows)
            for i in range(blocks):
                own = own_sum(i, state_in_ref, jac_ref.at[step], cols_ref, table, step)
                acc_ref[i] = jnp.where(keep[:, 0:1] > 0.0, own, 0.0)
        else:
            acc_ref[...] = z_ref[...]
        for d in range(n):
            q = me ^ d
            block = arrived[d - 1][pl.ds(0, cols)] if d else state_in_ref[send_ref[0, me]]
            stands = keep[:, d : d + 1] if fix else None
            add_coupled(block, iface_ref[step, 0, q], live_ref[0, q], recv_ref[0, q], acc_ref, stands)
        state_ref[...] = acc_ref[...].astype(state_ref.dtype)
        if send:
            for d in range(1, n):
                outgoing[d - 1][...] = state_ref[send_ref[0, me ^ d]]
        if store:
            copies += write_start([state_ref], store - 1, out_ref, sems)
            for copy in copies:
                copy.wait()

    if store:
        pl.when(tm == section)(join)
    else:
        join()
    if firsts:

        @pl.when(tm == 0)
        def _():
            made = first_states(
                opening, jac_ref, iface_ref, cols_ref, send_ref, recv_ref, live_ref, table_ref, handed, made_ref, acc_ref
            )
            for copy in write_start(made, 0, out_ref, sems):
                copy.wait()


def local(jac, block_cols, iface_jac, iface_send, iface_recv, iface_live, ctrl_node, ctrl_gain):
    steps, blocks, kinds, width, _ = jac.shape
    cols = ctrl_node.shape[0]
    tm = lax.axis_size("tm")
    n = lax.axis_size("net")
    col_parts = lax.axis_size("cols")
    node = ctrl_node[None]
    near = block_cols.T
    bf16 = functools.partial(jax.ShapeDtypeStruct, dtype=jnp.bfloat16)
    f32 = functools.partial(jax.ShapeDtypeStruct, dtype=jnp.float32)
    whole, one = bf16((blocks, cols, width)), bf16((cols, width))
    table_rows = GAIN + steps + -(GAIN + steps) % 8
    written = bf16((steps, cols, blocks * width))

    pinned = [
        pltpu.with_memory_space_constraint(x, pltpu.HBM)
        for x in (jac, iface_jac, near, iface_send, iface_recv, iface_live, node, ctrl_gain)
    ]
    table, state, *outgoing = pl.pallas_call(
        second_kernel,
        out_shape=[f32((cols, table_rows)), whole] + [bf16((cols + ROWS, width))] * (n - 1),
        in_specs=[HBM] * len(pinned),
        out_specs=[VMEM] * (n + 1),
        scratch_shapes=[
            pltpu.VMEM((blocks, kinds, width, width), jnp.bfloat16),
            pltpu.VMEM((n, width, width), jnp.bfloat16),
            *[pltpu.SMEM(x.shape, x.dtype) for x in (near, iface_send, iface_recv, iface_live)],
            *[pltpu.VMEM(x.shape, x.dtype) for x in (node, ctrl_gain)],
            pltpu.VMEM(whole.shape, jnp.bfloat16),
            pltpu.VMEM(whole.shape, jnp.float32),
            DMA((len(pinned),)),
        ],
        compiler_params=LIMIT,
    )(*pinned)

    def own(state, step):
        return pl.pallas_call(
            functools.partial(own_kernel, step),
            out_shape=f32(whole.shape),
            in_specs=[VMEM, VMEM, SMEM, VMEM],
            out_specs=VMEM,
            compiler_params=LIMIT,
        )(state, jac, near, table)

    def join(z, step, fix, state, arrived, send, section, opening=(), before=(), out=None, store=0):
        arrays = [*([jac, near] if fix else [z]), iface_jac, iface_send, iface_recv, iface_live, table, state]
        specs = [*([VMEM, SMEM] if fix else [VMEM]), VMEM, SMEM, SMEM, SMEM, VMEM, VMEM]
        arrays += arrived
        specs += [VMEM] * (n - 1)
        shapes = []
        scratch = [pltpu.VMEM(whole.shape, jnp.float32)]
        aliases = {}
        out_specs = []
        if store:
            if out is None:
                arrays += [*opening, *handed, jac, near]
                specs += [VMEM] * (len(opening) + n - 1) + [VMEM, SMEM]
            arrays += before
            specs += [VMEM] * len(before)
            if out is not None:
                aliases = {len(arrays): 0}
                arrays.append(out)
                specs.append(ANY)
            shapes.append(written)
            out_specs.append(ANY)
            scratch.insert(0, DMA((steps, blocks)))
            if out is None:
                scratch.insert(0, pltpu.VMEM((2, *whole.shape), jnp.bfloat16))
        if send:
            shapes += [whole] + [one] * (n - 1)
        else:
            scratch.insert(0, pltpu.VMEM(whole.shape, jnp.bfloat16))
        out_specs += [VMEM] * (len(shapes) - len(out_specs))
        firsts = len(opening) if store and out is None else 0
        return pl.pallas_call(
            functools.partial(join_kernel, step, fix, send, section, firsts, store),
            out_shape=shapes,
            in_specs=specs,
            out_specs=out_specs,
            input_output_aliases=aliases,
            scratch_shapes=scratch,
            compiler_params=LIMIT,
        )(*arrays)

    def swap(block, first, second, d):
        other = {first: second, second: first}
        pairs = []
        for a in range(tm):
            for q in range(n):
                for c in range(col_parts):
                    to = (other[a] * n + (q ^ d)) * col_parts + c if a in other else (a * n + q) * col_parts + (c ^ 1)
                    pairs.append(((a * n + q) * col_parts + c, to))
        return lax.ppermute(block, ("tm", "net", "cols"), pairs)

    def exchange(outgoing, first, second):
        order = range(1, n) if first != second else reversed(range(1, n))
        arrived = {d: swap(outgoing[d - 1], first, second, d) for d in order}
        return [arrived[d] for d in range(1, n)]

    opening = [state]
    out = None
    for r in range(1, tm):
        arrived = exchange(outgoing, r - 1, r)
        state = swap(state, r - 1, r, 0)
        if r == 1:
            handed = arrived
        before = []
        for s in range(steps):
            fix = r == 1 and s == 0
            if s > 0:
                arrived = exchange(outgoing, r, r)
            z = None if fix else own(state, s)
            if s < steps - 1:
                state, *outgoing = join(z, s, fix, state, arrived, True, r)
                before.append(state)
            elif r < tm - 1:
                out, state, *outgoing = join(z, s, fix, state, arrived, True, r, opening, before, out, steps)
            else:
                (out,) = join(z, s, fix, state, arrived, False, r, opening, before, out, steps)
    return out


def solution(mesh):
    return jax.shard_map(
        local,
        mesh=mesh,
        in_specs=(
            P("tm", "net", None, None, None),
            P("net", None),
            P("tm", "net", None, None, None),
            P("net", None),
            P("net", None),
            P("net", None),
            P("cols"),
            P("tm", "cols"),
        ),
        out_specs=P("tm", "cols", "net"),
        check_vma=False,
    )
```

```python
import functools

import jax
import jax.numpy as jnp
from jax import lax
from jax.experimental import pallas as pl
from jax.experimental.pallas import tpu as pltpu
from jax.sharding import PartitionSpec as P

VMEM = pl.BlockSpec(memory_space=pltpu.VMEM)
SMEM = pl.BlockSpec(memory_space=pltpu.SMEM)
HBM = pl.BlockSpec(memory_space=pltpu.HBM)
ANY = pl.BlockSpec(memory_space=pl.ANY)
LIMIT = pltpu.CompilerParams(vmem_limit_bytes=16 * 1024 * 1024)
DMA = pltpu.SemaphoreType.DMA

STATE, LANE, BLOCK, AWAY, GAIN = 0, 1, 2, 3, 4
ROWS = 16


def times_transposed(rows, block):
    return lax.dot_general(rows, block, (((1,), (1,)), ((), ())), preferred_element_type=jnp.float32)


def injected(table, step, first_state, width):
    lane = lax.broadcasted_iota(jnp.int32, (table.shape[0], width), 1)
    hit = table[:, STATE : STATE + 1] == (lane + first_state).astype(jnp.float32)
    return jnp.where(hit, table[:, GAIN + step : GAIN + step + 1], 0.0)


def own_sum(i, state_ref, jac_ref, cols_ref, table, step):
    blocks, _, width = state_ref.shape
    first = (lax.axis_index("net") * blocks + i) * width
    kinds = jac_ref.shape[1]
    rows = [state_ref[i]] + [state_ref[cols_ref[k - 1, i]] for k in range(1, kinds)]
    row_blocks = [jac_ref[i, k] for k in range(kinds)]
    total = times_transposed(jnp.concatenate(rows, axis=1), jnp.concatenate(row_blocks, axis=1))
    return total + injected(table, step, first, width)


def add_coupled(incoming, block, live, recv, z_ref, keep=None):
    mask = lax.broadcasted_iota(jnp.int32, z_ref.shape[1:], 1) < live
    if keep is not None:
        mask = jnp.logical_and(mask, keep > 0.0)
    z_ref[recv] += jnp.where(mask, times_transposed(incoming, block), 0.0)


def table_row(send_ref, partition, width):
    lane = lax.broadcasted_iota(jnp.int32, (1, width), 1)
    row = jnp.zeros((1, width), jnp.float32)
    for e in range(lax.axis_size("net")):
        row = jnp.where(lane == e, send_ref[0, partition ^ e].astype(jnp.float32), row)
    return row


def kept(table, rows):
    away, block = table[:, AWAY : AWAY + 1], table[:, BLOCK : BLOCK + 1]
    sent = jnp.broadcast_to(rows[0], (table.shape[0], rows[0].shape[1]))
    for d in range(1, len(rows)):
        sent = jnp.where(away == float(d), rows[d], sent)
    lane = lax.broadcasted_iota(jnp.int32, sent.shape, 1).astype(jnp.float32)
    return jnp.where(jnp.logical_or(away == lane, block == sent), 1.0, 0.0)


def second_kernel(*refs):
    jac_hbm, iface_hbm, *small, table_ref, state_ref = refs[:10]
    n = lax.axis_size("net")
    me = lax.axis_index("net")
    outgoing, refs = refs[10 : 9 + n], refs[9 + n :]
    jac_ref, iface_ref, *loaded, first_ref, z_ref, sems = refs
    cols_ref, send_ref, recv_ref, live_ref, node_ref, gain_ref = loaded
    blocks, cols, width = state_ref.shape
    loads = [
        pltpu.make_async_copy(source, target, sems.at[i])
        for i, (source, target) in enumerate(
            zip([jac_hbm.at[1], iface_hbm.at[1, 0], *small], [jac_ref, iface_ref, *loaded])
        )
    ]
    here = lax.axis_index("tm") == 0

    @pl.when(here)
    def _():
        for load in loads[:2]:
            load.start()

    for load in loads[2:]:
        load.start()
    for load in loads[2:]:
        load.wait()
    node = node_ref[...]
    block_of = node // width
    rows = [
        node,
        node - block_of * width,
        block_of % blocks,
        (block_of // blocks) ^ me,
    ]
    steps = gain_ref.shape[0]
    fill = -(GAIN + steps) % 8
    rows = [row.astype(jnp.float32) for row in rows] + [gain_ref[...], jnp.zeros((fill, cols), jnp.float32)]
    table_ref[...] = jnp.concatenate(rows, axis=0).T

    @pl.when(here)
    def _():
        table = table_ref[...]
        for i in range(blocks):
            first_ref[i] = injected(table, 0, (me * blocks + i) * width, width).astype(first_ref.dtype)
        lane = lax.broadcasted_iota(jnp.int32, (cols, width), 1).astype(jnp.float32)
        shot = jnp.where(lane == table[:, LANE : LANE + 1], table[:, GAIN : GAIN + 1], 0.0)
        loads[0].wait()
        for i in range(blocks):
            z_ref[i] = own_sum(i, first_ref, jac_ref, cols_ref, table, 1)
        loads[1].wait()
        away, block = table[:, AWAY : AWAY + 1], table[:, BLOCK : BLOCK + 1]
        mine = jnp.logical_or(away != 0.0, block == send_ref[0, me].astype(jnp.float32))
        shot = jnp.where(mine, shot, 0.0)
        for d in range(n):
            q = me ^ d
            sent = jnp.where(away == float(d), shot, 0.0).astype(first_ref.dtype)
            add_coupled(sent, iface_ref[q], live_ref[0, q], recv_ref[0, q], z_ref)
        state_ref[...] = z_ref[...].astype(state_ref.dtype)
        for d in range(1, n):
            outgoing[d - 1][pl.ds(0, cols)] = state_ref[send_ref[0, me ^ d]]

    for d in range(1, n):
        row = table_row(send_ref, me ^ d, width).astype(state_ref.dtype)
        outgoing[d - 1][pl.ds(cols, ROWS)] = jnp.broadcast_to(row, (ROWS, width))


def write_start(states, first, out_ref, sems):
    copies = []
    for s, state_ref in enumerate(states, first):
        width = state_ref.shape[2]
        for i in range(state_ref.shape[0]):
            copies.append(
                pltpu.make_async_copy(state_ref.at[i], out_ref.at[s, :, pl.ds(i * width, width)], sems.at[s, i])
            )
    for copy in copies:
        copy.start()
    return copies


def own_kernel(step, state_ref, jac_ref, cols_ref, table_ref, z_ref):
    table = table_ref[...]
    for i in range(state_ref.shape[0]):
        z_ref[i] = own_sum(i, state_ref, jac_ref.at[step], cols_ref, table, step)


def first_states(states, jac_ref, iface_ref, cols_ref, send_ref, recv_ref, live_ref, table_ref, handed, made_ref, z_ref):
    n = lax.axis_size("net")
    blocks, cols, width = z_ref.shape
    table = table_ref[...]
    made_ref[0] = jnp.zeros_like(made_ref[0])
    for i in range(blocks):
        z_ref[i] = own_sum(i, made_ref.at[0], jac_ref.at[0], cols_ref, table, 0)
    for q in range(n):
        add_coupled(made_ref[0, 0], iface_ref[0, 0, q], live_ref[0, q], recv_ref[0, q], z_ref)
    made_ref[0] = z_ref[...].astype(made_ref.dtype)
    me = lax.axis_index("net")
    rows = [table_row(send_ref, me, width)]
    rows += [block[cols : cols + 1].astype(jnp.float32) for block in handed]
    keep = kept(table, rows)[:, 0:1]
    for i in range(blocks):
        made_ref[1, i] = jnp.where(keep > 0.0, states[0][i], jnp.zeros_like(states[0][i]))
    return [made_ref.at[0], made_ref.at[1], *states[1:]]


def join_kernel(step, fix, send, section, firsts, store, *refs):
    n = lax.axis_size("net")
    me = lax.axis_index("net")
    tm = lax.axis_index("tm")
    if fix:
        jac_ref, cols_ref, *refs = refs
    else:
        z_ref, *refs = refs
    iface_ref, send_ref, recv_ref, live_ref, table_ref, *refs = refs
    arrived, state_in_ref, refs = refs[: n - 1][::-1], refs[n - 1], refs[n:]
    acc_ref = refs.pop()
    blocks, cols, width = acc_ref.shape
    before = []
    if store:
        sems = refs.pop()
        if firsts:
            made_ref = refs.pop()
            opening, refs = refs[:firsts], refs[firsts:]
            handed, refs = refs[: n - 1], refs[n - 1 :]
            jac_ref, cols_ref = refs.pop(0), refs.pop(0)
        before, refs = refs[: store - 1], refs[store - 1 :]
        if not firsts:
            refs.pop(0)
        out_ref = refs.pop(0)
    state_ref, *outgoing = refs

    def join():
        if store:
            copies = write_start(before, 0, out_ref, sems)
        if fix:
            table = table_ref[...]
            rows = [table_row(send_ref, me, width)]
            rows += [arrived[d - 1][cols : cols + 1].astype(jnp.float32) for d in range(1, n)]
            keep = kept(table, rows)
            for i in range(blocks):
                own = own_sum(i, state_in_ref, jac_ref.at[step], cols_ref, table, step)
                acc_ref[i] = jnp.where(keep[:, 0:1] > 0.0, own, 0.0)
        else:
            acc_ref[...] = z_ref[...]
        for d in range(n):
            q = me ^ d
            block = arrived[d - 1][pl.ds(0, cols)] if d else state_in_ref[send_ref[0, me]]
            stands = keep[:, d : d + 1] if fix else None
            add_coupled(block, iface_ref[step, 0, q], live_ref[0, q], recv_ref[0, q], acc_ref, stands)
        state_ref[...] = acc_ref[...].astype(state_ref.dtype)
        if send:
            for d in range(1, n):
                outgoing[d - 1][...] = state_ref[send_ref[0, me ^ d]]
        if store:
            copies += write_start([state_ref], store - 1, out_ref, sems)
            for copy in copies:
                copy.wait()

    if store:
        pl.when(tm == section)(join)
    else:
        join()
    if firsts:

        @pl.when(tm == 0)
        def _():
            made = first_states(
                opening, jac_ref, iface_ref, cols_ref, send_ref, recv_ref, live_ref, table_ref, handed, made_ref, acc_ref
            )
            for copy in write_start(made, 0, out_ref, sems):
                copy.wait()


def local(jac, block_cols, iface_jac, iface_send, iface_recv, iface_live, ctrl_node, ctrl_gain):
    steps, blocks, kinds, width, _ = jac.shape
    cols = ctrl_node.shape[0]
    tm = lax.axis_size("tm")
    n = lax.axis_size("net")
    col_parts = lax.axis_size("cols")
    node = ctrl_node[None]
    near = block_cols.T
    bf16 = functools.partial(jax.ShapeDtypeStruct, dtype=jnp.bfloat16)
    f32 = functools.partial(jax.ShapeDtypeStruct, dtype=jnp.float32)
    whole, one = bf16((blocks, cols, width)), bf16((cols, width))
    table_rows = GAIN + steps + -(GAIN + steps) % 8
    written = bf16((steps, cols, blocks * width))

    pinned = [
        pltpu.with_memory_space_constraint(x, pltpu.HBM)
        for x in (jac, iface_jac, near, iface_send, iface_recv, iface_live, node, ctrl_gain)
    ]
    table, state, *outgoing = pl.pallas_call(
        second_kernel,
        out_shape=[f32((cols, table_rows)), whole] + [bf16((cols + ROWS, width))] * (n - 1),
        in_specs=[HBM] * len(pinned),
        out_specs=[VMEM] * (n + 1),
        scratch_shapes=[
            pltpu.VMEM((blocks, kinds, width, width), jnp.bfloat16),
            pltpu.VMEM((n, width, width), jnp.bfloat16),
            *[pltpu.SMEM(x.shape, x.dtype) for x in (near, iface_send, iface_recv, iface_live)],
            *[pltpu.VMEM(x.shape, x.dtype) for x in (node, ctrl_gain)],
            pltpu.VMEM(whole.shape, jnp.bfloat16),
            pltpu.VMEM(whole.shape, jnp.float32),
            DMA((len(pinned),)),
        ],
        compiler_params=LIMIT,
    )(*pinned)

    def own(state, step):
        return pl.pallas_call(
            functools.partial(own_kernel, step),
            out_shape=f32(whole.shape),
            in_specs=[VMEM, VMEM, SMEM, VMEM],
            out_specs=VMEM,
            compiler_params=LIMIT,
        )(state, jac, near, table)

    def join(z, step, fix, state, arrived, send, section, opening=(), before=(), out=None, store=0):
        arrays = [*([jac, near] if fix else [z]), iface_jac, iface_send, iface_recv, iface_live, table]
        specs = [*([VMEM, SMEM] if fix else [VMEM]), VMEM, SMEM, SMEM, SMEM, VMEM]
        arrays += [*arrived[::-1], state]
        specs += [VMEM] * n
        shapes = []
        scratch = [pltpu.VMEM(whole.shape, jnp.float32)]
        aliases = {}
        out_specs = []
        if store:
            if out is None:
                arrays += [*opening, *handed, jac, near]
                specs += [VMEM] * (len(opening) + n - 1) + [VMEM, SMEM]
            arrays += before
            specs += [VMEM] * len(before)
            if out is not None:
                aliases = {len(arrays): 0}
                arrays.append(out)
                specs.append(ANY)
            shapes.append(written)
            out_specs.append(ANY)
            scratch.insert(0, DMA((steps, blocks)))
            if out is None:
                scratch.insert(0, pltpu.VMEM((2, *whole.shape), jnp.bfloat16))
        if send:
            shapes += [whole] + [one] * (n - 1)
        else:
            scratch.insert(0, pltpu.VMEM(whole.shape, jnp.bfloat16))
        out_specs += [VMEM] * (len(shapes) - len(out_specs))
        firsts = len(opening) if store and out is None else 0
        return pl.pallas_call(
            functools.partial(join_kernel, step, fix, send, section, firsts, store),
            out_shape=shapes,
            in_specs=specs,
            out_specs=out_specs,
            input_output_aliases=aliases,
            scratch_shapes=scratch,
            compiler_params=LIMIT,
        )(*arrays)

    def swap(block, first, second, d):
        other = {first: second, second: first}
        pairs = []
        for a in range(tm):
            for q in range(n):
                for c in range(col_parts):
                    to = (other[a] * n + (q ^ d)) * col_parts + c if a in other else (a * n + q) * col_parts + (c ^ 1)
                    pairs.append(((a * n + q) * col_parts + c, to))
        return lax.ppermute(block, ("tm", "net", "cols"), pairs)

    def exchange(outgoing, first, second):
        return [swap(outgoing[d - 1], first, second, d) for d in range(1, n)]

    opening = [state]
    out = None
    for r in range(1, tm):
        arrived = exchange(outgoing, r - 1, r)
        state = swap(state, r - 1, r, 0)
        if r == 1:
            handed = arrived
        before = []
        for s in range(steps):
            fix = r == 1 and s == 0
            if s > 0:
                arrived = exchange(outgoing, r, r)
            z = None if fix else own(state, s)
            if s < steps - 1:
                state, *outgoing = join(z, s, fix, state, arrived, True, r)
                before.append(state)
            elif r < tm - 1:
                out, state, *outgoing = join(z, s, fix, state, arrived, True, r, opening, before, out, steps)
            else:
                (out,) = join(z, s, fix, state, arrived, False, r, opening, before, out, steps)
    return out


def solution(mesh):
    return jax.shard_map(
        local,
        mesh=mesh,
        in_specs=(
            P("tm", "net", None, None, None),
            P("net", None),
            P("tm", "net", None, None, None),
            P("net", None),
            P("net", None),
            P("net", None),
            P("cols"),
            P("tm", "cols"),
        ),
        out_specs=P("tm", "cols", "net"),
        check_vma=False,
    )
```

```python
import functools

import jax
import jax.numpy as jnp
from jax import lax
from jax.experimental import pallas as pl
from jax.experimental.pallas import tpu as pltpu
from jax.sharding import PartitionSpec as P

VMEM = pl.BlockSpec(memory_space=pltpu.VMEM)
SMEM = pl.BlockSpec(memory_space=pltpu.SMEM)
HBM = pl.BlockSpec(memory_space=pltpu.HBM)
ANY = pl.BlockSpec(memory_space=pl.ANY)
LIMIT = pltpu.CompilerParams(vmem_limit_bytes=16 * 1024 * 1024)
DMA = pltpu.SemaphoreType.DMA

STATE, LANE, BLOCK, AWAY, GAIN = 0, 1, 2, 3, 4
ROWS = 16


def times_transposed(rows, block):
    return lax.dot_general(rows, block, (((1,), (1,)), ((), ())), preferred_element_type=jnp.float32)


def injected(table, step, first_state, width):
    lane = lax.broadcasted_iota(jnp.int32, (table.shape[0], width), 1)
    hit = table[:, STATE : STATE + 1] == (lane + first_state).astype(jnp.float32)
    return jnp.where(hit, table[:, GAIN + step : GAIN + step + 1], 0.0)


def near_by(state_ref, cols_ref):
    return lambda i, k: state_ref[cols_ref[k, i]]


def own_sum(i, state_ref, jac_ref, near, table, step):
    blocks, _, width = state_ref.shape
    first = (lax.axis_index("net") * blocks + i) * width
    kinds = jac_ref.shape[1]
    rows = [state_ref[i]] + [near(i, k) for k in range(kinds - 1)]
    row_blocks = [jac_ref[i, k] for k in range(kinds)]
    total = times_transposed(jnp.concatenate(rows, axis=1), jnp.concatenate(row_blocks, axis=1))
    return total + injected(table, step, first, width)


def picked(blocks, marks):
    total = blocks[0] * marks[0]
    for block, mark in zip(blocks[1:], marks[1:]):
        total += block * mark
    return total


def marks_layout(n, blocks, kinds):
    sent = n * blocks
    near = sent + n * blocks
    row = near + blocks * (kinds - 1) * blocks
    return sent, near, row, row + 1 + -(row + 1) % 8


def make_marks(marks_ref, blocks, kinds, cols_ref, send_ref, recv_ref, live_ref):
    n = lax.axis_size("net")
    me = lax.axis_index("net")
    width = marks_ref.shape[1]
    lane = lax.broadcasted_iota(jnp.int32, (1, width), 1)
    sent, near, own_row, _ = marks_layout(n, blocks, kinds)

    def put(row, mask):
        marks_ref[pl.ds(row, 1)] = jnp.where(mask, 1.0, 0.0)

    for d in range(n):
        q = me ^ d
        for i in range(blocks):
            put(d * blocks + i, lane < jnp.where(recv_ref[0, q] == i, live_ref[0, q], 0))
            put(sent + d * blocks + i, lane < jnp.where(send_ref[0, q] == i, width, 0))
    for i in range(blocks):
        for k in range(kinds - 1):
            for j in range(blocks):
                put(near + (i * (kinds - 1) + k) * blocks + j, lane < jnp.where(cols_ref[k, i] == j, width, 0))
    marks_ref[pl.ds(own_row, 1)] = table_row(send_ref, me, width)


def add_coupled(incoming, block, live, recv, z_ref):
    mask = lax.broadcasted_iota(jnp.int32, z_ref.shape[1:], 1) < live
    z_ref[recv] += jnp.where(mask, times_transposed(incoming, block), 0.0)


def table_row(send_ref, partition, width):
    lane = lax.broadcasted_iota(jnp.int32, (1, width), 1)
    row = jnp.zeros((1, width), jnp.float32)
    for e in range(lax.axis_size("net")):
        row = jnp.where(lane == e, send_ref[0, partition ^ e].astype(jnp.float32), row)
    return row


def kept(table, rows):
    away, block = table[:, AWAY : AWAY + 1], table[:, BLOCK : BLOCK + 1]
    sent = jnp.broadcast_to(rows[0], (table.shape[0], rows[0].shape[1]))
    for d in range(1, len(rows)):
        sent = jnp.where(away == float(d), rows[d], sent)
    lane = lax.broadcasted_iota(jnp.int32, sent.shape, 1).astype(jnp.float32)
    return jnp.where(jnp.logical_or(away == lane, block == sent), 1.0, 0.0)


def second_kernel(*refs):
    jac_hbm, iface_hbm, *small, table_ref, marks_ref, state_ref = refs[:11]
    n = lax.axis_size("net")
    me = lax.axis_index("net")
    outgoing, refs = refs[11 : 10 + n], refs[10 + n :]
    jac_ref, iface_ref, *loaded, first_ref, sems = refs
    cols_ref, send_ref, recv_ref, live_ref, node_ref, gain_ref = loaded
    blocks, cols, width = state_ref.shape
    loads = [
        pltpu.make_async_copy(source, target, sems.at[i])
        for i, (source, target) in enumerate(
            zip([jac_hbm.at[1], iface_hbm.at[1, 0], *small], [jac_ref, iface_ref, *loaded])
        )
    ]
    here = lax.axis_index("tm") == 0

    @pl.when(here)
    def _():
        for load in loads[:2]:
            load.start()

    for load in loads[2:]:
        load.start()
    for load in loads[2:]:
        load.wait()
    node = node_ref[...]
    block_of = node // width
    rows = [
        node,
        node - block_of * width,
        block_of % blocks,
        (block_of // blocks) ^ me,
    ]
    steps = gain_ref.shape[0]
    fill = -(GAIN + steps) % 8
    rows = [row.astype(jnp.float32) for row in rows] + [gain_ref[...], jnp.zeros((fill, cols), jnp.float32)]
    table_ref[...] = jnp.concatenate(rows, axis=0).T

    @pl.when(here)
    def _():
        table = table_ref[...]
        for i in range(blocks):
            first_ref[i] = injected(table, 0, (me * blocks + i) * width, width).astype(first_ref.dtype)
        lane = lax.broadcasted_iota(jnp.int32, (cols, width), 1).astype(jnp.float32)
        shot = jnp.where(lane == table[:, LANE : LANE + 1], table[:, GAIN : GAIN + 1], 0.0)
        away, block = table[:, AWAY : AWAY + 1], table[:, BLOCK : BLOCK + 1]
        mine = jnp.logical_or(away != 0.0, block == send_ref[0, me].astype(jnp.float32))
        shot = jnp.where(mine, shot, 0.0)
        live = recv = jnp.zeros_like(away)
        for d in range(n):
            live = jnp.where(away == float(d), live_ref[0, me ^ d].astype(jnp.float32), live)
            recv = jnp.where(away == float(d), recv_ref[0, me ^ d].astype(jnp.float32), recv)
        sent = [jnp.where(away == float(d), shot, 0.0).astype(first_ref.dtype) for d in range(n)]
        loads[1].wait()
        ifaces = jnp.concatenate([iface_ref[me ^ d] for d in range(n)], axis=1)
        coupled = times_transposed(jnp.concatenate(sent, axis=1), ifaces)
        coupled = jnp.where(lane < live, coupled, 0.0)
        loads[0].wait()
        for i in range(blocks):
            own = own_sum(i, first_ref, jac_ref, near_by(first_ref, cols_ref), table, 1)
            state_ref[i] = (own + jnp.where(recv == float(i), coupled, 0.0)).astype(state_ref.dtype)
        for d in range(1, n):
            outgoing[d - 1][pl.ds(0, cols)] = state_ref[send_ref[0, me ^ d]]

    @pl.when(jnp.logical_not(here))
    def _():
        make_marks(marks_ref, blocks, jac_ref.shape[1], cols_ref, send_ref, recv_ref, live_ref)

    for d in range(1, n):
        row = table_row(send_ref, me ^ d, width).astype(state_ref.dtype)
        outgoing[d - 1][pl.ds(cols, ROWS)] = jnp.broadcast_to(row, (ROWS, width))


def write_start(states, first, out_ref, sems):
    copies = []
    for s, state_ref in enumerate(states, first):
        width = state_ref.shape[2]
        for i in range(state_ref.shape[0]):
            copies.append(
                pltpu.make_async_copy(state_ref.at[i], out_ref.at[s, :, pl.ds(i * width, width)], sems.at[s, i])
            )
    for copy in copies:
        copy.start()
    return copies


def own_kernel(step, state_ref, jac_ref, cols_ref, table_ref, z_ref):
    table = table_ref[...]
    for i in range(state_ref.shape[0]):
        z_ref[i] = own_sum(i, state_ref, jac_ref.at[step], near_by(state_ref, cols_ref), table, step)


def first_states(opening, handed, jac_ref, iface_ref, ints, table_ref, made_ref, z_ref):
    cols_ref, send_ref, recv_ref, live_ref = ints
    n = lax.axis_size("net")
    blocks, cols, width = z_ref.shape
    table = table_ref[...]
    made_ref[0] = jnp.zeros_like(made_ref[0])
    for i in range(blocks):
        z_ref[i] = own_sum(i, made_ref.at[0], jac_ref.at[0], near_by(made_ref.at[0], cols_ref), table, 0)
    for q in range(n):
        add_coupled(made_ref[0, 0], iface_ref[0, 0, q], live_ref[0, q], recv_ref[0, q], z_ref)
    made_ref[0] = z_ref[...].astype(made_ref.dtype)
    rows = [table_row(send_ref, lax.axis_index("net"), width)]
    rows += [block[cols : cols + 1].astype(jnp.float32) for block in handed]
    keep = kept(table, rows)[:, 0:1]
    for i in range(blocks):
        made_ref[1, i] = jnp.where(keep > 0.0, opening[i], jnp.zeros_like(opening[i]))
    return [made_ref.at[0], made_ref.at[1]]


def joined(sums, step, iface_ref, marks_ref, state_ref, arrived, keep=None):
    n = lax.axis_size("net")
    me = lax.axis_index("net")
    blocks, cols, _ = state_ref.shape
    sent = marks_layout(n, blocks, 1)[0]
    for d in range(n):
        if d:
            block = arrived[d - 1][pl.ds(0, cols)]
        else:
            marks = [marks_ref[pl.ds(sent + j, 1)].astype(state_ref.dtype) for j in range(blocks)]
            block = picked([state_ref[j] for j in range(blocks)], marks)
        term = times_transposed(block, iface_ref[step, 0, me ^ d])
        if keep is not None:
            term *= keep[:, d : d + 1]
        sums = [total + term * marks_ref[pl.ds(d * blocks + i, 1)] for i, total in enumerate(sums)]
    return [total.astype(state_ref.dtype) for total in sums]


def give(made, marks_ref, state_ref, outgoing):
    blocks = len(made)
    n = lax.axis_size("net")
    sent = marks_layout(n, blocks, 1)[0]
    for i in range(blocks):
        state_ref[i] = made[i]
    for d in range(1, n) if outgoing else ():
        marks = [marks_ref[pl.ds(sent + d * blocks + j, 1)].astype(made[j].dtype) for j in range(blocks)]
        outgoing[d - 1][...] = picked(made, marks)


def join_kernel(step, fix, section, *refs):
    n = lax.axis_size("net")
    first_ref, iface_ref, table_ref, marks_ref, *refs = refs
    arrived, state_in_ref, state_ref, outgoing = refs[: n - 1][::-1], refs[n - 1], refs[n], refs[n + 1 :]
    blocks, cols, _ = state_in_ref.shape

    @pl.when(lax.axis_index("tm") == section)
    def _():
        keep = None
        if fix:
            kinds = first_ref.shape[2]
            table = table_ref[...]
            _, near, own_row, _ = marks_layout(n, blocks, kinds)
            state = [state_in_ref[j] for j in range(blocks)]

            def near_block(i, k):
                rows = [near + (i * (kinds - 1) + k) * blocks + j for j in range(blocks)]
                return picked(state, [marks_ref[pl.ds(row, 1)].astype(state_ref.dtype) for row in rows])

            rows = [marks_ref[pl.ds(own_row, 1)]]
            rows += [block[cols : cols + 1].astype(jnp.float32) for block in arrived]
            keep = kept(table, rows)
            sums = [
                own_sum(i, state_in_ref, first_ref.at[step], near_block, table, step) * keep[:, 0:1]
                for i in range(blocks)
            ]
        else:
            sums = [first_ref[i] for i in range(blocks)]
        made = joined(sums, step, iface_ref, marks_ref, state_in_ref, arrived, keep)
        give(made, marks_ref, state_ref, outgoing)


def close_kernel(step, section, firsts, send, before, *refs):
    n = lax.axis_size("net")
    *refs, sems = refs
    if firsts:
        *refs, made_ref, acc_ref, cols_ref, send_ref, recv_ref, live_ref, load_sems = refs
        ints = [cols_ref, send_ref, recv_ref, live_ref]
    z_ref, iface_ref, table_ref, marks_ref, *refs = refs
    arrived, state_in_ref, refs = refs[: n - 1][::-1], refs[n - 1], refs[n:]
    before, refs = refs[:before], refs[before:]
    if firsts:
        opening_ref, handed, jac_ref, sources, refs = refs[0], refs[1:n], refs[n], refs[n + 1 : n + 5], refs[n + 5 :]
    else:
        refs = refs[1:]
    out_ref, state_ref, *outgoing = refs

    @pl.when(lax.axis_index("tm") == section)
    def _():
        copies = write_start(before, 0, out_ref, sems)
        sums = [z_ref[i] for i in range(z_ref.shape[0])]
        made = joined(sums, step, iface_ref, marks_ref, state_in_ref, arrived)
        give(made, marks_ref, state_ref, outgoing)
        copies += write_start([state_ref], len(before), out_ref, sems)
        for copy in copies:
            copy.wait()

    if firsts:

        @pl.when(lax.axis_index("tm") == 0)
        def _():
            loads = [
                pltpu.make_async_copy(source, target, load_sems.at[i])
                for i, (source, target) in enumerate(zip(sources, ints))
            ]
            for load in loads:
                load.start()
            for load in loads:
                load.wait()
            made = first_states(opening_ref, handed, jac_ref, iface_ref, ints, table_ref, made_ref, acc_ref)
            for copy in write_start(made, 0, out_ref, sems):
                copy.wait()


def local(jac, block_cols, iface_jac, iface_send, iface_recv, iface_live, ctrl_node, ctrl_gain):
    steps, blocks, kinds, width, _ = jac.shape
    cols = ctrl_node.shape[0]
    tm = lax.axis_size("tm")
    n = lax.axis_size("net")
    col_parts = lax.axis_size("cols")
    node = ctrl_node[None]
    near = block_cols.T
    bf16 = functools.partial(jax.ShapeDtypeStruct, dtype=jnp.bfloat16)
    f32 = functools.partial(jax.ShapeDtypeStruct, dtype=jnp.float32)
    whole, one = bf16((blocks, cols, width)), bf16((cols, width))
    table_rows = GAIN + steps + -(GAIN + steps) % 8
    written = bf16((steps, cols, blocks * width))

    pinned = [
        pltpu.with_memory_space_constraint(x, pltpu.HBM)
        for x in (jac, iface_jac, near, iface_send, iface_recv, iface_live, node, ctrl_gain)
    ]
    marks_rows = marks_layout(n, blocks, kinds)[-1]
    table, marks, state, *outgoing = pl.pallas_call(
        second_kernel,
        out_shape=[f32((cols, table_rows)), f32((marks_rows, width)), whole]
        + [bf16((cols + ROWS, width))] * (n - 1),
        in_specs=[HBM] * len(pinned),
        out_specs=[VMEM] * (n + 2),
        scratch_shapes=[
            pltpu.VMEM((blocks, kinds, width, width), jnp.bfloat16),
            pltpu.VMEM((n, width, width), jnp.bfloat16),
            *[pltpu.SMEM(x.shape, x.dtype) for x in (near, iface_send, iface_recv, iface_live)],
            *[pltpu.VMEM(x.shape, x.dtype) for x in (node, ctrl_gain)],
            pltpu.VMEM(whole.shape, jnp.bfloat16),
            DMA((len(pinned),)),
        ],
        compiler_params=LIMIT,
    )(*pinned)

    def own(state, step):
        return pl.pallas_call(
            functools.partial(own_kernel, step),
            out_shape=f32(whole.shape),
            in_specs=[VMEM, VMEM, SMEM, VMEM],
            out_specs=VMEM,
            compiler_params=LIMIT,
        )(state, jac, near, table)

    def join(first, step, fix, state, arrived, section):
        return pl.pallas_call(
            functools.partial(join_kernel, step, fix, section),
            out_shape=[whole] + [one] * (n - 1),
            in_specs=[VMEM] * (n + 4),
            out_specs=[VMEM] * n,
            compiler_params=LIMIT,
        )(first, iface_jac, table, marks, *arrived[::-1], state)

    def close(z, step, state, arrived, section, before, out, send):
        firsts = out is None
        arrays = [z, iface_jac, table, marks, *arrived[::-1], state, *before]
        specs = [VMEM] * len(arrays)
        scratch = [DMA((steps, blocks))]
        aliases = {}
        if firsts:
            arrays += [opening, *handed, jac, *pinned[2:6]]
            specs += [VMEM] * (n + 1) + [HBM] * 4
            scratch = [
                pltpu.VMEM((2, *whole.shape), jnp.bfloat16),
                pltpu.VMEM(whole.shape, jnp.float32),
                *[pltpu.SMEM(x.shape, x.dtype) for x in pinned[2:6]],
                DMA((4,)),
            ] + scratch
        else:
            aliases = {len(arrays): 0}
            arrays.append(out)
            specs.append(ANY)
        shapes, out_specs = [written], [ANY]
        if send:
            shapes += [whole] + [one] * (n - 1)
            out_specs += [VMEM] * n
        else:
            scratch.insert(0, pltpu.VMEM(whole.shape, jnp.bfloat16))
        return pl.pallas_call(
            functools.partial(close_kernel, step, section, firsts, send, len(before)),
            out_shape=shapes,
            in_specs=specs,
            out_specs=out_specs,
            input_output_aliases=aliases,
            scratch_shapes=scratch,
            compiler_params=LIMIT,
        )(*arrays)

    def swap(block, first, second, d):
        other = {first: second, second: first}
        pairs = []
        for a in range(tm):
            for q in range(n):
                for c in range(col_parts):
                    to = (other[a] * n + (q ^ d)) * col_parts + c if a in other else (a * n + q) * col_parts + (c ^ 1)
                    pairs.append(((a * n + q) * col_parts + c, to))
        return lax.ppermute(block, ("tm", "net", "cols"), pairs)

    def exchange(outgoing, first, second):
        return [swap(outgoing[d - 1], first, second, d) for d in range(1, n)]

    opening = state
    out = None
    for r in range(1, tm):
        arrived = exchange(outgoing, r - 1, r)
        state = swap(state, r - 1, r, 0)
        if r == 1:
            handed = arrived
        before = []
        for s in range(steps):
            fix = r == 1 and s == 0
            if s > 0:
                arrived = exchange(outgoing, r, r)
            first = jac if fix else own(state, s)
            if s < steps - 1:
                state, *outgoing = join(first, s, fix, state, arrived, r)
                before.append(state)
            else:
                out, *rest = close(first, s, state, arrived, r, before, out, r < tm - 1)
                state, *outgoing = rest or [None]
    return out


def solution(mesh):
    return jax.shard_map(
        local,
        mesh=mesh,
        in_specs=(
            P("tm", "net", None, None, None),
            P("net", None),
            P("tm", "net", None, None, None),
            P("net", None),
            P("net", None),
            P("net", None),
            P("cols"),
            P("tm", "cols"),
        ),
        out_specs=P("tm", "cols", "net"),
        check_vma=False,
    )
```

```python
import functools

import jax
import jax.numpy as jnp
from jax import lax
from jax.experimental import pallas as pl
from jax.experimental.pallas import tpu as pltpu
from jax.sharding import PartitionSpec as P

VMEM = pl.BlockSpec(memory_space=pltpu.VMEM)
SMEM = pl.BlockSpec(memory_space=pltpu.SMEM)
HBM = pl.BlockSpec(memory_space=pltpu.HBM)
ANY = pl.BlockSpec(memory_space=pl.ANY)
LIMIT = pltpu.CompilerParams(vmem_limit_bytes=16 * 1024 * 1024)
DMA = pltpu.SemaphoreType.DMA

STATE, LANE, BLOCK, AWAY, GAIN = 0, 1, 2, 3, 4
ROWS = 16


def times_transposed(rows, block):
    return lax.dot_general(rows, block, (((1,), (1,)), ((), ())), preferred_element_type=jnp.float32)


def injected(table, step, first_state, width):
    lane = lax.broadcasted_iota(jnp.int32, (table.shape[0], width), 1)
    hit = table[:, STATE : STATE + 1] == (lane + first_state).astype(jnp.float32)
    return jnp.where(hit, table[:, GAIN + step : GAIN + step + 1], 0.0)


def near_by(state_ref, cols_ref):
    return lambda i, k: state_ref[cols_ref[k, i]]


def own_sum(i, state_ref, jac_ref, near, table, step):
    blocks, _, width = state_ref.shape
    first = (lax.axis_index("net") * blocks + i) * width
    kinds = jac_ref.shape[1]
    rows = [state_ref[i]] + [near(i, k) for k in range(kinds - 1)]
    row_blocks = [jac_ref[i, k] for k in range(kinds)]
    total = times_transposed(jnp.concatenate(rows, axis=1), jnp.concatenate(row_blocks, axis=1))
    return total + injected(table, step, first, width)


def picked(blocks, marks):
    total = blocks[0] * marks[0]
    for block, mark in zip(blocks[1:], marks[1:]):
        total += block * mark
    return total


def marks_layout(n, blocks, kinds):
    sent = n * blocks
    near = sent + n * blocks
    row = near + blocks * (kinds - 1) * blocks
    return sent, near, row, row + 1 + -(row + 1) % 8


def make_marks(marks_ref, blocks, kinds, cols_ref, send_ref, recv_ref, live_ref):
    n = lax.axis_size("net")
    me = lax.axis_index("net")
    width = marks_ref.shape[1]
    lane = lax.broadcasted_iota(jnp.int32, (1, width), 1)
    sent, near, own_row, _ = marks_layout(n, blocks, kinds)

    def put(row, mask):
        marks_ref[pl.ds(row, 1)] = jnp.where(mask, 1.0, 0.0)

    for d in range(n):
        q = me ^ d
        for i in range(blocks):
            put(d * blocks + i, lane < jnp.where(recv_ref[0, q] == i, live_ref[0, q], 0))
            put(sent + d * blocks + i, lane < jnp.where(send_ref[0, q] == i, width, 0))
    for i in range(blocks):
        for k in range(kinds - 1):
            for j in range(blocks):
                put(near + (i * (kinds - 1) + k) * blocks + j, lane < jnp.where(cols_ref[k, i] == j, width, 0))
    marks_ref[pl.ds(own_row, 1)] = table_row(send_ref, me, width)


def add_coupled(incoming, block, live, recv, z_ref):
    mask = lax.broadcasted_iota(jnp.int32, z_ref.shape[1:], 1) < live
    z_ref[recv] += jnp.where(mask, times_transposed(incoming, block), 0.0)


def table_row(send_ref, partition, width):
    lane = lax.broadcasted_iota(jnp.int32, (1, width), 1)
    row = jnp.zeros((1, width), jnp.float32)
    for e in range(lax.axis_size("net")):
        row = jnp.where(lane == e, send_ref[0, partition ^ e].astype(jnp.float32), row)
    return row


def kept(table, rows):
    away, block = table[:, AWAY : AWAY + 1], table[:, BLOCK : BLOCK + 1]
    sent = jnp.broadcast_to(rows[0], (table.shape[0], rows[0].shape[1]))
    for d in range(1, len(rows)):
        sent = jnp.where(away == float(d), rows[d], sent)
    lane = lax.broadcasted_iota(jnp.int32, sent.shape, 1).astype(jnp.float32)
    return jnp.where(jnp.logical_or(away == lane, block == sent), 1.0, 0.0)


def second_kernel(*refs):
    jac_hbm, iface_hbm, *small, table_ref, marks_ref, state_ref = refs[:11]
    n = lax.axis_size("net")
    me = lax.axis_index("net")
    outgoing, refs = refs[11 : 10 + n], refs[10 + n :]
    jac_ref, iface_ref, *loaded, first_ref, sems = refs
    cols_ref, send_ref, recv_ref, live_ref, node_ref, gain_ref = loaded
    blocks, cols, width = state_ref.shape
    loads = [
        pltpu.make_async_copy(source, target, sems.at[i])
        for i, (source, target) in enumerate(
            zip([jac_hbm.at[1], iface_hbm.at[1, 0], *small], [jac_ref, iface_ref, *loaded])
        )
    ]
    here = lax.axis_index("tm") == 0

    @pl.when(here)
    def _():
        for load in loads[:2]:
            load.start()

    for load in loads[2:]:
        load.start()
    for load in loads[2:]:
        load.wait()
    node = node_ref[...]
    block_of = node // width
    rows = [
        node,
        node - block_of * width,
        block_of % blocks,
        (block_of // blocks) ^ me,
    ]
    steps = gain_ref.shape[0]
    fill = -(GAIN + steps) % 8
    rows = [row.astype(jnp.float32) for row in rows] + [gain_ref[...], jnp.zeros((fill, cols), jnp.float32)]
    table_ref[...] = jnp.concatenate(rows, axis=0).T

    @pl.when(here)
    def _():
        table = table_ref[...]
        for i in range(blocks):
            first_ref[i] = injected(table, 0, (me * blocks + i) * width, width).astype(first_ref.dtype)
        lane = lax.broadcasted_iota(jnp.int32, (cols, width), 1).astype(jnp.float32)
        shot = jnp.where(lane == table[:, LANE : LANE + 1], table[:, GAIN : GAIN + 1], 0.0)
        away, block = table[:, AWAY : AWAY + 1], table[:, BLOCK : BLOCK + 1]
        mine = jnp.logical_or(away != 0.0, block == send_ref[0, me].astype(jnp.float32))
        shot = jnp.where(mine, shot, 0.0)
        live = recv = jnp.zeros_like(away)
        for d in range(n):
            live = jnp.where(away == float(d), live_ref[0, me ^ d].astype(jnp.float32), live)
            recv = jnp.where(away == float(d), recv_ref[0, me ^ d].astype(jnp.float32), recv)
        sent = [jnp.where(away == float(d), shot, 0.0).astype(first_ref.dtype) for d in range(n)]
        loads[1].wait()
        ifaces = jnp.concatenate([iface_ref[me ^ d] for d in range(n)], axis=1)
        coupled = times_transposed(jnp.concatenate(sent, axis=1), ifaces)
        coupled = jnp.where(lane < live, coupled, 0.0)
        loads[0].wait()
        for i in range(blocks):
            own = own_sum(i, first_ref, jac_ref, near_by(first_ref, cols_ref), table, 1)
            state_ref[i] = (own + jnp.where(recv == float(i), coupled, 0.0)).astype(state_ref.dtype)
        for d in range(1, n):
            outgoing[d - 1][pl.ds(0, cols)] = state_ref[send_ref[0, me ^ d]]

    @pl.when(jnp.logical_not(here))
    def _():
        make_marks(marks_ref, blocks, jac_ref.shape[1], cols_ref, send_ref, recv_ref, live_ref)

    for d in range(1, n):
        row = table_row(send_ref, me ^ d, width).astype(state_ref.dtype)
        outgoing[d - 1][pl.ds(cols, ROWS)] = jnp.broadcast_to(row, (ROWS, width))


def write_start(states, first, out_ref, sems):
    copies = []
    for s, state_ref in enumerate(states, first):
        width = state_ref.shape[2]
        for i in range(state_ref.shape[0]):
            copies.append(
                pltpu.make_async_copy(state_ref.at[i], out_ref.at[s, :, pl.ds(i * width, width)], sems.at[s, i])
            )
    for copy in copies:
        copy.start()
    return copies


def own_kernel(step, state_ref, jac_ref, cols_ref, table_ref, z_ref):
    table = table_ref[...]
    for i in range(state_ref.shape[0]):
        z_ref[i] = own_sum(i, state_ref, jac_ref.at[step], near_by(state_ref, cols_ref), table, step)


def first_states(opening, handed, jac_ref, iface_ref, ints, table_ref, made_ref, z_ref):
    cols_ref, send_ref, recv_ref, live_ref = ints
    n = lax.axis_size("net")
    blocks, cols, width = z_ref.shape
    table = table_ref[...]
    made_ref[0] = jnp.zeros_like(made_ref[0])
    for i in range(blocks):
        z_ref[i] = own_sum(i, made_ref.at[0], jac_ref.at[0], near_by(made_ref.at[0], cols_ref), table, 0)
    for q in range(n):
        add_coupled(made_ref[0, 0], iface_ref[0, 0, q], live_ref[0, q], recv_ref[0, q], z_ref)
    made_ref[0] = z_ref[...].astype(made_ref.dtype)
    rows = [table_row(send_ref, lax.axis_index("net"), width)]
    rows += [block[cols : cols + 1].astype(jnp.float32) for block in handed]
    keep = kept(table, rows)[:, 0:1]
    for i in range(blocks):
        made_ref[1, i] = jnp.where(keep > 0.0, opening[i], jnp.zeros_like(opening[i]))
    return [made_ref.at[0], made_ref.at[1]]


def joined(sums, step, iface_ref, marks_ref, state_ref, arrived, keep=None):
    n = lax.axis_size("net")
    me = lax.axis_index("net")
    blocks, cols, _ = state_ref.shape
    sent = marks_layout(n, blocks, 1)[0]
    for d in range(n):
        if d:
            block = arrived[d - 1][pl.ds(0, cols)]
        else:
            marks = [marks_ref[pl.ds(sent + j, 1)].astype(state_ref.dtype) for j in range(blocks)]
            block = picked([state_ref[j] for j in range(blocks)], marks)
        term = times_transposed(block, iface_ref[step, 0, me ^ d])
        if keep is not None:
            term *= keep[:, d : d + 1]
        sums = [total + term * marks_ref[pl.ds(d * blocks + i, 1)] for i, total in enumerate(sums)]
    return [total.astype(state_ref.dtype) for total in sums]


def give(made, marks_ref, state_ref, outgoing):
    blocks = len(made)
    n = lax.axis_size("net")
    sent = marks_layout(n, blocks, 1)[0]
    for i in range(blocks):
        state_ref[i] = made[i]
    for d in range(1, n) if outgoing else ():
        marks = [marks_ref[pl.ds(sent + d * blocks + j, 1)].astype(made[j].dtype) for j in range(blocks)]
        outgoing[d - 1][...] = picked(made, marks)


def join_kernel(step, fix, section, *refs):
    n = lax.axis_size("net")
    first_ref, iface_ref, table_ref, marks_ref, *refs = refs
    arrived, state_in_ref, state_ref, outgoing = refs[: n - 1][::-1], refs[n - 1], refs[n], refs[n + 1 :]
    blocks, cols, _ = state_in_ref.shape

    @pl.when(lax.axis_index("tm") == section)
    def _():
        keep = None
        if fix:
            kinds = first_ref.shape[2]
            table = table_ref[...]
            _, near, own_row, _ = marks_layout(n, blocks, kinds)
            state = [state_in_ref[j] for j in range(blocks)]

            def near_block(i, k):
                rows = [near + (i * (kinds - 1) + k) * blocks + j for j in range(blocks)]
                return picked(state, [marks_ref[pl.ds(row, 1)].astype(state_ref.dtype) for row in rows])

            rows = [marks_ref[pl.ds(own_row, 1)]]
            rows += [block[cols : cols + 1].astype(jnp.float32) for block in arrived]
            keep = kept(table, rows)
            sums = [
                own_sum(i, state_in_ref, first_ref.at[step], near_block, table, step) * keep[:, 0:1]
                for i in range(blocks)
            ]
        else:
            sums = [first_ref[i] for i in range(blocks)]
        made = joined(sums, step, iface_ref, marks_ref, state_in_ref, arrived, keep)
        give(made, marks_ref, state_ref, outgoing)


def close_kernel(step, section, firsts, send, before, *refs):
    n = lax.axis_size("net")
    *refs, sems = refs
    if firsts:
        *refs, made_ref, acc_ref, cols_ref, send_ref, recv_ref, live_ref, load_sems = refs
        ints = [cols_ref, send_ref, recv_ref, live_ref]
    z_ref, iface_ref, table_ref, marks_ref, *refs = refs
    arrived, state_in_ref, refs = refs[: n - 1][::-1], refs[n - 1], refs[n:]
    before, refs = refs[:before], refs[before:]
    if firsts:
        opening_ref, handed, jac_ref, sources, refs = refs[0], refs[1:n], refs[n], refs[n + 1 : n + 5], refs[n + 5 :]
    else:
        refs = refs[1:]
    out_ref, state_ref, *outgoing = refs

    @pl.when(lax.axis_index("tm") == section)
    def _():
        copies = write_start(before, 0, out_ref, sems)
        sums = [z_ref[i] for i in range(z_ref.shape[0])]
        made = joined(sums, step, iface_ref, marks_ref, state_in_ref, arrived)
        give(made, marks_ref, state_ref, outgoing)
        copies += write_start([state_ref], len(before), out_ref, sems)
        for copy in copies:
            copy.wait()

    if firsts:

        @pl.when(lax.axis_index("tm") == 0)
        def _():
            loads = [
                pltpu.make_async_copy(source, target, load_sems.at[i])
                for i, (source, target) in enumerate(zip(sources, ints))
            ]
            for load in loads:
                load.start()
            for load in loads:
                load.wait()
            made = first_states(opening_ref, handed, jac_ref, iface_ref, ints, table_ref, made_ref, acc_ref)
            for copy in write_start(made, 0, out_ref, sems):
                copy.wait()


def local(jac, block_cols, iface_jac, iface_send, iface_recv, iface_live, ctrl_node, ctrl_gain):
    steps, blocks, kinds, width, _ = jac.shape
    cols = ctrl_node.shape[0]
    tm = lax.axis_size("tm")
    n = lax.axis_size("net")
    col_parts = lax.axis_size("cols")
    node = ctrl_node[None]
    near = block_cols.T
    bf16 = functools.partial(jax.ShapeDtypeStruct, dtype=jnp.bfloat16)
    f32 = functools.partial(jax.ShapeDtypeStruct, dtype=jnp.float32)
    whole, one = bf16((blocks, cols, width)), bf16((cols, width))
    table_rows = GAIN + steps + -(GAIN + steps) % 8
    written = bf16((steps, cols, blocks * width))

    pinned = [
        pltpu.with_memory_space_constraint(x, pltpu.HBM)
        for x in (jac, iface_jac, near, iface_send, iface_recv, iface_live, node, ctrl_gain)
    ]
    marks_rows = marks_layout(n, blocks, kinds)[-1]
    table, marks, state, *outgoing = pl.pallas_call(
        second_kernel,
        out_shape=[f32((cols, table_rows)), f32((marks_rows, width)), whole]
        + [bf16((cols + ROWS, width))] * (n - 1),
        in_specs=[HBM] * len(pinned),
        out_specs=[VMEM] * (n + 2),
        scratch_shapes=[
            pltpu.VMEM((blocks, kinds, width, width), jnp.bfloat16),
            pltpu.VMEM((n, width, width), jnp.bfloat16),
            *[pltpu.SMEM(x.shape, x.dtype) for x in (near, iface_send, iface_recv, iface_live)],
            *[pltpu.VMEM(x.shape, x.dtype) for x in (node, ctrl_gain)],
            pltpu.VMEM(whole.shape, jnp.bfloat16),
            DMA((len(pinned),)),
        ],
        compiler_params=LIMIT,
    )(*pinned)

    def own(state, step):
        return pl.pallas_call(
            functools.partial(own_kernel, step),
            out_shape=f32(whole.shape),
            in_specs=[VMEM, VMEM, SMEM, VMEM],
            out_specs=VMEM,
            compiler_params=LIMIT,
        )(state, jac, near, table)

    def join(first, step, fix, state, arrived, section):
        return pl.pallas_call(
            functools.partial(join_kernel, step, fix, section),
            out_shape=[whole] + [one] * (n - 1),
            in_specs=[VMEM] * (n + 4),
            out_specs=[VMEM] * n,
            compiler_params=LIMIT,
        )(first, iface_jac, table, marks, *arrived[::-1], state)

    def close(z, step, state, arrived, section, before, out, send):
        firsts = out is None
        arrays = [z, iface_jac, table, marks, *arrived[::-1], state, *before]
        specs = [VMEM] * len(arrays)
        scratch = [DMA((steps, blocks))]
        aliases = {}
        if firsts:
            arrays += [opening, *handed, jac, *pinned[2:6]]
            specs += [VMEM] * (n + 1) + [HBM] * 4
            scratch = [
                pltpu.VMEM((2, *whole.shape), jnp.bfloat16),
                pltpu.VMEM(whole.shape, jnp.float32),
                *[pltpu.SMEM(x.shape, x.dtype) for x in pinned[2:6]],
                DMA((4,)),
            ] + scratch
        else:
            aliases = {len(arrays): 0}
            arrays.append(out)
            specs.append(ANY)
        shapes, out_specs = [written], [ANY]
        if send:
            shapes += [whole] + [one] * (n - 1)
            out_specs += [VMEM] * n
        else:
            scratch.insert(0, pltpu.VMEM(whole.shape, jnp.bfloat16))
        return pl.pallas_call(
            functools.partial(close_kernel, step, section, firsts, send, len(before)),
            out_shape=shapes,
            in_specs=specs,
            out_specs=out_specs,
            input_output_aliases=aliases,
            scratch_shapes=scratch,
            compiler_params=LIMIT,
        )(*arrays)

    def swap(block, first, second, d):
        other = {first: second, second: first}
        pairs = []
        for a in range(tm):
            for q in range(n):
                for c in range(col_parts):
                    to = (other[a] * n + (q ^ d)) * col_parts + c if a in other else (a * n + q) * col_parts + (c ^ 1)
                    pairs.append(((a * n + q) * col_parts + c, to))
        return lax.ppermute(block, ("tm", "net", "cols"), pairs)

    def exchange(outgoing, first, second):
        return [swap(outgoing[d - 1], first, second, d) for d in range(1, n)]

    opening = state
    out = None
    for r in range(1, tm):
        arrived = exchange(outgoing, r - 1, r)
        state = lax.ppermute(state, "tm", [(r - 1, r)])
        if r == 1:
            handed = arrived
        before = []
        for s in range(steps):
            fix = r == 1 and s == 0
            if s > 0:
                arrived = exchange(outgoing, r, r)
            first = jac if fix else own(state, s)
            if s < steps - 1:
                state, *outgoing = join(first, s, fix, state, arrived, r)
                before.append(state)
            else:
                out, *rest = close(first, s, state, arrived, r, before, out, r < tm - 1)
                state, *outgoing = rest or [None]
    return out


def solution(mesh):
    return jax.shard_map(
        local,
        mesh=mesh,
        in_specs=(
            P("tm", "net", None, None, None),
            P("net", None),
            P("tm", "net", None, None, None),
            P("net", None),
            P("net", None),
            P("net", None),
            P("cols"),
            P("tm", "cols"),
        ),
        out_specs=P("tm", "cols", "net"),
        check_vma=False,
    )
```

```python
import functools

import jax
import jax.numpy as jnp
from jax import lax
from jax.experimental import pallas as pl
from jax.experimental.pallas import tpu as pltpu
from jax.sharding import PartitionSpec as P

VMEM = pl.BlockSpec(memory_space=pltpu.VMEM)
SMEM = pl.BlockSpec(memory_space=pltpu.SMEM)
HBM = pl.BlockSpec(memory_space=pltpu.HBM)
ANY = pl.BlockSpec(memory_space=pl.ANY)
LIMIT = pltpu.CompilerParams(vmem_limit_bytes=16 * 1024 * 1024)
DMA = pltpu.SemaphoreType.DMA

STATE, LANE, BLOCK, AWAY, GAIN = 0, 1, 2, 3, 4
ROWS = 16


def turn(d, n, col):
    return jnp.where(jnp.logical_and(col % 2 == 1, d > 0), n - d, d)


def partner(partition, d):
    return partition ^ turn(d, lax.axis_size("net"), lax.axis_index("cols"))


def times_transposed(rows, block):
    return lax.dot_general(rows, block, (((1,), (1,)), ((), ())), preferred_element_type=jnp.float32)


def injected(table, step, first_state, width):
    lane = lax.broadcasted_iota(jnp.int32, (table.shape[0], width), 1)
    hit = table[:, STATE : STATE + 1] == (lane + first_state).astype(jnp.float32)
    return jnp.where(hit, table[:, GAIN + step : GAIN + step + 1], 0.0)


def near_by(state_ref, cols_ref):
    return lambda i, k: state_ref[cols_ref[k, i]]


def own_sum(i, state_ref, jac_ref, near, table, step):
    blocks, _, width = state_ref.shape
    first = (lax.axis_index("net") * blocks + i) * width
    kinds = jac_ref.shape[1]
    rows = [state_ref[i]] + [near(i, k) for k in range(kinds - 1)]
    row_blocks = [jac_ref[i, k] for k in range(kinds)]
    total = times_transposed(jnp.concatenate(rows, axis=1), jnp.concatenate(row_blocks, axis=1))
    return total + injected(table, step, first, width)


def picked(blocks, marks):
    total = blocks[0] * marks[0]
    for block, mark in zip(blocks[1:], marks[1:]):
        total += block * mark
    return total


def marks_layout(n, blocks, kinds):
    sent = n * blocks
    near = sent + n * blocks
    row = near + blocks * (kinds - 1) * blocks
    return sent, near, row, row + 1 + -(row + 1) % 8


def make_marks(marks_ref, blocks, kinds, cols_ref, send_ref, recv_ref, live_ref):
    n = lax.axis_size("net")
    me = lax.axis_index("net")
    width = marks_ref.shape[1]
    lane = lax.broadcasted_iota(jnp.int32, (1, width), 1)
    sent, near, own_row, _ = marks_layout(n, blocks, kinds)

    def put(row, mask):
        marks_ref[pl.ds(row, 1)] = jnp.where(mask, 1.0, 0.0)

    for d in range(n):
        q = partner(me, d)
        for i in range(blocks):
            put(d * blocks + i, lane < jnp.where(recv_ref[0, q] == i, live_ref[0, q], 0))
            put(sent + d * blocks + i, lane < jnp.where(send_ref[0, q] == i, width, 0))
    for i in range(blocks):
        for k in range(kinds - 1):
            for j in range(blocks):
                put(near + (i * (kinds - 1) + k) * blocks + j, lane < jnp.where(cols_ref[k, i] == j, width, 0))
    marks_ref[pl.ds(own_row, 1)] = table_row(send_ref, me, width)


def add_coupled(incoming, block, live, recv, z_ref):
    mask = lax.broadcasted_iota(jnp.int32, z_ref.shape[1:], 1) < live
    z_ref[recv] += jnp.where(mask, times_transposed(incoming, block), 0.0)


def table_row(send_ref, partition, width):
    lane = lax.broadcasted_iota(jnp.int32, (1, width), 1)
    row = jnp.zeros((1, width), jnp.float32)
    for e in range(lax.axis_size("net")):
        row = jnp.where(lane == e, send_ref[0, partner(partition, e)].astype(jnp.float32), row)
    return row


def kept(table, rows):
    away, block = table[:, AWAY : AWAY + 1], table[:, BLOCK : BLOCK + 1]
    sent = jnp.broadcast_to(rows[0], (table.shape[0], rows[0].shape[1]))
    for d in range(1, len(rows)):
        sent = jnp.where(away == float(d), rows[d], sent)
    lane = lax.broadcasted_iota(jnp.int32, sent.shape, 1).astype(jnp.float32)
    return jnp.where(jnp.logical_or(away == lane, block == sent), 1.0, 0.0)


def second_kernel(*refs):
    jac_hbm, iface_hbm, *small, table_ref, marks_ref, state_ref = refs[:11]
    n = lax.axis_size("net")
    me = lax.axis_index("net")
    outgoing, refs = refs[11 : 10 + n], refs[10 + n :]
    jac_ref, iface_ref, *loaded, first_ref, sems = refs
    cols_ref, send_ref, recv_ref, live_ref, node_ref, gain_ref = loaded
    blocks, cols, width = state_ref.shape
    loads = [
        pltpu.make_async_copy(source, target, sems.at[i])
        for i, (source, target) in enumerate(
            zip([jac_hbm.at[1], iface_hbm.at[1, 0], *small], [jac_ref, iface_ref, *loaded])
        )
    ]
    here = lax.axis_index("tm") == 0

    @pl.when(here)
    def _():
        for load in loads[:2]:
            load.start()

    for load in loads[2:]:
        load.start()
    for load in loads[2:]:
        load.wait()
    node = node_ref[...]
    block_of = node // width
    rows = [
        node,
        node - block_of * width,
        block_of % blocks,
        turn((block_of // blocks) ^ me, n, lax.axis_index("cols")),
    ]
    steps = gain_ref.shape[0]
    fill = -(GAIN + steps) % 8
    rows = [row.astype(jnp.float32) for row in rows] + [gain_ref[...], jnp.zeros((fill, cols), jnp.float32)]
    table_ref[...] = jnp.concatenate(rows, axis=0).T

    @pl.when(here)
    def _():
        table = table_ref[...]
        for i in range(blocks):
            first_ref[i] = injected(table, 0, (me * blocks + i) * width, width).astype(first_ref.dtype)
        lane = lax.broadcasted_iota(jnp.int32, (cols, width), 1).astype(jnp.float32)
        shot = jnp.where(lane == table[:, LANE : LANE + 1], table[:, GAIN : GAIN + 1], 0.0)
        away, block = table[:, AWAY : AWAY + 1], table[:, BLOCK : BLOCK + 1]
        mine = jnp.logical_or(away != 0.0, block == send_ref[0, me].astype(jnp.float32))
        shot = jnp.where(mine, shot, 0.0)
        live = recv = jnp.zeros_like(away)
        for d in range(n):
            live = jnp.where(away == float(d), live_ref[0, partner(me, d)].astype(jnp.float32), live)
            recv = jnp.where(away == float(d), recv_ref[0, partner(me, d)].astype(jnp.float32), recv)
        sent = [jnp.where(away == float(d), shot, 0.0).astype(first_ref.dtype) for d in range(n)]
        loads[1].wait()
        ifaces = jnp.concatenate([iface_ref[partner(me, d)] for d in range(n)], axis=1)
        coupled = times_transposed(jnp.concatenate(sent, axis=1), ifaces)
        coupled = jnp.where(lane < live, coupled, 0.0)
        loads[0].wait()
        for i in range(blocks):
            own = own_sum(i, first_ref, jac_ref, near_by(first_ref, cols_ref), table, 1)
            state_ref[i] = (own + jnp.where(recv == float(i), coupled, 0.0)).astype(state_ref.dtype)
        for d in range(1, n):
            outgoing[d - 1][pl.ds(0, cols)] = state_ref[send_ref[0, partner(me, d)]]

    @pl.when(jnp.logical_not(here))
    def _():
        make_marks(marks_ref, blocks, jac_ref.shape[1], cols_ref, send_ref, recv_ref, live_ref)

    for d in range(1, n):
        row = table_row(send_ref, partner(me, d), width).astype(state_ref.dtype)
        outgoing[d - 1][pl.ds(cols, ROWS)] = jnp.broadcast_to(row, (ROWS, width))


def write_start(states, first, out_ref, sems):
    copies = []
    for s, state_ref in enumerate(states, first):
        width = state_ref.shape[2]
        for i in range(state_ref.shape[0]):
            copies.append(
                pltpu.make_async_copy(state_ref.at[i], out_ref.at[s, :, pl.ds(i * width, width)], sems.at[s, i])
            )
    for copy in copies:
        copy.start()
    return copies


def own_kernel(step, state_ref, jac_ref, cols_ref, table_ref, z_ref):
    table = table_ref[...]
    for i in range(state_ref.shape[0]):
        z_ref[i] = own_sum(i, state_ref, jac_ref.at[step], near_by(state_ref, cols_ref), table, step)


def first_states(opening, handed, jac_ref, iface_ref, ints, table_ref, made_ref, z_ref):
    cols_ref, send_ref, recv_ref, live_ref = ints
    n = lax.axis_size("net")
    blocks, cols, width = z_ref.shape
    table = table_ref[...]
    made_ref[0] = jnp.zeros_like(made_ref[0])
    for i in range(blocks):
        z_ref[i] = own_sum(i, made_ref.at[0], jac_ref.at[0], near_by(made_ref.at[0], cols_ref), table, 0)
    for q in range(n):
        add_coupled(made_ref[0, 0], iface_ref[0, 0, q], live_ref[0, q], recv_ref[0, q], z_ref)
    made_ref[0] = z_ref[...].astype(made_ref.dtype)
    rows = [table_row(send_ref, lax.axis_index("net"), width)]
    rows += [block[cols : cols + 1].astype(jnp.float32) for block in handed]
    keep = kept(table, rows)[:, 0:1]
    for i in range(blocks):
        made_ref[1, i] = jnp.where(keep > 0.0, opening[i], jnp.zeros_like(opening[i]))
    return [made_ref.at[0], made_ref.at[1]]


def joined(sums, step, iface_ref, marks_ref, state_ref, arrived, keep=None):
    n = lax.axis_size("net")
    me = lax.axis_index("net")
    blocks, cols, _ = state_ref.shape
    sent = marks_layout(n, blocks, 1)[0]
    for d in range(n):
        if d:
            block = arrived[d - 1][pl.ds(0, cols)]
        else:
            marks = [marks_ref[pl.ds(sent + j, 1)].astype(state_ref.dtype) for j in range(blocks)]
            block = picked([state_ref[j] for j in range(blocks)], marks)
        term = times_transposed(block, iface_ref[step, 0, partner(me, d)])
        if keep is not None:
            term *= keep[:, d : d + 1]
        sums = [total + term * marks_ref[pl.ds(d * blocks + i, 1)] for i, total in enumerate(sums)]
    return [total.astype(state_ref.dtype) for total in sums]


def give(made, marks_ref, state_ref, outgoing):
    blocks = len(made)
    n = lax.axis_size("net")
    sent = marks_layout(n, blocks, 1)[0]
    for i in range(blocks):
        state_ref[i] = made[i]
    for d in range(1, n) if outgoing else ():
        marks = [marks_ref[pl.ds(sent + d * blocks + j, 1)].astype(made[j].dtype) for j in range(blocks)]
        outgoing[d - 1][...] = picked(made, marks)


def join_kernel(step, fix, section, *refs):
    n = lax.axis_size("net")
    first_ref, iface_ref, table_ref, marks_ref, *refs = refs
    arrived, state_in_ref, state_ref, outgoing = refs[: n - 1][::-1], refs[n - 1], refs[n], refs[n + 1 :]
    blocks, cols, _ = state_in_ref.shape

    @pl.when(lax.axis_index("tm") == section)
    def _():
        keep = None
        if fix:
            kinds = first_ref.shape[2]
            table = table_ref[...]
            _, near, own_row, _ = marks_layout(n, blocks, kinds)
            state = [state_in_ref[j] for j in range(blocks)]

            def near_block(i, k):
                rows = [near + (i * (kinds - 1) + k) * blocks + j for j in range(blocks)]
                return picked(state, [marks_ref[pl.ds(row, 1)].astype(state_ref.dtype) for row in rows])

            rows = [marks_ref[pl.ds(own_row, 1)]]
            rows += [block[cols : cols + 1].astype(jnp.float32) for block in arrived]
            keep = kept(table, rows)
            sums = [
                own_sum(i, state_in_ref, first_ref.at[step], near_block, table, step) * keep[:, 0:1]
                for i in range(blocks)
            ]
        else:
            sums = [first_ref[i] for i in range(blocks)]
        made = joined(sums, step, iface_ref, marks_ref, state_in_ref, arrived, keep)
        give(made, marks_ref, state_ref, outgoing)


def close_kernel(step, section, firsts, send, before, *refs):
    n = lax.axis_size("net")
    *refs, sems = refs
    if firsts:
        *refs, made_ref, acc_ref, cols_ref, send_ref, recv_ref, live_ref, load_sems = refs
        ints = [cols_ref, send_ref, recv_ref, live_ref]
    z_ref, iface_ref, table_ref, marks_ref, *refs = refs
    arrived, state_in_ref, refs = refs[: n - 1][::-1], refs[n - 1], refs[n:]
    before, refs = refs[:before], refs[before:]
    if firsts:
        opening_ref, handed, jac_ref, sources, refs = refs[0], refs[1:n], refs[n], refs[n + 1 : n + 5], refs[n + 5 :]
    else:
        refs = refs[1:]
    out_ref, state_ref, *outgoing = refs

    @pl.when(lax.axis_index("tm") == section)
    def _():
        copies = write_start(before, 0, out_ref, sems)
        sums = [z_ref[i] for i in range(z_ref.shape[0])]
        made = joined(sums, step, iface_ref, marks_ref, state_in_ref, arrived)
        give(made, marks_ref, state_ref, outgoing)
        copies += write_start([state_ref], len(before), out_ref, sems)
        for copy in copies:
            copy.wait()

    if firsts:

        @pl.when(lax.axis_index("tm") == 0)
        def _():
            loads = [
                pltpu.make_async_copy(source, target, load_sems.at[i])
                for i, (source, target) in enumerate(zip(sources, ints))
            ]
            for load in loads:
                load.start()
            for load in loads:
                load.wait()
            made = first_states(opening_ref, handed, jac_ref, iface_ref, ints, table_ref, made_ref, acc_ref)
            for copy in write_start(made, 0, out_ref, sems):
                copy.wait()


def local(jac, block_cols, iface_jac, iface_send, iface_recv, iface_live, ctrl_node, ctrl_gain):
    steps, blocks, kinds, width, _ = jac.shape
    cols = ctrl_node.shape[0]
    tm = lax.axis_size("tm")
    n = lax.axis_size("net")
    col_parts = lax.axis_size("cols")
    node = ctrl_node[None]
    near = block_cols.T
    bf16 = functools.partial(jax.ShapeDtypeStruct, dtype=jnp.bfloat16)
    f32 = functools.partial(jax.ShapeDtypeStruct, dtype=jnp.float32)
    whole, one = bf16((blocks, cols, width)), bf16((cols, width))
    table_rows = GAIN + steps + -(GAIN + steps) % 8
    written = bf16((steps, cols, blocks * width))

    pinned = [
        pltpu.with_memory_space_constraint(x, pltpu.HBM)
        for x in (jac, iface_jac, near, iface_send, iface_recv, iface_live, node, ctrl_gain)
    ]
    marks_rows = marks_layout(n, blocks, kinds)[-1]
    table, marks, state, *outgoing = pl.pallas_call(
        second_kernel,
        out_shape=[f32((cols, table_rows)), f32((marks_rows, width)), whole]
        + [bf16((cols + ROWS, width))] * (n - 1),
        in_specs=[HBM] * len(pinned),
        out_specs=[VMEM] * (n + 2),
        scratch_shapes=[
            pltpu.VMEM((blocks, kinds, width, width), jnp.bfloat16),
            pltpu.VMEM((n, width, width), jnp.bfloat16),
            *[pltpu.SMEM(x.shape, x.dtype) for x in (near, iface_send, iface_recv, iface_live)],
            *[pltpu.VMEM(x.shape, x.dtype) for x in (node, ctrl_gain)],
            pltpu.VMEM(whole.shape, jnp.bfloat16),
            DMA((len(pinned),)),
        ],
        compiler_params=LIMIT,
    )(*pinned)

    def own(state, step):
        return pl.pallas_call(
            functools.partial(own_kernel, step),
            out_shape=f32(whole.shape),
            in_specs=[VMEM, VMEM, SMEM, VMEM],
            out_specs=VMEM,
            compiler_params=LIMIT,
        )(state, jac, near, table)

    def join(first, step, fix, state, arrived, section):
        return pl.pallas_call(
            functools.partial(join_kernel, step, fix, section),
            out_shape=[whole] + [one] * (n - 1),
            in_specs=[VMEM] * (n + 4),
            out_specs=[VMEM] * n,
            compiler_params=LIMIT,
        )(first, iface_jac, table, marks, *arrived[::-1], state)

    def close(z, step, state, arrived, section, before, out, send):
        firsts = out is None
        arrays = [z, iface_jac, table, marks, *arrived[::-1], state, *before]
        specs = [VMEM] * len(arrays)
        scratch = [DMA((steps, blocks))]
        aliases = {}
        if firsts:
            arrays += [opening, *handed, jac, *pinned[2:6]]
            specs += [VMEM] * (n + 1) + [HBM] * 4
            scratch = [
                pltpu.VMEM((2, *whole.shape), jnp.bfloat16),
                pltpu.VMEM(whole.shape, jnp.float32),
                *[pltpu.SMEM(x.shape, x.dtype) for x in pinned[2:6]],
                DMA((4,)),
            ] + scratch
        else:
            aliases = {len(arrays): 0}
            arrays.append(out)
            specs.append(ANY)
        shapes, out_specs = [written], [ANY]
        if send:
            shapes += [whole] + [one] * (n - 1)
            out_specs += [VMEM] * n
        else:
            scratch.insert(0, pltpu.VMEM(whole.shape, jnp.bfloat16))
        return pl.pallas_call(
            functools.partial(close_kernel, step, section, firsts, send, len(before)),
            out_shape=shapes,
            in_specs=specs,
            out_specs=out_specs,
            input_output_aliases=aliases,
            scratch_shapes=scratch,
            compiler_params=LIMIT,
        )(*arrays)

    def swap(block, first, second, d):
        other = {first: second, second: first}
        pairs = []
        for a in range(tm):
            for q in range(n):
                for c in range(col_parts):
                    p = q ^ (n - d if c % 2 == 1 and d > 0 else d)
                    to = (other[a] * n + p) * col_parts + c if a in other else (a * n + q) * col_parts + (c ^ 1)
                    pairs.append(((a * n + q) * col_parts + c, to))
        return lax.ppermute(block, ("tm", "net", "cols"), pairs)

    def exchange(outgoing, first, second):
        return [swap(outgoing[d - 1], first, second, d) for d in range(1, n)]

    opening = state
    out = None
    for r in range(1, tm):
        arrived = exchange(outgoing, r - 1, r)
        state = swap(state, r - 1, r, 0)
        if r == 1:
            handed = arrived
        before = []
        for s in range(steps):
            fix = r == 1 and s == 0
            if s > 0:
                arrived = exchange(outgoing, r, r)
            first = jac if fix else own(state, s)
            if s < steps - 1:
                state, *outgoing = join(first, s, fix, state, arrived, r)
                before.append(state)
            else:
                out, *rest = close(first, s, state, arrived, r, before, out, r < tm - 1)
                state, *outgoing = rest or [None]
    return out


def solution(mesh):
    return jax.shard_map(
        local,
        mesh=mesh,
        in_specs=(
            P("tm", "net", None, None, None),
            P("net", None),
            P("tm", "net", None, None, None),
            P("net", None),
            P("net", None),
            P("net", None),
            P("cols"),
            P("tm", "cols"),
        ),
        out_specs=P("tm", "cols", "net"),
        check_vma=False,
    )
```

```python
import functools

import jax
import jax.numpy as jnp
from jax import lax
from jax.experimental import pallas as pl
from jax.experimental.pallas import tpu as pltpu
from jax.sharding import PartitionSpec as P

VMEM = pl.BlockSpec(memory_space=pltpu.VMEM)
SMEM = pl.BlockSpec(memory_space=pltpu.SMEM)
HBM = pl.BlockSpec(memory_space=pltpu.HBM)
ANY = pl.BlockSpec(memory_space=pl.ANY)
LIMIT = pltpu.CompilerParams(vmem_limit_bytes=16 * 1024 * 1024)
DMA = pltpu.SemaphoreType.DMA

STATE, LANE, BLOCK, AWAY, GAIN = 0, 1, 2, 3, 4
ROWS = 16


def times_transposed(rows, block):
    return lax.dot_general(rows, block, (((1,), (1,)), ((), ())), preferred_element_type=jnp.float32)


def hits(table, i, blocks, width):
    first_state = (lax.axis_index("net") * blocks + i) * width
    lane = lax.broadcasted_iota(jnp.int32, (table.shape[0], width), 1)
    return table[:, STATE : STATE + 1] == (lane + first_state).astype(jnp.float32)


def injected(table, step, hit):
    return jnp.where(hit, table[:, GAIN + step : GAIN + step + 1], 0.0)


def near_by(state_ref, cols_ref):
    return lambda i, k: state_ref[cols_ref[k, i]]


def own_sum(i, state_ref, jac_ref, near, table, step, hit=None):
    blocks, _, width = state_ref.shape
    if hit is None:
        hit = hits(table, i, blocks, width)
    kinds = jac_ref.shape[1]
    rows = [state_ref[i]] + [near(i, k) for k in range(kinds - 1)]
    row_blocks = [jac_ref[i, k] for k in range(kinds)]
    total = times_transposed(jnp.concatenate(rows, axis=1), jnp.concatenate(row_blocks, axis=1))
    return total + injected(table, step, hit)


def picked(blocks, marks):
    total = blocks[0] * marks[0]
    for block, mark in zip(blocks[1:], marks[1:]):
        total += block * mark
    return total


def marks_layout(n, blocks, kinds):
    sent = n * blocks
    near = sent + n * blocks
    row = near + blocks * (kinds - 1) * blocks
    return sent, near, row, row + 1 + -(row + 1) % 8


def make_marks(marks_ref, blocks, kinds, cols_ref, send_ref, recv_ref, live_ref):
    n = lax.axis_size("net")
    me = lax.axis_index("net")
    width = marks_ref.shape[1]
    lane = lax.broadcasted_iota(jnp.int32, (1, width), 1)
    sent, near, own_row, _ = marks_layout(n, blocks, kinds)

    def put(row, mask):
        marks_ref[pl.ds(row, 1)] = jnp.where(mask, 1.0, 0.0)

    for d in range(n):
        q = me ^ d
        for i in range(blocks):
            put(d * blocks + i, lane < jnp.where(recv_ref[0, q] == i, live_ref[0, q], 0))
            put(sent + d * blocks + i, lane < jnp.where(send_ref[0, q] == i, width, 0))
    for i in range(blocks):
        for k in range(kinds - 1):
            for j in range(blocks):
                put(near + (i * (kinds - 1) + k) * blocks + j, lane < jnp.where(cols_ref[k, i] == j, width, 0))
    marks_ref[pl.ds(own_row, 1)] = table_row(send_ref, me, width)


def add_coupled(incoming, block, live, recv, z_ref):
    mask = lax.broadcasted_iota(jnp.int32, z_ref.shape[1:], 1) < live
    z_ref[recv] += jnp.where(mask, times_transposed(incoming, block), 0.0)


def table_row(send_ref, partition, width):
    lane = lax.broadcasted_iota(jnp.int32, (1, width), 1)
    row = jnp.zeros((1, width), jnp.float32)
    for e in range(lax.axis_size("net")):
        row = jnp.where(lane == e, send_ref[0, partition ^ e].astype(jnp.float32), row)
    return row


def kept(table, rows):
    away, block = table[:, AWAY : AWAY + 1], table[:, BLOCK : BLOCK + 1]
    sent = jnp.broadcast_to(rows[0], (table.shape[0], rows[0].shape[1]))
    for d in range(1, len(rows)):
        sent = jnp.where(away == float(d), rows[d], sent)
    lane = lax.broadcasted_iota(jnp.int32, sent.shape, 1).astype(jnp.float32)
    return jnp.where(jnp.logical_or(away == lane, block == sent), 1.0, 0.0)


def second_kernel(*refs):
    jac_hbm, iface_hbm, *small, table_ref, marks_ref, state_ref = refs[:11]
    n = lax.axis_size("net")
    me = lax.axis_index("net")
    outgoing, refs = refs[11 : 10 + n], refs[10 + n :]
    jac_ref, iface_ref, *loaded, first_ref, sems = refs
    cols_ref, send_ref, recv_ref, live_ref, node_ref, gain_ref = loaded
    blocks, cols, width = state_ref.shape
    sources = [jac_hbm.at[1], iface_hbm.at[1, 0], *small]
    loads = [
        pltpu.make_async_copy(source, target, sems.at[i])
        for i, (source, target) in enumerate(zip(sources, [jac_ref, iface_ref, *loaded]))
    ]
    here = lax.axis_index("tm") == 0
    for load in loads[6:]:
        load.start()

    @pl.when(here)
    def _():
        for load in loads[:2]:
            load.start()

    for load in loads[2:6]:
        load.start()
    for load in loads[6:]:
        load.wait()
    node = node_ref[...]
    block_of = node // width
    rows = [
        node,
        node - block_of * width,
        block_of % blocks,
        (block_of // blocks) ^ me,
    ]
    steps = gain_ref.shape[0]
    fill = -(GAIN + steps) % 8
    rows = [row.astype(jnp.float32) for row in rows] + [gain_ref[...], jnp.zeros((fill, cols), jnp.float32)]
    table_ref[...] = jnp.concatenate(rows, axis=0).T

    @pl.when(here)
    def _():
        table = table_ref[...]
        hit = [hits(table, i, blocks, width) for i in range(blocks)]
        for i in range(blocks):
            first_ref[i] = injected(table, 0, hit[i]).astype(first_ref.dtype)
        lane = lax.broadcasted_iota(jnp.int32, (cols, width), 1).astype(jnp.float32)
        shot = jnp.where(lane == table[:, LANE : LANE + 1], table[:, GAIN : GAIN + 1], 0.0)
        away, block = table[:, AWAY : AWAY + 1], table[:, BLOCK : BLOCK + 1]
        for load in loads[2:6]:
            load.wait()
        mine = jnp.logical_or(away != 0.0, block == send_ref[0, me].astype(jnp.float32))
        shot = jnp.where(mine, shot, 0.0)
        live = recv = jnp.zeros_like(away)
        for d in range(n):
            live = jnp.where(away == float(d), live_ref[0, me ^ d].astype(jnp.float32), live)
            recv = jnp.where(away == float(d), recv_ref[0, me ^ d].astype(jnp.float32), recv)
        sent = [jnp.where(away == float(d), shot, 0.0).astype(first_ref.dtype) for d in range(n)]
        loads[1].wait()
        ifaces = jnp.concatenate([iface_ref[me ^ d] for d in range(n)], axis=1)
        coupled = times_transposed(jnp.concatenate(sent, axis=1), ifaces)
        coupled = jnp.where(lane < live, coupled, 0.0)
        loads[0].wait()
        for i in range(blocks):
            own = own_sum(i, first_ref, jac_ref, near_by(first_ref, cols_ref), table, 1, hit[i])
            state_ref[i] = (own + jnp.where(recv == float(i), coupled, 0.0)).astype(state_ref.dtype)
        for d in range(1, n):
            outgoing[d - 1][pl.ds(0, cols)] = state_ref[send_ref[0, me ^ d]]

    @pl.when(jnp.logical_not(here))
    def _():
        for load in loads[2:6]:
            load.wait()
        make_marks(marks_ref, blocks, jac_ref.shape[1], cols_ref, send_ref, recv_ref, live_ref)

    for d in range(1, n):
        row = table_row(send_ref, me ^ d, width).astype(state_ref.dtype)
        outgoing[d - 1][pl.ds(cols, ROWS)] = jnp.broadcast_to(row, (ROWS, width))


def write_start(states, first, out_ref, sems):
    copies = []
    for s, state_ref in enumerate(states, first):
        width = state_ref.shape[2]
        for i in range(state_ref.shape[0]):
            copies.append(
                pltpu.make_async_copy(state_ref.at[i], out_ref.at[s, :, pl.ds(i * width, width)], sems.at[s, i])
            )
    for copy in copies:
        copy.start()
    return copies


def own_kernel(step, state_ref, jac_ref, iface_ref, table_ref, marks_ref, z_ref):
    table = table_ref[...]
    n = lax.axis_size("net")
    blocks = state_ref.shape[0]
    kinds = jac_ref.shape[2]
    sent, near, _, _ = marks_layout(n, blocks, kinds)
    state = [state_ref[j] for j in range(blocks)]

    def pick(row):
        return picked(state, [marks_ref[pl.ds(row + j, 1)].astype(state_ref.dtype) for j in range(blocks)])

    def near_block(i, k):
        return pick(near + (i * (kinds - 1) + k) * blocks)

    @pl.when(lax.axis_index("tm") > 0)
    def _():
        term = times_transposed(pick(sent), iface_ref[step, 0, lax.axis_index("net")])
        for i in range(blocks):
            own = own_sum(i, state_ref, jac_ref.at[step], near_block, table, step)
            z_ref[i] = own + term * marks_ref[pl.ds(i, 1)]


def first_states(opening, handed, jac_ref, iface_ref, ints, table_ref, made_ref, z_ref):
    cols_ref, send_ref, recv_ref, live_ref = ints
    n = lax.axis_size("net")
    blocks, cols, width = z_ref.shape
    table = table_ref[...]
    made_ref[0] = jnp.zeros_like(made_ref[0])
    for i in range(blocks):
        z_ref[i] = own_sum(i, made_ref.at[0], jac_ref.at[0], near_by(made_ref.at[0], cols_ref), table, 0)
    for q in range(n):
        add_coupled(made_ref[0, 0], iface_ref[0, 0, q], live_ref[0, q], recv_ref[0, q], z_ref)
    made_ref[0] = z_ref[...].astype(made_ref.dtype)
    rows = [table_row(send_ref, lax.axis_index("net"), width)]
    rows += [block[cols : cols + 1].astype(jnp.float32) for block in handed]
    keep = kept(table, rows)[:, 0:1]
    for i in range(blocks):
        made_ref[1, i] = jnp.where(keep > 0.0, opening[i], jnp.zeros_like(opening[i]))
    return [made_ref.at[0], made_ref.at[1]]


def joined(sums, step, iface_ref, marks_ref, arrived, keep=None):
    me = lax.axis_index("net")
    blocks, cols = len(sums), sums[0].shape[0]
    if keep is not None:
        sums = [total * keep[:, 0:1] for total in sums]
    for d, block in enumerate(arrived, 1):
        term = times_transposed(block[pl.ds(0, cols)], iface_ref[step, 0, me ^ d])
        if keep is not None:
            term *= keep[:, d : d + 1]
        sums = [total + term * marks_ref[pl.ds(d * blocks + i, 1)] for i, total in enumerate(sums)]
    return [total.astype(jnp.bfloat16) for total in sums]


def give(made, marks_ref, state_ref, outgoing):
    blocks = len(made)
    n = lax.axis_size("net")
    sent = marks_layout(n, blocks, 1)[0]
    for i in range(blocks):
        state_ref[i] = made[i]
    for d in range(1, n) if outgoing else ():
        marks = [marks_ref[pl.ds(sent + d * blocks + j, 1)].astype(made[j].dtype) for j in range(blocks)]
        outgoing[d - 1][...] = picked(made, marks)


def join_kernel(step, fix, section, z_ref, iface_ref, table_ref, marks_ref, *refs):
    n = lax.axis_size("net")
    arrived, state_ref, outgoing = refs[: n - 1][::-1], refs[n - 1], refs[n:]
    blocks, cols, _ = z_ref.shape

    @pl.when(lax.axis_index("tm") == section)
    def _():
        keep = None
        if fix:
            rows = [marks_ref[pl.ds(marks_layout(n, blocks, fix)[2], 1)]]
            rows += [block[cols : cols + 1].astype(jnp.float32) for block in arrived]
            keep = kept(table_ref[...], rows)
        made = joined([z_ref[i] for i in range(blocks)], step, iface_ref, marks_ref, arrived, keep)
        give(made, marks_ref, state_ref, outgoing)


def close_kernel(step, section, firsts, send, before, *refs):
    n = lax.axis_size("net")
    *refs, sems = refs
    if firsts:
        *refs, made_ref, acc_ref, cols_ref, send_ref, recv_ref, live_ref, load_sems = refs
        ints = [cols_ref, send_ref, recv_ref, live_ref]
    z_ref, iface_ref, table_ref, marks_ref, *refs = refs
    arrived, refs = refs[: n - 1][::-1], refs[n - 1 :]
    before, refs = refs[:before], refs[before:]
    if firsts:
        opening_ref, handed, jac_ref, sources, refs = refs[0], refs[1:n], refs[n], refs[n + 1 : n + 5], refs[n + 5 :]
    else:
        refs = refs[1:]
    out_ref, state_ref, *outgoing = refs

    @pl.when(lax.axis_index("tm") == section)
    def _():
        copies = write_start(before, 0, out_ref, sems)
        sums = [z_ref[i] for i in range(z_ref.shape[0])]
        made = joined(sums, step, iface_ref, marks_ref, arrived)
        give(made, marks_ref, state_ref, outgoing)
        copies += write_start([state_ref], len(before), out_ref, sems)
        for copy in copies:
            copy.wait()

    if firsts:

        @pl.when(lax.axis_index("tm") == 0)
        def _():
            loads = [
                pltpu.make_async_copy(source, target, load_sems.at[i])
                for i, (source, target) in enumerate(zip(sources, ints))
            ]
            for load in loads:
                load.start()
            for load in loads:
                load.wait()
            made = first_states(opening_ref, handed, jac_ref, iface_ref, ints, table_ref, made_ref, acc_ref)
            for copy in write_start(made, 0, out_ref, sems):
                copy.wait()


def local(jac, block_cols, iface_jac, iface_send, iface_recv, iface_live, ctrl_node, ctrl_gain):
    steps, blocks, kinds, width, _ = jac.shape
    cols = ctrl_node.shape[0]
    tm = lax.axis_size("tm")
    n = lax.axis_size("net")
    col_parts = lax.axis_size("cols")
    node = ctrl_node[None]
    near = block_cols.T
    bf16 = functools.partial(jax.ShapeDtypeStruct, dtype=jnp.bfloat16)
    f32 = functools.partial(jax.ShapeDtypeStruct, dtype=jnp.float32)
    whole, one = bf16((blocks, cols, width)), bf16((cols, width))
    table_rows = GAIN + steps + -(GAIN + steps) % 8
    written = bf16((steps, cols, blocks * width))

    pinned = [
        pltpu.with_memory_space_constraint(x, pltpu.HBM)
        for x in (jac, iface_jac, near, iface_send, iface_recv, iface_live, node, ctrl_gain)
    ]
    marks_rows = marks_layout(n, blocks, kinds)[-1]
    table, marks, state, *outgoing = pl.pallas_call(
        second_kernel,
        out_shape=[f32((cols, table_rows)), f32((marks_rows, width)), whole]
        + [bf16((cols + ROWS, width))] * (n - 1),
        in_specs=[HBM] * len(pinned),
        out_specs=[VMEM] * (n + 2),
        scratch_shapes=[
            pltpu.VMEM((blocks, kinds, width, width), jnp.bfloat16),
            pltpu.VMEM((n, width, width), jnp.bfloat16),
            *[pltpu.SMEM(x.shape, x.dtype) for x in (near, iface_send, iface_recv, iface_live)],
            *[pltpu.VMEM(x.shape, x.dtype) for x in (node, ctrl_gain)],
            pltpu.VMEM(whole.shape, jnp.bfloat16),
            DMA((len(pinned),)),
        ],
        compiler_params=LIMIT,
    )(*pinned)

    def own(state, step):
        return pl.pallas_call(
            functools.partial(own_kernel, step),
            out_shape=f32(whole.shape),
            in_specs=[VMEM] * 5,
            out_specs=VMEM,
            compiler_params=LIMIT,
        )(state, jac, iface_jac, table, marks)

    def join(z, step, fix, arrived, section):
        return pl.pallas_call(
            functools.partial(join_kernel, step, kinds if fix else 0, section),
            out_shape=[whole] + [one] * (n - 1),
            in_specs=[VMEM] * (n + 3),
            out_specs=[VMEM] * n,
            compiler_params=LIMIT,
        )(z, iface_jac, table, marks, *arrived[::-1])

    def close(z, step, arrived, section, before, out, send):
        firsts = out is None
        arrays = [z, iface_jac, table, marks, *arrived[::-1], *before]
        specs = [VMEM] * len(arrays)
        scratch = [DMA((steps, blocks))]
        aliases = {}
        if firsts:
            arrays += [opening, *handed, jac, *pinned[2:6]]
            specs += [VMEM] * (n + 1) + [HBM] * 4
            scratch = [
                pltpu.VMEM((2, *whole.shape), jnp.bfloat16),
                pltpu.VMEM(whole.shape, jnp.float32),
                *[pltpu.SMEM(x.shape, x.dtype) for x in pinned[2:6]],
                DMA((4,)),
            ] + scratch
        else:
            aliases = {len(arrays): 0}
            arrays.append(out)
            specs.append(ANY)
        shapes, out_specs = [written], [ANY]
        if send:
            shapes += [whole] + [one] * (n - 1)
            out_specs += [VMEM] * n
        else:
            scratch.insert(0, pltpu.VMEM(whole.shape, jnp.bfloat16))
        return pl.pallas_call(
            functools.partial(close_kernel, step, section, firsts, send, len(before)),
            out_shape=shapes,
            in_specs=specs,
            out_specs=out_specs,
            input_output_aliases=aliases,
            scratch_shapes=scratch,
            compiler_params=LIMIT,
        )(*arrays)

    def swap(block, first, second, d):
        other = {first: second, second: first}
        pairs = []
        for a in range(tm):
            for q in range(n):
                for c in range(col_parts):
                    to = (other[a] * n + (q ^ d)) * col_parts + c if a in other else (a * n + q) * col_parts + (c ^ 1)
                    pairs.append(((a * n + q) * col_parts + c, to))
        return lax.ppermute(block, ("tm", "net", "cols"), pairs)

    def exchange(outgoing, first, second):
        return [swap(outgoing[d - 1], first, second, d) for d in range(1, n)]

    opening = state
    out = None
    for r in range(1, tm):
        arrived = exchange(outgoing, r - 1, r)
        state = swap(state, r - 1, r, 0)
        if r == 1:
            handed = arrived
        before = []
        for s in range(steps):
            fix = r == 1 and s == 0
            if s > 0:
                arrived = exchange(outgoing, r, r)
            z = own(state, s)
            if s < steps - 1:
                state, *outgoing = join(z, s, fix, arrived, r)
                before.append(state)
            else:
                out, *rest = close(z, s, arrived, r, before, out, r < tm - 1)
                state, *outgoing = rest or [None]
    return out


def solution(mesh):
    return jax.shard_map(
        local,
        mesh=mesh,
        in_specs=(
            P("tm", "net", None, None, None),
            P("net", None),
            P("tm", "net", None, None, None),
            P("net", None),
            P("net", None),
            P("net", None),
            P("cols"),
            P("tm", "cols"),
        ),
        out_specs=P("tm", "cols", "net"),
        check_vma=False,
    )
```

```python
import functools

import jax
import jax.numpy as jnp
from jax import lax
from jax.experimental import pallas as pl
from jax.experimental.pallas import tpu as pltpu
from jax.sharding import PartitionSpec as P

VMEM = pl.BlockSpec(memory_space=pltpu.VMEM)
SMEM = pl.BlockSpec(memory_space=pltpu.SMEM)
HBM = pl.BlockSpec(memory_space=pltpu.HBM)
ANY = pl.BlockSpec(memory_space=pl.ANY)
LIMIT = pltpu.CompilerParams(vmem_limit_bytes=16 * 1024 * 1024)
DMA = pltpu.SemaphoreType.DMA

STATE, LANE, BLOCK, AWAY, GAIN = 0, 1, 2, 3, 4
ROWS = 16


def times_transposed(rows, block):
    return lax.dot_general(rows, block, (((1,), (1,)), ((), ())), preferred_element_type=jnp.float32)


def hits(table, i, blocks, width):
    first_state = (lax.axis_index("net") * blocks + i) * width
    lane = lax.broadcasted_iota(jnp.int32, (table.shape[0], width), 1)
    return table[:, STATE : STATE + 1] == (lane + first_state).astype(jnp.float32)


def injected(table, step, hit):
    return jnp.where(hit, table[:, GAIN + step : GAIN + step + 1], 0.0)


def near_by(state_ref, cols_ref):
    return lambda i, k: state_ref[cols_ref[k, i]]


def own_sum(i, state_ref, jac_ref, near, table, step, hit=None):
    blocks, _, width = state_ref.shape
    if hit is None:
        hit = hits(table, i, blocks, width)
    kinds = jac_ref.shape[1]
    rows = [state_ref[i]] + [near(i, k) for k in range(kinds - 1)]
    row_blocks = [jac_ref[i, k] for k in range(kinds)]
    total = times_transposed(jnp.concatenate(rows, axis=1), jnp.concatenate(row_blocks, axis=1))
    return total + injected(table, step, hit)


def picked(blocks, marks):
    total = blocks[0] * marks[0]
    for block, mark in zip(blocks[1:], marks[1:]):
        total += block * mark
    return total


def marks_layout(n, blocks, kinds):
    sent = n * blocks
    near = sent + n * blocks
    row = near + blocks * (kinds - 1) * blocks
    return sent, near, row, row + 1 + -(row + 1) % 8


def make_marks(marks_ref, blocks, kinds, cols_ref, send_ref, recv_ref, live_ref):
    n = lax.axis_size("net")
    me = lax.axis_index("net")
    width = marks_ref.shape[1]
    lane = lax.broadcasted_iota(jnp.int32, (1, width), 1)
    sent, near, own_row, _ = marks_layout(n, blocks, kinds)

    def put(row, mask):
        marks_ref[pl.ds(row, 1)] = jnp.where(mask, 1.0, 0.0)

    for d in range(n):
        q = me ^ d
        for i in range(blocks):
            put(d * blocks + i, lane < jnp.where(recv_ref[0, q] == i, live_ref[0, q], 0))
            put(sent + d * blocks + i, lane < jnp.where(send_ref[0, q] == i, width, 0))
    for i in range(blocks):
        for k in range(kinds - 1):
            for j in range(blocks):
                put(near + (i * (kinds - 1) + k) * blocks + j, lane < jnp.where(cols_ref[k, i] == j, width, 0))
    marks_ref[pl.ds(own_row, 1)] = table_row(send_ref, me, width)


def add_coupled(incoming, block, live, recv, z_ref):
    mask = lax.broadcasted_iota(jnp.int32, z_ref.shape[1:], 1) < live
    z_ref[recv] += jnp.where(mask, times_transposed(incoming, block), 0.0)


def table_row(send_ref, partition, width):
    lane = lax.broadcasted_iota(jnp.int32, (1, width), 1)
    row = jnp.zeros((1, width), jnp.float32)
    for e in range(lax.axis_size("net")):
        row = jnp.where(lane == e, send_ref[0, partition ^ e].astype(jnp.float32), row)
    return row


def kept(table, rows):
    away, block = table[:, AWAY : AWAY + 1], table[:, BLOCK : BLOCK + 1]
    sent = jnp.broadcast_to(rows[0], (table.shape[0], rows[0].shape[1]))
    for d in range(1, len(rows)):
        sent = jnp.where(away == float(d), rows[d], sent)
    lane = lax.broadcasted_iota(jnp.int32, sent.shape, 1).astype(jnp.float32)
    return jnp.where(jnp.logical_or(away == lane, block == sent), 1.0, 0.0)


def second_kernel(*refs):
    jac_hbm, iface_hbm, *small, table_ref, marks_ref, state_ref = refs[:11]
    n = lax.axis_size("net")
    me = lax.axis_index("net")
    outgoing, refs = refs[11 : 10 + n], refs[10 + n :]
    jac_ref, iface_ref, *loaded, first_ref, sems = refs
    cols_ref, send_ref, recv_ref, live_ref, node_ref, gain_ref = loaded
    blocks, cols, width = state_ref.shape
    sources = [jac_hbm.at[1], iface_hbm.at[1, 0], *small]
    loads = [
        pltpu.make_async_copy(source, target, sems.at[i])
        for i, (source, target) in enumerate(zip(sources, [jac_ref, iface_ref, *loaded]))
    ]
    here = lax.axis_index("tm") == 0
    for load in loads[6:]:
        load.start()

    @pl.when(here)
    def _():
        for load in loads[:2]:
            load.start()

    for load in loads[2:6]:
        load.start()
    for load in loads[6:]:
        load.wait()
    node = node_ref[...]
    block_of = node // width
    rows = [
        node,
        node - block_of * width,
        block_of % blocks,
        (block_of // blocks) ^ me,
    ]
    steps = gain_ref.shape[0]
    fill = -(GAIN + steps) % 8
    rows = [row.astype(jnp.float32) for row in rows] + [gain_ref[...], jnp.zeros((fill, cols), jnp.float32)]
    table_ref[...] = jnp.concatenate(rows, axis=0).T

    @pl.when(here)
    def _():
        table = table_ref[...]
        hit = [hits(table, i, blocks, width) for i in range(blocks)]
        for i in range(blocks):
            first_ref[i] = injected(table, 0, hit[i]).astype(first_ref.dtype)
        lane = lax.broadcasted_iota(jnp.int32, (cols, width), 1).astype(jnp.float32)
        shot = jnp.where(lane == table[:, LANE : LANE + 1], table[:, GAIN : GAIN + 1], 0.0)
        away, block = table[:, AWAY : AWAY + 1], table[:, BLOCK : BLOCK + 1]
        for load in loads[2:6]:
            load.wait()
        mine = jnp.logical_or(away != 0.0, block == send_ref[0, me].astype(jnp.float32))
        shot = jnp.where(mine, shot, 0.0)
        live = recv = jnp.zeros_like(away)
        for d in range(n):
            live = jnp.where(away == float(d), live_ref[0, me ^ d].astype(jnp.float32), live)
            recv = jnp.where(away == float(d), recv_ref[0, me ^ d].astype(jnp.float32), recv)
        sent = [jnp.where(away == float(d), shot, 0.0).astype(first_ref.dtype) for d in range(n)]
        loads[1].wait()
        ifaces = jnp.concatenate([iface_ref[me ^ d] for d in range(n)], axis=1)
        coupled = times_transposed(jnp.concatenate(sent, axis=1), ifaces)
        coupled = jnp.where(lane < live, coupled, 0.0)
        loads[0].wait()
        for i in range(blocks):
            own = own_sum(i, first_ref, jac_ref, near_by(first_ref, cols_ref), table, 1, hit[i])
            state_ref[i] = (own + jnp.where(recv == float(i), coupled, 0.0)).astype(state_ref.dtype)
        for d in range(1, n):
            outgoing[d - 1][pl.ds(0, cols)] = state_ref[send_ref[0, me ^ d]]

    @pl.when(jnp.logical_not(here))
    def _():
        for load in loads[2:6]:
            load.wait()
        make_marks(marks_ref, blocks, jac_ref.shape[1], cols_ref, send_ref, recv_ref, live_ref)

    for d in range(1, n):
        row = table_row(send_ref, me ^ d, width).astype(state_ref.dtype)
        outgoing[d - 1][pl.ds(cols, ROWS)] = jnp.broadcast_to(row, (ROWS, width))


def write_start(states, first, out_ref, sems):
    copies = []
    for s, state_ref in enumerate(states, first):
        width = state_ref.shape[2]
        for i in range(state_ref.shape[0]):
            copies.append(
                pltpu.make_async_copy(state_ref.at[i], out_ref.at[s, :, pl.ds(i * width, width)], sems.at[s, i])
            )
    for copy in copies:
        copy.start()
    return copies


def own_kernel(step, state_ref, jac_ref, iface_ref, table_ref, marks_ref, z_ref):
    table = table_ref[...]
    n = lax.axis_size("net")
    blocks = state_ref.shape[0]
    kinds = jac_ref.shape[2]
    sent, near, _, _ = marks_layout(n, blocks, kinds)
    state = [state_ref[j] for j in range(blocks)]

    def pick(row):
        return picked(state, [marks_ref[pl.ds(row + j, 1)].astype(state_ref.dtype) for j in range(blocks)])

    def near_block(i, k):
        return pick(near + (i * (kinds - 1) + k) * blocks)

    @pl.when(lax.axis_index("tm") > 0)
    def _():
        term = times_transposed(pick(sent), iface_ref[step, 0, lax.axis_index("net")])
        for i in range(blocks):
            own = own_sum(i, state_ref, jac_ref.at[step], near_block, table, step)
            z_ref[i] = own + term * marks_ref[pl.ds(i, 1)]


def first_states(opening, handed, jac_ref, iface_ref, ints, table_ref, made_ref, z_ref):
    cols_ref, send_ref, recv_ref, live_ref = ints
    n = lax.axis_size("net")
    blocks, cols, width = z_ref.shape
    table = table_ref[...]
    made_ref[0] = jnp.zeros_like(made_ref[0])
    for i in range(blocks):
        z_ref[i] = own_sum(i, made_ref.at[0], jac_ref.at[0], near_by(made_ref.at[0], cols_ref), table, 0)
    for q in range(n):
        add_coupled(made_ref[0, 0], iface_ref[0, 0, q], live_ref[0, q], recv_ref[0, q], z_ref)
    made_ref[0] = z_ref[...].astype(made_ref.dtype)
    rows = [table_row(send_ref, lax.axis_index("net"), width)]
    rows += [block[cols : cols + 1].astype(jnp.float32) for block in handed]
    keep = kept(table, rows)[:, 0:1]
    for i in range(blocks):
        made_ref[1, i] = jnp.where(keep > 0.0, opening[i], jnp.zeros_like(opening[i]))
    return [made_ref.at[0], made_ref.at[1]]


def joined(sums, step, iface_ref, marks_ref, arrived, keep=None):
    me = lax.axis_index("net")
    blocks, cols = len(sums), sums[0].shape[0]
    if keep is not None:
        sums = [total * keep[:, 0:1] for total in sums]
    for d, block in enumerate(arrived, 1):
        term = times_transposed(block[pl.ds(0, cols)], iface_ref[step, 0, me ^ d])
        if keep is not None:
            term *= keep[:, d : d + 1]
        sums = [total + term * marks_ref[pl.ds(d * blocks + i, 1)] for i, total in enumerate(sums)]
    return [total.astype(jnp.bfloat16) for total in sums]


def give(made, marks_ref, state_ref, outgoing):
    blocks = len(made)
    n = lax.axis_size("net")
    sent = marks_layout(n, blocks, 1)[0]
    for i in range(blocks):
        state_ref[i] = made[i]
    for d in range(1, n) if outgoing else ():
        marks = [marks_ref[pl.ds(sent + d * blocks + j, 1)].astype(made[j].dtype) for j in range(blocks)]
        outgoing[d - 1][...] = picked(made, marks)


def exchange_order(n, handed):
    return list(range(n - 1, 0, -1)) if handed else [*range(n // 2, n), *range(n // 2 - 1, 0, -1)]


def by_distance(refs, handed):
    order = exchange_order(len(refs) + 1, handed)
    return [refs[order.index(d)] for d in range(1, len(refs) + 1)]


def join_kernel(step, fix, section, z_ref, iface_ref, table_ref, marks_ref, *refs):
    n = lax.axis_size("net")
    arrived, state_ref, outgoing = by_distance(refs[: n - 1], step == 0), refs[n - 1], refs[n:]
    blocks, cols, _ = z_ref.shape

    @pl.when(lax.axis_index("tm") == section)
    def _():
        keep = None
        if fix:
            rows = [marks_ref[pl.ds(marks_layout(n, blocks, fix)[2], 1)]]
            rows += [block[cols : cols + 1].astype(jnp.float32) for block in arrived]
            keep = kept(table_ref[...], rows)
        made = joined([z_ref[i] for i in range(blocks)], step, iface_ref, marks_ref, arrived, keep)
        give(made, marks_ref, state_ref, outgoing)


def close_kernel(step, section, firsts, send, before, *refs):
    n = lax.axis_size("net")
    *refs, sems = refs
    if firsts:
        *refs, made_ref, acc_ref, cols_ref, send_ref, recv_ref, live_ref, load_sems = refs
        ints = [cols_ref, send_ref, recv_ref, live_ref]
    z_ref, iface_ref, table_ref, marks_ref, *refs = refs
    arrived, refs = by_distance(refs[: n - 1], False), refs[n - 1 :]
    before, refs = refs[:before], refs[before:]
    if firsts:
        opening_ref, handed, jac_ref, sources, refs = refs[0], refs[1:n], refs[n], refs[n + 1 : n + 5], refs[n + 5 :]
    else:
        refs = refs[1:]
    out_ref, state_ref, *outgoing = refs

    @pl.when(lax.axis_index("tm") == section)
    def _():
        copies = write_start(before, 0, out_ref, sems)
        sums = [z_ref[i] for i in range(z_ref.shape[0])]
        made = joined(sums, step, iface_ref, marks_ref, arrived)
        give(made, marks_ref, state_ref, outgoing)
        copies += write_start([state_ref], len(before), out_ref, sems)
        for copy in copies:
            copy.wait()

    if firsts:

        @pl.when(lax.axis_index("tm") == 0)
        def _():
            loads = [
                pltpu.make_async_copy(source, target, load_sems.at[i])
                for i, (source, target) in enumerate(zip(sources, ints))
            ]
            for load in loads:
                load.start()
            for load in loads:
                load.wait()
            made = first_states(opening_ref, handed, jac_ref, iface_ref, ints, table_ref, made_ref, acc_ref)
            for copy in write_start(made, 0, out_ref, sems):
                copy.wait()


def local(jac, block_cols, iface_jac, iface_send, iface_recv, iface_live, ctrl_node, ctrl_gain):
    steps, blocks, kinds, width, _ = jac.shape
    cols = ctrl_node.shape[0]
    tm = lax.axis_size("tm")
    n = lax.axis_size("net")
    col_parts = lax.axis_size("cols")
    node = ctrl_node[None]
    near = block_cols.T
    bf16 = functools.partial(jax.ShapeDtypeStruct, dtype=jnp.bfloat16)
    f32 = functools.partial(jax.ShapeDtypeStruct, dtype=jnp.float32)
    whole, one = bf16((blocks, cols, width)), bf16((cols, width))
    table_rows = GAIN + steps + -(GAIN + steps) % 8
    written = bf16((steps, cols, blocks * width))

    pinned = [
        pltpu.with_memory_space_constraint(x, pltpu.HBM)
        for x in (jac, iface_jac, near, iface_send, iface_recv, iface_live, node, ctrl_gain)
    ]
    marks_rows = marks_layout(n, blocks, kinds)[-1]
    table, marks, state, *outgoing = pl.pallas_call(
        second_kernel,
        out_shape=[f32((cols, table_rows)), f32((marks_rows, width)), whole]
        + [bf16((cols + ROWS, width))] * (n - 1),
        in_specs=[HBM] * len(pinned),
        out_specs=[VMEM] * (n + 2),
        scratch_shapes=[
            pltpu.VMEM((blocks, kinds, width, width), jnp.bfloat16),
            pltpu.VMEM((n, width, width), jnp.bfloat16),
            *[pltpu.SMEM(x.shape, x.dtype) for x in (near, iface_send, iface_recv, iface_live)],
            *[pltpu.VMEM(x.shape, x.dtype) for x in (node, ctrl_gain)],
            pltpu.VMEM(whole.shape, jnp.bfloat16),
            DMA((len(pinned),)),
        ],
        compiler_params=LIMIT,
    )(*pinned)

    def own(state, step):
        return pl.pallas_call(
            functools.partial(own_kernel, step),
            out_shape=f32(whole.shape),
            in_specs=[VMEM] * 5,
            out_specs=VMEM,
            compiler_params=LIMIT,
        )(state, jac, iface_jac, table, marks)

    def join(z, step, fix, arrived, section):
        return pl.pallas_call(
            functools.partial(join_kernel, step, kinds if fix else 0, section),
            out_shape=[whole] + [one] * (n - 1),
            in_specs=[VMEM] * (n + 3),
            out_specs=[VMEM] * n,
            compiler_params=LIMIT,
        )(z, iface_jac, table, marks, *[arrived[d - 1] for d in exchange_order(n, step == 0)])

    def close(z, step, arrived, section, before, out, send):
        firsts = out is None
        arrays = [z, iface_jac, table, marks, *[arrived[d - 1] for d in exchange_order(n, False)], *before]
        specs = [VMEM] * len(arrays)
        scratch = [DMA((steps, blocks))]
        aliases = {}
        if firsts:
            arrays += [opening, *handed, jac, *pinned[2:6]]
            specs += [VMEM] * (n + 1) + [HBM] * 4
            scratch = [
                pltpu.VMEM((2, *whole.shape), jnp.bfloat16),
                pltpu.VMEM(whole.shape, jnp.float32),
                *[pltpu.SMEM(x.shape, x.dtype) for x in pinned[2:6]],
                DMA((4,)),
            ] + scratch
        else:
            aliases = {len(arrays): 0}
            arrays.append(out)
            specs.append(ANY)
        shapes, out_specs = [written], [ANY]
        if send:
            shapes += [whole] + [one] * (n - 1)
            out_specs += [VMEM] * n
        else:
            scratch.insert(0, pltpu.VMEM(whole.shape, jnp.bfloat16))
        return pl.pallas_call(
            functools.partial(close_kernel, step, section, firsts, send, len(before)),
            out_shape=shapes,
            in_specs=specs,
            out_specs=out_specs,
            input_output_aliases=aliases,
            scratch_shapes=scratch,
            compiler_params=LIMIT,
        )(*arrays)

    def swap(block, first, second, d):
        other = {first: second, second: first}
        pairs = []
        for a in range(tm):
            for q in range(n):
                for c in range(col_parts):
                    to = (other[a] * n + (q ^ d)) * col_parts + c if a in other else (a * n + q) * col_parts + (c ^ 1)
                    pairs.append(((a * n + q) * col_parts + c, to))
        return lax.ppermute(block, ("tm", "net", "cols"), pairs)

    def exchange(outgoing, first, second):
        return [swap(outgoing[d - 1], first, second, d) for d in range(1, n)]

    opening = state
    out = None
    for r in range(1, tm):
        arrived = exchange(outgoing, r - 1, r)
        state = swap(state, r - 1, r, 0)
        if r == 1:
            handed = arrived
        before = []
        for s in range(steps):
            fix = r == 1 and s == 0
            if s > 0:
                arrived = exchange(outgoing, r, r)
            z = own(state, s)
            if s < steps - 1:
                state, *outgoing = join(z, s, fix, arrived, r)
                before.append(state)
            else:
                out, *rest = close(z, s, arrived, r, before, out, r < tm - 1)
                state, *outgoing = rest or [None]
    return out


def solution(mesh):
    return jax.shard_map(
        local,
        mesh=mesh,
        in_specs=(
            P("tm", "net", None, None, None),
            P("net", None),
            P("tm", "net", None, None, None),
            P("net", None),
            P("net", None),
            P("net", None),
            P("cols"),
            P("tm", "cols"),
        ),
        out_specs=P("tm", "cols", "net"),
        check_vma=False,
    )
```

```python
import functools

import jax
import jax.numpy as jnp
from jax import lax
from jax.experimental import pallas as pl
from jax.experimental.pallas import tpu as pltpu
from jax.sharding import PartitionSpec as P

VMEM = pl.BlockSpec(memory_space=pltpu.VMEM)
SMEM = pl.BlockSpec(memory_space=pltpu.SMEM)
HBM = pl.BlockSpec(memory_space=pltpu.HBM)
ANY = pl.BlockSpec(memory_space=pl.ANY)
LIMIT = pltpu.CompilerParams(vmem_limit_bytes=16 * 1024 * 1024)
DMA = pltpu.SemaphoreType.DMA

STATE, LANE, BLOCK, AWAY, GAIN = 0, 1, 2, 3, 4
ROWS = 16


def times_transposed(rows, block):
    return lax.dot_general(rows, block, (((1,), (1,)), ((), ())), preferred_element_type=jnp.float32)


def hits(table, i, blocks, width):
    first_state = (lax.axis_index("net") * blocks + i) * width
    lane = lax.broadcasted_iota(jnp.int32, (table.shape[0], width), 1)
    return table[:, STATE : STATE + 1] == (lane + first_state).astype(jnp.float32)


def injected(table, step, hit):
    return jnp.where(hit, table[:, GAIN + step : GAIN + step + 1], 0.0)


def near_by(state_ref, cols_ref):
    return lambda i, k: state_ref[cols_ref[k, i]]


def own_sum(i, state_ref, jac_ref, near, table, step, hit=None):
    blocks, _, width = state_ref.shape
    if hit is None:
        hit = hits(table, i, blocks, width)
    kinds = jac_ref.shape[1]
    rows = [state_ref[i]] + [near(i, k) for k in range(kinds - 1)]
    row_blocks = [jac_ref[i, k] for k in range(kinds)]
    total = times_transposed(jnp.concatenate(rows, axis=1), jnp.concatenate(row_blocks, axis=1))
    return total + injected(table, step, hit)


def picked(blocks, marks):
    total = blocks[0] * marks[0]
    for block, mark in zip(blocks[1:], marks[1:]):
        total += block * mark
    return total


def marks_layout(n, blocks, kinds):
    sent = n * blocks
    near = sent + n * blocks
    row = near + blocks * (kinds - 1) * blocks
    return sent, near, row, row + 1 + -(row + 1) % 8


def make_marks(marks_ref, blocks, kinds, cols_ref, send_ref, recv_ref, live_ref):
    n = lax.axis_size("net")
    me = lax.axis_index("net")
    width = marks_ref.shape[1]
    lane = lax.broadcasted_iota(jnp.int32, (1, width), 1)
    sent, near, own_row, _ = marks_layout(n, blocks, kinds)

    def put(row, mask):
        marks_ref[pl.ds(row, 1)] = jnp.where(mask, 1.0, 0.0)

    for d in range(n):
        q = me ^ d
        for i in range(blocks):
            put(d * blocks + i, lane < jnp.where(recv_ref[0, q] == i, live_ref[0, q], 0))
            put(sent + d * blocks + i, lane < jnp.where(send_ref[0, q] == i, width, 0))
    for i in range(blocks):
        for k in range(kinds - 1):
            for j in range(blocks):
                put(near + (i * (kinds - 1) + k) * blocks + j, lane < jnp.where(cols_ref[k, i] == j, width, 0))
    marks_ref[pl.ds(own_row, 1)] = table_row(send_ref, me, width)


def add_coupled(incoming, block, live, recv, z_ref):
    mask = lax.broadcasted_iota(jnp.int32, z_ref.shape[1:], 1) < live
    z_ref[recv] += jnp.where(mask, times_transposed(incoming, block), 0.0)


def table_row(send_ref, partition, width):
    lane = lax.broadcasted_iota(jnp.int32, (1, width), 1)
    row = jnp.zeros((1, width), jnp.float32)
    for e in range(lax.axis_size("net")):
        row = jnp.where(lane == e, send_ref[0, partition ^ e].astype(jnp.float32), row)
    return row


def kept(table, rows):
    away, block = table[:, AWAY : AWAY + 1], table[:, BLOCK : BLOCK + 1]
    sent = jnp.broadcast_to(rows[0], (table.shape[0], rows[0].shape[1]))
    for d in range(1, len(rows)):
        sent = jnp.where(away == float(d), rows[d], sent)
    lane = lax.broadcasted_iota(jnp.int32, sent.shape, 1).astype(jnp.float32)
    return jnp.where(jnp.logical_or(away == lane, block == sent), 1.0, 0.0)


def second_kernel(*refs):
    jac_hbm, iface_hbm, *small, table_ref, marks_ref, state_ref = refs[:11]
    n = lax.axis_size("net")
    me = lax.axis_index("net")
    outgoing, refs = refs[11 : 10 + n], refs[10 + n :]
    jac_ref, iface_ref, *loaded, first_ref, sems = refs
    cols_ref, send_ref, recv_ref, live_ref, node_ref, gain_ref = loaded
    blocks, cols, width = state_ref.shape
    sources = [jac_hbm.at[1], iface_hbm.at[1, 0], *small]
    loads = [
        pltpu.make_async_copy(source, target, sems.at[i])
        for i, (source, target) in enumerate(zip(sources, [jac_ref, iface_ref, *loaded]))
    ]
    here = lax.axis_index("tm") == 0
    for load in loads[6:]:
        load.start()

    @pl.when(here)
    def _():
        for load in loads[:2]:
            load.start()

    for load in loads[2:6]:
        load.start()
    for load in loads[6:]:
        load.wait()
    node = node_ref[...]
    block_of = node // width
    rows = [
        node,
        node - block_of * width,
        block_of % blocks,
        (block_of // blocks) ^ me,
    ]
    steps = gain_ref.shape[0]
    fill = -(GAIN + steps) % 8
    rows = [row.astype(jnp.float32) for row in rows] + [gain_ref[...], jnp.zeros((fill, cols), jnp.float32)]
    table_ref[...] = jnp.concatenate(rows, axis=0).T

    @pl.when(here)
    def _():
        table = table_ref[...]
        hit = [hits(table, i, blocks, width) for i in range(blocks)]
        for i in range(blocks):
            first_ref[i] = injected(table, 0, hit[i]).astype(first_ref.dtype)
        lane = lax.broadcasted_iota(jnp.int32, (cols, width), 1).astype(jnp.float32)
        shot = jnp.where(lane == table[:, LANE : LANE + 1], table[:, GAIN : GAIN + 1], 0.0)
        away, block = table[:, AWAY : AWAY + 1], table[:, BLOCK : BLOCK + 1]
        for load in loads[2:6]:
            load.wait()
        mine = jnp.logical_or(away != 0.0, block == send_ref[0, me].astype(jnp.float32))
        shot = jnp.where(mine, shot, 0.0)
        live = recv = jnp.zeros_like(away)
        for d in range(n):
            live = jnp.where(away == float(d), live_ref[0, me ^ d].astype(jnp.float32), live)
            recv = jnp.where(away == float(d), recv_ref[0, me ^ d].astype(jnp.float32), recv)
        sent = [jnp.where(away == float(d), shot, 0.0).astype(first_ref.dtype) for d in range(n)]
        loads[1].wait()
        ifaces = jnp.concatenate([iface_ref[me ^ d] for d in range(n)], axis=1)
        coupled = times_transposed(jnp.concatenate(sent, axis=1), ifaces)
        coupled = jnp.where(lane < live, coupled, 0.0)
        loads[0].wait()
        for i in range(blocks):
            own = own_sum(i, first_ref, jac_ref, near_by(first_ref, cols_ref), table, 1, hit[i])
            state_ref[i] = (own + jnp.where(recv == float(i), coupled, 0.0)).astype(state_ref.dtype)
        for d in range(1, n):
            outgoing[d - 1][pl.ds(0, cols)] = state_ref[send_ref[0, me ^ d]]

    @pl.when(jnp.logical_not(here))
    def _():
        for load in loads[2:6]:
            load.wait()
        make_marks(marks_ref, blocks, jac_ref.shape[1], cols_ref, send_ref, recv_ref, live_ref)

    for d in range(1, n):
        row = table_row(send_ref, me ^ d, width).astype(state_ref.dtype)
        outgoing[d - 1][pl.ds(cols, ROWS)] = jnp.broadcast_to(row, (ROWS, width))


def write_start(states, first, out_ref, sems):
    copies = []
    for s, state_ref in enumerate(states, first):
        width = state_ref.shape[2]
        for i in range(state_ref.shape[0]):
            copies.append(
                pltpu.make_async_copy(state_ref.at[i], out_ref.at[s, :, pl.ds(i * width, width)], sems.at[s, i])
            )
    for copy in copies:
        copy.start()
    return copies


def own_kernel(step, state_ref, jac_ref, iface_ref, table_ref, marks_ref, z_ref):
    table = table_ref[...]
    n = lax.axis_size("net")
    blocks = state_ref.shape[0]
    kinds = jac_ref.shape[2]
    sent, near, _, _ = marks_layout(n, blocks, kinds)
    state = [state_ref[j] for j in range(blocks)]

    def pick(row):
        return picked(state, [marks_ref[pl.ds(row + j, 1)].astype(state_ref.dtype) for j in range(blocks)])

    def near_block(i, k):
        return pick(near + (i * (kinds - 1) + k) * blocks)

    @pl.when(lax.axis_index("tm") > 0)
    def _():
        term = times_transposed(pick(sent), iface_ref[step, 0, lax.axis_index("net")])
        for i in range(blocks):
            own = own_sum(i, state_ref, jac_ref.at[step], near_block, table, step)
            z_ref[i] = own + term * marks_ref[pl.ds(i, 1)]


def first_states(opening, handed, jac_ref, iface_ref, ints, table_ref, made_ref, z_ref):
    cols_ref, send_ref, recv_ref, live_ref = ints
    n = lax.axis_size("net")
    blocks, cols, width = z_ref.shape
    table = table_ref[...]
    made_ref[0] = jnp.zeros_like(made_ref[0])
    for i in range(blocks):
        z_ref[i] = own_sum(i, made_ref.at[0], jac_ref.at[0], near_by(made_ref.at[0], cols_ref), table, 0)
    for q in range(n):
        add_coupled(made_ref[0, 0], iface_ref[0, 0, q], live_ref[0, q], recv_ref[0, q], z_ref)
    made_ref[0] = z_ref[...].astype(made_ref.dtype)
    rows = [table_row(send_ref, lax.axis_index("net"), width)]
    rows += [block[cols : cols + 1].astype(jnp.float32) for block in handed]
    keep = kept(table, rows)[:, 0:1]
    for i in range(blocks):
        made_ref[1, i] = jnp.where(keep > 0.0, opening[i], jnp.zeros_like(opening[i]))
    return [made_ref.at[0], made_ref.at[1]]


def joined(sums, step, iface_ref, marks_ref, arrived, keep=None):
    me = lax.axis_index("net")
    blocks, cols = len(sums), sums[0].shape[0]
    if keep is not None:
        sums = [total * keep[:, 0:1] for total in sums]
    for d, block in enumerate(arrived, 1):
        term = times_transposed(block[pl.ds(0, cols)], iface_ref[step, 0, me ^ d])
        if keep is not None:
            term *= keep[:, d : d + 1]
        sums = [total + term * marks_ref[pl.ds(d * blocks + i, 1)] for i, total in enumerate(sums)]
    return [total.astype(jnp.bfloat16) for total in sums]


def give(made, marks_ref, state_ref, outgoing):
    blocks = len(made)
    n = lax.axis_size("net")
    sent = marks_layout(n, blocks, 1)[0]
    for i in range(blocks):
        state_ref[i] = made[i]
    for d in range(1, n) if outgoing else ():
        marks = [marks_ref[pl.ds(sent + d * blocks + j, 1)].astype(made[j].dtype) for j in range(blocks)]
        outgoing[d - 1][...] = picked(made, marks)


def exchange_order(n, handed):
    return [*range(n // 2, n), *range(n // 2 - 1, 0, -1)] if handed else list(range(n - 1, 0, -1))


def by_distance(refs, handed):
    order = exchange_order(len(refs) + 1, handed)
    return [refs[order.index(d)] for d in range(1, len(refs) + 1)]


def join_kernel(step, fix, section, z_ref, iface_ref, table_ref, marks_ref, *refs):
    n = lax.axis_size("net")
    arrived, state_ref, outgoing = by_distance(refs[: n - 1], step == 0), refs[n - 1], refs[n:]
    blocks, cols, _ = z_ref.shape

    @pl.when(lax.axis_index("tm") == section)
    def _():
        keep = None
        if fix:
            rows = [marks_ref[pl.ds(marks_layout(n, blocks, fix)[2], 1)]]
            rows += [block[cols : cols + 1].astype(jnp.float32) for block in arrived]
            keep = kept(table_ref[...], rows)
        made = joined([z_ref[i] for i in range(blocks)], step, iface_ref, marks_ref, arrived, keep)
        give(made, marks_ref, state_ref, outgoing)


def close_kernel(step, section, firsts, send, before, *refs):
    n = lax.axis_size("net")
    *refs, sems = refs
    if firsts:
        *refs, made_ref, acc_ref, cols_ref, send_ref, recv_ref, live_ref, load_sems = refs
        ints = [cols_ref, send_ref, recv_ref, live_ref]
    z_ref, iface_ref, table_ref, marks_ref, *refs = refs
    arrived, refs = by_distance(refs[: n - 1], False), refs[n - 1 :]
    before, refs = refs[:before], refs[before:]
    if firsts:
        opening_ref, handed, jac_ref, sources, refs = refs[0], refs[1:n], refs[n], refs[n + 1 : n + 5], refs[n + 5 :]
    else:
        refs = refs[1:]
    out_ref, state_ref, *outgoing = refs

    @pl.when(lax.axis_index("tm") == section)
    def _():
        copies = write_start(before, 0, out_ref, sems)
        sums = [z_ref[i] for i in range(z_ref.shape[0])]
        made = joined(sums, step, iface_ref, marks_ref, arrived)
        give(made, marks_ref, state_ref, outgoing)
        copies += write_start([state_ref], len(before), out_ref, sems)
        for copy in copies:
            copy.wait()

    if firsts:

        @pl.when(lax.axis_index("tm") == 0)
        def _():
            loads = [
                pltpu.make_async_copy(source, target, load_sems.at[i])
                for i, (source, target) in enumerate(zip(sources, ints))
            ]
            for load in loads:
                load.start()
            for load in loads:
                load.wait()
            made = first_states(opening_ref, handed, jac_ref, iface_ref, ints, table_ref, made_ref, acc_ref)
            for copy in write_start(made, 0, out_ref, sems):
                copy.wait()


def local(jac, block_cols, iface_jac, iface_send, iface_recv, iface_live, ctrl_node, ctrl_gain):
    steps, blocks, kinds, width, _ = jac.shape
    cols = ctrl_node.shape[0]
    tm = lax.axis_size("tm")
    n = lax.axis_size("net")
    col_parts = lax.axis_size("cols")
    node = ctrl_node[None]
    near = block_cols.T
    bf16 = functools.partial(jax.ShapeDtypeStruct, dtype=jnp.bfloat16)
    f32 = functools.partial(jax.ShapeDtypeStruct, dtype=jnp.float32)
    whole, one = bf16((blocks, cols, width)), bf16((cols, width))
    table_rows = GAIN + steps + -(GAIN + steps) % 8
    written = bf16((steps, cols, blocks * width))

    pinned = [
        pltpu.with_memory_space_constraint(x, pltpu.HBM)
        for x in (jac, iface_jac, near, iface_send, iface_recv, iface_live, node, ctrl_gain)
    ]
    marks_rows = marks_layout(n, blocks, kinds)[-1]
    table, marks, state, *outgoing = pl.pallas_call(
        second_kernel,
        out_shape=[f32((cols, table_rows)), f32((marks_rows, width)), whole]
        + [bf16((cols + ROWS, width))] * (n - 1),
        in_specs=[HBM] * len(pinned),
        out_specs=[VMEM] * (n + 2),
        scratch_shapes=[
            pltpu.VMEM((blocks, kinds, width, width), jnp.bfloat16),
            pltpu.VMEM((n, width, width), jnp.bfloat16),
            *[pltpu.SMEM(x.shape, x.dtype) for x in (near, iface_send, iface_recv, iface_live)],
            *[pltpu.VMEM(x.shape, x.dtype) for x in (node, ctrl_gain)],
            pltpu.VMEM(whole.shape, jnp.bfloat16),
            DMA((len(pinned),)),
        ],
        compiler_params=LIMIT,
    )(*pinned)

    def own(state, step):
        return pl.pallas_call(
            functools.partial(own_kernel, step),
            out_shape=f32(whole.shape),
            in_specs=[VMEM] * 5,
            out_specs=VMEM,
            compiler_params=LIMIT,
        )(state, jac, iface_jac, table, marks)

    def join(z, step, fix, arrived, section):
        return pl.pallas_call(
            functools.partial(join_kernel, step, kinds if fix else 0, section),
            out_shape=[whole] + [one] * (n - 1),
            in_specs=[VMEM] * (n + 3),
            out_specs=[VMEM] * n,
            compiler_params=LIMIT,
        )(z, iface_jac, table, marks, *[arrived[d - 1] for d in exchange_order(n, step == 0)])

    def close(z, step, arrived, section, before, out, send):
        firsts = out is None
        arrays = [z, iface_jac, table, marks, *[arrived[d - 1] for d in exchange_order(n, False)], *before]
        specs = [VMEM] * len(arrays)
        scratch = [DMA((steps, blocks))]
        aliases = {}
        if firsts:
            arrays += [opening, *handed, jac, *pinned[2:6]]
            specs += [VMEM] * (n + 1) + [HBM] * 4
            scratch = [
                pltpu.VMEM((2, *whole.shape), jnp.bfloat16),
                pltpu.VMEM(whole.shape, jnp.float32),
                *[pltpu.SMEM(x.shape, x.dtype) for x in pinned[2:6]],
                DMA((4,)),
            ] + scratch
        else:
            aliases = {len(arrays): 0}
            arrays.append(out)
            specs.append(ANY)
        shapes, out_specs = [written], [ANY]
        if send:
            shapes += [whole] + [one] * (n - 1)
            out_specs += [VMEM] * n
        else:
            scratch.insert(0, pltpu.VMEM(whole.shape, jnp.bfloat16))
        return pl.pallas_call(
            functools.partial(close_kernel, step, section, firsts, send, len(before)),
            out_shape=shapes,
            in_specs=specs,
            out_specs=out_specs,
            input_output_aliases=aliases,
            scratch_shapes=scratch,
            compiler_params=LIMIT,
        )(*arrays)

    def swap(block, first, second, d):
        other = {first: second, second: first}
        pairs = []
        for a in range(tm):
            for q in range(n):
                for c in range(col_parts):
                    to = (other[a] * n + (q ^ d)) * col_parts + c if a in other else (a * n + q) * col_parts + (c ^ 1)
                    pairs.append(((a * n + q) * col_parts + c, to))
        return lax.ppermute(block, ("tm", "net", "cols"), pairs)

    def exchange(outgoing, first, second):
        return [swap(outgoing[d - 1], first, second, d) for d in range(1, n)]

    opening = state
    out = None
    for r in range(1, tm):
        arrived = exchange(outgoing, r - 1, r)
        state = swap(state, r - 1, r, 0)
        if r == 1:
            handed = arrived
        before = []
        for s in range(steps):
            fix = r == 1 and s == 0
            if s > 0:
                arrived = exchange(outgoing, r, r)
            z = own(state, s)
            if s < steps - 1:
                state, *outgoing = join(z, s, fix, arrived, r)
                before.append(state)
            else:
                out, *rest = close(z, s, arrived, r, before, out, r < tm - 1)
                state, *outgoing = rest or [None]
    return out


def solution(mesh):
    return jax.shard_map(
        local,
        mesh=mesh,
        in_specs=(
            P("tm", "net", None, None, None),
            P("net", None),
            P("tm", "net", None, None, None),
            P("net", None),
            P("net", None),
            P("net", None),
            P("cols"),
            P("tm", "cols"),
        ),
        out_specs=P("tm", "cols", "net"),
        check_vma=False,
    )
```

```python
import functools

import jax
import jax.numpy as jnp
from jax import lax
from jax.experimental import pallas as pl
from jax.experimental.pallas import tpu as pltpu
from jax.sharding import PartitionSpec as P

VMEM = pl.BlockSpec(memory_space=pltpu.VMEM)
SMEM = pl.BlockSpec(memory_space=pltpu.SMEM)
HBM = pl.BlockSpec(memory_space=pltpu.HBM)
ANY = pl.BlockSpec(memory_space=pl.ANY)
LIMIT = pltpu.CompilerParams(vmem_limit_bytes=16 * 1024 * 1024)
DMA = pltpu.SemaphoreType.DMA

STATE, LANE, BLOCK, AWAY, GAIN = 0, 1, 2, 3, 4
PANELS = 2
ROWS = 16


def times_transposed(rows, block):
    return lax.dot_general(rows, block, (((1,), (1,)), ((), ())), preferred_element_type=jnp.float32)


def hits(table, i, blocks, width):
    first_state = (lax.axis_index("net") * blocks + i) * width
    lane = lax.broadcasted_iota(jnp.int32, (table.shape[0], width), 1)
    return table[:, STATE : STATE + 1] == (lane + first_state).astype(jnp.float32)


def injected(table, step, hit):
    return jnp.where(hit, table[:, GAIN + step : GAIN + step + 1], 0.0)


def near_by(state_ref, cols_ref):
    return lambda i, k: state_ref[cols_ref[k, i]]


def own_sum(i, state_ref, jac_ref, near, table, step, hit=None):
    blocks, _, width = state_ref.shape
    if hit is None:
        hit = hits(table, i, blocks, width)
    kinds = jac_ref.shape[1]
    rows = [state_ref[i]] + [near(i, k) for k in range(kinds - 1)]
    row_blocks = [jac_ref[i, k] for k in range(kinds)]
    total = times_transposed(jnp.concatenate(rows, axis=1), jnp.concatenate(row_blocks, axis=1))
    return total + injected(table, step, hit)


def picked(blocks, marks):
    total = blocks[0] * marks[0]
    for block, mark in zip(blocks[1:], marks[1:]):
        total += block * mark
    return total


def marks_layout(n, blocks, kinds):
    sent = n * blocks
    near = sent + n * blocks
    row = near + blocks * (kinds - 1) * blocks
    return sent, near, row, row + 1 + -(row + 1) % 8


def make_marks(marks_ref, blocks, kinds, cols_ref, send_ref, recv_ref, live_ref):
    n = lax.axis_size("net")
    me = lax.axis_index("net")
    width = marks_ref.shape[1]
    lane = lax.broadcasted_iota(jnp.int32, (1, width), 1)
    sent, near, own_row, _ = marks_layout(n, blocks, kinds)

    def put(row, mask):
        marks_ref[pl.ds(row, 1)] = jnp.where(mask, 1.0, 0.0)

    for d in range(n):
        q = me ^ d
        for i in range(blocks):
            put(d * blocks + i, lane < jnp.where(recv_ref[0, q] == i, live_ref[0, q], 0))
            put(sent + d * blocks + i, lane < jnp.where(send_ref[0, q] == i, width, 0))
    for i in range(blocks):
        for k in range(kinds - 1):
            for j in range(blocks):
                put(near + (i * (kinds - 1) + k) * blocks + j, lane < jnp.where(cols_ref[k, i] == j, width, 0))
    marks_ref[pl.ds(own_row, 1)] = table_row(send_ref, me, width)


def add_coupled(incoming, block, live, recv, z_ref):
    mask = lax.broadcasted_iota(jnp.int32, z_ref.shape[1:], 1) < live
    z_ref[recv] += jnp.where(mask, times_transposed(incoming, block), 0.0)


def table_row(send_ref, partition, width):
    lane = lax.broadcasted_iota(jnp.int32, (1, width), 1)
    row = jnp.zeros((1, width), jnp.float32)
    for e in range(lax.axis_size("net")):
        row = jnp.where(lane == e, send_ref[0, partition ^ e].astype(jnp.float32), row)
    return row


def kept(table, rows):
    away, block = table[:, AWAY : AWAY + 1], table[:, BLOCK : BLOCK + 1]
    sent = jnp.broadcast_to(rows[0], (table.shape[0], rows[0].shape[1]))
    for d in range(1, len(rows)):
        sent = jnp.where(away == float(d), rows[d], sent)
    lane = lax.broadcasted_iota(jnp.int32, sent.shape, 1).astype(jnp.float32)
    return jnp.where(jnp.logical_or(away == lane, block == sent), 1.0, 0.0)


def second_kernel(*refs):
    jac_hbm, iface_hbm, *small, table_ref, marks_ref, state_ref = refs[:11]
    n = lax.axis_size("net")
    me = lax.axis_index("net")
    outgoing, (jac_ref, iface_ref, *loaded, first_ref, sems) = refs[11:-10], refs[-10:]
    cols_ref, send_ref, recv_ref, live_ref, node_ref, gain_ref = loaded
    blocks, cols, width = state_ref.shape
    panel = cols // PANELS
    sources = [jac_hbm.at[1], iface_hbm.at[1, 0], *small]
    loads = [
        pltpu.make_async_copy(source, target, sems.at[i])
        for i, (source, target) in enumerate(zip(sources, [jac_ref, iface_ref, *loaded]))
    ]
    here = lax.axis_index("tm") == 0
    for load in loads[6:]:
        load.start()

    @pl.when(here)
    def _():
        for load in loads[:2]:
            load.start()

    for load in loads[2:6]:
        load.start()
    for load in loads[6:]:
        load.wait()
    node = node_ref[...]
    block_of = node // width
    rows = [
        node,
        node - block_of * width,
        block_of % blocks,
        (block_of // blocks) ^ me,
    ]
    steps = gain_ref.shape[0]
    fill = -(GAIN + steps) % 8
    rows = [row.astype(jnp.float32) for row in rows] + [gain_ref[...], jnp.zeros((fill, cols), jnp.float32)]
    table_ref[...] = jnp.concatenate(rows, axis=0).T

    @pl.when(here)
    def _():
        table = table_ref[...]
        hit = [hits(table, i, blocks, width) for i in range(blocks)]
        for i in range(blocks):
            first_ref[i] = injected(table, 0, hit[i]).astype(first_ref.dtype)
        lane = lax.broadcasted_iota(jnp.int32, (cols, width), 1).astype(jnp.float32)
        shot = jnp.where(lane == table[:, LANE : LANE + 1], table[:, GAIN : GAIN + 1], 0.0)
        away, block = table[:, AWAY : AWAY + 1], table[:, BLOCK : BLOCK + 1]
        for load in loads[2:6]:
            load.wait()
        mine = jnp.logical_or(away != 0.0, block == send_ref[0, me].astype(jnp.float32))
        shot = jnp.where(mine, shot, 0.0)
        live = recv = jnp.zeros_like(away)
        for d in range(n):
            live = jnp.where(away == float(d), live_ref[0, me ^ d].astype(jnp.float32), live)
            recv = jnp.where(away == float(d), recv_ref[0, me ^ d].astype(jnp.float32), recv)
        sent = [jnp.where(away == float(d), shot, 0.0).astype(first_ref.dtype) for d in range(n)]
        loads[1].wait()
        ifaces = jnp.concatenate([iface_ref[me ^ d] for d in range(n)], axis=1)
        coupled = times_transposed(jnp.concatenate(sent, axis=1), ifaces)
        coupled = jnp.where(lane < live, coupled, 0.0)
        loads[0].wait()
        for i in range(blocks):
            own = own_sum(i, first_ref, jac_ref, near_by(first_ref, cols_ref), table, 1, hit[i])
            state_ref[i] = (own + jnp.where(recv == float(i), coupled, 0.0)).astype(state_ref.dtype)
        for h in range(PANELS):
            for d in range(1, n):
                block = state_ref[send_ref[0, me ^ d], pl.ds(h * panel, panel)]
                outgoing[h * (n - 1) + d - 1][pl.ds(0, panel)] = block

    @pl.when(jnp.logical_not(here))
    def _():
        for load in loads[2:6]:
            load.wait()
        make_marks(marks_ref, blocks, jac_ref.shape[1], cols_ref, send_ref, recv_ref, live_ref)

    for d in range(1, n):
        row = table_row(send_ref, me ^ d, width).astype(state_ref.dtype)
        outgoing[d - 1][pl.ds(panel, ROWS)] = jnp.broadcast_to(row, (ROWS, width))


def write_start(states, first, out_ref, sems, row=0):
    copies = []
    for s, state_ref in enumerate(states, first):
        blocks, cols, width = state_ref.shape
        for i in range(blocks):
            target = out_ref.at[s, pl.ds(row, cols), pl.ds(i * width, width)]
            copies.append(pltpu.make_async_copy(state_ref.at[i], target, sems.at[s, i]))
    for copy in copies:
        copy.start()
    return copies


def own_kernel(step, row, state_ref, jac_ref, iface_ref, table_ref, marks_ref, z_ref):
    n = lax.axis_size("net")
    blocks, cols, _ = state_ref.shape
    table = table_ref[pl.ds(row, cols)]
    kinds = jac_ref.shape[2]
    sent, near, _, _ = marks_layout(n, blocks, kinds)
    state = [state_ref[j] for j in range(blocks)]

    def pick(row):
        return picked(state, [marks_ref[pl.ds(row + j, 1)].astype(state_ref.dtype) for j in range(blocks)])

    def near_block(i, k):
        return pick(near + (i * (kinds - 1) + k) * blocks)

    @pl.when(lax.axis_index("tm") > 0)
    def _():
        term = times_transposed(pick(sent), iface_ref[step, 0, lax.axis_index("net")])
        for i in range(blocks):
            own = own_sum(i, state_ref, jac_ref.at[step], near_block, table, step)
            z_ref[i] = own + term * marks_ref[pl.ds(i, 1)]


def first_states(opening, handed, jac_ref, iface_ref, ints, table_ref, made_ref, z_ref):
    cols_ref, send_ref, recv_ref, live_ref = ints
    n = lax.axis_size("net")
    blocks, cols, width = z_ref.shape
    table = table_ref[...]
    made_ref[0] = jnp.zeros_like(made_ref[0])
    for i in range(blocks):
        z_ref[i] = own_sum(i, made_ref.at[0], jac_ref.at[0], near_by(made_ref.at[0], cols_ref), table, 0)
    for q in range(n):
        add_coupled(made_ref[0, 0], iface_ref[0, 0, q], live_ref[0, q], recv_ref[0, q], z_ref)
    made_ref[0] = z_ref[...].astype(made_ref.dtype)
    rows = [table_row(send_ref, lax.axis_index("net"), width)]
    rows += [block[cols // PANELS : cols // PANELS + 1].astype(jnp.float32) for block in handed]
    keep = kept(table, rows)[:, 0:1]
    for i in range(blocks):
        made_ref[1, i] = jnp.where(keep > 0.0, opening[i], jnp.zeros_like(opening[i]))
    return [made_ref.at[0], made_ref.at[1]]


def joined(sums, step, iface_ref, marks_ref, arrived, keep=None):
    me = lax.axis_index("net")
    blocks, cols = len(sums), sums[0].shape[0]
    if keep is not None:
        sums = [total * keep[:, 0:1] for total in sums]
    for d, block in enumerate(arrived, 1):
        term = times_transposed(block[pl.ds(0, cols)], iface_ref[step, 0, me ^ d])
        if keep is not None:
            term *= keep[:, d : d + 1]
        sums = [total + term * marks_ref[pl.ds(d * blocks + i, 1)] for i, total in enumerate(sums)]
    return [total.astype(jnp.bfloat16) for total in sums]


def give(made, marks_ref, state_ref, outgoing):
    blocks = len(made)
    n = lax.axis_size("net")
    sent = marks_layout(n, blocks, 1)[0]
    for i in range(blocks):
        state_ref[i] = made[i]
    for d in range(1, n) if outgoing else ():
        marks = [marks_ref[pl.ds(sent + d * blocks + j, 1)].astype(made[j].dtype) for j in range(blocks)]
        outgoing[d - 1][...] = picked(made, marks)


def exchange_order(n, handed):
    return [*range(n // 2, n), *range(n // 2 - 1, 0, -1)] if handed else list(range(n - 1, 0, -1))


def by_distance(refs, handed):
    order = exchange_order(len(refs) + 1, handed)
    return [refs[order.index(d)] for d in range(1, len(refs) + 1)]


def join_kernel(step, fix, section, row, z_row, z_ref, iface_ref, table_ref, marks_ref, *refs):
    n = lax.axis_size("net")
    arrived, (state_ref, *outgoing) = by_distance(refs[: n - 1], step == 0), refs[-n:]
    carriers = by_distance(refs[-n - (n - 1) : -n], step == 0)
    blocks, cols, _ = state_ref.shape

    @pl.when(lax.axis_index("tm") == section)
    def _():
        keep = None
        if fix:
            rows = [marks_ref[pl.ds(marks_layout(n, blocks, fix)[2], 1)]]
            rows += [block[cols : cols + 1].astype(jnp.float32) for block in carriers]
            keep = kept(table_ref[pl.ds(row, cols)], rows)
        sums = [z_ref[i, pl.ds(z_row, cols)] for i in range(blocks)]
        give(joined(sums, step, iface_ref, marks_ref, arrived, keep), marks_ref, state_ref, outgoing)


def close_kernel(step, section, row, firsts, send, before, *refs):
    n = lax.axis_size("net")
    *refs, sems = refs
    if firsts:
        *refs, made_ref, acc_ref, cols_ref, send_ref, recv_ref, live_ref, load_sems = refs
        ints = [cols_ref, send_ref, recv_ref, live_ref]
    z_ref, iface_ref, table_ref, marks_ref, *refs = refs
    arrived, refs = by_distance(refs[: n - 1], False), refs[n - 1 :]
    before, refs = refs[:before], refs[before:]
    if firsts:
        opening_ref, handed, jac_ref, sources, refs = refs[0], refs[1:n], refs[n], refs[n + 1 : n + 5], refs[n + 5 :]
    else:
        refs = refs[1:]
    out_ref, state_ref, *outgoing = refs

    @pl.when(lax.axis_index("tm") == section)
    def _():
        copies = write_start(before, 0, out_ref, sems, row)
        sums = [z_ref[i] for i in range(z_ref.shape[0])]
        made = joined(sums, step, iface_ref, marks_ref, arrived)
        give(made, marks_ref, state_ref, outgoing)
        copies += write_start([state_ref], len(before), out_ref, sems, row)
        for copy in copies:
            copy.wait()

    if firsts:

        @pl.when(lax.axis_index("tm") == 0)
        def _():
            loads = [
                pltpu.make_async_copy(source, target, load_sems.at[i])
                for i, (source, target) in enumerate(zip(sources, ints))
            ]
            for load in loads:
                load.start()
            for load in loads:
                load.wait()
            made = first_states(opening_ref, handed, jac_ref, iface_ref, ints, table_ref, made_ref, acc_ref)
            for copy in write_start(made, 0, out_ref, sems):
                copy.wait()


def local(jac, block_cols, iface_jac, iface_send, iface_recv, iface_live, ctrl_node, ctrl_gain):
    steps, blocks, kinds, width, _ = jac.shape
    cols = ctrl_node.shape[0]
    tm = lax.axis_size("tm")
    n = lax.axis_size("net")
    col_parts = lax.axis_size("cols")
    node = ctrl_node[None]
    near = block_cols.T
    bf16 = functools.partial(jax.ShapeDtypeStruct, dtype=jnp.bfloat16)
    f32 = functools.partial(jax.ShapeDtypeStruct, dtype=jnp.float32)
    panel = cols // PANELS
    whole, part, one = bf16((blocks, cols, width)), bf16((blocks, panel, width)), bf16((panel, width))
    table_rows = GAIN + steps + -(GAIN + steps) % 8
    written = bf16((steps, cols, blocks * width))

    pinned = [
        pltpu.with_memory_space_constraint(x, pltpu.HBM)
        for x in (jac, iface_jac, near, iface_send, iface_recv, iface_live, node, ctrl_gain)
    ]
    marks_rows = marks_layout(n, blocks, kinds)[-1]
    table, marks, state, *outgoing = pl.pallas_call(
        second_kernel,
        out_shape=[f32((cols, table_rows)), f32((marks_rows, width)), whole]
        + [bf16((panel + ROWS, width))] * (n - 1)
        + [one] * ((PANELS - 1) * (n - 1)),
        in_specs=[HBM] * len(pinned),
        out_specs=[VMEM] * (3 + PANELS * (n - 1)),
        scratch_shapes=[
            pltpu.VMEM((blocks, kinds, width, width), jnp.bfloat16),
            pltpu.VMEM((n, width, width), jnp.bfloat16),
            *[pltpu.SMEM(x.shape, x.dtype) for x in (near, iface_send, iface_recv, iface_live)],
            *[pltpu.VMEM(x.shape, x.dtype) for x in (node, ctrl_gain)],
            pltpu.VMEM(whole.shape, jnp.bfloat16),
            DMA((len(pinned),)),
        ],
        compiler_params=LIMIT,
    )(*pinned)

    def own(state, step, row):
        return pl.pallas_call(
            functools.partial(own_kernel, step, row),
            out_shape=f32(state.shape),
            in_specs=[VMEM] * 5,
            out_specs=VMEM,
            compiler_params=LIMIT,
        )(state, jac, iface_jac, table, marks)

    def ordered(arrived, step):
        return [arrived[d - 1] for d in exchange_order(n, step == 0)]

    def join(z, z_row, step, fix, arrived, carriers, section, row):
        arrays = [z, iface_jac, table, marks, *ordered(arrived, step)]
        if carriers is not arrived:
            arrays += ordered(carriers, step)
        return pl.pallas_call(
            functools.partial(join_kernel, step, kinds if fix else 0, section, row, z_row),
            out_shape=[part] + [one] * (n - 1),
            in_specs=[VMEM] * len(arrays),
            out_specs=[VMEM] * n,
            compiler_params=LIMIT,
        )(*arrays)

    def close(z, step, arrived, section, row, before, out, send):
        firsts = out is None
        arrays = [z, iface_jac, table, marks, *ordered(arrived, step), *before]
        specs = [VMEM] * len(arrays)
        scratch = [DMA((steps, blocks))]
        aliases = {}
        if firsts:
            arrays += [opening, *handed, jac, *pinned[2:6]]
            specs += [VMEM] * (n + 1) + [HBM] * 4
            scratch = [
                pltpu.VMEM((2, *whole.shape), jnp.bfloat16),
                pltpu.VMEM(whole.shape, jnp.float32),
                *[pltpu.SMEM(x.shape, x.dtype) for x in pinned[2:6]],
                DMA((4,)),
            ] + scratch
        else:
            aliases = {len(arrays): 0}
            arrays.append(out)
            specs.append(ANY)
        shapes, out_specs = [written], [ANY]
        if send:
            shapes += [part] + [one] * (n - 1)
            out_specs += [VMEM] * n
        else:
            scratch.insert(0, pltpu.VMEM(part.shape, jnp.bfloat16))
        return pl.pallas_call(
            functools.partial(close_kernel, step, section, row, firsts, send, len(before)),
            out_shape=shapes,
            in_specs=specs,
            out_specs=out_specs,
            input_output_aliases=aliases,
            scratch_shapes=scratch,
            compiler_params=LIMIT,
        )(*arrays)

    def swap(block, first, second, d):
        other = {first: second, second: first}
        pairs = []
        for a in range(tm):
            for q in range(n):
                for c in range(col_parts):
                    to = (other[a] * n + (q ^ d)) * col_parts + c if a in other else (a * n + q) * col_parts + (c ^ 1)
                    pairs.append(((a * n + q) * col_parts + c, to))
        return lax.ppermute(block, ("tm", "net", "cols"), pairs)

    def exchange(outgoing, first, second):
        return [swap(outgoing[d - 1], first, second, d) for d in range(1, n)]

    opening = state
    sends = [outgoing[h * (n - 1) : (h + 1) * (n - 1)] for h in range(PANELS)]
    states = [None] * PANELS
    out = None
    for r in range(1, tm):
        arrived = [exchange(blocks_out, r - 1, r) for blocks_out in sends]
        if r == 1:
            handed = arrived[0]
            z = own(swap(state, 0, 1, 0), 0, 0)
            sums = [(z, h * panel) for h in range(PANELS)]
        else:
            sums = [(own(swap(states[h], r - 1, r, 0), 0, h * panel), 0) for h in range(PANELS)]
        before = [[] for _ in range(PANELS)]
        for s in range(steps):
            if s > 0:
                arrived = [exchange(blocks_out, r, r) for blocks_out in sends]
                sums = [(own(states[h], s, h * panel), 0) for h in range(PANELS)]
            for h in range(PANELS):
                row = h * panel
                if s < steps - 1:
                    states[h], *sends[h] = join(*sums[h], s, r == 1 and s == 0, arrived[h], arrived[0] if s == 0 and r == 1 else arrived[h], r, row)
                    before[h].append(states[h])
                else:
                    out, *rest = close(sums[h][0], s, arrived[h], r, row, before[h], out, r < tm - 1)
                    states[h], *sends[h] = rest or [None]
    return out


def solution(mesh):
    return jax.shard_map(
        local,
        mesh=mesh,
        in_specs=(
            P("tm", "net", None, None, None),
            P("net", None),
            P("tm", "net", None, None, None),
            P("net", None),
            P("net", None),
            P("net", None),
            P("cols"),
            P("tm", "cols"),
        ),
        out_specs=P("tm", "cols", "net"),
        check_vma=False,
    )
```

```python
import functools

import jax
import jax.numpy as jnp
from jax import lax
from jax.experimental import pallas as pl
from jax.experimental.pallas import tpu as pltpu
from jax.sharding import PartitionSpec as P

VMEM = pl.BlockSpec(memory_space=pltpu.VMEM)
SMEM = pl.BlockSpec(memory_space=pltpu.SMEM)
HBM = pl.BlockSpec(memory_space=pltpu.HBM)
ANY = pl.BlockSpec(memory_space=pl.ANY)
LIMIT = pltpu.CompilerParams(vmem_limit_bytes=16 * 1024 * 1024)
DMA = pltpu.SemaphoreType.DMA

STATE, LANE, BLOCK, AWAY, GAIN = 0, 1, 2, 3, 4
ROWS = 16


def times_transposed(rows, block):
    return lax.dot_general(rows, block, (((1,), (1,)), ((), ())), preferred_element_type=jnp.float32)


def hits(table, i, blocks, width):
    first_state = (lax.axis_index("net") * blocks + i) * width
    lane = lax.broadcasted_iota(jnp.int32, (table.shape[0], width), 1)
    return table[:, STATE : STATE + 1] == (lane + first_state).astype(jnp.float32)


def injected(table, step, hit):
    return jnp.where(hit, table[:, GAIN + step : GAIN + step + 1], 0.0)


def near_by(state_ref, cols_ref):
    return lambda i, k: state_ref[cols_ref[k, i]]


def products(i, state_ref, jac_ref, near):
    kinds = jac_ref.shape[1]
    rows = [state_ref[i]] + [near(i, k) for k in range(kinds - 1)]
    row_blocks = [jac_ref[i, k] for k in range(kinds)]
    return times_transposed(jnp.concatenate(rows, axis=1), jnp.concatenate(row_blocks, axis=1))


def own_sum(i, state_ref, jac_ref, near, table, step):
    blocks, _, width = state_ref.shape
    return products(i, state_ref, jac_ref, near) + injected(table, step, hits(table, i, blocks, width))


def picked(blocks, marks):
    total = blocks[0] * marks[0]
    for block, mark in zip(blocks[1:], marks[1:]):
        total += block * mark
    return total


def marks_layout(n, blocks, kinds):
    sent = n * blocks
    near = sent + n * blocks
    row = near + blocks * (kinds - 1) * blocks
    return sent, near, row, row + 1 + -(row + 1) % 8


def make_marks(marks_ref, blocks, kinds, cols_ref, send_ref, recv_ref, live_ref):
    n = lax.axis_size("net")
    me = lax.axis_index("net")
    width = marks_ref.shape[1]
    lane = lax.broadcasted_iota(jnp.int32, (1, width), 1)
    sent, near, own_row, _ = marks_layout(n, blocks, kinds)

    def put(row, mask):
        marks_ref[pl.ds(row, 1)] = jnp.where(mask, 1.0, 0.0)

    for d in range(n):
        q = me ^ d
        for i in range(blocks):
            put(d * blocks + i, lane < jnp.where(recv_ref[0, q] == i, live_ref[0, q], 0))
            put(sent + d * blocks + i, lane < jnp.where(send_ref[0, q] == i, width, 0))
    for i in range(blocks):
        for k in range(kinds - 1):
            for j in range(blocks):
                put(near + (i * (kinds - 1) + k) * blocks + j, lane < jnp.where(cols_ref[k, i] == j, width, 0))
    marks_ref[pl.ds(own_row, 1)] = table_row(send_ref, me, width)


def add_coupled(incoming, block, live, recv, z_ref):
    mask = lax.broadcasted_iota(jnp.int32, z_ref.shape[1:], 1) < live
    z_ref[recv] += jnp.where(mask, times_transposed(incoming, block), 0.0)


def table_row(send_ref, partition, width):
    lane = lax.broadcasted_iota(jnp.int32, (1, width), 1)
    row = jnp.zeros((1, width), jnp.float32)
    for e in range(lax.axis_size("net")):
        row = jnp.where(lane == e, send_ref[0, partition ^ e].astype(jnp.float32), row)
    return row


def kept(table, rows):
    away, block = table[:, AWAY : AWAY + 1], table[:, BLOCK : BLOCK + 1]
    sent = jnp.broadcast_to(rows[0], (table.shape[0], rows[0].shape[1]))
    for d in range(1, len(rows)):
        sent = jnp.where(away == float(d), rows[d], sent)
    lane = lax.broadcasted_iota(jnp.int32, sent.shape, 1).astype(jnp.float32)
    return jnp.where(jnp.logical_or(away == lane, block == sent), 1.0, 0.0)


def second_kernel(*refs):
    jac_hbm, iface_hbm, *small, table_ref, marks_ref, state_ref = refs[:11]
    n = lax.axis_size("net")
    me = lax.axis_index("net")
    outgoing, refs = refs[11 : 10 + n], refs[10 + n :]
    jac_ref, iface_ref, *loaded, first_ref, sems = refs
    cols_ref, send_ref, recv_ref, live_ref, node_ref, gain_ref = loaded
    blocks, cols, width = state_ref.shape
    sources = [jac_hbm.at[1], iface_hbm.at[1, 0], *small]
    loads = [
        pltpu.make_async_copy(source, target, sems.at[i])
        for i, (source, target) in enumerate(zip(sources, [jac_ref, iface_ref, *loaded]))
    ]
    here = lax.axis_index("tm") == 0
    for load in loads[6:]:
        load.start()

    @pl.when(here)
    def _():
        for load in loads[:2]:
            load.start()

    for load in loads[2:6]:
        load.start()
    for load in loads[6:]:
        load.wait()
    node = node_ref[...]
    block_of = node // width
    rows = [
        node,
        node - block_of * width,
        block_of % blocks,
        (block_of // blocks) ^ me,
    ]
    steps = gain_ref.shape[0]
    fill = -(GAIN + steps) % 8
    rows = [row.astype(jnp.float32) for row in rows] + [gain_ref[...], jnp.zeros((fill, cols), jnp.float32)]
    table_ref[...] = jnp.concatenate(rows, axis=0).T

    @pl.when(here)
    def _():
        table = table_ref[...]

        def spread(column):
            return jnp.broadcast_to(column, (cols, width))

        lane = lax.broadcasted_iota(jnp.int32, (cols, width), 1).astype(jnp.float32)
        place = spread(table[:, STATE : STATE + 1] - (me * blocks * width).astype(jnp.float32)) - lane
        gain = spread(table[:, GAIN : GAIN + 1])
        later_gain = spread(table[:, GAIN + 1 : GAIN + 2])
        hit = [place == float(i * width) for i in range(blocks)]
        for i in range(blocks):
            first_ref[i] = jnp.where(hit[i], gain, 0.0).astype(first_ref.dtype)
        away, block = table[:, AWAY : AWAY + 1], table[:, BLOCK : BLOCK + 1]
        for load in loads[2:6]:
            load.wait()
        mine = jnp.logical_or(away != 0.0, block == send_ref[0, me].astype(jnp.float32))
        shot_lane = spread(jnp.where(mine, table[:, LANE : LANE + 1], -1.0))
        shot = jnp.where(lane == shot_lane, gain, 0.0)
        live = recv = jnp.zeros_like(away)
        for d in range(n):
            live = jnp.where(away == float(d), live_ref[0, me ^ d].astype(jnp.float32), live)
            recv = jnp.where(away == float(d), recv_ref[0, me ^ d].astype(jnp.float32), recv)
        away, live, recv = spread(away), spread(live), spread(recv)
        sent = [jnp.where(away == float(d), shot, 0.0).astype(first_ref.dtype) for d in range(n)]
        loads[1].wait()
        ifaces = jnp.concatenate([iface_ref[me ^ d] for d in range(n)], axis=1)
        coupled = times_transposed(jnp.concatenate(sent, axis=1), ifaces)
        coupled = jnp.where(lane < live, coupled, 0.0)
        loads[0].wait()
        for i in range(blocks):
            own = products(i, first_ref, jac_ref, near_by(first_ref, cols_ref))
            own += jnp.where(hit[i], later_gain, 0.0)
            state_ref[i] = (own + jnp.where(recv == float(i), coupled, 0.0)).astype(state_ref.dtype)
        for d in range(1, n):
            outgoing[d - 1][pl.ds(0, cols)] = state_ref[send_ref[0, me ^ d]]

    @pl.when(jnp.logical_not(here))
    def _():
        for load in loads[2:6]:
            load.wait()
        make_marks(marks_ref, blocks, jac_ref.shape[1], cols_ref, send_ref, recv_ref, live_ref)

    for d in range(1, n):
        row = table_row(send_ref, me ^ d, width).astype(state_ref.dtype)
        outgoing[d - 1][pl.ds(cols, ROWS)] = jnp.broadcast_to(row, (ROWS, width))


def write_start(states, first, out_ref, sems):
    copies = []
    for s, state_ref in enumerate(states, first):
        width = state_ref.shape[2]
        for i in range(state_ref.shape[0]):
            copies.append(
                pltpu.make_async_copy(state_ref.at[i], out_ref.at[s, :, pl.ds(i * width, width)], sems.at[s, i])
            )
    for copy in copies:
        copy.start()
    return copies


def own_kernel(step, state_ref, jac_ref, iface_ref, table_ref, marks_ref, z_ref):
    table = table_ref[...]
    n = lax.axis_size("net")
    blocks = state_ref.shape[0]
    kinds = jac_ref.shape[2]
    sent, near, _, _ = marks_layout(n, blocks, kinds)
    state = [state_ref[j] for j in range(blocks)]

    def pick(row):
        return picked(state, [marks_ref[pl.ds(row + j, 1)].astype(state_ref.dtype) for j in range(blocks)])

    def near_block(i, k):
        return pick(near + (i * (kinds - 1) + k) * blocks)

    @pl.when(lax.axis_index("tm") > 0)
    def _():
        term = times_transposed(pick(sent), iface_ref[step, 0, lax.axis_index("net")])
        for i in range(blocks):
            own = own_sum(i, state_ref, jac_ref.at[step], near_block, table, step)
            z_ref[i] = own + term * marks_ref[pl.ds(i, 1)]


def first_states(opening, handed, jac_ref, iface_ref, ints, table_ref, made_ref, z_ref):
    cols_ref, send_ref, recv_ref, live_ref = ints
    n = lax.axis_size("net")
    blocks, cols, width = z_ref.shape
    table = table_ref[...]
    made_ref[0] = jnp.zeros_like(made_ref[0])
    for i in range(blocks):
        z_ref[i] = own_sum(i, made_ref.at[0], jac_ref.at[0], near_by(made_ref.at[0], cols_ref), table, 0)
    for q in range(n):
        add_coupled(made_ref[0, 0], iface_ref[0, 0, q], live_ref[0, q], recv_ref[0, q], z_ref)
    made_ref[0] = z_ref[...].astype(made_ref.dtype)
    rows = [table_row(send_ref, lax.axis_index("net"), width)]
    rows += [block[cols : cols + 1].astype(jnp.float32) for block in handed]
    keep = kept(table, rows)[:, 0:1]
    for i in range(blocks):
        made_ref[1, i] = jnp.where(keep > 0.0, opening[i], jnp.zeros_like(opening[i]))
    return [made_ref.at[0], made_ref.at[1]]


def joined(sums, step, iface_ref, marks_ref, arrived, keep=None):
    me = lax.axis_index("net")
    blocks, cols = len(sums), sums[0].shape[0]
    if keep is not None:
        sums = [total * keep[:, 0:1] for total in sums]
    for d, block in enumerate(arrived, 1):
        term = times_transposed(block[pl.ds(0, cols)], iface_ref[step, 0, me ^ d])
        if keep is not None:
            term *= keep[:, d : d + 1]
        sums = [total + term * marks_ref[pl.ds(d * blocks + i, 1)] for i, total in enumerate(sums)]
    return [total.astype(jnp.bfloat16) for total in sums]


def give(made, marks_ref, state_ref, outgoing):
    blocks = len(made)
    n = lax.axis_size("net")
    sent = marks_layout(n, blocks, 1)[0]
    for i in range(blocks):
        state_ref[i] = made[i]
    for d in range(1, n) if outgoing else ():
        marks = [marks_ref[pl.ds(sent + d * blocks + j, 1)].astype(made[j].dtype) for j in range(blocks)]
        outgoing[d - 1][...] = picked(made, marks)


def exchange_order(n, handed):
    return [*range(n // 2, n), *range(n // 2 - 1, 0, -1)] if handed else list(range(1, n))


def by_distance(refs, handed):
    order = exchange_order(len(refs) + 1, handed)
    return [refs[order.index(d)] for d in range(1, len(refs) + 1)]


def join_kernel(step, fix, section, z_ref, iface_ref, table_ref, marks_ref, *refs):
    n = lax.axis_size("net")
    arrived, state_ref, outgoing = by_distance(refs[: n - 1], step == 0), refs[n - 1], refs[n:]
    blocks, cols, _ = z_ref.shape

    @pl.when(lax.axis_index("tm") == section)
    def _():
        keep = None
        if fix:
            rows = [marks_ref[pl.ds(marks_layout(n, blocks, fix)[2], 1)]]
            rows += [block[cols : cols + 1].astype(jnp.float32) for block in arrived]
            keep = kept(table_ref[...], rows)
        made = joined([z_ref[i] for i in range(blocks)], step, iface_ref, marks_ref, arrived, keep)
        give(made, marks_ref, state_ref, outgoing)


def close_kernel(step, section, firsts, send, before, *refs):
    n = lax.axis_size("net")
    *refs, sems = refs
    if firsts:
        *refs, made_ref, acc_ref, cols_ref, send_ref, recv_ref, live_ref, load_sems = refs
        ints = [cols_ref, send_ref, recv_ref, live_ref]
    z_ref, iface_ref, table_ref, marks_ref, *refs = refs
    arrived, refs = by_distance(refs[: n - 1], False), refs[n - 1 :]
    before, refs = refs[:before], refs[before:]
    if firsts:
        opening_ref, handed, jac_ref, sources, refs = refs[0], refs[1:n], refs[n], refs[n + 1 : n + 5], refs[n + 5 :]
    else:
        refs = refs[1:]
    out_ref, state_ref, *outgoing = refs

    @pl.when(lax.axis_index("tm") == section)
    def _():
        copies = write_start(before, 0, out_ref, sems)
        sums = [z_ref[i] for i in range(z_ref.shape[0])]
        made = joined(sums, step, iface_ref, marks_ref, arrived)
        give(made, marks_ref, state_ref, outgoing)
        copies += write_start([state_ref], len(before), out_ref, sems)
        for copy in copies:
            copy.wait()

    if firsts:

        @pl.when(lax.axis_index("tm") == 0)
        def _():
            loads = [
                pltpu.make_async_copy(source, target, load_sems.at[i])
                for i, (source, target) in enumerate(zip(sources, ints))
            ]
            for load in loads:
                load.start()
            for load in loads:
                load.wait()
            made = first_states(opening_ref, handed, jac_ref, iface_ref, ints, table_ref, made_ref, acc_ref)
            for copy in write_start(made, 0, out_ref, sems):
                copy.wait()


def local(jac, block_cols, iface_jac, iface_send, iface_recv, iface_live, ctrl_node, ctrl_gain):
    steps, blocks, kinds, width, _ = jac.shape
    cols = ctrl_node.shape[0]
    tm = lax.axis_size("tm")
    n = lax.axis_size("net")
    col_parts = lax.axis_size("cols")
    node = ctrl_node[None]
    near = block_cols.T
    bf16 = functools.partial(jax.ShapeDtypeStruct, dtype=jnp.bfloat16)
    f32 = functools.partial(jax.ShapeDtypeStruct, dtype=jnp.float32)
    whole, one = bf16((blocks, cols, width)), bf16((cols, width))
    table_rows = GAIN + steps + -(GAIN + steps) % 8
    written = bf16((steps, cols, blocks * width))

    pinned = [
        pltpu.with_memory_space_constraint(x, pltpu.HBM)
        for x in (jac, iface_jac, near, iface_send, iface_recv, iface_live, node, ctrl_gain)
    ]
    marks_rows = marks_layout(n, blocks, kinds)[-1]
    table, marks, state, *outgoing = pl.pallas_call(
        second_kernel,
        out_shape=[f32((cols, table_rows)), f32((marks_rows, width)), whole]
        + [bf16((cols + ROWS, width))] * (n - 1),
        in_specs=[HBM] * len(pinned),
        out_specs=[VMEM] * (n + 2),
        scratch_shapes=[
            pltpu.VMEM((blocks, kinds, width, width), jnp.bfloat16),
            pltpu.VMEM((n, width, width), jnp.bfloat16),
            *[pltpu.SMEM(x.shape, x.dtype) for x in (near, iface_send, iface_recv, iface_live)],
            *[pltpu.VMEM(x.shape, x.dtype) for x in (node, ctrl_gain)],
            pltpu.VMEM(whole.shape, jnp.bfloat16),
            DMA((len(pinned),)),
        ],
        compiler_params=LIMIT,
    )(*pinned)

    def own(state, step):
        return pl.pallas_call(
            functools.partial(own_kernel, step),
            out_shape=f32(whole.shape),
            in_specs=[VMEM] * 5,
            out_specs=VMEM,
            compiler_params=LIMIT,
        )(state, jac, iface_jac, table, marks)

    def join(z, step, fix, arrived, section):
        return pl.pallas_call(
            functools.partial(join_kernel, step, kinds if fix else 0, section),
            out_shape=[whole] + [one] * (n - 1),
            in_specs=[VMEM] * (n + 3),
            out_specs=[VMEM] * n,
            compiler_params=LIMIT,
        )(z, iface_jac, table, marks, *[arrived[d - 1] for d in exchange_order(n, step == 0)])

    def close(z, step, arrived, section, before, out, send):
        firsts = out is None
        arrays = [z, iface_jac, table, marks, *[arrived[d - 1] for d in exchange_order(n, False)], *before]
        specs = [VMEM] * len(arrays)
        scratch = [DMA((steps, blocks))]
        aliases = {}
        if firsts:
            arrays += [opening, *handed, jac, *pinned[2:6]]
            specs += [VMEM] * (n + 1) + [HBM] * 4
            scratch = [
                pltpu.VMEM((2, *whole.shape), jnp.bfloat16),
                pltpu.VMEM(whole.shape, jnp.float32),
                *[pltpu.SMEM(x.shape, x.dtype) for x in pinned[2:6]],
                DMA((4,)),
            ] + scratch
        else:
            aliases = {len(arrays): 0}
            arrays.append(out)
            specs.append(ANY)
        shapes, out_specs = [written], [ANY]
        if send:
            shapes += [whole] + [one] * (n - 1)
            out_specs += [VMEM] * n
        else:
            scratch.insert(0, pltpu.VMEM(whole.shape, jnp.bfloat16))
        return pl.pallas_call(
            functools.partial(close_kernel, step, section, firsts, send, len(before)),
            out_shape=shapes,
            in_specs=specs,
            out_specs=out_specs,
            input_output_aliases=aliases,
            scratch_shapes=scratch,
            compiler_params=LIMIT,
        )(*arrays)

    def swap(block, first, second, d):
        other = {first: second, second: first}
        pairs = []
        for a in range(tm):
            for q in range(n):
                for c in range(col_parts):
                    to = (other[a] * n + (q ^ d)) * col_parts + c if a in other else (a * n + q) * col_parts + (c ^ 1)
                    pairs.append(((a * n + q) * col_parts + c, to))
        return lax.ppermute(block, ("tm", "net", "cols"), pairs)

    def exchange(outgoing, first, second):
        return [swap(outgoing[d - 1], first, second, d) for d in range(1, n)]

    opening = state
    out = None
    for r in range(1, tm):
        arrived = exchange(outgoing, r - 1, r)
        state = swap(state, r - 1, r, 0)
        if r == 1:
            handed = arrived
        before = []
        for s in range(steps):
            fix = r == 1 and s == 0
            if s > 0:
                arrived = exchange(outgoing, r, r)
            z = own(state, s)
            if s < steps - 1:
                state, *outgoing = join(z, s, fix, arrived, r)
                before.append(state)
            else:
                out, *rest = close(z, s, arrived, r, before, out, r < tm - 1)
                state, *outgoing = rest or [None]
    return out


def solution(mesh):
    return jax.shard_map(
        local,
        mesh=mesh,
        in_specs=(
            P("tm", "net", None, None, None),
            P("net", None),
            P("tm", "net", None, None, None),
            P("net", None),
            P("net", None),
            P("net", None),
            P("cols"),
            P("tm", "cols"),
        ),
        out_specs=P("tm", "cols", "net"),
        check_vma=False,
    )
```

```python
import functools

import jax
import jax.numpy as jnp
from jax import lax
from jax.experimental import pallas as pl
from jax.experimental.pallas import tpu as pltpu
from jax.sharding import PartitionSpec as P

VMEM = pl.BlockSpec(memory_space=pltpu.VMEM)
SMEM = pl.BlockSpec(memory_space=pltpu.SMEM)
HBM = pl.BlockSpec(memory_space=pltpu.HBM)
ANY = pl.BlockSpec(memory_space=pl.ANY)
LIMIT = pltpu.CompilerParams(vmem_limit_bytes=16 * 1024 * 1024)
DMA = pltpu.SemaphoreType.DMA

STATE, LANE, BLOCK, AWAY, GAIN = 0, 1, 2, 3, 4
ROWS = 16


def times_transposed(rows, block):
    return lax.dot_general(rows, block, (((1,), (1,)), ((), ())), preferred_element_type=jnp.float32)


def hits(table, i, blocks, width):
    first_state = (lax.axis_index("net") * blocks + i) * width
    lane = lax.broadcasted_iota(jnp.int32, (table.shape[0], width), 1)
    return table[:, STATE : STATE + 1] == (lane + first_state).astype(jnp.float32)


def injected(table, step, hit):
    return jnp.where(hit, table[:, GAIN + step : GAIN + step + 1], 0.0)


def near_by(state_ref, cols_ref):
    return lambda i, k: state_ref[cols_ref[k, i]]


def products(i, state_ref, jac_ref, near):
    kinds = jac_ref.shape[1]
    rows = [state_ref[i]] + [near(i, k) for k in range(kinds - 1)]
    row_blocks = [jac_ref[i, k] for k in range(kinds)]
    return times_transposed(jnp.concatenate(rows, axis=1), jnp.concatenate(row_blocks, axis=1))


def own_sum(i, state_ref, jac_ref, near, table, step):
    blocks, _, width = state_ref.shape
    return products(i, state_ref, jac_ref, near) + injected(table, step, hits(table, i, blocks, width))


def picked(blocks, marks):
    total = blocks[0] * marks[0]
    for block, mark in zip(blocks[1:], marks[1:]):
        total += block * mark
    return total


def marks_layout(n, blocks, kinds):
    sent = n * blocks
    near = sent + n * blocks
    row = near + blocks * (kinds - 1) * blocks
    return sent, near, row, row + 1 + -(row + 1) % 8


def make_marks(marks_ref, blocks, kinds, cols_ref, send_ref, recv_ref, live_ref):
    n = lax.axis_size("net")
    me = lax.axis_index("net")
    width = marks_ref.shape[1]
    lane = lax.broadcasted_iota(jnp.int32, (1, width), 1)
    sent, near, own_row, _ = marks_layout(n, blocks, kinds)

    def put(row, mask):
        marks_ref[pl.ds(row, 1)] = jnp.where(mask, 1.0, 0.0)

    for d in range(n):
        q = me ^ d
        for i in range(blocks):
            put(d * blocks + i, lane < jnp.where(recv_ref[0, q] == i, live_ref[0, q], 0))
            put(sent + d * blocks + i, lane < jnp.where(send_ref[0, q] == i, width, 0))
    for i in range(blocks):
        for k in range(kinds - 1):
            for j in range(blocks):
                put(near + (i * (kinds - 1) + k) * blocks + j, lane < jnp.where(cols_ref[k, i] == j, width, 0))
    marks_ref[pl.ds(own_row, 1)] = table_row(send_ref, me, width)


def add_coupled(incoming, block, live, recv, z_ref):
    mask = lax.broadcasted_iota(jnp.int32, z_ref.shape[1:], 1) < live
    z_ref[recv] += jnp.where(mask, times_transposed(incoming, block), 0.0)


def table_row(send_ref, partition, width):
    lane = lax.broadcasted_iota(jnp.int32, (1, width), 1)
    row = jnp.zeros((1, width), jnp.float32)
    for e in range(lax.axis_size("net")):
        row = jnp.where(lane == e, send_ref[0, partition ^ e].astype(jnp.float32), row)
    return row


def kept(table, rows):
    away, block = table[:, AWAY : AWAY + 1], table[:, BLOCK : BLOCK + 1]
    sent = jnp.broadcast_to(rows[0], (table.shape[0], rows[0].shape[1]))
    for d in range(1, len(rows)):
        sent = jnp.where(away == float(d), rows[d], sent)
    lane = lax.broadcasted_iota(jnp.int32, sent.shape, 1).astype(jnp.float32)
    return jnp.where(jnp.logical_or(away == lane, block == sent), 1.0, 0.0)


def second_kernel(*refs):
    jac_hbm, iface_hbm, *small, table_ref, marks_ref, state_ref = refs[:11]
    n = lax.axis_size("net")
    me = lax.axis_index("net")
    outgoing, refs = refs[11 : 10 + n], refs[10 + n :]
    jac_ref, iface_ref, *loaded, first_ref, sems = refs
    cols_ref, send_ref, recv_ref, live_ref, node_ref, gain_ref = loaded
    blocks, cols, width = state_ref.shape
    sources = [jac_hbm.at[1], iface_hbm.at[1, 0], *small]
    loads = [
        pltpu.make_async_copy(source, target, sems.at[i])
        for i, (source, target) in enumerate(zip(sources, [jac_ref, iface_ref, *loaded]))
    ]
    here = lax.axis_index("tm") == 0
    for load in loads[6:]:
        load.start()

    @pl.when(here)
    def _():
        for load in loads[:2]:
            load.start()

    for load in loads[2:6]:
        load.start()
    for load in loads[6:]:
        load.wait()
    node = node_ref[...]
    block_of = node // width
    rows = [
        node,
        node - block_of * width,
        block_of % blocks,
        (block_of // blocks) ^ me,
    ]
    steps = gain_ref.shape[0]
    fill = -(GAIN + steps) % 8
    rows = [row.astype(jnp.float32) for row in rows] + [gain_ref[...], jnp.zeros((fill, cols), jnp.float32)]
    table_ref[...] = jnp.concatenate(rows, axis=0).T

    @pl.when(here)
    def _():
        table = table_ref[...]

        def spread(column):
            return jnp.broadcast_to(column, (cols, width))

        lane = lax.broadcasted_iota(jnp.int32, (cols, width), 1).astype(jnp.float32)
        place = spread(table[:, STATE : STATE + 1] - (me * blocks * width).astype(jnp.float32)) - lane
        gain = spread(table[:, GAIN : GAIN + 1])
        later_gain = spread(table[:, GAIN + 1 : GAIN + 2])
        hit = [place == float(i * width) for i in range(blocks)]
        for i in range(blocks):
            first_ref[i] = jnp.where(hit[i], gain, 0.0).astype(first_ref.dtype)
        away, block = table[:, AWAY : AWAY + 1], table[:, BLOCK : BLOCK + 1]
        for load in loads[2:6]:
            load.wait()
        mine = jnp.logical_or(away != 0.0, block == send_ref[0, me].astype(jnp.float32))
        shot_lane = spread(jnp.where(mine, table[:, LANE : LANE + 1], -1.0))
        shot = jnp.where(lane == shot_lane, gain, 0.0)
        live = recv = jnp.zeros_like(away)
        for d in range(n):
            live = jnp.where(away == float(d), live_ref[0, me ^ d].astype(jnp.float32), live)
            recv = jnp.where(away == float(d), recv_ref[0, me ^ d].astype(jnp.float32), recv)
        away, live, recv = spread(away), spread(live), spread(recv)
        sent = [jnp.where(away == float(d), shot, 0.0).astype(first_ref.dtype) for d in range(n)]
        loads[1].wait()
        ifaces = jnp.concatenate([iface_ref[me ^ d] for d in range(n)], axis=1)
        coupled = times_transposed(jnp.concatenate(sent, axis=1), ifaces)
        coupled = jnp.where(lane < live, coupled, 0.0)
        loads[0].wait()
        for i in range(blocks):
            own = products(i, first_ref, jac_ref, near_by(first_ref, cols_ref))
            own += jnp.where(hit[i], later_gain, 0.0)
            state_ref[i] = (own + jnp.where(recv == float(i), coupled, 0.0)).astype(state_ref.dtype)
        for d in range(1, n):
            outgoing[d - 1][pl.ds(0, cols)] = state_ref[send_ref[0, me ^ d]]

    @pl.when(jnp.logical_not(here))
    def _():
        for load in loads[2:6]:
            load.wait()
        make_marks(marks_ref, blocks, jac_ref.shape[1], cols_ref, send_ref, recv_ref, live_ref)

    for d in range(1, n):
        row = table_row(send_ref, me ^ d, width).astype(state_ref.dtype)
        outgoing[d - 1][pl.ds(cols, ROWS)] = jnp.broadcast_to(row, (ROWS, width))


def write_start(states, first, out_ref, sems):
    copies = []
    for s, state_ref in enumerate(states, first):
        width = state_ref.shape[2]
        for i in range(state_ref.shape[0]):
            copies.append(
                pltpu.make_async_copy(state_ref.at[i], out_ref.at[s, :, pl.ds(i * width, width)], sems.at[s, i])
            )
    for copy in copies:
        copy.start()
    return copies


def own_kernel(step, state_ref, jac_ref, iface_ref, table_ref, marks_ref, z_ref):
    table = table_ref[...]
    n = lax.axis_size("net")
    blocks = state_ref.shape[0]
    kinds = jac_ref.shape[2]
    sent, near, _, _ = marks_layout(n, blocks, kinds)
    state = [state_ref[j] for j in range(blocks)]

    def pick(row):
        return picked(state, [marks_ref[pl.ds(row + j, 1)].astype(state_ref.dtype) for j in range(blocks)])

    def near_block(i, k):
        return pick(near + (i * (kinds - 1) + k) * blocks)

    @pl.when(lax.axis_index("tm") > 0)
    def _():
        term = times_transposed(pick(sent), iface_ref[step, 0, lax.axis_index("net")])
        for i in range(blocks):
            own = own_sum(i, state_ref, jac_ref.at[step], near_block, table, step)
            z_ref[i] = own + term * marks_ref[pl.ds(i, 1)]


def first_states(opening, handed, jac_ref, iface_ref, ints, table_ref, made_ref, z_ref):
    cols_ref, send_ref, recv_ref, live_ref = ints
    n = lax.axis_size("net")
    blocks, cols, width = z_ref.shape
    table = table_ref[...]
    made_ref[0] = jnp.zeros_like(made_ref[0])
    for i in range(blocks):
        z_ref[i] = own_sum(i, made_ref.at[0], jac_ref.at[0], near_by(made_ref.at[0], cols_ref), table, 0)
    for q in range(n):
        add_coupled(made_ref[0, 0], iface_ref[0, 0, q], live_ref[0, q], recv_ref[0, q], z_ref)
    made_ref[0] = z_ref[...].astype(made_ref.dtype)
    rows = [table_row(send_ref, lax.axis_index("net"), width)]
    rows += [block[cols : cols + 1].astype(jnp.float32) for block in handed]
    keep = kept(table, rows)[:, 0:1]
    for i in range(blocks):
        made_ref[1, i] = jnp.where(keep > 0.0, opening[i], jnp.zeros_like(opening[i]))
    return [made_ref.at[0], made_ref.at[1]]


def joined(sums, step, iface_ref, marks_ref, arrived, keep=None):
    me = lax.axis_index("net")
    blocks, cols = len(sums), sums[0].shape[0]
    if keep is not None:
        sums = [total * keep[:, 0:1] for total in sums]
    for d, block in enumerate(arrived, 1):
        term = times_transposed(block[pl.ds(0, cols)], iface_ref[step, 0, me ^ d])
        if keep is not None:
            term *= keep[:, d : d + 1]
        sums = [total + term * marks_ref[pl.ds(d * blocks + i, 1)] for i, total in enumerate(sums)]
    return [total.astype(jnp.bfloat16) for total in sums]


def give(made, marks_ref, state_ref, outgoing):
    blocks = len(made)
    n = lax.axis_size("net")
    sent = marks_layout(n, blocks, 1)[0]
    for i in range(blocks):
        state_ref[i] = made[i]
    for d in range(1, n) if outgoing else ():
        marks = [marks_ref[pl.ds(sent + d * blocks + j, 1)].astype(made[j].dtype) for j in range(blocks)]
        outgoing[d - 1][...] = picked(made, marks)


def exchange_order(n, handed):
    return [*range(n // 2, n), *range(n // 2 - 1, 0, -1)] if handed else [1, *range(n - 1, 1, -1)]


def by_distance(refs, handed):
    order = exchange_order(len(refs) + 1, handed)
    return [refs[order.index(d)] for d in range(1, len(refs) + 1)]


def join_kernel(step, fix, section, z_ref, iface_ref, table_ref, marks_ref, *refs):
    n = lax.axis_size("net")
    arrived, state_ref, outgoing = by_distance(refs[: n - 1], step == 0), refs[n - 1], refs[n:]
    blocks, cols, _ = z_ref.shape

    @pl.when(lax.axis_index("tm") == section)
    def _():
        keep = None
        if fix:
            rows = [marks_ref[pl.ds(marks_layout(n, blocks, fix)[2], 1)]]
            rows += [block[cols : cols + 1].astype(jnp.float32) for block in arrived]
            keep = kept(table_ref[...], rows)
        made = joined([z_ref[i] for i in range(blocks)], step, iface_ref, marks_ref, arrived, keep)
        give(made, marks_ref, state_ref, outgoing)


def close_kernel(step, section, firsts, send, before, *refs):
    n = lax.axis_size("net")
    *refs, sems = refs
    if firsts:
        *refs, made_ref, acc_ref, cols_ref, send_ref, recv_ref, live_ref, load_sems = refs
        ints = [cols_ref, send_ref, recv_ref, live_ref]
    z_ref, iface_ref, table_ref, marks_ref, *refs = refs
    arrived, refs = by_distance(refs[: n - 1], False), refs[n - 1 :]
    before, refs = refs[:before], refs[before:]
    if firsts:
        opening_ref, handed, jac_ref, sources, refs = refs[0], refs[1:n], refs[n], refs[n + 1 : n + 5], refs[n + 5 :]
    else:
        refs = refs[1:]
    out_ref, state_ref, *outgoing = refs

    @pl.when(lax.axis_index("tm") == section)
    def _():
        copies = write_start(before, 0, out_ref, sems)
        sums = [z_ref[i] for i in range(z_ref.shape[0])]
        made = joined(sums, step, iface_ref, marks_ref, arrived)
        give(made, marks_ref, state_ref, outgoing)
        copies += write_start([state_ref], len(before), out_ref, sems)
        for copy in copies:
            copy.wait()

    if firsts:

        @pl.when(lax.axis_index("tm") == 0)
        def _():
            loads = [
                pltpu.make_async_copy(source, target, load_sems.at[i])
                for i, (source, target) in enumerate(zip(sources, ints))
            ]
            for load in loads:
                load.start()
            for load in loads:
                load.wait()
            made = first_states(opening_ref, handed, jac_ref, iface_ref, ints, table_ref, made_ref, acc_ref)
            for copy in write_start(made, 0, out_ref, sems):
                copy.wait()


def local(jac, block_cols, iface_jac, iface_send, iface_recv, iface_live, ctrl_node, ctrl_gain):
    steps, blocks, kinds, width, _ = jac.shape
    cols = ctrl_node.shape[0]
    tm = lax.axis_size("tm")
    n = lax.axis_size("net")
    col_parts = lax.axis_size("cols")
    node = ctrl_node[None]
    near = block_cols.T
    bf16 = functools.partial(jax.ShapeDtypeStruct, dtype=jnp.bfloat16)
    f32 = functools.partial(jax.ShapeDtypeStruct, dtype=jnp.float32)
    whole, one = bf16((blocks, cols, width)), bf16((cols, width))
    table_rows = GAIN + steps + -(GAIN + steps) % 8
    written = bf16((steps, cols, blocks * width))

    pinned = [
        pltpu.with_memory_space_constraint(x, pltpu.HBM)
        for x in (jac, iface_jac, near, iface_send, iface_recv, iface_live, node, ctrl_gain)
    ]
    marks_rows = marks_layout(n, blocks, kinds)[-1]
    table, marks, state, *outgoing = pl.pallas_call(
        second_kernel,
        out_shape=[f32((cols, table_rows)), f32((marks_rows, width)), whole]
        + [bf16((cols + ROWS, width))] * (n - 1),
        in_specs=[HBM] * len(pinned),
        out_specs=[VMEM] * (n + 2),
        scratch_shapes=[
            pltpu.VMEM((blocks, kinds, width, width), jnp.bfloat16),
            pltpu.VMEM((n, width, width), jnp.bfloat16),
            *[pltpu.SMEM(x.shape, x.dtype) for x in (near, iface_send, iface_recv, iface_live)],
            *[pltpu.VMEM(x.shape, x.dtype) for x in (node, ctrl_gain)],
            pltpu.VMEM(whole.shape, jnp.bfloat16),
            DMA((len(pinned),)),
        ],
        compiler_params=LIMIT,
    )(*pinned)

    def own(state, step):
        return pl.pallas_call(
            functools.partial(own_kernel, step),
            out_shape=f32(whole.shape),
            in_specs=[VMEM] * 5,
            out_specs=VMEM,
            compiler_params=LIMIT,
        )(state, jac, iface_jac, table, marks)

    def join(z, step, fix, arrived, section):
        return pl.pallas_call(
            functools.partial(join_kernel, step, kinds if fix else 0, section),
            out_shape=[whole] + [one] * (n - 1),
            in_specs=[VMEM] * (n + 3),
            out_specs=[VMEM] * n,
            compiler_params=LIMIT,
        )(z, iface_jac, table, marks, *[arrived[d - 1] for d in exchange_order(n, step == 0)])

    def close(z, step, arrived, section, before, out, send):
        firsts = out is None
        arrays = [z, iface_jac, table, marks, *[arrived[d - 1] for d in exchange_order(n, False)], *before]
        specs = [VMEM] * len(arrays)
        scratch = [DMA((steps, blocks))]
        aliases = {}
        if firsts:
            arrays += [opening, *handed, jac, *pinned[2:6]]
            specs += [VMEM] * (n + 1) + [HBM] * 4
            scratch = [
                pltpu.VMEM((2, *whole.shape), jnp.bfloat16),
                pltpu.VMEM(whole.shape, jnp.float32),
                *[pltpu.SMEM(x.shape, x.dtype) for x in pinned[2:6]],
                DMA((4,)),
            ] + scratch
        else:
            aliases = {len(arrays): 0}
            arrays.append(out)
            specs.append(ANY)
        shapes, out_specs = [written], [ANY]
        if send:
            shapes += [whole] + [one] * (n - 1)
            out_specs += [VMEM] * n
        else:
            scratch.insert(0, pltpu.VMEM(whole.shape, jnp.bfloat16))
        return pl.pallas_call(
            functools.partial(close_kernel, step, section, firsts, send, len(before)),
            out_shape=shapes,
            in_specs=specs,
            out_specs=out_specs,
            input_output_aliases=aliases,
            scratch_shapes=scratch,
            compiler_params=LIMIT,
        )(*arrays)

    def swap(block, first, second, d):
        other = {first: second, second: first}
        pairs = []
        for a in range(tm):
            for q in range(n):
                for c in range(col_parts):
                    to = (other[a] * n + (q ^ d)) * col_parts + c if a in other else (a * n + q) * col_parts + (c ^ 1)
                    pairs.append(((a * n + q) * col_parts + c, to))
        return lax.ppermute(block, ("tm", "net", "cols"), pairs)

    def exchange(outgoing, first, second):
        return [swap(outgoing[d - 1], first, second, d) for d in range(1, n)]

    opening = state
    out = None
    for r in range(1, tm):
        arrived = exchange(outgoing, r - 1, r)
        state = swap(state, r - 1, r, 0)
        if r == 1:
            handed = arrived
        before = []
        for s in range(steps):
            fix = r == 1 and s == 0
            if s > 0:
                arrived = exchange(outgoing, r, r)
            z = own(state, s)
            if s < steps - 1:
                state, *outgoing = join(z, s, fix, arrived, r)
                before.append(state)
            else:
                out, *rest = close(z, s, arrived, r, before, out, r < tm - 1)
                state, *outgoing = rest or [None]
    return out


def solution(mesh):
    return jax.shard_map(
        local,
        mesh=mesh,
        in_specs=(
            P("tm", "net", None, None, None),
            P("net", None),
            P("tm", "net", None, None, None),
            P("net", None),
            P("net", None),
            P("net", None),
            P("cols"),
            P("tm", "cols"),
        ),
        out_specs=P("tm", "cols", "net"),
        check_vma=False,
    )
```

```python
import functools

import jax
import jax.numpy as jnp
from jax import lax
from jax.experimental import pallas as pl
from jax.experimental.pallas import tpu as pltpu
from jax.sharding import PartitionSpec as P

VMEM = pl.BlockSpec(memory_space=pltpu.VMEM)
SMEM = pl.BlockSpec(memory_space=pltpu.SMEM)
HBM = pl.BlockSpec(memory_space=pltpu.HBM)
ANY = pl.BlockSpec(memory_space=pl.ANY)
LIMIT = pltpu.CompilerParams(vmem_limit_bytes=16 * 1024 * 1024)
DMA = pltpu.SemaphoreType.DMA

STATE, LANE, BLOCK, AWAY, GAIN = 0, 1, 2, 3, 4
ROWS = 16


def times_transposed(rows, block):
    return lax.dot_general(rows, block, (((1,), (1,)), ((), ())), preferred_element_type=jnp.float32)


def hits(table, i, blocks, width):
    first_state = (lax.axis_index("net") * blocks + i) * width
    lane = lax.broadcasted_iota(jnp.int32, (table.shape[0], width), 1)
    return table[:, STATE : STATE + 1] == (lane + first_state).astype(jnp.float32)


def injected(table, step, hit):
    return jnp.where(hit, table[:, GAIN + step : GAIN + step + 1], 0.0)


def near_by(state_ref, cols_ref):
    return lambda i, k: state_ref[cols_ref[k, i]]


def products(i, state_ref, jac_ref, near):
    kinds = jac_ref.shape[1]
    rows = [state_ref[i]] + [near(i, k) for k in range(kinds - 1)]
    row_blocks = [jac_ref[i, k] for k in range(kinds)]
    return times_transposed(jnp.concatenate(rows, axis=1), jnp.concatenate(row_blocks, axis=1))


def own_sum(i, state_ref, jac_ref, near, table, step):
    blocks, _, width = state_ref.shape
    return products(i, state_ref, jac_ref, near) + injected(table, step, hits(table, i, blocks, width))


def picked(blocks, marks):
    total = blocks[0] * marks[0]
    for block, mark in zip(blocks[1:], marks[1:]):
        total += block * mark
    return total


def marks_layout(n, blocks, kinds):
    sent = n * blocks
    near = sent + n * blocks
    row = near + blocks * (kinds - 1) * blocks
    return sent, near, row, row + 1 + -(row + 1) % 8


def make_marks(marks_ref, blocks, kinds, cols_ref, send_ref, recv_ref, live_ref):
    n = lax.axis_size("net")
    me = lax.axis_index("net")
    width = marks_ref.shape[1]
    lane = lax.broadcasted_iota(jnp.int32, (1, width), 1)
    sent, near, own_row, _ = marks_layout(n, blocks, kinds)

    def put(row, mask):
        marks_ref[pl.ds(row, 1)] = jnp.where(mask, 1.0, 0.0)

    for d in range(n):
        q = me ^ d
        for i in range(blocks):
            put(d * blocks + i, lane < jnp.where(recv_ref[0, q] == i, live_ref[0, q], 0))
            put(sent + d * blocks + i, lane < jnp.where(send_ref[0, q] == i, width, 0))
    for i in range(blocks):
        for k in range(kinds - 1):
            for j in range(blocks):
                put(near + (i * (kinds - 1) + k) * blocks + j, lane < jnp.where(cols_ref[k, i] == j, width, 0))
    marks_ref[pl.ds(own_row, 1)] = table_row(send_ref, me, width)


def add_coupled(incoming, block, live, recv, z_ref):
    mask = lax.broadcasted_iota(jnp.int32, z_ref.shape[1:], 1) < live
    z_ref[recv] += jnp.where(mask, times_transposed(incoming, block), 0.0)


def table_row(send_ref, partition, width):
    lane = lax.broadcasted_iota(jnp.int32, (1, width), 1)
    row = jnp.zeros((1, width), jnp.float32)
    for e in range(lax.axis_size("net")):
        row = jnp.where(lane == e, send_ref[0, partition ^ e].astype(jnp.float32), row)
    return row


def kept(table, rows):
    away, block = table[:, AWAY : AWAY + 1], table[:, BLOCK : BLOCK + 1]
    sent = jnp.broadcast_to(rows[0], (table.shape[0], rows[0].shape[1]))
    for d in range(1, len(rows)):
        sent = jnp.where(away == float(d), rows[d], sent)
    lane = lax.broadcasted_iota(jnp.int32, sent.shape, 1).astype(jnp.float32)
    return jnp.where(jnp.logical_or(away == lane, block == sent), 1.0, 0.0)


def second_kernel(*refs):
    jac_hbm, iface_hbm, *small, table_ref, marks_ref, state_ref = refs[:11]
    n = lax.axis_size("net")
    me = lax.axis_index("net")
    outgoing, refs = refs[11 : 10 + n], refs[10 + n :]
    jac_ref, iface_ref, *loaded, first_ref, sems = refs
    cols_ref, send_ref, recv_ref, live_ref, node_ref, gain_ref = loaded
    blocks, cols, width = state_ref.shape
    sources = [jac_hbm.at[1], iface_hbm.at[1, 0], *small]
    loads = [
        pltpu.make_async_copy(source, target, sems.at[i])
        for i, (source, target) in enumerate(zip(sources, [jac_ref, iface_ref, *loaded]))
    ]
    here = lax.axis_index("tm") == 0
    for load in loads[6:]:
        load.start()

    @pl.when(here)
    def _():
        for load in loads[:2]:
            load.start()

    for load in loads[2:6]:
        load.start()
    for load in loads[6:]:
        load.wait()
    node = node_ref[...]
    block_of = node // width
    rows = [
        node,
        node - block_of * width,
        block_of % blocks,
        (block_of // blocks) ^ me,
    ]
    steps = gain_ref.shape[0]
    fill = -(GAIN + steps) % 8
    rows = [row.astype(jnp.float32) for row in rows] + [gain_ref[...], jnp.zeros((fill, cols), jnp.float32)]
    table_ref[...] = jnp.concatenate(rows, axis=0).T

    @pl.when(here)
    def _():
        table = table_ref[...]

        def spread(column):
            return jnp.broadcast_to(column, (cols, width))

        lane = lax.broadcasted_iota(jnp.int32, (cols, width), 1).astype(jnp.float32)
        place = spread(table[:, STATE : STATE + 1] - (me * blocks * width).astype(jnp.float32)) - lane
        gain = spread(table[:, GAIN : GAIN + 1])
        later_gain = spread(table[:, GAIN + 1 : GAIN + 2])
        hit = [place == float(i * width) for i in range(blocks)]
        for i in range(blocks):
            first_ref[i] = jnp.where(hit[i], gain, 0.0).astype(first_ref.dtype)
        away, block = table[:, AWAY : AWAY + 1], table[:, BLOCK : BLOCK + 1]
        for load in loads[2:6]:
            load.wait()
        mine = jnp.logical_or(away != 0.0, block == send_ref[0, me].astype(jnp.float32))
        shot_lane = spread(jnp.where(mine, table[:, LANE : LANE + 1], -1.0))
        shot = jnp.where(lane == shot_lane, gain, 0.0)
        live = recv = jnp.zeros_like(away)
        for d in range(n):
            live = jnp.where(away == float(d), live_ref[0, me ^ d].astype(jnp.float32), live)
            recv = jnp.where(away == float(d), recv_ref[0, me ^ d].astype(jnp.float32), recv)
        away, live, recv = spread(away), spread(live), spread(recv)
        sent = [jnp.where(away == float(d), shot, 0.0).astype(first_ref.dtype) for d in range(n)]
        loads[1].wait()
        ifaces = jnp.concatenate([iface_ref[me ^ d] for d in range(n)], axis=1)
        coupled = times_transposed(jnp.concatenate(sent, axis=1), ifaces)
        coupled = jnp.where(lane < live, coupled, 0.0)
        loads[0].wait()
        for i in range(blocks):
            own = products(i, first_ref, jac_ref, near_by(first_ref, cols_ref))
            own += jnp.where(hit[i], later_gain, 0.0)
            state_ref[i] = (own + jnp.where(recv == float(i), coupled, 0.0)).astype(state_ref.dtype)
        for d in range(1, n):
            outgoing[d - 1][pl.ds(0, cols)] = state_ref[send_ref[0, me ^ d]]

    @pl.when(jnp.logical_not(here))
    def _():
        for load in loads[2:6]:
            load.wait()
        make_marks(marks_ref, blocks, jac_ref.shape[1], cols_ref, send_ref, recv_ref, live_ref)

    for d in range(1, n):
        row = table_row(send_ref, me ^ d, width).astype(state_ref.dtype)
        outgoing[d - 1][pl.ds(cols, ROWS)] = jnp.broadcast_to(row, (ROWS, width))


def write_start(states, first, out_ref, sems):
    copies = []
    for s, state_ref in enumerate(states, first):
        width = state_ref.shape[2]
        for i in range(state_ref.shape[0]):
            copies.append(
                pltpu.make_async_copy(state_ref.at[i], out_ref.at[s, :, pl.ds(i * width, width)], sems.at[s, i])
            )
    for copy in copies:
        copy.start()
    return copies


def own_kernel(step, state_ref, jac_ref, iface_ref, table_ref, marks_ref, z_ref):
    table = table_ref[...]
    n = lax.axis_size("net")
    blocks = state_ref.shape[0]
    kinds = jac_ref.shape[2]
    sent, near, _, _ = marks_layout(n, blocks, kinds)
    state = [state_ref[j] for j in range(blocks)]

    def pick(row):
        return picked(state, [marks_ref[pl.ds(row + j, 1)].astype(state_ref.dtype) for j in range(blocks)])

    def near_block(i, k):
        return pick(near + (i * (kinds - 1) + k) * blocks)

    @pl.when(lax.axis_index("tm") > 0)
    def _():
        term = times_transposed(pick(sent), iface_ref[step, 0, lax.axis_index("net")])
        for i in range(blocks):
            own = own_sum(i, state_ref, jac_ref.at[step], near_block, table, step)
            z_ref[i] = own + term * marks_ref[pl.ds(i, 1)]


def first_states(opening, handed, jac_ref, iface_ref, ints, table_ref, made_ref, z_ref):
    cols_ref, send_ref, recv_ref, live_ref = ints
    n = lax.axis_size("net")
    blocks, cols, width = z_ref.shape
    table = table_ref[...]
    made_ref[0] = jnp.zeros_like(made_ref[0])
    for i in range(blocks):
        z_ref[i] = own_sum(i, made_ref.at[0], jac_ref.at[0], near_by(made_ref.at[0], cols_ref), table, 0)
    for q in range(n):
        add_coupled(made_ref[0, 0], iface_ref[0, 0, q], live_ref[0, q], recv_ref[0, q], z_ref)
    made_ref[0] = z_ref[...].astype(made_ref.dtype)
    rows = [table_row(send_ref, lax.axis_index("net"), width)]
    rows += [block[cols : cols + 1].astype(jnp.float32) for block in handed]
    keep = kept(table, rows)[:, 0:1]
    for i in range(blocks):
        made_ref[1, i] = jnp.where(keep > 0.0, opening[i], jnp.zeros_like(opening[i]))
    return [made_ref.at[0], made_ref.at[1]]


def joined(sums, step, iface_ref, marks_ref, arrived, keep=None):
    me = lax.axis_index("net")
    blocks, cols = len(sums), sums[0].shape[0]
    if keep is not None:
        sums = [total * keep[:, 0:1] for total in sums]
    for d, block in enumerate(arrived, 1):
        term = times_transposed(block[pl.ds(0, cols)], iface_ref[step, 0, me ^ d])
        if keep is not None:
            term *= keep[:, d : d + 1]
        sums = [total + term * marks_ref[pl.ds(d * blocks + i, 1)] for i, total in enumerate(sums)]
    return [total.astype(jnp.bfloat16) for total in sums]


def give(made, marks_ref, state_ref, outgoing):
    blocks = len(made)
    n = lax.axis_size("net")
    sent = marks_layout(n, blocks, 1)[0]
    for i in range(blocks):
        state_ref[i] = made[i]
    for d in range(1, n) if outgoing else ():
        marks = [marks_ref[pl.ds(sent + d * blocks + j, 1)].astype(made[j].dtype) for j in range(blocks)]
        outgoing[d - 1][...] = picked(made, marks)


def exchange_order(n, handed):
    near = [n // 2, *[d for d in range(1, n) if d != n // 2]]
    return near if handed else list(range(n - 1, 0, -1))


def by_distance(refs, handed):
    order = exchange_order(len(refs) + 1, handed)
    return [refs[order.index(d)] for d in range(1, len(refs) + 1)]


def join_kernel(step, fix, section, z_ref, iface_ref, table_ref, marks_ref, *refs):
    n = lax.axis_size("net")
    arrived, state_ref, outgoing = by_distance(refs[: n - 1], step == 0), refs[n - 1], refs[n:]
    blocks, cols, _ = z_ref.shape

    @pl.when(lax.axis_index("tm") == section)
    def _():
        keep = None
        if fix:
            rows = [marks_ref[pl.ds(marks_layout(n, blocks, fix)[2], 1)]]
            rows += [block[cols : cols + 1].astype(jnp.float32) for block in arrived]
            keep = kept(table_ref[...], rows)
        made = joined([z_ref[i] for i in range(blocks)], step, iface_ref, marks_ref, arrived, keep)
        give(made, marks_ref, state_ref, outgoing)


def close_kernel(step, section, firsts, send, before, *refs):
    n = lax.axis_size("net")
    *refs, sems = refs
    if firsts:
        *refs, made_ref, acc_ref, cols_ref, send_ref, recv_ref, live_ref, load_sems = refs
        ints = [cols_ref, send_ref, recv_ref, live_ref]
    z_ref, iface_ref, table_ref, marks_ref, *refs = refs
    arrived, refs = by_distance(refs[: n - 1], False), refs[n - 1 :]
    before, refs = refs[:before], refs[before:]
    if firsts:
        opening_ref, handed, jac_ref, sources, refs = refs[0], refs[1:n], refs[n], refs[n + 1 : n + 5], refs[n + 5 :]
    else:
        refs = refs[1:]
    out_ref, state_ref, *outgoing = refs

    @pl.when(lax.axis_index("tm") == section)
    def _():
        copies = write_start(before, 0, out_ref, sems)
        sums = [z_ref[i] for i in range(z_ref.shape[0])]
        made = joined(sums, step, iface_ref, marks_ref, arrived)
        give(made, marks_ref, state_ref, outgoing)
        copies += write_start([state_ref], len(before), out_ref, sems)
        for copy in copies:
            copy.wait()

    if firsts:

        @pl.when(lax.axis_index("tm") == 0)
        def _():
            loads = [
                pltpu.make_async_copy(source, target, load_sems.at[i])
                for i, (source, target) in enumerate(zip(sources, ints))
            ]
            for load in loads:
                load.start()
            for load in loads:
                load.wait()
            made = first_states(opening_ref, handed, jac_ref, iface_ref, ints, table_ref, made_ref, acc_ref)
            for copy in write_start(made, 0, out_ref, sems):
                copy.wait()


def local(jac, block_cols, iface_jac, iface_send, iface_recv, iface_live, ctrl_node, ctrl_gain):
    steps, blocks, kinds, width, _ = jac.shape
    cols = ctrl_node.shape[0]
    tm = lax.axis_size("tm")
    n = lax.axis_size("net")
    col_parts = lax.axis_size("cols")
    node = ctrl_node[None]
    near = block_cols.T
    bf16 = functools.partial(jax.ShapeDtypeStruct, dtype=jnp.bfloat16)
    f32 = functools.partial(jax.ShapeDtypeStruct, dtype=jnp.float32)
    whole, one = bf16((blocks, cols, width)), bf16((cols, width))
    table_rows = GAIN + steps + -(GAIN + steps) % 8
    written = bf16((steps, cols, blocks * width))

    pinned = [
        pltpu.with_memory_space_constraint(x, pltpu.HBM)
        for x in (jac, iface_jac, near, iface_send, iface_recv, iface_live, node, ctrl_gain)
    ]
    marks_rows = marks_layout(n, blocks, kinds)[-1]
    table, marks, state, *outgoing = pl.pallas_call(
        second_kernel,
        out_shape=[f32((cols, table_rows)), f32((marks_rows, width)), whole]
        + [bf16((cols + ROWS, width))] * (n - 1),
        in_specs=[HBM] * len(pinned),
        out_specs=[VMEM] * (n + 2),
        scratch_shapes=[
            pltpu.VMEM((blocks, kinds, width, width), jnp.bfloat16),
            pltpu.VMEM((n, width, width), jnp.bfloat16),
            *[pltpu.SMEM(x.shape, x.dtype) for x in (near, iface_send, iface_recv, iface_live)],
            *[pltpu.VMEM(x.shape, x.dtype) for x in (node, ctrl_gain)],
            pltpu.VMEM(whole.shape, jnp.bfloat16),
            DMA((len(pinned),)),
        ],
        compiler_params=LIMIT,
    )(*pinned)

    def own(state, step):
        return pl.pallas_call(
            functools.partial(own_kernel, step),
            out_shape=f32(whole.shape),
            in_specs=[VMEM] * 5,
            out_specs=VMEM,
            compiler_params=LIMIT,
        )(state, jac, iface_jac, table, marks)

    def join(z, step, fix, arrived, section):
        return pl.pallas_call(
            functools.partial(join_kernel, step, kinds if fix else 0, section),
            out_shape=[whole] + [one] * (n - 1),
            in_specs=[VMEM] * (n + 3),
            out_specs=[VMEM] * n,
            compiler_params=LIMIT,
        )(z, iface_jac, table, marks, *[arrived[d - 1] for d in exchange_order(n, step == 0)])

    def close(z, step, arrived, section, before, out, send):
        firsts = out is None
        arrays = [z, iface_jac, table, marks, *[arrived[d - 1] for d in exchange_order(n, False)], *before]
        specs = [VMEM] * len(arrays)
        scratch = [DMA((steps, blocks))]
        aliases = {}
        if firsts:
            arrays += [opening, *handed, jac, *pinned[2:6]]
            specs += [VMEM] * (n + 1) + [HBM] * 4
            scratch = [
                pltpu.VMEM((2, *whole.shape), jnp.bfloat16),
                pltpu.VMEM(whole.shape, jnp.float32),
                *[pltpu.SMEM(x.shape, x.dtype) for x in pinned[2:6]],
                DMA((4,)),
            ] + scratch
        else:
            aliases = {len(arrays): 0}
            arrays.append(out)
            specs.append(ANY)
        shapes, out_specs = [written], [ANY]
        if send:
            shapes += [whole] + [one] * (n - 1)
            out_specs += [VMEM] * n
        else:
            scratch.insert(0, pltpu.VMEM(whole.shape, jnp.bfloat16))
        return pl.pallas_call(
            functools.partial(close_kernel, step, section, firsts, send, len(before)),
            out_shape=shapes,
            in_specs=specs,
            out_specs=out_specs,
            input_output_aliases=aliases,
            scratch_shapes=scratch,
            compiler_params=LIMIT,
        )(*arrays)

    def swap(block, first, second, d):
        other = {first: second, second: first}
        pairs = []
        for a in range(tm):
            for q in range(n):
                for c in range(col_parts):
                    to = (other[a] * n + (q ^ d)) * col_parts + c if a in other else (a * n + q) * col_parts + (c ^ 1)
                    pairs.append(((a * n + q) * col_parts + c, to))
        return lax.ppermute(block, ("tm", "net", "cols"), pairs)

    def exchange(outgoing, first, second):
        return [swap(outgoing[d - 1], first, second, d) for d in range(1, n)]

    opening = state
    out = None
    for r in range(1, tm):
        arrived = exchange(outgoing, r - 1, r)
        state = swap(state, r - 1, r, 0)
        if r == 1:
            handed = arrived
        before = []
        for s in range(steps):
            fix = r == 1 and s == 0
            if s > 0:
                arrived = exchange(outgoing, r, r)
            z = own(state, s)
            if s < steps - 1:
                state, *outgoing = join(z, s, fix, arrived, r)
                before.append(state)
            else:
                out, *rest = close(z, s, arrived, r, before, out, r < tm - 1)
                state, *outgoing = rest or [None]
    return out


def solution(mesh):
    return jax.shard_map(
        local,
        mesh=mesh,
        in_specs=(
            P("tm", "net", None, None, None),
            P("net", None),
            P("tm", "net", None, None, None),
            P("net", None),
            P("net", None),
            P("net", None),
            P("cols"),
            P("tm", "cols"),
        ),
        out_specs=P("tm", "cols", "net"),
        check_vma=False,
    )
```

```python
import functools

import jax
import jax.numpy as jnp
from jax import lax
from jax.experimental import pallas as pl
from jax.experimental.pallas import tpu as pltpu
from jax.sharding import PartitionSpec as P

VMEM = pl.BlockSpec(memory_space=pltpu.VMEM)
SMEM = pl.BlockSpec(memory_space=pltpu.SMEM)
HBM = pl.BlockSpec(memory_space=pltpu.HBM)
ANY = pl.BlockSpec(memory_space=pl.ANY)
LIMIT = pltpu.CompilerParams(vmem_limit_bytes=16 * 1024 * 1024)
DMA = pltpu.SemaphoreType.DMA

STATE, LANE, BLOCK, AWAY, GAIN = 0, 1, 2, 3, 4
ROWS = 16


def times_transposed(rows, block):
    return lax.dot_general(rows, block, (((1,), (1,)), ((), ())), preferred_element_type=jnp.float32)


def hits(table, i, blocks, width):
    first_state = (lax.axis_index("net") * blocks + i) * width
    lane = lax.broadcasted_iota(jnp.int32, (table.shape[0], width), 1)
    return table[:, STATE : STATE + 1] == (lane + first_state).astype(jnp.float32)


def injected(table, step, hit):
    return jnp.where(hit, table[:, GAIN + step : GAIN + step + 1], 0.0)


def near_by(state_ref, cols_ref):
    return lambda i, k: state_ref[cols_ref[k, i]]


def products(i, state_ref, jac_ref, near):
    kinds = jac_ref.shape[1]
    rows = [state_ref[i]] + [near(i, k) for k in range(kinds - 1)]
    row_blocks = [jac_ref[i, k] for k in range(kinds)]
    return times_transposed(jnp.concatenate(rows, axis=1), jnp.concatenate(row_blocks, axis=1))


def own_sum(i, state_ref, jac_ref, near, table, step):
    blocks, _, width = state_ref.shape
    return products(i, state_ref, jac_ref, near) + injected(table, step, hits(table, i, blocks, width))


def picked(blocks, marks):
    total = blocks[0] * marks[0]
    for block, mark in zip(blocks[1:], marks[1:]):
        total += block * mark
    return total


def marks_layout(n, blocks, kinds):
    sent = n * blocks
    near = sent + n * blocks
    row = near + blocks * (kinds - 1) * blocks
    return sent, near, row, row + 1 + -(row + 1) % 8


def make_marks(marks_ref, blocks, kinds, cols_ref, send_ref, recv_ref, live_ref):
    n = lax.axis_size("net")
    me = lax.axis_index("net")
    width = marks_ref.shape[1]
    lane = lax.broadcasted_iota(jnp.int32, (1, width), 1)
    sent, near, own_row, _ = marks_layout(n, blocks, kinds)

    def put(row, mask):
        marks_ref[pl.ds(row, 1)] = jnp.where(mask, 1.0, 0.0)

    for d in range(n):
        q = me ^ d
        for i in range(blocks):
            put(d * blocks + i, lane < jnp.where(recv_ref[0, q] == i, live_ref[0, q], 0))
            put(sent + d * blocks + i, lane < jnp.where(send_ref[0, q] == i, width, 0))
    for i in range(blocks):
        for k in range(kinds - 1):
            for j in range(blocks):
                put(near + (i * (kinds - 1) + k) * blocks + j, lane < jnp.where(cols_ref[k, i] == j, width, 0))
    marks_ref[pl.ds(own_row, 1)] = table_row(send_ref, me, width)


def add_coupled(incoming, block, live, recv, z_ref):
    mask = lax.broadcasted_iota(jnp.int32, z_ref.shape[1:], 1) < live
    z_ref[recv] += jnp.where(mask, times_transposed(incoming, block), 0.0)


def table_row(send_ref, partition, width):
    lane = lax.broadcasted_iota(jnp.int32, (1, width), 1)
    row = jnp.zeros((1, width), jnp.float32)
    for e in range(lax.axis_size("net")):
        row = jnp.where(lane == e, send_ref[0, partition ^ e].astype(jnp.float32), row)
    return row


def kept(table, rows):
    away, block = table[:, AWAY : AWAY + 1], table[:, BLOCK : BLOCK + 1]
    sent = jnp.broadcast_to(rows[0], (table.shape[0], rows[0].shape[1]))
    for d in range(1, len(rows)):
        sent = jnp.where(away == float(d), rows[d], sent)
    lane = lax.broadcasted_iota(jnp.int32, sent.shape, 1).astype(jnp.float32)
    return jnp.where(jnp.logical_or(away == lane, block == sent), 1.0, 0.0)


def second_kernel(*refs):
    jac_hbm, iface_hbm, *small, table_ref, marks_ref, state_ref = refs[:11]
    n = lax.axis_size("net")
    me = lax.axis_index("net")
    outgoing, refs = refs[11 : 10 + n], refs[10 + n :]
    jac_ref, iface_ref, *loaded, first_ref, sems = refs
    cols_ref, send_ref, recv_ref, live_ref, node_ref, gain_ref = loaded
    blocks, cols, width = state_ref.shape
    sources = [jac_hbm.at[1], iface_hbm.at[1, 0], *small]
    loads = [
        pltpu.make_async_copy(source, target, sems.at[i])
        for i, (source, target) in enumerate(zip(sources, [jac_ref, iface_ref, *loaded]))
    ]
    here = lax.axis_index("tm") == 0
    for load in loads[6:]:
        load.start()

    @pl.when(here)
    def _():
        for load in loads[:2]:
            load.start()

    for load in loads[2:6]:
        load.start()
    for load in loads[6:]:
        load.wait()
    node = node_ref[...]
    block_of = node // width
    rows = [
        node,
        node - block_of * width,
        block_of % blocks,
        (block_of // blocks) ^ me,
    ]
    steps = gain_ref.shape[0]
    fill = -(GAIN + steps) % 8
    rows = [row.astype(jnp.float32) for row in rows] + [gain_ref[...], jnp.zeros((fill, cols), jnp.float32)]
    table_ref[...] = jnp.concatenate(rows, axis=0).T

    @pl.when(here)
    def _():
        table = table_ref[...]

        def spread(column):
            return jnp.broadcast_to(column, (cols, width))

        lane = lax.broadcasted_iota(jnp.int32, (cols, width), 1).astype(jnp.float32)
        place = spread(table[:, STATE : STATE + 1] - (me * blocks * width).astype(jnp.float32)) - lane
        gain = spread(table[:, GAIN : GAIN + 1])
        later_gain = spread(table[:, GAIN + 1 : GAIN + 2])
        hit = [place == float(i * width) for i in range(blocks)]
        for i in range(blocks):
            first_ref[i] = jnp.where(hit[i], gain, 0.0).astype(first_ref.dtype)
        away, block = table[:, AWAY : AWAY + 1], table[:, BLOCK : BLOCK + 1]
        for load in loads[2:6]:
            load.wait()
        mine = jnp.logical_or(away != 0.0, block == send_ref[0, me].astype(jnp.float32))
        shot_lane = spread(jnp.where(mine, table[:, LANE : LANE + 1], -1.0))
        shot = jnp.where(lane == shot_lane, gain, 0.0)
        live = recv = jnp.zeros_like(away)
        for d in range(n):
            live = jnp.where(away == float(d), live_ref[0, me ^ d].astype(jnp.float32), live)
            recv = jnp.where(away == float(d), recv_ref[0, me ^ d].astype(jnp.float32), recv)
        away, live, recv = spread(away), spread(live), spread(recv)
        sent = [jnp.where(away == float(d), shot, 0.0).astype(first_ref.dtype) for d in range(n)]
        loads[1].wait()
        ifaces = jnp.concatenate([iface_ref[me ^ d] for d in range(n)], axis=1)
        coupled = times_transposed(jnp.concatenate(sent, axis=1), ifaces)
        coupled = jnp.where(lane < live, coupled, 0.0)
        loads[0].wait()
        for i in range(blocks):
            own = products(i, first_ref, jac_ref, near_by(first_ref, cols_ref))
            own += jnp.where(hit[i], later_gain, 0.0)
            state_ref[i] = (own + jnp.where(recv == float(i), coupled, 0.0)).astype(state_ref.dtype)
        for d in range(1, n):
            outgoing[d - 1][pl.ds(0, cols)] = state_ref[send_ref[0, me ^ d]]

    @pl.when(jnp.logical_not(here))
    def _():
        for load in loads[2:6]:
            load.wait()
        make_marks(marks_ref, blocks, jac_ref.shape[1], cols_ref, send_ref, recv_ref, live_ref)

    for d in range(1, n):
        row = table_row(send_ref, me ^ d, width).astype(state_ref.dtype)
        outgoing[d - 1][pl.ds(cols, ROWS)] = jnp.broadcast_to(row, (ROWS, width))


def write_start(states, first, out_ref, sems):
    copies = []
    for s, state_ref in enumerate(states, first):
        width = state_ref.shape[2]
        for i in range(state_ref.shape[0]):
            copies.append(
                pltpu.make_async_copy(state_ref.at[i], out_ref.at[s, :, pl.ds(i * width, width)], sems.at[s, i])
            )
    for copy in copies:
        copy.start()
    return copies


def own_kernel(step, state_ref, jac_ref, iface_ref, table_ref, marks_ref, z_ref):
    table = table_ref[...]
    n = lax.axis_size("net")
    blocks = state_ref.shape[0]
    kinds = jac_ref.shape[2]
    sent, near, _, _ = marks_layout(n, blocks, kinds)
    state = [state_ref[j] for j in range(blocks)]

    def pick(row):
        return picked(state, [marks_ref[pl.ds(row + j, 1)].astype(state_ref.dtype) for j in range(blocks)])

    def near_block(i, k):
        return pick(near + (i * (kinds - 1) + k) * blocks)

    @pl.when(lax.axis_index("tm") > 0)
    def _():
        term = times_transposed(pick(sent), iface_ref[step, 0, lax.axis_index("net")])
        for i in range(blocks):
            own = own_sum(i, state_ref, jac_ref.at[step], near_block, table, step)
            z_ref[i] = own + term * marks_ref[pl.ds(i, 1)]


def first_states(opening, handed, jac_ref, iface_ref, ints, table_ref, made_ref, z_ref):
    cols_ref, send_ref, recv_ref, live_ref = ints
    n = lax.axis_size("net")
    blocks, cols, width = z_ref.shape
    table = table_ref[...]
    made_ref[0] = jnp.zeros_like(made_ref[0])
    for i in range(blocks):
        z_ref[i] = own_sum(i, made_ref.at[0], jac_ref.at[0], near_by(made_ref.at[0], cols_ref), table, 0)
    for q in range(n):
        add_coupled(made_ref[0, 0], iface_ref[0, 0, q], live_ref[0, q], recv_ref[0, q], z_ref)
    made_ref[0] = z_ref[...].astype(made_ref.dtype)
    rows = [table_row(send_ref, lax.axis_index("net"), width)]
    rows += [block[cols : cols + 1].astype(jnp.float32) for block in handed]
    keep = kept(table, rows)[:, 0:1]
    for i in range(blocks):
        made_ref[1, i] = jnp.where(keep > 0.0, opening[i], jnp.zeros_like(opening[i]))
    return [made_ref.at[0], made_ref.at[1]]


def joined(sums, step, iface_ref, marks_ref, arrived, keep=None):
    me = lax.axis_index("net")
    blocks, cols = len(sums), sums[0].shape[0]
    if keep is not None:
        sums = [total * keep[:, 0:1] for total in sums]
    for d, block in enumerate(arrived, 1):
        term = times_transposed(block[pl.ds(0, cols)], iface_ref[step, 0, me ^ d])
        if keep is not None:
            term *= keep[:, d : d + 1]
        sums = [total + term * marks_ref[pl.ds(d * blocks + i, 1)] for i, total in enumerate(sums)]
    return [total.astype(jnp.bfloat16) for total in sums]


def give(made, marks_ref, state_ref, outgoing):
    blocks = len(made)
    n = lax.axis_size("net")
    sent = marks_layout(n, blocks, 1)[0]
    for i in range(blocks):
        state_ref[i] = made[i]
    for d in range(1, n) if outgoing else ():
        marks = [marks_ref[pl.ds(sent + d * blocks + j, 1)].astype(made[j].dtype) for j in range(blocks)]
        outgoing[d - 1][...] = picked(made, marks)


def exchange_order(n, handed):
    handing = [*range(n // 2, n), *range(n // 2 - 1, 0, -1)]
    return handing if handed else [n - 1, *range(1, n - 1)]


def by_distance(refs, handed):
    order = exchange_order(len(refs) + 1, handed)
    return [refs[order.index(d)] for d in range(1, len(refs) + 1)]


def join_kernel(step, fix, section, z_ref, iface_ref, table_ref, marks_ref, *refs):
    n = lax.axis_size("net")
    arrived, state_ref, outgoing = by_distance(refs[: n - 1], step == 0), refs[n - 1], refs[n:]
    blocks, cols, _ = z_ref.shape

    @pl.when(lax.axis_index("tm") == section)
    def _():
        keep = None
        if fix:
            rows = [marks_ref[pl.ds(marks_layout(n, blocks, fix)[2], 1)]]
            rows += [block[cols : cols + 1].astype(jnp.float32) for block in arrived]
            keep = kept(table_ref[...], rows)
        made = joined([z_ref[i] for i in range(blocks)], step, iface_ref, marks_ref, arrived, keep)
        give(made, marks_ref, state_ref, outgoing)


def close_kernel(step, section, firsts, send, before, *refs):
    n = lax.axis_size("net")
    *refs, sems = refs
    if firsts:
        *refs, made_ref, acc_ref, cols_ref, send_ref, recv_ref, live_ref, load_sems = refs
        ints = [cols_ref, send_ref, recv_ref, live_ref]
    z_ref, iface_ref, table_ref, marks_ref, *refs = refs
    arrived, refs = by_distance(refs[: n - 1], False), refs[n - 1 :]
    before, refs = refs[:before], refs[before:]
    if firsts:
        opening_ref, handed, jac_ref, sources, refs = refs[0], refs[1:n], refs[n], refs[n + 1 : n + 5], refs[n + 5 :]
    else:
        refs = refs[1:]
    out_ref, state_ref, *outgoing = refs

    @pl.when(lax.axis_index("tm") == section)
    def _():
        copies = write_start(before, 0, out_ref, sems)
        sums = [z_ref[i] for i in range(z_ref.shape[0])]
        made = joined(sums, step, iface_ref, marks_ref, arrived)
        give(made, marks_ref, state_ref, outgoing)
        copies += write_start([state_ref], len(before), out_ref, sems)
        for copy in copies:
            copy.wait()

    if firsts:

        @pl.when(lax.axis_index("tm") == 0)
        def _():
            loads = [
                pltpu.make_async_copy(source, target, load_sems.at[i])
                for i, (source, target) in enumerate(zip(sources, ints))
            ]
            for load in loads:
                load.start()
            for load in loads:
                load.wait()
            made = first_states(opening_ref, handed, jac_ref, iface_ref, ints, table_ref, made_ref, acc_ref)
            for copy in write_start(made, 0, out_ref, sems):
                copy.wait()


def local(jac, block_cols, iface_jac, iface_send, iface_recv, iface_live, ctrl_node, ctrl_gain):
    steps, blocks, kinds, width, _ = jac.shape
    cols = ctrl_node.shape[0]
    tm = lax.axis_size("tm")
    n = lax.axis_size("net")
    col_parts = lax.axis_size("cols")
    node = ctrl_node[None]
    near = block_cols.T
    bf16 = functools.partial(jax.ShapeDtypeStruct, dtype=jnp.bfloat16)
    f32 = functools.partial(jax.ShapeDtypeStruct, dtype=jnp.float32)
    whole, one = bf16((blocks, cols, width)), bf16((cols, width))
    table_rows = GAIN + steps + -(GAIN + steps) % 8
    written = bf16((steps, cols, blocks * width))

    pinned = [
        pltpu.with_memory_space_constraint(x, pltpu.HBM)
        for x in (jac, iface_jac, near, iface_send, iface_recv, iface_live, node, ctrl_gain)
    ]
    marks_rows = marks_layout(n, blocks, kinds)[-1]
    table, marks, state, *outgoing = pl.pallas_call(
        second_kernel,
        out_shape=[f32((cols, table_rows)), f32((marks_rows, width)), whole]
        + [bf16((cols + ROWS, width))] * (n - 1),
        in_specs=[HBM] * len(pinned),
        out_specs=[VMEM] * (n + 2),
        scratch_shapes=[
            pltpu.VMEM((blocks, kinds, width, width), jnp.bfloat16),
            pltpu.VMEM((n, width, width), jnp.bfloat16),
            *[pltpu.SMEM(x.shape, x.dtype) for x in (near, iface_send, iface_recv, iface_live)],
            *[pltpu.VMEM(x.shape, x.dtype) for x in (node, ctrl_gain)],
            pltpu.VMEM(whole.shape, jnp.bfloat16),
            DMA((len(pinned),)),
        ],
        compiler_params=LIMIT,
    )(*pinned)

    def own(state, step):
        return pl.pallas_call(
            functools.partial(own_kernel, step),
            out_shape=f32(whole.shape),
            in_specs=[VMEM] * 5,
            out_specs=VMEM,
            compiler_params=LIMIT,
        )(state, jac, iface_jac, table, marks)

    def join(z, step, fix, arrived, section):
        return pl.pallas_call(
            functools.partial(join_kernel, step, kinds if fix else 0, section),
            out_shape=[whole] + [one] * (n - 1),
            in_specs=[VMEM] * (n + 3),
            out_specs=[VMEM] * n,
            compiler_params=LIMIT,
        )(z, iface_jac, table, marks, *[arrived[d - 1] for d in exchange_order(n, step == 0)])

    def close(z, step, arrived, section, before, out, send):
        firsts = out is None
        arrays = [z, iface_jac, table, marks, *[arrived[d - 1] for d in exchange_order(n, False)], *before]
        specs = [VMEM] * len(arrays)
        scratch = [DMA((steps, blocks))]
        aliases = {}
        if firsts:
            arrays += [opening, *handed, jac, *pinned[2:6]]
            specs += [VMEM] * (n + 1) + [HBM] * 4
            scratch = [
                pltpu.VMEM((2, *whole.shape), jnp.bfloat16),
                pltpu.VMEM(whole.shape, jnp.float32),
                *[pltpu.SMEM(x.shape, x.dtype) for x in pinned[2:6]],
                DMA((4,)),
            ] + scratch
        else:
            aliases = {len(arrays): 0}
            arrays.append(out)
            specs.append(ANY)
        shapes, out_specs = [written], [ANY]
        if send:
            shapes += [whole] + [one] * (n - 1)
            out_specs += [VMEM] * n
        else:
            scratch.insert(0, pltpu.VMEM(whole.shape, jnp.bfloat16))
        return pl.pallas_call(
            functools.partial(close_kernel, step, section, firsts, send, len(before)),
            out_shape=shapes,
            in_specs=specs,
            out_specs=out_specs,
            input_output_aliases=aliases,
            scratch_shapes=scratch,
            compiler_params=LIMIT,
        )(*arrays)

    def swap(block, first, second, d):
        other = {first: second, second: first}
        pairs = []
        for a in range(tm):
            for q in range(n):
                for c in range(col_parts):
                    to = (other[a] * n + (q ^ d)) * col_parts + c if a in other else (a * n + q) * col_parts + (c ^ 1)
                    pairs.append(((a * n + q) * col_parts + c, to))
        return lax.ppermute(block, ("tm", "net", "cols"), pairs)

    def exchange(outgoing, first, second):
        return [swap(outgoing[d - 1], first, second, d) for d in range(1, n)]

    opening = state
    out = None
    for r in range(1, tm):
        arrived = exchange(outgoing, r - 1, r)
        state = swap(state, r - 1, r, 0)
        if r == 1:
            handed = arrived
        before = []
        for s in range(steps):
            fix = r == 1 and s == 0
            if s > 0:
                arrived = exchange(outgoing, r, r)
            z = own(state, s)
            if s < steps - 1:
                state, *outgoing = join(z, s, fix, arrived, r)
                before.append(state)
            else:
                out, *rest = close(z, s, arrived, r, before, out, r < tm - 1)
                state, *outgoing = rest or [None]
    return out


def solution(mesh):
    return jax.shard_map(
        local,
        mesh=mesh,
        in_specs=(
            P("tm", "net", None, None, None),
            P("net", None),
            P("tm", "net", None, None, None),
            P("net", None),
            P("net", None),
            P("net", None),
            P("cols"),
            P("tm", "cols"),
        ),
        out_specs=P("tm", "cols", "net"),
        check_vma=False,
    )
```

```python
import functools

import jax
import jax.numpy as jnp
from jax import lax
from jax.experimental import pallas as pl
from jax.experimental.pallas import tpu as pltpu
from jax.sharding import PartitionSpec as P

VMEM = pl.BlockSpec(memory_space=pltpu.VMEM)
SMEM = pl.BlockSpec(memory_space=pltpu.SMEM)
HBM = pl.BlockSpec(memory_space=pltpu.HBM)
ANY = pl.BlockSpec(memory_space=pl.ANY)
LIMIT = pltpu.CompilerParams(vmem_limit_bytes=16 * 1024 * 1024)
DMA = pltpu.SemaphoreType.DMA

STATE, LANE, BLOCK, AWAY, GAIN = 0, 1, 2, 3, 4
ROWS = 16


def times_transposed(rows, block):
    return lax.dot_general(rows, block, (((1,), (1,)), ((), ())), preferred_element_type=jnp.float32)


def hits(table, i, blocks, width):
    first_state = (lax.axis_index("net") * blocks + i) * width
    lane = lax.broadcasted_iota(jnp.int32, (table.shape[0], width), 1)
    return table[:, STATE : STATE + 1] == (lane + first_state).astype(jnp.float32)


def injected(table, step, hit):
    return jnp.where(hit, table[:, GAIN + step : GAIN + step + 1], 0.0)


def near_by(state_ref, cols_ref):
    return lambda i, k: state_ref[cols_ref[k, i]]


def own_sum(i, state_ref, jac_ref, near, table, step, hit=None):
    blocks, _, width = state_ref.shape
    if hit is None:
        hit = hits(table, i, blocks, width)
    kinds = jac_ref.shape[1]
    rows = [state_ref[i]] + [near(i, k) for k in range(kinds - 1)]
    row_blocks = [jac_ref[i, k] for k in range(kinds)]
    total = times_transposed(jnp.concatenate(rows, axis=1), jnp.concatenate(row_blocks, axis=1))
    return total + injected(table, step, hit)


def picked(blocks, marks):
    total = blocks[0] * marks[0]
    for block, mark in zip(blocks[1:], marks[1:]):
        total += block * mark
    return total


def marks_layout(n, blocks, kinds):
    sent = n * blocks
    near = sent + n * blocks
    row = near + blocks * (kinds - 1) * blocks
    return sent, near, row, row + 1 + -(row + 1) % 8


def make_marks(marks_ref, blocks, kinds, cols_ref, send_ref, recv_ref, live_ref):
    n = lax.axis_size("net")
    me = lax.axis_index("net")
    width = marks_ref.shape[1]
    lane = lax.broadcasted_iota(jnp.int32, (1, width), 1)
    sent, near, own_row, _ = marks_layout(n, blocks, kinds)

    def put(row, mask):
        marks_ref[pl.ds(row, 1)] = jnp.where(mask, 1.0, 0.0)

    for d in range(n):
        q = me ^ d
        for i in range(blocks):
            put(d * blocks + i, lane < jnp.where(recv_ref[0, q] == i, live_ref[0, q], 0))
            put(sent + d * blocks + i, lane < jnp.where(send_ref[0, q] == i, width, 0))
    for i in range(blocks):
        for k in range(kinds - 1):
            for j in range(blocks):
                put(near + (i * (kinds - 1) + k) * blocks + j, lane < jnp.where(cols_ref[k, i] == j, width, 0))
    marks_ref[pl.ds(own_row, 1)] = table_row(send_ref, me, width)


def add_coupled(incoming, block, live, recv, z_ref):
    mask = lax.broadcasted_iota(jnp.int32, z_ref.shape[1:], 1) < live
    z_ref[recv] += jnp.where(mask, times_transposed(incoming, block), 0.0)


def table_row(send_ref, partition, width):
    lane = lax.broadcasted_iota(jnp.int32, (1, width), 1)
    row = jnp.zeros((1, width), jnp.float32)
    for e in range(lax.axis_size("net")):
        row = jnp.where(lane == e, send_ref[0, partition ^ e].astype(jnp.float32), row)
    return row


def kept(table, rows):
    away, block = table[:, AWAY : AWAY + 1], table[:, BLOCK : BLOCK + 1]
    sent = jnp.broadcast_to(rows[0], (table.shape[0], rows[0].shape[1]))
    for d in range(1, len(rows)):
        sent = jnp.where(away == float(d), rows[d], sent)
    lane = lax.broadcasted_iota(jnp.int32, sent.shape, 1).astype(jnp.float32)
    return jnp.where(jnp.logical_or(away == lane, block == sent), 1.0, 0.0)


def second_kernel(*refs):
    jac_hbm, iface_hbm, *small, table_ref, marks_ref, state_ref = refs[:11]
    n = lax.axis_size("net")
    me = lax.axis_index("net")
    outgoing, refs = refs[11 : 10 + n], refs[10 + n :]
    jac_ref, iface_ref, *loaded, first_ref, sems = refs
    cols_ref, send_ref, recv_ref, live_ref, node_ref, gain_ref = loaded
    blocks, cols, width = state_ref.shape
    sources = [jac_hbm.at[1], iface_hbm.at[1, 0], *small]
    loads = [
        pltpu.make_async_copy(source, target, sems.at[i])
        for i, (source, target) in enumerate(zip(sources, [jac_ref, iface_ref, *loaded]))
    ]
    here = lax.axis_index("tm") == 0
    for load in loads[6:]:
        load.start()

    @pl.when(here)
    def _():
        for load in loads[:2]:
            load.start()

    for load in loads[2:6]:
        load.start()
    for load in loads[6:]:
        load.wait()
    node = node_ref[...]
    block_of = node // width
    rows = [
        node,
        node - block_of * width,
        block_of % blocks,
        (block_of // blocks) ^ me,
    ]
    steps = gain_ref.shape[0]
    fill = -(GAIN + steps) % 8
    rows = [row.astype(jnp.float32) for row in rows] + [gain_ref[...], jnp.zeros((fill, cols), jnp.float32)]
    table_ref[...] = jnp.concatenate(rows, axis=0).T

    @pl.when(here)
    def _():
        table = table_ref[...]
        hit = [hits(table, i, blocks, width) for i in range(blocks)]
        for i in range(blocks):
            first_ref[i] = injected(table, 0, hit[i]).astype(first_ref.dtype)
        lane = lax.broadcasted_iota(jnp.int32, (cols, width), 1).astype(jnp.float32)
        shot = jnp.where(lane == table[:, LANE : LANE + 1], table[:, GAIN : GAIN + 1], 0.0)
        away, block = table[:, AWAY : AWAY + 1], table[:, BLOCK : BLOCK + 1]
        for load in loads[2:6]:
            load.wait()
        mine = jnp.logical_or(away != 0.0, block == send_ref[0, me].astype(jnp.float32))
        shot = jnp.where(mine, shot, 0.0)
        live = recv = jnp.zeros_like(away)
        for d in range(n):
            live = jnp.where(away == float(d), live_ref[0, me ^ d].astype(jnp.float32), live)
            recv = jnp.where(away == float(d), recv_ref[0, me ^ d].astype(jnp.float32), recv)
        sent = [jnp.where(away == float(d), shot, 0.0).astype(first_ref.dtype) for d in range(n)]
        loads[1].wait()
        ifaces = jnp.concatenate([iface_ref[me ^ d] for d in range(n)], axis=1)
        coupled = times_transposed(jnp.concatenate(sent, axis=1), ifaces)
        coupled = jnp.where(lane < live, coupled, 0.0)
        loads[0].wait()
        for i in range(blocks):
            own = own_sum(i, first_ref, jac_ref, near_by(first_ref, cols_ref), table, 1, hit[i])
            state_ref[i] = (own + jnp.where(recv == float(i), coupled, 0.0)).astype(state_ref.dtype)
        for d in range(1, n):
            outgoing[d - 1][pl.ds(0, cols)] = state_ref[send_ref[0, me ^ d]]

    @pl.when(jnp.logical_not(here))
    def _():
        for load in loads[2:6]:
            load.wait()
        make_marks(marks_ref, blocks, jac_ref.shape[1], cols_ref, send_ref, recv_ref, live_ref)

    for d in range(1, n):
        row = table_row(send_ref, me ^ d, width).astype(state_ref.dtype)
        outgoing[d - 1][pl.ds(cols, ROWS)] = jnp.broadcast_to(row, (ROWS, width))


def write_start(states, first, out_ref, sems):
    copies = []
    for s, state_ref in enumerate(states, first):
        width = state_ref.shape[2]
        for i in range(state_ref.shape[0]):
            copies.append(
                pltpu.make_async_copy(state_ref.at[i], out_ref.at[s, :, pl.ds(i * width, width)], sems.at[s, i])
            )
    for copy in copies:
        copy.start()
    return copies


def own_kernel(step, state_ref, jac_ref, iface_ref, table_ref, marks_ref, z_ref):
    table = table_ref[...]
    n = lax.axis_size("net")
    blocks = state_ref.shape[0]
    kinds = jac_ref.shape[2]
    sent, near, _, _ = marks_layout(n, blocks, kinds)
    state = [state_ref[j] for j in range(blocks)]

    def pick(row):
        return picked(state, [marks_ref[pl.ds(row + j, 1)].astype(state_ref.dtype) for j in range(blocks)])

    def near_block(i, k):
        return pick(near + (i * (kinds - 1) + k) * blocks)

    @pl.when(lax.axis_index("tm") > 0)
    def _():
        term = times_transposed(pick(sent), iface_ref[step, 0, lax.axis_index("net")])
        for i in range(blocks):
            own = own_sum(i, state_ref, jac_ref.at[step], near_block, table, step)
            z_ref[i] = own + term * marks_ref[pl.ds(i, 1)]


def first_states(opening, handed, jac_ref, iface_ref, ints, table_ref, made_ref, z_ref):
    cols_ref, send_ref, recv_ref, live_ref = ints
    n = lax.axis_size("net")
    blocks, cols, width = z_ref.shape
    table = table_ref[...]
    made_ref[0] = jnp.zeros_like(made_ref[0])
    for i in range(blocks):
        z_ref[i] = own_sum(i, made_ref.at[0], jac_ref.at[0], near_by(made_ref.at[0], cols_ref), table, 0)
    for q in range(n):
        add_coupled(made_ref[0, 0], iface_ref[0, 0, q], live_ref[0, q], recv_ref[0, q], z_ref)
    made_ref[0] = z_ref[...].astype(made_ref.dtype)
    rows = [table_row(send_ref, lax.axis_index("net"), width)]
    rows += [block[cols : cols + 1].astype(jnp.float32) for block in handed]
    keep = kept(table, rows)[:, 0:1]
    for i in range(blocks):
        made_ref[1, i] = jnp.where(keep > 0.0, opening[i], jnp.zeros_like(opening[i]))
    return [made_ref.at[0], made_ref.at[1]]


def joined(sums, step, iface_ref, marks_ref, arrived, keep=None):
    me = lax.axis_index("net")
    blocks, cols = len(sums), sums[0].shape[0]
    if keep is not None:
        sums = [total * keep[:, 0:1] for total in sums]
    for d, block in enumerate(arrived, 1):
        term = times_transposed(block[pl.ds(0, cols)], iface_ref[step, 0, me ^ d])
        if keep is not None:
            term *= keep[:, d : d + 1]
        sums = [total + term * marks_ref[pl.ds(d * blocks + i, 1)] for i, total in enumerate(sums)]
    return [total.astype(jnp.bfloat16) for total in sums]


def give(made, marks_ref, state_ref, outgoing):
    blocks = len(made)
    n = lax.axis_size("net")
    sent = marks_layout(n, blocks, 1)[0]
    for i in range(blocks):
        state_ref[i] = made[i]
    for d in range(1, n) if outgoing else ():
        marks = [marks_ref[pl.ds(sent + d * blocks + j, 1)].astype(made[j].dtype) for j in range(blocks)]
        outgoing[d - 1][...] = picked(made, marks)


def exchange_order(n, handed):
    return [n - 1, *range(1, n - 1)] if handed else list(range(n - 1, 0, -1))


def by_distance(refs, handed):
    order = exchange_order(len(refs) + 1, handed)
    return [refs[order.index(d)] for d in range(1, len(refs) + 1)]


def join_kernel(step, fix, section, z_ref, iface_ref, table_ref, marks_ref, *refs):
    n = lax.axis_size("net")
    arrived, state_ref, outgoing = by_distance(refs[: n - 1], step == 0), refs[n - 1], refs[n:]
    blocks, cols, _ = z_ref.shape

    @pl.when(lax.axis_index("tm") == section)
    def _():
        keep = None
        if fix:
            rows = [marks_ref[pl.ds(marks_layout(n, blocks, fix)[2], 1)]]
            rows += [block[cols : cols + 1].astype(jnp.float32) for block in arrived]
            keep = kept(table_ref[...], rows)
        made = joined([z_ref[i] for i in range(blocks)], step, iface_ref, marks_ref, arrived, keep)
        give(made, marks_ref, state_ref, outgoing)


def close_kernel(step, section, firsts, send, before, *refs):
    n = lax.axis_size("net")
    *refs, sems = refs
    if firsts:
        *refs, made_ref, acc_ref, cols_ref, send_ref, recv_ref, live_ref, load_sems = refs
        ints = [cols_ref, send_ref, recv_ref, live_ref]
    z_ref, iface_ref, table_ref, marks_ref, *refs = refs
    arrived, refs = by_distance(refs[: n - 1], False), refs[n - 1 :]
    before, refs = refs[:before], refs[before:]
    if firsts:
        opening_ref, handed, jac_ref, sources, refs = refs[0], refs[1:n], refs[n], refs[n + 1 : n + 5], refs[n + 5 :]
    else:
        refs = refs[1:]
    out_ref, state_ref, *outgoing = refs

    @pl.when(lax.axis_index("tm") == section)
    def _():
        copies = write_start(before, 0, out_ref, sems)
        sums = [z_ref[i] for i in range(z_ref.shape[0])]
        made = joined(sums, step, iface_ref, marks_ref, arrived)
        give(made, marks_ref, state_ref, outgoing)
        copies += write_start([state_ref], len(before), out_ref, sems)
        for copy in copies:
            copy.wait()

    if firsts:

        @pl.when(lax.axis_index("tm") == 0)
        def _():
            loads = [
                pltpu.make_async_copy(source, target, load_sems.at[i])
                for i, (source, target) in enumerate(zip(sources, ints))
            ]
            for load in loads:
                load.start()
            for load in loads:
                load.wait()
            made = first_states(opening_ref, handed, jac_ref, iface_ref, ints, table_ref, made_ref, acc_ref)
            for copy in write_start(made, 0, out_ref, sems):
                copy.wait()


def local(jac, block_cols, iface_jac, iface_send, iface_recv, iface_live, ctrl_node, ctrl_gain):
    steps, blocks, kinds, width, _ = jac.shape
    cols = ctrl_node.shape[0]
    tm = lax.axis_size("tm")
    n = lax.axis_size("net")
    col_parts = lax.axis_size("cols")
    node = ctrl_node[None]
    near = block_cols.T
    bf16 = functools.partial(jax.ShapeDtypeStruct, dtype=jnp.bfloat16)
    f32 = functools.partial(jax.ShapeDtypeStruct, dtype=jnp.float32)
    whole, one = bf16((blocks, cols, width)), bf16((cols, width))
    table_rows = GAIN + steps + -(GAIN + steps) % 8
    written = bf16((steps, cols, blocks * width))

    pinned = [
        pltpu.with_memory_space_constraint(x, pltpu.HBM)
        for x in (jac, iface_jac, near, iface_send, iface_recv, iface_live, node, ctrl_gain)
    ]
    marks_rows = marks_layout(n, blocks, kinds)[-1]
    table, marks, state, *outgoing = pl.pallas_call(
        second_kernel,
        out_shape=[f32((cols, table_rows)), f32((marks_rows, width)), whole]
        + [bf16((cols + ROWS, width))] * (n - 1),
        in_specs=[HBM] * len(pinned),
        out_specs=[VMEM] * (n + 2),
        scratch_shapes=[
            pltpu.VMEM((blocks, kinds, width, width), jnp.bfloat16),
            pltpu.VMEM((n, width, width), jnp.bfloat16),
            *[pltpu.SMEM(x.shape, x.dtype) for x in (near, iface_send, iface_recv, iface_live)],
            *[pltpu.VMEM(x.shape, x.dtype) for x in (node, ctrl_gain)],
            pltpu.VMEM(whole.shape, jnp.bfloat16),
            DMA((len(pinned),)),
        ],
        compiler_params=LIMIT,
    )(*pinned)

    def own(state, step):
        return pl.pallas_call(
            functools.partial(own_kernel, step),
            out_shape=f32(whole.shape),
            in_specs=[VMEM] * 5,
            out_specs=VMEM,
            compiler_params=LIMIT,
        )(state, jac, iface_jac, table, marks)

    def join(z, step, fix, arrived, section):
        return pl.pallas_call(
            functools.partial(join_kernel, step, kinds if fix else 0, section),
            out_shape=[whole] + [one] * (n - 1),
            in_specs=[VMEM] * (n + 3),
            out_specs=[VMEM] * n,
            compiler_params=LIMIT,
        )(z, iface_jac, table, marks, *[arrived[d - 1] for d in exchange_order(n, step == 0)])

    def close(z, step, arrived, section, before, out, send):
        firsts = out is None
        arrays = [z, iface_jac, table, marks, *[arrived[d - 1] for d in exchange_order(n, False)], *before]
        specs = [VMEM] * len(arrays)
        scratch = [DMA((steps, blocks))]
        aliases = {}
        if firsts:
            arrays += [opening, *handed, jac, *pinned[2:6]]
            specs += [VMEM] * (n + 1) + [HBM] * 4
            scratch = [
                pltpu.VMEM((2, *whole.shape), jnp.bfloat16),
                pltpu.VMEM(whole.shape, jnp.float32),
                *[pltpu.SMEM(x.shape, x.dtype) for x in pinned[2:6]],
                DMA((4,)),
            ] + scratch
        else:
            aliases = {len(arrays): 0}
            arrays.append(out)
            specs.append(ANY)
        shapes, out_specs = [written], [ANY]
        if send:
            shapes += [whole] + [one] * (n - 1)
            out_specs += [VMEM] * n
        else:
            scratch.insert(0, pltpu.VMEM(whole.shape, jnp.bfloat16))
        return pl.pallas_call(
            functools.partial(close_kernel, step, section, firsts, send, len(before)),
            out_shape=shapes,
            in_specs=specs,
            out_specs=out_specs,
            input_output_aliases=aliases,
            scratch_shapes=scratch,
            compiler_params=LIMIT,
        )(*arrays)

    def swap(block, first, second, d):
        other = {first: second, second: first}
        pairs = []
        for a in range(tm):
            for q in range(n):
                for c in range(col_parts):
                    to = (other[a] * n + (q ^ d)) * col_parts + c if a in other else (a * n + q) * col_parts + (c ^ 1)
                    pairs.append(((a * n + q) * col_parts + c, to))
        return lax.ppermute(block, ("tm", "net", "cols"), pairs)

    def exchange(outgoing, first, second):
        return [swap(outgoing[d - 1], first, second, d) for d in range(1, n)]

    opening = state
    out = None
    for r in range(1, tm):
        arrived = exchange(outgoing, r - 1, r)
        state = swap(state, r - 1, r, 0)
        if r == 1:
            handed = arrived
        before = []
        for s in range(steps):
            fix = r == 1 and s == 0
            if s > 0:
                arrived = exchange(outgoing, r, r)
            z = own(state, s)
            if s < steps - 1:
                state, *outgoing = join(z, s, fix, arrived, r)
                before.append(state)
            else:
                out, *rest = close(z, s, arrived, r, before, out, r < tm - 1)
                state, *outgoing = rest or [None]
    return out


def solution(mesh):
    return jax.shard_map(
        local,
        mesh=mesh,
        in_specs=(
            P("tm", "net", None, None, None),
            P("net", None),
            P("tm", "net", None, None, None),
            P("net", None),
            P("net", None),
            P("net", None),
            P("cols"),
            P("tm", "cols"),
        ),
        out_specs=P("tm", "cols", "net"),
        check_vma=False,
    )
```

```python
import functools

import jax
import jax.numpy as jnp
from jax import lax
from jax.experimental import pallas as pl
from jax.experimental.pallas import tpu as pltpu
from jax.sharding import PartitionSpec as P

VMEM = pl.BlockSpec(memory_space=pltpu.VMEM)
SMEM = pl.BlockSpec(memory_space=pltpu.SMEM)
HBM = pl.BlockSpec(memory_space=pltpu.HBM)
ANY = pl.BlockSpec(memory_space=pl.ANY)
LIMIT = pltpu.CompilerParams(vmem_limit_bytes=16 * 1024 * 1024)
DMA = pltpu.SemaphoreType.DMA

STATE, LANE, BLOCK, AWAY, GAIN = 0, 1, 2, 3, 4
ROWS = 16


def times_transposed(rows, block):
    return lax.dot_general(rows, block, (((1,), (1,)), ((), ())), preferred_element_type=jnp.float32)


def hits(table, i, blocks, width):
    first_state = (lax.axis_index("net") * blocks + i) * width
    lane = lax.broadcasted_iota(jnp.int32, (table.shape[0], width), 1)
    return table[:, STATE : STATE + 1] == (lane + first_state).astype(jnp.float32)


def injected(table, step, hit):
    return jnp.where(hit, table[:, GAIN + step : GAIN + step + 1], 0.0)


def near_by(state_ref, cols_ref):
    return lambda i, k: state_ref[cols_ref[k, i]]


def own_sum(i, state_ref, jac_ref, near, table, step, hit=None):
    blocks, _, width = state_ref.shape
    if hit is None:
        hit = hits(table, i, blocks, width)
    kinds = jac_ref.shape[1]
    rows = [state_ref[i]] + [near(i, k) for k in range(kinds - 1)]
    row_blocks = [jac_ref[i, k] for k in range(kinds)]
    total = times_transposed(jnp.concatenate(rows, axis=1), jnp.concatenate(row_blocks, axis=1))
    return total + injected(table, step, hit)


def picked(blocks, marks):
    total = blocks[0] * marks[0]
    for block, mark in zip(blocks[1:], marks[1:]):
        total += block * mark
    return total


def marks_layout(n, blocks, kinds):
    sent = n * blocks
    near = sent + n * blocks
    row = near + blocks * (kinds - 1) * blocks
    return sent, near, row, row + 1 + -(row + 1) % 8


def make_marks(marks_ref, blocks, kinds, cols_ref, send_ref, recv_ref, live_ref):
    n = lax.axis_size("net")
    me = lax.axis_index("net")
    width = marks_ref.shape[1]
    lane = lax.broadcasted_iota(jnp.int32, (1, width), 1)
    sent, near, own_row, _ = marks_layout(n, blocks, kinds)

    def put(row, mask):
        marks_ref[pl.ds(row, 1)] = jnp.where(mask, 1.0, 0.0)

    for d in range(n):
        q = me ^ d
        for i in range(blocks):
            put(d * blocks + i, lane < jnp.where(recv_ref[0, q] == i, live_ref[0, q], 0))
            put(sent + d * blocks + i, lane < jnp.where(send_ref[0, q] == i, width, 0))
    for i in range(blocks):
        for k in range(kinds - 1):
            for j in range(blocks):
                put(near + (i * (kinds - 1) + k) * blocks + j, lane < jnp.where(cols_ref[k, i] == j, width, 0))
    marks_ref[pl.ds(own_row, 1)] = table_row(send_ref, me, width)


def add_coupled(incoming, block, live, recv, z_ref):
    mask = lax.broadcasted_iota(jnp.int32, z_ref.shape[1:], 1) < live
    z_ref[recv] += jnp.where(mask, times_transposed(incoming, block), 0.0)


def table_row(send_ref, partition, width):
    lane = lax.broadcasted_iota(jnp.int32, (1, width), 1)
    row = jnp.zeros((1, width), jnp.float32)
    for e in range(lax.axis_size("net")):
        row = jnp.where(lane == e, send_ref[0, partition ^ e].astype(jnp.float32), row)
    return row


def kept(table, rows):
    away, block = table[:, AWAY : AWAY + 1], table[:, BLOCK : BLOCK + 1]
    sent = jnp.broadcast_to(rows[0], (table.shape[0], rows[0].shape[1]))
    for d in range(1, len(rows)):
        sent = jnp.where(away == float(d), rows[d], sent)
    lane = lax.broadcasted_iota(jnp.int32, sent.shape, 1).astype(jnp.float32)
    return jnp.where(jnp.logical_or(away == lane, block == sent), 1.0, 0.0)


def second_kernel(*refs):
    jac_hbm, iface_hbm, *small, table_ref, marks_ref, state_ref = refs[:11]
    n = lax.axis_size("net")
    me = lax.axis_index("net")
    outgoing, refs = refs[11 : 10 + n], refs[10 + n :]
    jac_ref, iface_ref, *loaded, first_ref, sems = refs
    cols_ref, send_ref, recv_ref, live_ref, node_ref, gain_ref = loaded
    blocks, cols, width = state_ref.shape
    sources = [jac_hbm.at[1], iface_hbm.at[1, 0], *small]
    loads = [
        pltpu.make_async_copy(source, target, sems.at[i])
        for i, (source, target) in enumerate(zip(sources, [jac_ref, iface_ref, *loaded]))
    ]
    here = lax.axis_index("tm") == 0
    for load in loads[6:]:
        load.start()

    @pl.when(here)
    def _():
        for load in loads[:2]:
            load.start()

    for load in loads[2:6]:
        load.start()
    for load in loads[6:]:
        load.wait()
    node = node_ref[...]
    block_of = node // width
    rows = [
        node,
        node - block_of * width,
        block_of % blocks,
        (block_of // blocks) ^ me,
    ]
    steps = gain_ref.shape[0]
    fill = -(GAIN + steps) % 8
    rows = [row.astype(jnp.float32) for row in rows] + [gain_ref[...], jnp.zeros((fill, cols), jnp.float32)]
    table_ref[...] = jnp.concatenate(rows, axis=0).T

    @pl.when(here)
    def _():
        table = table_ref[...]
        hit = [hits(table, i, blocks, width) for i in range(blocks)]
        for i in range(blocks):
            first_ref[i] = injected(table, 0, hit[i]).astype(first_ref.dtype)
        lane = lax.broadcasted_iota(jnp.int32, (cols, width), 1).astype(jnp.float32)
        shot = jnp.where(lane == table[:, LANE : LANE + 1], table[:, GAIN : GAIN + 1], 0.0)
        away, block = table[:, AWAY : AWAY + 1], table[:, BLOCK : BLOCK + 1]
        for load in loads[2:6]:
            load.wait()
        mine = jnp.logical_or(away != 0.0, block == send_ref[0, me].astype(jnp.float32))
        shot = jnp.where(mine, shot, 0.0)
        live = recv = jnp.zeros_like(away)
        for d in range(n):
            live = jnp.where(away == float(d), live_ref[0, me ^ d].astype(jnp.float32), live)
            recv = jnp.where(away == float(d), recv_ref[0, me ^ d].astype(jnp.float32), recv)
        sent = [jnp.where(away == float(d), shot, 0.0).astype(first_ref.dtype) for d in range(n)]
        loads[1].wait()
        ifaces = jnp.concatenate([iface_ref[me ^ d] for d in range(n)], axis=1)
        coupled = times_transposed(jnp.concatenate(sent, axis=1), ifaces)
        coupled = jnp.where(lane < live, coupled, 0.0)
        loads[0].wait()
        for i in range(blocks):
            own = own_sum(i, first_ref, jac_ref, near_by(first_ref, cols_ref), table, 1, hit[i])
            state_ref[i] = (own + jnp.where(recv == float(i), coupled, 0.0)).astype(state_ref.dtype)
        for d in range(1, n):
            outgoing[d - 1][pl.ds(0, cols)] = state_ref[send_ref[0, me ^ d]]

    @pl.when(jnp.logical_not(here))
    def _():
        for load in loads[2:6]:
            load.wait()
        make_marks(marks_ref, blocks, jac_ref.shape[1], cols_ref, send_ref, recv_ref, live_ref)

    for d in range(1, n):
        row = table_row(send_ref, me ^ d, width).astype(state_ref.dtype)
        outgoing[d - 1][pl.ds(cols, ROWS)] = jnp.broadcast_to(row, (ROWS, width))


def write_copies(states, first, out_ref, sems):
    copies = []
    for s, state_ref in enumerate(states, first):
        width = state_ref.shape[2]
        for i in range(state_ref.shape[0]):
            copies.append(
                pltpu.make_async_copy(state_ref.at[i], out_ref.at[s, :, pl.ds(i * width, width)], sems.at[s, i])
            )
    return copies


def write(states, first, out_ref, sems):
    copies = write_copies(states, first, out_ref, sems)
    for copy in copies:
        copy.start()
    for copy in copies:
        copy.wait()


def own_kernel(step, state_ref, jac_ref, iface_ref, table_ref, marks_ref, z_ref):
    table = table_ref[...]
    n = lax.axis_size("net")
    blocks = state_ref.shape[0]
    kinds = jac_ref.shape[2]
    sent, near, _, _ = marks_layout(n, blocks, kinds)
    state = [state_ref[j] for j in range(blocks)]

    def pick(row):
        return picked(state, [marks_ref[pl.ds(row + j, 1)].astype(state_ref.dtype) for j in range(blocks)])

    def near_block(i, k):
        return pick(near + (i * (kinds - 1) + k) * blocks)

    @pl.when(lax.axis_index("tm") > 0)
    def _():
        term = times_transposed(pick(sent), iface_ref[step, 0, lax.axis_index("net")])
        for i in range(blocks):
            own = own_sum(i, state_ref, jac_ref.at[step], near_block, table, step)
            z_ref[i] = own + term * marks_ref[pl.ds(i, 1)]


def first_states(opening, handed, jac_ref, iface_ref, ints, table_ref, made_ref, z_ref):
    cols_ref, send_ref, recv_ref, live_ref = ints
    n = lax.axis_size("net")
    blocks, cols, width = z_ref.shape
    table = table_ref[...]
    made_ref[0] = jnp.zeros_like(made_ref[0])
    for i in range(blocks):
        z_ref[i] = own_sum(i, made_ref.at[0], jac_ref.at[0], near_by(made_ref.at[0], cols_ref), table, 0)
    for q in range(n):
        add_coupled(made_ref[0, 0], iface_ref[0, 0, q], live_ref[0, q], recv_ref[0, q], z_ref)
    made_ref[0] = z_ref[...].astype(made_ref.dtype)
    rows = [table_row(send_ref, lax.axis_index("net"), width)]
    rows += [block[cols : cols + 1].astype(jnp.float32) for block in handed]
    keep = kept(table, rows)[:, 0:1]
    for i in range(blocks):
        made_ref[1, i] = jnp.where(keep > 0.0, opening[i], jnp.zeros_like(opening[i]))
    return [made_ref.at[0], made_ref.at[1]]


def joined(sums, step, iface_ref, marks_ref, arrived, keep=None):
    me = lax.axis_index("net")
    blocks, cols = len(sums), sums[0].shape[0]
    if keep is not None:
        sums = [total * keep[:, 0:1] for total in sums]
    for d, block in enumerate(arrived, 1):
        term = times_transposed(block[pl.ds(0, cols)], iface_ref[step, 0, me ^ d])
        if keep is not None:
            term *= keep[:, d : d + 1]
        sums = [total + term * marks_ref[pl.ds(d * blocks + i, 1)] for i, total in enumerate(sums)]
    return [total.astype(jnp.bfloat16) for total in sums]


def give(made, marks_ref, state_ref, outgoing):
    blocks = len(made)
    n = lax.axis_size("net")
    sent = marks_layout(n, blocks, 1)[0]
    for i in range(blocks):
        state_ref[i] = made[i]
    for d in range(1, n) if outgoing else ():
        marks = [marks_ref[pl.ds(sent + d * blocks + j, 1)].astype(made[j].dtype) for j in range(blocks)]
        outgoing[d - 1][...] = picked(made, marks)


def exchange_order(n, handed):
    return [*range(n // 2, n), *range(n // 2 - 1, 0, -1)] if handed else list(range(n - 1, 0, -1))


def by_distance(refs, handed):
    order = exchange_order(len(refs) + 1, handed)
    return [refs[order.index(d)] for d in range(1, len(refs) + 1)]


def join_kernel(step, fix, section, z_ref, iface_ref, table_ref, marks_ref, *refs):
    n = lax.axis_size("net")
    arrived, state_ref, outgoing = by_distance(refs[: n - 1], step == 0), refs[n - 1], refs[n:]
    blocks, cols, _ = z_ref.shape

    @pl.when(lax.axis_index("tm") == section)
    def _():
        keep = None
        if fix:
            rows = [marks_ref[pl.ds(marks_layout(n, blocks, fix)[2], 1)]]
            rows += [block[cols : cols + 1].astype(jnp.float32) for block in arrived]
            keep = kept(table_ref[...], rows)
        made = joined([z_ref[i] for i in range(blocks)], step, iface_ref, marks_ref, arrived, keep)
        give(made, marks_ref, state_ref, outgoing)


def write_kernel(step, section, firsts, before, state_ref, jac_ref, iface_ref, table_ref, marks_ref, *refs):
    n = lax.axis_size("net")
    *refs, sems = refs
    before, refs = refs[:before], refs[before:]
    if firsts:
        *refs, made_ref, acc_ref, cols_ref, send_ref, recv_ref, live_ref, load_sems = refs
        ints = [cols_ref, send_ref, recv_ref, live_ref]
        opening_ref, handed, sources, (z_ref, out_ref) = refs[0], refs[1:n], refs[n : n + 4], refs[n + 4 :]
    else:
        _, z_ref, out_ref = refs
    here = lax.axis_index("tm") == section

    @pl.when(here)
    def _():
        for copy in write_copies(before, 0, out_ref, sems):
            copy.start()

    own_kernel(step, state_ref, jac_ref, iface_ref, table_ref, marks_ref, z_ref)

    @pl.when(here)
    def _():
        for copy in write_copies(before, 0, out_ref, sems):
            copy.wait()

    if firsts:

        @pl.when(lax.axis_index("tm") == 0)
        def _():
            loads = [
                pltpu.make_async_copy(source, target, load_sems.at[i])
                for i, (source, target) in enumerate(zip(sources, ints))
            ]
            for load in loads:
                load.start()
            for load in loads:
                load.wait()
            made = first_states(opening_ref, handed, jac_ref, iface_ref, ints, table_ref, made_ref, acc_ref)
            write(made, 0, out_ref, sems)


def close_kernel(step, section, place, z_ref, iface_ref, marks_ref, *refs):
    n = lax.axis_size("net")
    arrived, (_, out_ref, state_ref, *outgoing, sems) = by_distance(refs[: n - 1], False), refs[n - 1 :]

    @pl.when(lax.axis_index("tm") == section)
    def _():
        sums = [z_ref[i] for i in range(z_ref.shape[0])]
        give(joined(sums, step, iface_ref, marks_ref, arrived), marks_ref, state_ref, outgoing)
        write([state_ref], place, out_ref, sems)


def local(jac, block_cols, iface_jac, iface_send, iface_recv, iface_live, ctrl_node, ctrl_gain):
    steps, blocks, kinds, width, _ = jac.shape
    cols = ctrl_node.shape[0]
    tm = lax.axis_size("tm")
    n = lax.axis_size("net")
    col_parts = lax.axis_size("cols")
    node = ctrl_node[None]
    near = block_cols.T
    bf16 = functools.partial(jax.ShapeDtypeStruct, dtype=jnp.bfloat16)
    f32 = functools.partial(jax.ShapeDtypeStruct, dtype=jnp.float32)
    whole, one = bf16((blocks, cols, width)), bf16((cols, width))
    table_rows = GAIN + steps + -(GAIN + steps) % 8
    written = bf16((steps, cols, blocks * width))

    pinned = [
        pltpu.with_memory_space_constraint(x, pltpu.HBM)
        for x in (jac, iface_jac, near, iface_send, iface_recv, iface_live, node, ctrl_gain)
    ]
    marks_rows = marks_layout(n, blocks, kinds)[-1]
    table, marks, state, *outgoing = pl.pallas_call(
        second_kernel,
        out_shape=[f32((cols, table_rows)), f32((marks_rows, width)), whole]
        + [bf16((cols + ROWS, width))] * (n - 1),
        in_specs=[HBM] * len(pinned),
        out_specs=[VMEM] * (n + 2),
        scratch_shapes=[
            pltpu.VMEM((blocks, kinds, width, width), jnp.bfloat16),
            pltpu.VMEM((n, width, width), jnp.bfloat16),
            *[pltpu.SMEM(x.shape, x.dtype) for x in (near, iface_send, iface_recv, iface_live)],
            *[pltpu.VMEM(x.shape, x.dtype) for x in (node, ctrl_gain)],
            pltpu.VMEM(whole.shape, jnp.bfloat16),
            DMA((len(pinned),)),
        ],
        compiler_params=LIMIT,
    )(*pinned)

    def own(state, step):
        return pl.pallas_call(
            functools.partial(own_kernel, step),
            out_shape=f32(whole.shape),
            in_specs=[VMEM] * 5,
            out_specs=VMEM,
            compiler_params=LIMIT,
        )(state, jac, iface_jac, table, marks)

    def join(z, step, fix, arrived, section):
        return pl.pallas_call(
            functools.partial(join_kernel, step, kinds if fix else 0, section),
            out_shape=[whole] + [one] * (n - 1),
            in_specs=[VMEM] * (n + 3),
            out_specs=[VMEM] * n,
            compiler_params=LIMIT,
        )(z, iface_jac, table, marks, *[arrived[d - 1] for d in exchange_order(n, step == 0)])

    def own_and_write(state, step, section, before, out):
        firsts = out is None
        arrays = [state, jac, iface_jac, table, marks, *before]
        specs = [VMEM] * len(arrays)
        scratch = [DMA((steps, blocks))]
        aliases = {}
        if firsts:
            arrays += [opening, *handed, *pinned[2:6]]
            specs += [VMEM] * n + [HBM] * 4
            scratch = [
                pltpu.VMEM((2, *whole.shape), jnp.bfloat16),
                pltpu.VMEM(whole.shape, jnp.float32),
                *[pltpu.SMEM(x.shape, x.dtype) for x in pinned[2:6]],
                DMA((4,)),
            ] + scratch
        else:
            aliases = {len(arrays): 1}
            arrays.append(out)
            specs.append(ANY)
        return pl.pallas_call(
            functools.partial(write_kernel, step, section, firsts, len(before)),
            out_shape=[f32(whole.shape), written],
            in_specs=specs,
            out_specs=[VMEM, ANY],
            input_output_aliases=aliases,
            scratch_shapes=scratch,
            compiler_params=LIMIT,
        )(*arrays)

    def close(z, step, arrived, section, out, send):
        ordered = [arrived[d - 1] for d in exchange_order(n, False)]
        return pl.pallas_call(
            functools.partial(close_kernel, step, section, steps - 1),
            out_shape=[written] + ([whole] + [one] * (n - 1) if send else []),
            in_specs=[VMEM] * (n + 2) + [ANY],
            out_specs=[ANY] + [VMEM] * (n if send else 0),
            input_output_aliases={n + 2: 0},
            scratch_shapes=([] if send else [pltpu.VMEM(whole.shape, jnp.bfloat16)]) + [DMA((steps, blocks))],
            compiler_params=LIMIT,
        )(z, iface_jac, marks, *ordered, out)

    def swap(block, first, second, d):
        other = {first: second, second: first}
        pairs = []
        for a in range(tm):
            for q in range(n):
                for c in range(col_parts):
                    to = (other[a] * n + (q ^ d)) * col_parts + c if a in other else (a * n + q) * col_parts + (c ^ 1)
                    pairs.append(((a * n + q) * col_parts + c, to))
        return lax.ppermute(block, ("tm", "net", "cols"), pairs)

    def exchange(outgoing, first, second):
        return [swap(outgoing[d - 1], first, second, d) for d in range(1, n)]

    opening = state
    out = None
    for r in range(1, tm):
        arrived = exchange(outgoing, r - 1, r)
        state = swap(state, r - 1, r, 0)
        if r == 1:
            handed = arrived
        before = []
        for s in range(steps):
            fix = r == 1 and s == 0
            if s > 0:
                arrived = exchange(outgoing, r, r)
            if s < steps - 1:
                state, *outgoing = join(own(state, s), s, fix, arrived, r)
                before.append(state)
            else:
                z, out = own_and_write(state, s, r, before, out)
                out, *rest = close(z, s, arrived, r, out, r < tm - 1)
                state, *outgoing = rest or [None]
    return out


def solution(mesh):
    return jax.shard_map(
        local,
        mesh=mesh,
        in_specs=(
            P("tm", "net", None, None, None),
            P("net", None),
            P("tm", "net", None, None, None),
            P("net", None),
            P("net", None),
            P("net", None),
            P("cols"),
            P("tm", "cols"),
        ),
        out_specs=P("tm", "cols", "net"),
        check_vma=False,
    )
```

```python
import functools

import jax
import jax.numpy as jnp
from jax import lax
from jax.experimental import pallas as pl
from jax.experimental.pallas import tpu as pltpu
from jax.sharding import PartitionSpec as P

VMEM = pl.BlockSpec(memory_space=pltpu.VMEM)
SMEM = pl.BlockSpec(memory_space=pltpu.SMEM)
HBM = pl.BlockSpec(memory_space=pltpu.HBM)
ANY = pl.BlockSpec(memory_space=pl.ANY)
LIMIT = pltpu.CompilerParams(vmem_limit_bytes=16 * 1024 * 1024)
DMA = pltpu.SemaphoreType.DMA

STATE, LANE, BLOCK, AWAY, GAIN = 0, 1, 2, 3, 4
ROWS = 16


def times_transposed(rows, block):
    return lax.dot_general(rows, block, (((1,), (1,)), ((), ())), preferred_element_type=jnp.float32)


def hits(table, i, blocks, width):
    first_state = (lax.axis_index("net") * blocks + i) * width
    lane = lax.broadcasted_iota(jnp.int32, (table.shape[0], width), 1)
    return table[:, STATE : STATE + 1] == (lane + first_state).astype(jnp.float32)


def injected(table, step, hit):
    return jnp.where(hit, table[:, GAIN + step : GAIN + step + 1], 0.0)


def near_by(state_ref, cols_ref):
    return lambda i, k: state_ref[cols_ref[k, i]]


def own_sum(i, state_ref, jac_ref, near, table, step, hit=None):
    blocks, _, width = state_ref.shape
    if hit is None:
        hit = hits(table, i, blocks, width)
    kinds = jac_ref.shape[1]
    rows = [state_ref[i]] + [near(i, k) for k in range(kinds - 1)]
    row_blocks = [jac_ref[i, k] for k in range(kinds)]
    total = times_transposed(jnp.concatenate(rows, axis=1), jnp.concatenate(row_blocks, axis=1))
    return total + injected(table, step, hit)


def picked(blocks, marks):
    total = blocks[0] * marks[0]
    for block, mark in zip(blocks[1:], marks[1:]):
        total += block * mark
    return total


def marks_layout(n, blocks, kinds):
    sent = n * blocks
    near = sent + n * blocks
    row = near + blocks * (kinds - 1) * blocks
    return sent, near, row, row + 1 + -(row + 1) % 8


def make_marks(marks_ref, blocks, kinds, cols_ref, send_ref, recv_ref, live_ref):
    n = lax.axis_size("net")
    me = lax.axis_index("net")
    width = marks_ref.shape[1]
    lane = lax.broadcasted_iota(jnp.int32, (1, width), 1)
    sent, near, own_row, _ = marks_layout(n, blocks, kinds)

    def put(row, mask):
        marks_ref[pl.ds(row, 1)] = jnp.where(mask, 1.0, 0.0)

    for d in range(n):
        q = me ^ d
        for i in range(blocks):
            put(d * blocks + i, lane < jnp.where(recv_ref[0, q] == i, live_ref[0, q], 0))
            put(sent + d * blocks + i, lane < jnp.where(send_ref[0, q] == i, width, 0))
    for i in range(blocks):
        for k in range(kinds - 1):
            for j in range(blocks):
                put(near + (i * (kinds - 1) + k) * blocks + j, lane < jnp.where(cols_ref[k, i] == j, width, 0))
    marks_ref[pl.ds(own_row, 1)] = table_row(send_ref, me, width)


def add_coupled(incoming, block, live, recv, z_ref):
    mask = lax.broadcasted_iota(jnp.int32, z_ref.shape[1:], 1) < live
    z_ref[recv] += jnp.where(mask, times_transposed(incoming, block), 0.0)


def table_row(send_ref, partition, width):
    lane = lax.broadcasted_iota(jnp.int32, (1, width), 1)
    row = jnp.zeros((1, width), jnp.float32)
    for e in range(lax.axis_size("net")):
        row = jnp.where(lane == e, send_ref[0, partition ^ e].astype(jnp.float32), row)
    return row


def kept(table, rows):
    away, block = table[:, AWAY : AWAY + 1], table[:, BLOCK : BLOCK + 1]
    sent = jnp.broadcast_to(rows[0], (table.shape[0], rows[0].shape[1]))
    for d in range(1, len(rows)):
        sent = jnp.where(away == float(d), rows[d], sent)
    lane = lax.broadcasted_iota(jnp.int32, sent.shape, 1).astype(jnp.float32)
    return jnp.where(jnp.logical_or(away == lane, block == sent), 1.0, 0.0)


def second_kernel(*refs):
    jac_hbm, iface_hbm, *small, table_ref, marks_ref, state_ref = refs[:11]
    n = lax.axis_size("net")
    me = lax.axis_index("net")
    outgoing, refs = refs[11 : 10 + n], refs[10 + n :]
    jac_ref, iface_ref, *loaded, first_ref, sems = refs
    cols_ref, send_ref, recv_ref, live_ref, node_ref, gain_ref = loaded
    blocks, cols, width = state_ref.shape
    sources = [jac_hbm.at[1], iface_hbm.at[1, 0], *small]
    loads = [
        pltpu.make_async_copy(source, target, sems.at[i])
        for i, (source, target) in enumerate(zip(sources, [jac_ref, iface_ref, *loaded]))
    ]
    here = lax.axis_index("tm") == 0
    for load in loads[6:]:
        load.start()

    @pl.when(here)
    def _():
        for load in loads[:2]:
            load.start()

    for load in loads[2:6]:
        load.start()
    for load in loads[6:]:
        load.wait()
    node = node_ref[...]
    block_of = node // width
    rows = [
        node,
        node - block_of * width,
        block_of % blocks,
        (block_of // blocks) ^ me,
    ]
    steps = gain_ref.shape[0]
    fill = -(GAIN + steps) % 8
    rows = [row.astype(jnp.float32) for row in rows] + [gain_ref[...], jnp.zeros((fill, cols), jnp.float32)]
    table_ref[...] = jnp.concatenate(rows, axis=0).T

    @pl.when(here)
    def _():
        table = table_ref[...]
        hit = [hits(table, i, blocks, width) for i in range(blocks)]
        for i in range(blocks):
            first_ref[i] = injected(table, 0, hit[i]).astype(first_ref.dtype)
        lane = lax.broadcasted_iota(jnp.int32, (cols, width), 1).astype(jnp.float32)
        shot = jnp.where(lane == table[:, LANE : LANE + 1], table[:, GAIN : GAIN + 1], 0.0)
        away, block = table[:, AWAY : AWAY + 1], table[:, BLOCK : BLOCK + 1]
        for load in loads[2:6]:
            load.wait()
        mine = jnp.logical_or(away != 0.0, block == send_ref[0, me].astype(jnp.float32))
        shot = jnp.where(mine, shot, 0.0)
        live = recv = jnp.zeros_like(away)
        for d in range(n):
            live = jnp.where(away == float(d), live_ref[0, me ^ d].astype(jnp.float32), live)
            recv = jnp.where(away == float(d), recv_ref[0, me ^ d].astype(jnp.float32), recv)
        sent = [jnp.where(away == float(d), shot, 0.0).astype(first_ref.dtype) for d in range(n)]
        loads[1].wait()
        ifaces = jnp.concatenate([iface_ref[me ^ d] for d in range(n)], axis=1)
        coupled = times_transposed(jnp.concatenate(sent, axis=1), ifaces)
        coupled = jnp.where(lane < live, coupled, 0.0)
        loads[0].wait()
        for i in range(blocks):
            own = own_sum(i, first_ref, jac_ref, near_by(first_ref, cols_ref), table, 1, hit[i])
            state_ref[i] = (own + jnp.where(recv == float(i), coupled, 0.0)).astype(state_ref.dtype)
        for d in range(1, n):
            outgoing[d - 1][pl.ds(0, cols)] = state_ref[send_ref[0, me ^ d]]

    @pl.when(jnp.logical_not(here))
    def _():
        for load in loads[2:6]:
            load.wait()
        make_marks(marks_ref, blocks, jac_ref.shape[1], cols_ref, send_ref, recv_ref, live_ref)

    for d in range(1, n):
        row = table_row(send_ref, me ^ d, width).astype(state_ref.dtype)
        outgoing[d - 1][pl.ds(cols, ROWS)] = jnp.broadcast_to(row, (ROWS, width))


def write_copies(states, first, out_ref, sems):
    copies = []
    for s, state_ref in enumerate(states, first):
        width = state_ref.shape[2]
        for i in range(state_ref.shape[0]):
            copies.append(
                pltpu.make_async_copy(state_ref.at[i], out_ref.at[s, :, pl.ds(i * width, width)], sems.at[s, i])
            )
    return copies


def write(states, first, out_ref, sems):
    copies = write_copies(states, first, out_ref, sems)
    for copy in copies:
        copy.start()
    for copy in copies:
        copy.wait()


def own_kernel(step, state_ref, jac_ref, iface_ref, table_ref, marks_ref, z_ref):
    table = table_ref[...]
    n = lax.axis_size("net")
    blocks = state_ref.shape[0]
    kinds = jac_ref.shape[2]
    sent, near, _, _ = marks_layout(n, blocks, kinds)
    state = [state_ref[j] for j in range(blocks)]

    def pick(row):
        return picked(state, [marks_ref[pl.ds(row + j, 1)].astype(state_ref.dtype) for j in range(blocks)])

    def near_block(i, k):
        return pick(near + (i * (kinds - 1) + k) * blocks)

    @pl.when(lax.axis_index("tm") > 0)
    def _():
        term = times_transposed(pick(sent), iface_ref[step, 0, lax.axis_index("net")])
        for i in range(blocks):
            own = own_sum(i, state_ref, jac_ref.at[step], near_block, table, step)
            z_ref[i] = own + term * marks_ref[pl.ds(i, 1)]


def first_states(opening, handed, jac_ref, iface_ref, ints, table_ref, made_ref, z_ref):
    cols_ref, send_ref, recv_ref, live_ref = ints
    n = lax.axis_size("net")
    blocks, cols, width = z_ref.shape
    table = table_ref[...]
    made_ref[0] = jnp.zeros_like(made_ref[0])
    for i in range(blocks):
        z_ref[i] = own_sum(i, made_ref.at[0], jac_ref.at[0], near_by(made_ref.at[0], cols_ref), table, 0)
    for q in range(n):
        add_coupled(made_ref[0, 0], iface_ref[0, 0, q], live_ref[0, q], recv_ref[0, q], z_ref)
    made_ref[0] = z_ref[...].astype(made_ref.dtype)
    rows = [table_row(send_ref, lax.axis_index("net"), width)]
    rows += [block[cols : cols + 1].astype(jnp.float32) for block in handed]
    keep = kept(table, rows)[:, 0:1]
    for i in range(blocks):
        made_ref[1, i] = jnp.where(keep > 0.0, opening[i], jnp.zeros_like(opening[i]))
    return [made_ref.at[0], made_ref.at[1]]


def joined(sums, step, iface_ref, marks_ref, arrived, keep=None):
    me = lax.axis_index("net")
    blocks, cols = len(sums), sums[0].shape[0]
    if keep is not None:
        sums = [total * keep[:, 0:1] for total in sums]
    for d, block in enumerate(arrived, 1):
        term = times_transposed(block[pl.ds(0, cols)], iface_ref[step, 0, me ^ d])
        if keep is not None:
            term *= keep[:, d : d + 1]
        sums = [total + term * marks_ref[pl.ds(d * blocks + i, 1)] for i, total in enumerate(sums)]
    return [total.astype(jnp.bfloat16) for total in sums]


def give(made, marks_ref, state_ref, outgoing):
    blocks = len(made)
    n = lax.axis_size("net")
    sent = marks_layout(n, blocks, 1)[0]
    for i in range(blocks) if state_ref is not None else ():
        state_ref[i] = made[i]
    for d in range(1, n) if outgoing else ():
        marks = [marks_ref[pl.ds(sent + d * blocks + j, 1)].astype(made[j].dtype) for j in range(blocks)]
        outgoing[d - 1][...] = picked(made, marks)


def exchange_order(n, handed):
    return [*range(n // 2, n), *range(n // 2 - 1, 0, -1)] if handed else list(range(n - 1, 0, -1))


def by_distance(refs, handed):
    order = exchange_order(len(refs) + 1, handed)
    return [refs[order.index(d)] for d in range(1, len(refs) + 1)]


def join_kernel(step, fix, section, z_ref, iface_ref, table_ref, marks_ref, *refs):
    n = lax.axis_size("net")
    arrived, state_ref, outgoing = by_distance(refs[: n - 1], step == 0), refs[n - 1], refs[n:]
    blocks, cols, _ = z_ref.shape

    @pl.when(lax.axis_index("tm") == section)
    def _():
        keep = None
        if fix:
            rows = [marks_ref[pl.ds(marks_layout(n, blocks, fix)[2], 1)]]
            rows += [block[cols : cols + 1].astype(jnp.float32) for block in arrived]
            keep = kept(table_ref[...], rows)
        made = joined([z_ref[i] for i in range(blocks)], step, iface_ref, marks_ref, arrived, keep)
        give(made, marks_ref, state_ref, outgoing)


def write_kernel(step, section, firsts, before, state_ref, jac_ref, iface_ref, table_ref, marks_ref, *refs):
    n = lax.axis_size("net")
    *refs, sems = refs
    before, refs = refs[:before], refs[before:]
    if firsts:
        *refs, made_ref, acc_ref, cols_ref, send_ref, recv_ref, live_ref, load_sems = refs
        ints = [cols_ref, send_ref, recv_ref, live_ref]
        opening_ref, handed, sources, (z_ref, out_ref) = refs[0], refs[1:n], refs[n : n + 4], refs[n + 4 :]
    else:
        _, z_ref, out_ref = refs
    here = lax.axis_index("tm") == section

    @pl.when(here)
    def _():
        for copy in write_copies(before, 0, out_ref, sems):
            copy.start()

    own_kernel(step, state_ref, jac_ref, iface_ref, table_ref, marks_ref, z_ref)

    @pl.when(here)
    def _():
        for copy in write_copies(before, 0, out_ref, sems):
            copy.wait()

    if firsts:

        @pl.when(lax.axis_index("tm") == 0)
        def _():
            loads = [
                pltpu.make_async_copy(source, target, load_sems.at[i])
                for i, (source, target) in enumerate(zip(sources, ints))
            ]
            for load in loads:
                load.start()
            for load in loads:
                load.wait()
            made = first_states(opening_ref, handed, jac_ref, iface_ref, ints, table_ref, made_ref, acc_ref)
            write(made, 0, out_ref, sems)


def close_kernel(step, section, place, z_ref, iface_ref, marks_ref, *refs):
    n = lax.axis_size("net")
    arrived, (_, out_ref, state_ref, *outgoing, sems) = by_distance(refs[: n - 1], False), refs[n - 1 :]

    @pl.when(lax.axis_index("tm") == section)
    def _():
        me = lax.axis_index("net")
        blocks = z_ref.shape[0]
        terms = [times_transposed(block[...], iface_ref[step, 0, me ^ d]) for d, block in enumerate(arrived, 1)]
        copies = write_copies([state_ref], place, out_ref, sems)
        made = []
        for i in range(blocks):
            total = z_ref[i]
            for d, term in enumerate(terms, 1):
                total += term * marks_ref[pl.ds(d * blocks + i, 1)]
            made.append(total.astype(state_ref.dtype))
            state_ref[i] = made[i]
            copies[i].start()
        if outgoing:
            give(made, marks_ref, None, outgoing)
        for copy in copies:
            copy.wait()


def local(jac, block_cols, iface_jac, iface_send, iface_recv, iface_live, ctrl_node, ctrl_gain):
    steps, blocks, kinds, width, _ = jac.shape
    cols = ctrl_node.shape[0]
    tm = lax.axis_size("tm")
    n = lax.axis_size("net")
    col_parts = lax.axis_size("cols")
    node = ctrl_node[None]
    near = block_cols.T
    bf16 = functools.partial(jax.ShapeDtypeStruct, dtype=jnp.bfloat16)
    f32 = functools.partial(jax.ShapeDtypeStruct, dtype=jnp.float32)
    whole, one = bf16((blocks, cols, width)), bf16((cols, width))
    table_rows = GAIN + steps + -(GAIN + steps) % 8
    written = bf16((steps, cols, blocks * width))

    pinned = [
        pltpu.with_memory_space_constraint(x, pltpu.HBM)
        for x in (jac, iface_jac, near, iface_send, iface_recv, iface_live, node, ctrl_gain)
    ]
    marks_rows = marks_layout(n, blocks, kinds)[-1]
    table, marks, state, *outgoing = pl.pallas_call(
        second_kernel,
        out_shape=[f32((cols, table_rows)), f32((marks_rows, width)), whole]
        + [bf16((cols + ROWS, width))] * (n - 1),
        in_specs=[HBM] * len(pinned),
        out_specs=[VMEM] * (n + 2),
        scratch_shapes=[
            pltpu.VMEM((blocks, kinds, width, width), jnp.bfloat16),
            pltpu.VMEM((n, width, width), jnp.bfloat16),
            *[pltpu.SMEM(x.shape, x.dtype) for x in (near, iface_send, iface_recv, iface_live)],
            *[pltpu.VMEM(x.shape, x.dtype) for x in (node, ctrl_gain)],
            pltpu.VMEM(whole.shape, jnp.bfloat16),
            DMA((len(pinned),)),
        ],
        compiler_params=LIMIT,
    )(*pinned)

    def own(state, step):
        return pl.pallas_call(
            functools.partial(own_kernel, step),
            out_shape=f32(whole.shape),
            in_specs=[VMEM] * 5,
            out_specs=VMEM,
            compiler_params=LIMIT,
        )(state, jac, iface_jac, table, marks)

    def join(z, step, fix, arrived, section):
        return pl.pallas_call(
            functools.partial(join_kernel, step, kinds if fix else 0, section),
            out_shape=[whole] + [one] * (n - 1),
            in_specs=[VMEM] * (n + 3),
            out_specs=[VMEM] * n,
            compiler_params=LIMIT,
        )(z, iface_jac, table, marks, *[arrived[d - 1] for d in exchange_order(n, step == 0)])

    def own_and_write(state, step, section, before, out):
        firsts = out is None
        arrays = [state, jac, iface_jac, table, marks, *before]
        specs = [VMEM] * len(arrays)
        scratch = [DMA((steps, blocks))]
        aliases = {}
        if firsts:
            arrays += [opening, *handed, *pinned[2:6]]
            specs += [VMEM] * n + [HBM] * 4
            scratch = [
                pltpu.VMEM((2, *whole.shape), jnp.bfloat16),
                pltpu.VMEM(whole.shape, jnp.float32),
                *[pltpu.SMEM(x.shape, x.dtype) for x in pinned[2:6]],
                DMA((4,)),
            ] + scratch
        else:
            aliases = {len(arrays): 1}
            arrays.append(out)
            specs.append(ANY)
        return pl.pallas_call(
            functools.partial(write_kernel, step, section, firsts, len(before)),
            out_shape=[f32(whole.shape), written],
            in_specs=specs,
            out_specs=[VMEM, ANY],
            input_output_aliases=aliases,
            scratch_shapes=scratch,
            compiler_params=LIMIT,
        )(*arrays)

    def close(z, step, arrived, section, out, send):
        ordered = [arrived[d - 1] for d in exchange_order(n, False)]
        return pl.pallas_call(
            functools.partial(close_kernel, step, section, steps - 1),
            out_shape=[written] + ([whole] + [one] * (n - 1) if send else []),
            in_specs=[VMEM] * (n + 2) + [ANY],
            out_specs=[ANY] + [VMEM] * (n if send else 0),
            input_output_aliases={n + 2: 0},
            scratch_shapes=([] if send else [pltpu.VMEM(whole.shape, jnp.bfloat16)]) + [DMA((steps, blocks))],
            compiler_params=LIMIT,
        )(z, iface_jac, marks, *ordered, out)

    def swap(block, first, second, d):
        other = {first: second, second: first}
        pairs = []
        for a in range(tm):
            for q in range(n):
                for c in range(col_parts):
                    to = (other[a] * n + (q ^ d)) * col_parts + c if a in other else (a * n + q) * col_parts + (c ^ 1)
                    pairs.append(((a * n + q) * col_parts + c, to))
        return lax.ppermute(block, ("tm", "net", "cols"), pairs)

    def exchange(outgoing, first, second):
        return [swap(outgoing[d - 1], first, second, d) for d in range(1, n)]

    opening = state
    out = None
    for r in range(1, tm):
        arrived = exchange(outgoing, r - 1, r)
        state = swap(state, r - 1, r, 0)
        if r == 1:
            handed = arrived
        before = []
        for s in range(steps):
            fix = r == 1 and s == 0
            if s > 0:
                arrived = exchange(outgoing, r, r)
            if s < steps - 1:
                state, *outgoing = join(own(state, s), s, fix, arrived, r)
                before.append(state)
            else:
                z, out = own_and_write(state, s, r, before, out)
                out, *rest = close(z, s, arrived, r, out, r < tm - 1)
                state, *outgoing = rest or [None]
    return out


def solution(mesh):
    return jax.shard_map(
        local,
        mesh=mesh,
        in_specs=(
            P("tm", "net", None, None, None),
            P("net", None),
            P("tm", "net", None, None, None),
            P("net", None),
            P("net", None),
            P("net", None),
            P("cols"),
            P("tm", "cols"),
        ),
        out_specs=P("tm", "cols", "net"),
        check_vma=False,
    )
```

```python
import functools

import jax
import jax.numpy as jnp
from jax import lax
from jax.experimental import pallas as pl
from jax.experimental.pallas import tpu as pltpu
from jax.sharding import PartitionSpec as P

VMEM = pl.BlockSpec(memory_space=pltpu.VMEM)
SMEM = pl.BlockSpec(memory_space=pltpu.SMEM)
HBM = pl.BlockSpec(memory_space=pltpu.HBM)
ANY = pl.BlockSpec(memory_space=pl.ANY)
LIMIT = pltpu.CompilerParams(vmem_limit_bytes=16 * 1024 * 1024)
DMA = pltpu.SemaphoreType.DMA

STATE, LANE, BLOCK, AWAY, GAIN = 0, 1, 2, 3, 4
ROWS = 16


def times_transposed(rows, block):
    return lax.dot_general(rows, block, (((1,), (1,)), ((), ())), preferred_element_type=jnp.float32)


def hits(table, i, blocks, width):
    first_state = (lax.axis_index("net") * blocks + i) * width
    lane = lax.broadcasted_iota(jnp.int32, (table.shape[0], width), 1)
    return table[:, STATE : STATE + 1] == (lane + first_state).astype(jnp.float32)


def injected(table, step, hit):
    return jnp.where(hit, table[:, GAIN + step : GAIN + step + 1], 0.0)


def near_by(state_ref, cols_ref):
    return lambda i, k: state_ref[cols_ref[k, i]]


def own_sum(i, state_ref, jac_ref, near, table, step, hit=None):
    blocks, _, width = state_ref.shape
    if hit is None:
        hit = hits(table, i, blocks, width)
    kinds = jac_ref.shape[1]
    rows = [state_ref[i]] + [near(i, k) for k in range(kinds - 1)]
    row_blocks = [jac_ref[i, k] for k in range(kinds)]
    total = times_transposed(jnp.concatenate(rows, axis=1), jnp.concatenate(row_blocks, axis=1))
    return total + injected(table, step, hit)


def picked(blocks, marks):
    total = blocks[0] * marks[0]
    for block, mark in zip(blocks[1:], marks[1:]):
        total += block * mark
    return total


def marks_layout(n, blocks, kinds):
    sent = n * blocks
    near = sent + n * blocks
    row = near + blocks * (kinds - 1) * blocks
    return sent, near, row, row + 1 + -(row + 1) % 8


def make_marks(marks_ref, blocks, kinds, cols_ref, send_ref, recv_ref, live_ref):
    n = lax.axis_size("net")
    me = lax.axis_index("net")
    width = marks_ref.shape[1]
    lane = lax.broadcasted_iota(jnp.int32, (1, width), 1)
    sent, near, own_row, _ = marks_layout(n, blocks, kinds)

    def put(row, mask):
        marks_ref[pl.ds(row, 1)] = jnp.where(mask, 1.0, 0.0)

    for d in range(n):
        q = me ^ d
        for i in range(blocks):
            put(d * blocks + i, lane < jnp.where(recv_ref[0, q] == i, live_ref[0, q], 0))
            put(sent + d * blocks + i, lane < jnp.where(send_ref[0, q] == i, width, 0))
    for i in range(blocks):
        for k in range(kinds - 1):
            for j in range(blocks):
                put(near + (i * (kinds - 1) + k) * blocks + j, lane < jnp.where(cols_ref[k, i] == j, width, 0))
    marks_ref[pl.ds(own_row, 1)] = table_row(send_ref, me, width)


def add_coupled(incoming, block, live, recv, z_ref):
    mask = lax.broadcasted_iota(jnp.int32, z_ref.shape[1:], 1) < live
    z_ref[recv] += jnp.where(mask, times_transposed(incoming, block), 0.0)


def table_row(send_ref, partition, width):
    lane = lax.broadcasted_iota(jnp.int32, (1, width), 1)
    row = jnp.zeros((1, width), jnp.float32)
    for e in range(lax.axis_size("net")):
        row = jnp.where(lane == e, send_ref[0, partition ^ e].astype(jnp.float32), row)
    return row


def kept(table, rows):
    away, block = table[:, AWAY : AWAY + 1], table[:, BLOCK : BLOCK + 1]
    sent = jnp.broadcast_to(rows[0], (table.shape[0], rows[0].shape[1]))
    for d in range(1, len(rows)):
        sent = jnp.where(away == float(d), rows[d], sent)
    lane = lax.broadcasted_iota(jnp.int32, sent.shape, 1).astype(jnp.float32)
    return jnp.where(jnp.logical_or(away == lane, block == sent), 1.0, 0.0)


def second_kernel(*refs):
    jac_hbm, iface_hbm, *small, table_ref, marks_ref, state_ref = refs[:11]
    n = lax.axis_size("net")
    me = lax.axis_index("net")
    outgoing, refs = refs[11 : 10 + n], refs[10 + n :]
    jac_ref, iface_ref, *loaded, first_ref, sems = refs
    cols_ref, send_ref, recv_ref, live_ref, node_ref, gain_ref = loaded
    blocks, cols, width = state_ref.shape
    sources = [jac_hbm.at[1], iface_hbm.at[1, 0], *small]
    loads = [
        pltpu.make_async_copy(source, target, sems.at[i])
        for i, (source, target) in enumerate(zip(sources, [jac_ref, iface_ref, *loaded]))
    ]
    here = lax.axis_index("tm") == 0
    for load in loads[6:]:
        load.start()

    @pl.when(here)
    def _():
        for load in loads[:2]:
            load.start()

    for load in loads[2:6]:
        load.start()
    for load in loads[6:]:
        load.wait()
    node = node_ref[...]
    block_of = node // width
    rows = [
        node,
        node - block_of * width,
        block_of % blocks,
        (block_of // blocks) ^ me,
    ]
    steps = gain_ref.shape[0]
    fill = -(GAIN + steps) % 8
    rows = [row.astype(jnp.float32) for row in rows] + [gain_ref[...], jnp.zeros((fill, cols), jnp.float32)]
    table_ref[...] = jnp.concatenate(rows, axis=0).T

    @pl.when(here)
    def _():
        table = table_ref[...]
        hit = [hits(table, i, blocks, width) for i in range(blocks)]
        for i in range(blocks):
            first_ref[i] = injected(table, 0, hit[i]).astype(first_ref.dtype)
        lane = lax.broadcasted_iota(jnp.int32, (cols, width), 1).astype(jnp.float32)
        shot = jnp.where(lane == table[:, LANE : LANE + 1], table[:, GAIN : GAIN + 1], 0.0)
        away, block = table[:, AWAY : AWAY + 1], table[:, BLOCK : BLOCK + 1]
        for load in loads[2:6]:
            load.wait()
        mine = jnp.logical_or(away != 0.0, block == send_ref[0, me].astype(jnp.float32))
        shot = jnp.where(mine, shot, 0.0)
        live = recv = jnp.zeros_like(away)
        for d in range(n):
            live = jnp.where(away == float(d), live_ref[0, me ^ d].astype(jnp.float32), live)
            recv = jnp.where(away == float(d), recv_ref[0, me ^ d].astype(jnp.float32), recv)
        sent = [jnp.where(away == float(d), shot, 0.0).astype(first_ref.dtype) for d in range(n)]
        loads[1].wait()
        ifaces = jnp.concatenate([iface_ref[me ^ d] for d in range(n)], axis=1)
        coupled = times_transposed(jnp.concatenate(sent, axis=1), ifaces)
        coupled = jnp.where(lane < live, coupled, 0.0)
        loads[0].wait()
        for i in range(blocks):
            own = own_sum(i, first_ref, jac_ref, near_by(first_ref, cols_ref), table, 1, hit[i])
            state_ref[i] = (own + jnp.where(recv == float(i), coupled, 0.0)).astype(state_ref.dtype)
        for d in range(1, n):
            outgoing[d - 1][pl.ds(0, cols)] = state_ref[send_ref[0, me ^ d]]

    @pl.when(jnp.logical_not(here))
    def _():
        for load in loads[2:6]:
            load.wait()
        make_marks(marks_ref, blocks, jac_ref.shape[1], cols_ref, send_ref, recv_ref, live_ref)

    for d in range(1, n):
        row = table_row(send_ref, me ^ d, width).astype(state_ref.dtype)
        outgoing[d - 1][pl.ds(cols, ROWS)] = jnp.broadcast_to(row, (ROWS, width))


def write_copies(states, first, out_ref, sems):
    copies = []
    for s, state_ref in enumerate(states, first):
        width = state_ref.shape[2]
        for i in range(state_ref.shape[0]):
            copies.append(
                pltpu.make_async_copy(state_ref.at[i], out_ref.at[s, :, pl.ds(i * width, width)], sems.at[s, i])
            )
    return copies


def write(states, first, out_ref, sems):
    copies = write_copies(states, first, out_ref, sems)
    for copy in copies:
        copy.start()
    for copy in copies:
        copy.wait()


def own_kernel(step, state_ref, jac_ref, iface_ref, table_ref, marks_ref, z_ref):
    table = table_ref[...]
    n = lax.axis_size("net")
    blocks = state_ref.shape[0]
    kinds = jac_ref.shape[2]
    sent, near, _, _ = marks_layout(n, blocks, kinds)
    state = [state_ref[j] for j in range(blocks)]

    def pick(row):
        return picked(state, [marks_ref[pl.ds(row + j, 1)].astype(state_ref.dtype) for j in range(blocks)])

    def near_block(i, k):
        return pick(near + (i * (kinds - 1) + k) * blocks)

    @pl.when(lax.axis_index("tm") > 0)
    def _():
        term = times_transposed(pick(sent), iface_ref[step, 0, lax.axis_index("net")])
        for i in range(blocks):
            own = own_sum(i, state_ref, jac_ref.at[step], near_block, table, step)
            z_ref[i] = own + term * marks_ref[pl.ds(i, 1)]


def first_states(opening, handed, jac_ref, iface_ref, ints, table_ref, made_ref, z_ref):
    cols_ref, send_ref, recv_ref, live_ref = ints
    n = lax.axis_size("net")
    blocks, cols, width = z_ref.shape
    table = table_ref[...]
    made_ref[0] = jnp.zeros_like(made_ref[0])
    for i in range(blocks):
        z_ref[i] = own_sum(i, made_ref.at[0], jac_ref.at[0], near_by(made_ref.at[0], cols_ref), table, 0)
    for q in range(n):
        add_coupled(made_ref[0, 0], iface_ref[0, 0, q], live_ref[0, q], recv_ref[0, q], z_ref)
    made_ref[0] = z_ref[...].astype(made_ref.dtype)
    rows = [table_row(send_ref, lax.axis_index("net"), width)]
    rows += [block[cols : cols + 1].astype(jnp.float32) for block in handed]
    keep = kept(table, rows)[:, 0:1]
    for i in range(blocks):
        made_ref[1, i] = jnp.where(keep > 0.0, opening[i], jnp.zeros_like(opening[i]))
    return [made_ref.at[0], made_ref.at[1]]


def joined(sums, step, iface_ref, marks_ref, arrived, keep=None):
    me = lax.axis_index("net")
    blocks, cols = len(sums), sums[0].shape[0]
    if keep is not None:
        sums = [total * keep[:, 0:1] for total in sums]
    for d, block in enumerate(arrived, 1):
        term = times_transposed(block[pl.ds(0, cols)], iface_ref[step, 0, me ^ d])
        if keep is not None:
            term *= keep[:, d : d + 1]
        sums = [total + term * marks_ref[pl.ds(d * blocks + i, 1)] for i, total in enumerate(sums)]
    return [total.astype(jnp.bfloat16) for total in sums]


def give(made, marks_ref, state_ref, outgoing):
    blocks = len(made)
    n = lax.axis_size("net")
    sent = marks_layout(n, blocks, 1)[0]
    for i in range(blocks):
        state_ref[i] = made[i]
    for d in range(1, n) if outgoing else ():
        marks = [marks_ref[pl.ds(sent + d * blocks + j, 1)].astype(made[j].dtype) for j in range(blocks)]
        outgoing[d - 1][...] = picked(made, marks)


def exchange_order(n, handed):
    return [*range(n // 2, n), *range(n // 2 - 1, 0, -1)]


def by_distance(refs, handed):
    order = exchange_order(len(refs) + 1, handed)
    return [refs[order.index(d)] for d in range(1, len(refs) + 1)]


def join_kernel(step, fix, section, z_ref, iface_ref, table_ref, marks_ref, *refs):
    n = lax.axis_size("net")
    arrived, state_ref, outgoing = by_distance(refs[: n - 1], step == 0), refs[n - 1], refs[n:]
    blocks, cols, _ = z_ref.shape

    @pl.when(lax.axis_index("tm") == section)
    def _():
        keep = None
        if fix:
            rows = [marks_ref[pl.ds(marks_layout(n, blocks, fix)[2], 1)]]
            rows += [block[cols : cols + 1].astype(jnp.float32) for block in arrived]
            keep = kept(table_ref[...], rows)
        made = joined([z_ref[i] for i in range(blocks)], step, iface_ref, marks_ref, arrived, keep)
        give(made, marks_ref, state_ref, outgoing)


def write_kernel(step, section, firsts, before, state_ref, jac_ref, iface_ref, table_ref, marks_ref, *refs):
    n = lax.axis_size("net")
    *refs, sems = refs
    before, refs = refs[:before], refs[before:]
    if firsts:
        *refs, made_ref, acc_ref, cols_ref, send_ref, recv_ref, live_ref, load_sems = refs
        ints = [cols_ref, send_ref, recv_ref, live_ref]
        opening_ref, handed, sources, (z_ref, out_ref) = refs[0], refs[1:n], refs[n : n + 4], refs[n + 4 :]
    else:
        _, z_ref, out_ref = refs
    here = lax.axis_index("tm") == section

    @pl.when(here)
    def _():
        for copy in write_copies(before, 0, out_ref, sems):
            copy.start()

    own_kernel(step, state_ref, jac_ref, iface_ref, table_ref, marks_ref, z_ref)

    @pl.when(here)
    def _():
        for copy in write_copies(before, 0, out_ref, sems):
            copy.wait()

    if firsts:

        @pl.when(lax.axis_index("tm") == 0)
        def _():
            loads = [
                pltpu.make_async_copy(source, target, load_sems.at[i])
                for i, (source, target) in enumerate(zip(sources, ints))
            ]
            for load in loads:
                load.start()
            for load in loads:
                load.wait()
            made = first_states(opening_ref, handed, jac_ref, iface_ref, ints, table_ref, made_ref, acc_ref)
            write(made, 0, out_ref, sems)


def close_kernel(step, section, place, z_ref, iface_ref, marks_ref, *refs):
    n = lax.axis_size("net")
    arrived, (_, out_ref, state_ref, *outgoing, sems) = by_distance(refs[: n - 1], False), refs[n - 1 :]

    @pl.when(lax.axis_index("tm") == section)
    def _():
        sums = [z_ref[i] for i in range(z_ref.shape[0])]
        give(joined(sums, step, iface_ref, marks_ref, arrived), marks_ref, state_ref, outgoing)
        write([state_ref], place, out_ref, sems)


def local(jac, block_cols, iface_jac, iface_send, iface_recv, iface_live, ctrl_node, ctrl_gain):
    steps, blocks, kinds, width, _ = jac.shape
    cols = ctrl_node.shape[0]
    tm = lax.axis_size("tm")
    n = lax.axis_size("net")
    col_parts = lax.axis_size("cols")
    node = ctrl_node[None]
    near = block_cols.T
    bf16 = functools.partial(jax.ShapeDtypeStruct, dtype=jnp.bfloat16)
    f32 = functools.partial(jax.ShapeDtypeStruct, dtype=jnp.float32)
    whole, one = bf16((blocks, cols, width)), bf16((cols, width))
    table_rows = GAIN + steps + -(GAIN + steps) % 8
    written = bf16((steps, cols, blocks * width))

    pinned = [
        pltpu.with_memory_space_constraint(x, pltpu.HBM)
        for x in (jac, iface_jac, near, iface_send, iface_recv, iface_live, node, ctrl_gain)
    ]
    marks_rows = marks_layout(n, blocks, kinds)[-1]
    table, marks, state, *outgoing = pl.pallas_call(
        second_kernel,
        out_shape=[f32((cols, table_rows)), f32((marks_rows, width)), whole]
        + [bf16((cols + ROWS, width))] * (n - 1),
        in_specs=[HBM] * len(pinned),
        out_specs=[VMEM] * (n + 2),
        scratch_shapes=[
            pltpu.VMEM((blocks, kinds, width, width), jnp.bfloat16),
            pltpu.VMEM((n, width, width), jnp.bfloat16),
            *[pltpu.SMEM(x.shape, x.dtype) for x in (near, iface_send, iface_recv, iface_live)],
            *[pltpu.VMEM(x.shape, x.dtype) for x in (node, ctrl_gain)],
            pltpu.VMEM(whole.shape, jnp.bfloat16),
            DMA((len(pinned),)),
        ],
        compiler_params=LIMIT,
    )(*pinned)

    def own(state, step):
        return pl.pallas_call(
            functools.partial(own_kernel, step),
            out_shape=f32(whole.shape),
            in_specs=[VMEM] * 5,
            out_specs=VMEM,
            compiler_params=LIMIT,
        )(state, jac, iface_jac, table, marks)

    def join(z, step, fix, arrived, section):
        return pl.pallas_call(
            functools.partial(join_kernel, step, kinds if fix else 0, section),
            out_shape=[whole] + [one] * (n - 1),
            in_specs=[VMEM] * (n + 3),
            out_specs=[VMEM] * n,
            compiler_params=LIMIT,
        )(z, iface_jac, table, marks, *[arrived[d - 1] for d in exchange_order(n, step == 0)])

    def own_and_write(state, step, section, before, out):
        firsts = out is None
        arrays = [state, jac, iface_jac, table, marks, *before]
        specs = [VMEM] * len(arrays)
        scratch = [DMA((steps, blocks))]
        aliases = {}
        if firsts:
            arrays += [opening, *handed, *pinned[2:6]]
            specs += [VMEM] * n + [HBM] * 4
            scratch = [
                pltpu.VMEM((2, *whole.shape), jnp.bfloat16),
                pltpu.VMEM(whole.shape, jnp.float32),
                *[pltpu.SMEM(x.shape, x.dtype) for x in pinned[2:6]],
                DMA((4,)),
            ] + scratch
        else:
            aliases = {len(arrays): 1}
            arrays.append(out)
            specs.append(ANY)
        return pl.pallas_call(
            functools.partial(write_kernel, step, section, firsts, len(before)),
            out_shape=[f32(whole.shape), written],
            in_specs=specs,
            out_specs=[VMEM, ANY],
            input_output_aliases=aliases,
            scratch_shapes=scratch,
            compiler_params=LIMIT,
        )(*arrays)

    def close(z, step, arrived, section, out, send):
        ordered = [arrived[d - 1] for d in exchange_order(n, False)]
        return pl.pallas_call(
            functools.partial(close_kernel, step, section, steps - 1),
            out_shape=[written] + ([whole] + [one] * (n - 1) if send else []),
            in_specs=[VMEM] * (n + 2) + [ANY],
            out_specs=[ANY] + [VMEM] * (n if send else 0),
            input_output_aliases={n + 2: 0},
            scratch_shapes=([] if send else [pltpu.VMEM(whole.shape, jnp.bfloat16)]) + [DMA((steps, blocks))],
            compiler_params=LIMIT,
        )(z, iface_jac, marks, *ordered, out)

    def swap(block, first, second, d):
        other = {first: second, second: first}
        pairs = []
        for a in range(tm):
            for q in range(n):
                for c in range(col_parts):
                    to = (other[a] * n + (q ^ d)) * col_parts + c if a in other else (a * n + q) * col_parts + (c ^ 1)
                    pairs.append(((a * n + q) * col_parts + c, to))
        return lax.ppermute(block, ("tm", "net", "cols"), pairs)

    def exchange(outgoing, first, second):
        return [swap(outgoing[d - 1], first, second, d) for d in range(1, n)]

    opening = state
    out = None
    for r in range(1, tm):
        arrived = exchange(outgoing, r - 1, r)
        state = swap(state, r - 1, r, 0)
        if r == 1:
            handed = arrived
        before = []
        for s in range(steps):
            fix = r == 1 and s == 0
            if s > 0:
                arrived = exchange(outgoing, r, r)
            if s < steps - 1:
                state, *outgoing = join(own(state, s), s, fix, arrived, r)
                before.append(state)
            else:
                z, out = own_and_write(state, s, r, before, out)
                out, *rest = close(z, s, arrived, r, out, r < tm - 1)
                state, *outgoing = rest or [None]
    return out


def solution(mesh):
    return jax.shard_map(
        local,
        mesh=mesh,
        in_specs=(
            P("tm", "net", None, None, None),
            P("net", None),
            P("tm", "net", None, None, None),
            P("net", None),
            P("net", None),
            P("net", None),
            P("cols"),
            P("tm", "cols"),
        ),
        out_specs=P("tm", "cols", "net"),
        check_vma=False,
    )
```

```python
import functools

import jax
import jax.numpy as jnp
from jax import lax
from jax.experimental import pallas as pl
from jax.experimental.pallas import tpu as pltpu
from jax.sharding import PartitionSpec as P

VMEM = pl.BlockSpec(memory_space=pltpu.VMEM)
SMEM = pl.BlockSpec(memory_space=pltpu.SMEM)
HBM = pl.BlockSpec(memory_space=pltpu.HBM)
ANY = pl.BlockSpec(memory_space=pl.ANY)
LIMIT = pltpu.CompilerParams(vmem_limit_bytes=16 * 1024 * 1024)
DMA = pltpu.SemaphoreType.DMA

STATE, LANE, BLOCK, AWAY, GAIN = 0, 1, 2, 3, 4
ROWS = 16


def times_transposed(rows, block):
    return lax.dot_general(rows, block, (((1,), (1,)), ((), ())), preferred_element_type=jnp.float32)


def hits(table, i, blocks, width):
    first_state = (lax.axis_index("net") * blocks + i) * width
    lane = lax.broadcasted_iota(jnp.int32, (table.shape[0], width), 1)
    return table[:, STATE : STATE + 1] == (lane + first_state).astype(jnp.float32)


def injected(table, step, hit):
    return jnp.where(hit, table[:, GAIN + step : GAIN + step + 1], 0.0)


def near_by(state_ref, cols_ref):
    return lambda i, k: state_ref[cols_ref[k, i]]


def own_sum(i, state_ref, jac_ref, near, table, step, hit=None):
    blocks, _, width = state_ref.shape
    if hit is None:
        hit = hits(table, i, blocks, width)
    kinds = jac_ref.shape[1]
    rows = [state_ref[i]] + [near(i, k) for k in range(kinds - 1)]
    row_blocks = [jac_ref[i, k] for k in range(kinds)]
    total = times_transposed(jnp.concatenate(rows, axis=1), jnp.concatenate(row_blocks, axis=1))
    return total + injected(table, step, hit)


def picked(blocks, marks):
    total = blocks[0] * marks[0]
    for block, mark in zip(blocks[1:], marks[1:]):
        total += block * mark
    return total


def marks_layout(n, blocks, kinds):
    sent = n * blocks
    near = sent + n * blocks
    row = near + blocks * (kinds - 1) * blocks
    return sent, near, row, row + 1 + -(row + 1) % 8


def make_marks(marks_ref, blocks, kinds, cols_ref, send_ref, recv_ref, live_ref):
    n = lax.axis_size("net")
    me = lax.axis_index("net")
    width = marks_ref.shape[1]
    lane = lax.broadcasted_iota(jnp.int32, (1, width), 1)
    sent, near, own_row, _ = marks_layout(n, blocks, kinds)

    def put(row, mask):
        marks_ref[pl.ds(row, 1)] = jnp.where(mask, 1.0, 0.0)

    for d in range(n):
        q = me ^ d
        for i in range(blocks):
            put(d * blocks + i, lane < jnp.where(recv_ref[0, q] == i, live_ref[0, q], 0))
            put(sent + d * blocks + i, lane < jnp.where(send_ref[0, q] == i, width, 0))
    for i in range(blocks):
        for k in range(kinds - 1):
            for j in range(blocks):
                put(near + (i * (kinds - 1) + k) * blocks + j, lane < jnp.where(cols_ref[k, i] == j, width, 0))
    marks_ref[pl.ds(own_row, 1)] = table_row(send_ref, me, width)


def add_coupled(incoming, block, live, recv, z_ref):
    mask = lax.broadcasted_iota(jnp.int32, z_ref.shape[1:], 1) < live
    z_ref[recv] += jnp.where(mask, times_transposed(incoming, block), 0.0)


def table_row(send_ref, partition, width):
    lane = lax.broadcasted_iota(jnp.int32, (1, width), 1)
    row = jnp.zeros((1, width), jnp.float32)
    for e in range(lax.axis_size("net")):
        row = jnp.where(lane == e, send_ref[0, partition ^ e].astype(jnp.float32), row)
    return row


def kept(table, rows):
    away, block = table[:, AWAY : AWAY + 1], table[:, BLOCK : BLOCK + 1]
    sent = jnp.broadcast_to(rows[0], (table.shape[0], rows[0].shape[1]))
    for d in range(1, len(rows)):
        sent = jnp.where(away == float(d), rows[d], sent)
    lane = lax.broadcasted_iota(jnp.int32, sent.shape, 1).astype(jnp.float32)
    return jnp.where(jnp.logical_or(away == lane, block == sent), 1.0, 0.0)


def second_kernel(*refs):
    jac_hbm, iface_hbm, *small, table_ref, marks_ref, state_ref = refs[:11]
    n = lax.axis_size("net")
    me = lax.axis_index("net")
    outgoing, refs = refs[11 : 10 + n], refs[10 + n :]
    jac_ref, iface_ref, *loaded, first_ref, sems = refs
    cols_ref, send_ref, recv_ref, live_ref, node_ref, gain_ref = loaded
    blocks, cols, width = state_ref.shape
    sources = [jac_hbm.at[1], iface_hbm.at[1, 0], *small]
    loads = [
        pltpu.make_async_copy(source, target, sems.at[i])
        for i, (source, target) in enumerate(zip(sources, [jac_ref, iface_ref, *loaded]))
    ]
    here = lax.axis_index("tm") == 0
    for load in loads[6:]:
        load.start()

    @pl.when(here)
    def _():
        for load in loads[:2]:
            load.start()

    for load in loads[2:6]:
        load.start()
    for load in loads[6:]:
        load.wait()
    node = node_ref[...]
    block_of = node // width
    rows = [
        node,
        node - block_of * width,
        block_of % blocks,
        (block_of // blocks) ^ me,
    ]
    steps = gain_ref.shape[0]
    fill = -(GAIN + steps) % 8
    rows = [row.astype(jnp.float32) for row in rows] + [gain_ref[...], jnp.zeros((fill, cols), jnp.float32)]
    table_ref[...] = jnp.concatenate(rows, axis=0).T

    @pl.when(here)
    def _():
        table = table_ref[...]
        hit = [hits(table, i, blocks, width) for i in range(blocks)]
        for i in range(blocks):
            first_ref[i] = injected(table, 0, hit[i]).astype(first_ref.dtype)
        lane = lax.broadcasted_iota(jnp.int32, (cols, width), 1).astype(jnp.float32)
        shot = jnp.where(lane == table[:, LANE : LANE + 1], table[:, GAIN : GAIN + 1], 0.0)
        away, block = table[:, AWAY : AWAY + 1], table[:, BLOCK : BLOCK + 1]
        for load in loads[2:6]:
            load.wait()
        mine = jnp.logical_or(away != 0.0, block == send_ref[0, me].astype(jnp.float32))
        shot = jnp.where(mine, shot, 0.0)
        live = recv = jnp.zeros_like(away)
        for d in range(n):
            live = jnp.where(away == float(d), live_ref[0, me ^ d].astype(jnp.float32), live)
            recv = jnp.where(away == float(d), recv_ref[0, me ^ d].astype(jnp.float32), recv)
        sent = [jnp.where(away == float(d), shot, 0.0).astype(first_ref.dtype) for d in range(n)]
        loads[1].wait()
        ifaces = jnp.concatenate([iface_ref[me ^ d] for d in range(n)], axis=1)
        coupled = times_transposed(jnp.concatenate(sent, axis=1), ifaces)
        coupled = jnp.where(lane < live, coupled, 0.0)
        loads[0].wait()
        for i in range(blocks):
            own = own_sum(i, first_ref, jac_ref, near_by(first_ref, cols_ref), table, 1, hit[i])
            state_ref[i] = (own + jnp.where(recv == float(i), coupled, 0.0)).astype(state_ref.dtype)
        for d in range(1, n):
            outgoing[d - 1][pl.ds(0, cols)] = state_ref[send_ref[0, me ^ d]]

    @pl.when(jnp.logical_not(here))
    def _():
        for load in loads[2:6]:
            load.wait()
        make_marks(marks_ref, blocks, jac_ref.shape[1], cols_ref, send_ref, recv_ref, live_ref)

    for d in range(1, n):
        row = table_row(send_ref, me ^ d, width).astype(state_ref.dtype)
        outgoing[d - 1][pl.ds(cols, ROWS)] = jnp.broadcast_to(row, (ROWS, width))


def write_copies(states, first, out_ref, sems):
    copies = []
    for s, state_ref in enumerate(states, first):
        width = state_ref.shape[2]
        for i in range(state_ref.shape[0]):
            copies.append(
                pltpu.make_async_copy(state_ref.at[i], out_ref.at[s, :, pl.ds(i * width, width)], sems.at[s, i])
            )
    return copies


def write(states, first, out_ref, sems):
    copies = write_copies(states, first, out_ref, sems)
    for copy in copies:
        copy.start()
    for copy in copies:
        copy.wait()


def own_kernel(step, state_ref, jac_ref, iface_ref, table_ref, marks_ref, z_ref):
    table = table_ref[...]
    n = lax.axis_size("net")
    blocks = state_ref.shape[0]
    kinds = jac_ref.shape[2]
    sent, near, _, _ = marks_layout(n, blocks, kinds)
    state = [state_ref[j] for j in range(blocks)]

    def pick(row):
        return picked(state, [marks_ref[pl.ds(row + j, 1)].astype(state_ref.dtype) for j in range(blocks)])

    def near_block(i, k):
        return pick(near + (i * (kinds - 1) + k) * blocks)

    @pl.when(lax.axis_index("tm") > 0)
    def _():
        term = times_transposed(pick(sent), iface_ref[step, 0, lax.axis_index("net")])
        for i in range(blocks):
            own = own_sum(i, state_ref, jac_ref.at[step], near_block, table, step)
            z_ref[i] = own + term * marks_ref[pl.ds(i, 1)]


def first_states(opening, handed, jac_ref, iface_ref, ints, table_ref, made_ref, z_ref):
    cols_ref, send_ref, recv_ref, live_ref = ints
    n = lax.axis_size("net")
    blocks, cols, width = z_ref.shape
    table = table_ref[...]
    made_ref[0] = jnp.zeros_like(made_ref[0])
    for i in range(blocks):
        z_ref[i] = own_sum(i, made_ref.at[0], jac_ref.at[0], near_by(made_ref.at[0], cols_ref), table, 0)
    for q in range(n):
        add_coupled(made_ref[0, 0], iface_ref[0, 0, q], live_ref[0, q], recv_ref[0, q], z_ref)
    made_ref[0] = z_ref[...].astype(made_ref.dtype)
    rows = [table_row(send_ref, lax.axis_index("net"), width)]
    rows += [block[cols : cols + 1].astype(jnp.float32) for block in handed]
    keep = kept(table, rows)[:, 0:1]
    for i in range(blocks):
        made_ref[1, i] = jnp.where(keep > 0.0, opening[i], jnp.zeros_like(opening[i]))
    return [made_ref.at[0], made_ref.at[1]]


def joined(sums, step, iface_ref, marks_ref, arrived, keep=None):
    me = lax.axis_index("net")
    blocks, cols = len(sums), sums[0].shape[0]
    if keep is not None:
        sums = [total * keep[:, 0:1] for total in sums]
    for d, block in enumerate(arrived, 1):
        term = times_transposed(block[pl.ds(0, cols)], iface_ref[step, 0, me ^ d])
        if keep is not None:
            term *= keep[:, d : d + 1]
        sums = [total + term * marks_ref[pl.ds(d * blocks + i, 1)] for i, total in enumerate(sums)]
    return [total.astype(jnp.bfloat16) for total in sums]


def give(made, marks_ref, state_ref, outgoing):
    blocks = len(made)
    n = lax.axis_size("net")
    sent = marks_layout(n, blocks, 1)[0]
    for i in range(blocks):
        state_ref[i] = made[i]
    for d in range(1, n) if outgoing else ():
        marks = [marks_ref[pl.ds(sent + d * blocks + j, 1)].astype(made[j].dtype) for j in range(blocks)]
        outgoing[d - 1][...] = picked(made, marks)


def exchange_order(n, handed):
    return [1, *range(n - 1, 1, -1)] if handed else list(range(n - 1, 0, -1))


def by_distance(refs, handed):
    order = exchange_order(len(refs) + 1, handed)
    return [refs[order.index(d)] for d in range(1, len(refs) + 1)]


def join_kernel(step, fix, section, z_ref, iface_ref, table_ref, marks_ref, *refs):
    n = lax.axis_size("net")
    arrived, state_ref, outgoing = by_distance(refs[: n - 1], step == 0), refs[n - 1], refs[n:]
    blocks, cols, _ = z_ref.shape

    @pl.when(lax.axis_index("tm") == section)
    def _():
        keep = None
        if fix:
            rows = [marks_ref[pl.ds(marks_layout(n, blocks, fix)[2], 1)]]
            rows += [block[cols : cols + 1].astype(jnp.float32) for block in arrived]
            keep = kept(table_ref[...], rows)
        made = joined([z_ref[i] for i in range(blocks)], step, iface_ref, marks_ref, arrived, keep)
        give(made, marks_ref, state_ref, outgoing)


def write_kernel(step, section, firsts, before, state_ref, jac_ref, iface_ref, table_ref, marks_ref, *refs):
    n = lax.axis_size("net")
    *refs, sems = refs
    before, refs = refs[:before], refs[before:]
    if firsts:
        *refs, made_ref, acc_ref, cols_ref, send_ref, recv_ref, live_ref, load_sems = refs
        ints = [cols_ref, send_ref, recv_ref, live_ref]
        opening_ref, handed, sources, (z_ref, out_ref) = refs[0], refs[1:n], refs[n : n + 4], refs[n + 4 :]
    else:
        _, z_ref, out_ref = refs
    here = lax.axis_index("tm") == section

    @pl.when(here)
    def _():
        for copy in write_copies(before, 0, out_ref, sems):
            copy.start()

    own_kernel(step, state_ref, jac_ref, iface_ref, table_ref, marks_ref, z_ref)

    @pl.when(here)
    def _():
        for copy in write_copies(before, 0, out_ref, sems):
            copy.wait()

    if firsts:

        @pl.when(lax.axis_index("tm") == 0)
        def _():
            loads = [
                pltpu.make_async_copy(source, target, load_sems.at[i])
                for i, (source, target) in enumerate(zip(sources, ints))
            ]
            for load in loads:
                load.start()
            for load in loads:
                load.wait()
            made = first_states(opening_ref, handed, jac_ref, iface_ref, ints, table_ref, made_ref, acc_ref)
            write(made, 0, out_ref, sems)


def close_kernel(step, section, place, z_ref, iface_ref, marks_ref, *refs):
    n = lax.axis_size("net")
    arrived, (_, out_ref, state_ref, *outgoing, sems) = by_distance(refs[: n - 1], False), refs[n - 1 :]

    @pl.when(lax.axis_index("tm") == section)
    def _():
        sums = [z_ref[i] for i in range(z_ref.shape[0])]
        give(joined(sums, step, iface_ref, marks_ref, arrived), marks_ref, state_ref, outgoing)
        write([state_ref], place, out_ref, sems)


def local(jac, block_cols, iface_jac, iface_send, iface_recv, iface_live, ctrl_node, ctrl_gain):
    steps, blocks, kinds, width, _ = jac.shape
    cols = ctrl_node.shape[0]
    tm = lax.axis_size("tm")
    n = lax.axis_size("net")
    col_parts = lax.axis_size("cols")
    node = ctrl_node[None]
    near = block_cols.T
    bf16 = functools.partial(jax.ShapeDtypeStruct, dtype=jnp.bfloat16)
    f32 = functools.partial(jax.ShapeDtypeStruct, dtype=jnp.float32)
    whole, one = bf16((blocks, cols, width)), bf16((cols, width))
    table_rows = GAIN + steps + -(GAIN + steps) % 8
    written = bf16((steps, cols, blocks * width))

    pinned = [
        pltpu.with_memory_space_constraint(x, pltpu.HBM)
        for x in (jac, iface_jac, near, iface_send, iface_recv, iface_live, node, ctrl_gain)
    ]
    marks_rows = marks_layout(n, blocks, kinds)[-1]
    table, marks, state, *outgoing = pl.pallas_call(
        second_kernel,
        out_shape=[f32((cols, table_rows)), f32((marks_rows, width)), whole]
        + [bf16((cols + ROWS, width))] * (n - 1),
        in_specs=[HBM] * len(pinned),
        out_specs=[VMEM] * (n + 2),
        scratch_shapes=[
            pltpu.VMEM((blocks, kinds, width, width), jnp.bfloat16),
            pltpu.VMEM((n, width, width), jnp.bfloat16),
            *[pltpu.SMEM(x.shape, x.dtype) for x in (near, iface_send, iface_recv, iface_live)],
            *[pltpu.VMEM(x.shape, x.dtype) for x in (node, ctrl_gain)],
            pltpu.VMEM(whole.shape, jnp.bfloat16),
            DMA((len(pinned),)),
        ],
        compiler_params=LIMIT,
    )(*pinned)

    def own(state, step):
        return pl.pallas_call(
            functools.partial(own_kernel, step),
            out_shape=f32(whole.shape),
            in_specs=[VMEM] * 5,
            out_specs=VMEM,
            compiler_params=LIMIT,
        )(state, jac, iface_jac, table, marks)

    def join(z, step, fix, arrived, section):
        return pl.pallas_call(
            functools.partial(join_kernel, step, kinds if fix else 0, section),
            out_shape=[whole] + [one] * (n - 1),
            in_specs=[VMEM] * (n + 3),
            out_specs=[VMEM] * n,
            compiler_params=LIMIT,
        )(z, iface_jac, table, marks, *[arrived[d - 1] for d in exchange_order(n, step == 0)])

    def own_and_write(state, step, section, before, out):
        firsts = out is None
        arrays = [state, jac, iface_jac, table, marks, *before]
        specs = [VMEM] * len(arrays)
        scratch = [DMA((steps, blocks))]
        aliases = {}
        if firsts:
            arrays += [opening, *handed, *pinned[2:6]]
            specs += [VMEM] * n + [HBM] * 4
            scratch = [
                pltpu.VMEM((2, *whole.shape), jnp.bfloat16),
                pltpu.VMEM(whole.shape, jnp.float32),
                *[pltpu.SMEM(x.shape, x.dtype) for x in pinned[2:6]],
                DMA((4,)),
            ] + scratch
        else:
            aliases = {len(arrays): 1}
            arrays.append(out)
            specs.append(ANY)
        return pl.pallas_call(
            functools.partial(write_kernel, step, section, firsts, len(before)),
            out_shape=[f32(whole.shape), written],
            in_specs=specs,
            out_specs=[VMEM, ANY],
            input_output_aliases=aliases,
            scratch_shapes=scratch,
            compiler_params=LIMIT,
        )(*arrays)

    def close(z, step, arrived, section, out, send):
        ordered = [arrived[d - 1] for d in exchange_order(n, False)]
        return pl.pallas_call(
            functools.partial(close_kernel, step, section, steps - 1),
            out_shape=[written] + ([whole] + [one] * (n - 1) if send else []),
            in_specs=[VMEM] * (n + 2) + [ANY],
            out_specs=[ANY] + [VMEM] * (n if send else 0),
            input_output_aliases={n + 2: 0},
            scratch_shapes=([] if send else [pltpu.VMEM(whole.shape, jnp.bfloat16)]) + [DMA((steps, blocks))],
            compiler_params=LIMIT,
        )(z, iface_jac, marks, *ordered, out)

    def swap(block, first, second, d):
        other = {first: second, second: first}
        pairs = []
        for a in range(tm):
            for q in range(n):
                for c in range(col_parts):
                    to = (other[a] * n + (q ^ d)) * col_parts + c if a in other else (a * n + q) * col_parts + (c ^ 1)
                    pairs.append(((a * n + q) * col_parts + c, to))
        return lax.ppermute(block, ("tm", "net", "cols"), pairs)

    def exchange(outgoing, first, second):
        return [swap(outgoing[d - 1], first, second, d) for d in range(1, n)]

    opening = state
    out = None
    for r in range(1, tm):
        arrived = exchange(outgoing, r - 1, r)
        state = swap(state, r - 1, r, 0)
        if r == 1:
            handed = arrived
        before = []
        for s in range(steps):
            fix = r == 1 and s == 0
            if s > 0:
                arrived = exchange(outgoing, r, r)
            if s < steps - 1:
                state, *outgoing = join(own(state, s), s, fix, arrived, r)
                before.append(state)
            else:
                z, out = own_and_write(state, s, r, before, out)
                out, *rest = close(z, s, arrived, r, out, r < tm - 1)
                state, *outgoing = rest or [None]
    return out


def solution(mesh):
    return jax.shard_map(
        local,
        mesh=mesh,
        in_specs=(
            P("tm", "net", None, None, None),
            P("net", None),
            P("tm", "net", None, None, None),
            P("net", None),
            P("net", None),
            P("net", None),
            P("cols"),
            P("tm", "cols"),
        ),
        out_specs=P("tm", "cols", "net"),
        check_vma=False,
    )
```

```python
import functools

import jax
import jax.numpy as jnp
from jax import lax
from jax.experimental import pallas as pl
from jax.experimental.pallas import tpu as pltpu
from jax.sharding import PartitionSpec as P

VMEM = pl.BlockSpec(memory_space=pltpu.VMEM)
SMEM = pl.BlockSpec(memory_space=pltpu.SMEM)
HBM = pl.BlockSpec(memory_space=pltpu.HBM)
ANY = pl.BlockSpec(memory_space=pl.ANY)
LIMIT = pltpu.CompilerParams(vmem_limit_bytes=16 * 1024 * 1024)
DMA = pltpu.SemaphoreType.DMA

STATE, LANE, BLOCK, AWAY, GAIN = 0, 1, 2, 3, 4
ROWS = 16


def times_transposed(rows, block):
    return lax.dot_general(rows, block, (((1,), (1,)), ((), ())), preferred_element_type=jnp.float32)


def hits(table, i, blocks, width):
    first_state = (lax.axis_index("net") * blocks + i) * width
    lane = lax.broadcasted_iota(jnp.int32, (table.shape[0], width), 1)
    return table[:, STATE : STATE + 1] == (lane + first_state).astype(jnp.float32)


def injected(table, step, hit):
    return jnp.where(hit, table[:, GAIN + step : GAIN + step + 1], 0.0)


def near_by(state_ref, cols_ref):
    return lambda i, k: state_ref[cols_ref[k, i]]


def products(i, state_ref, jac_ref, near):
    kinds = jac_ref.shape[1]
    rows = [state_ref[i]] + [near(i, k) for k in range(kinds - 1)]
    row_blocks = [jac_ref[i, k] for k in range(kinds)]
    return times_transposed(jnp.concatenate(rows, axis=1), jnp.concatenate(row_blocks, axis=1))


def own_sum(i, state_ref, jac_ref, near, table, step):
    blocks, _, width = state_ref.shape
    return products(i, state_ref, jac_ref, near) + injected(table, step, hits(table, i, blocks, width))


def picked(blocks, marks):
    total = blocks[0] * marks[0]
    for block, mark in zip(blocks[1:], marks[1:]):
        total += block * mark
    return total


def marks_layout(n, blocks, kinds):
    sent = n * blocks
    near = sent + n * blocks
    row = near + blocks * (kinds - 1) * blocks
    return sent, near, row, row + 1 + -(row + 1) % 8


def make_marks(marks_ref, blocks, kinds, cols_ref, send_ref, recv_ref, live_ref):
    n = lax.axis_size("net")
    me = lax.axis_index("net")
    width = marks_ref.shape[1]
    lane = lax.broadcasted_iota(jnp.int32, (1, width), 1)
    sent, near, own_row, _ = marks_layout(n, blocks, kinds)

    def put(row, mask):
        marks_ref[pl.ds(row, 1)] = jnp.where(mask, 1.0, 0.0)

    for d in range(n):
        q = me ^ d
        for i in range(blocks):
            put(d * blocks + i, lane < jnp.where(recv_ref[0, q] == i, live_ref[0, q], 0))
            put(sent + d * blocks + i, lane < jnp.where(send_ref[0, q] == i, width, 0))
    for i in range(blocks):
        for k in range(kinds - 1):
            for j in range(blocks):
                put(near + (i * (kinds - 1) + k) * blocks + j, lane < jnp.where(cols_ref[k, i] == j, width, 0))
    marks_ref[pl.ds(own_row, 1)] = table_row(send_ref, me, width)


def add_coupled(incoming, block, live, recv, z_ref):
    mask = lax.broadcasted_iota(jnp.int32, z_ref.shape[1:], 1) < live
    z_ref[recv] += jnp.where(mask, times_transposed(incoming, block), 0.0)


def table_row(send_ref, partition, width):
    lane = lax.broadcasted_iota(jnp.int32, (1, width), 1)
    row = jnp.zeros((1, width), jnp.float32)
    for e in range(lax.axis_size("net")):
        row = jnp.where(lane == e, send_ref[0, partition ^ e].astype(jnp.float32), row)
    return row


def kept(table, rows):
    away, block = table[:, AWAY : AWAY + 1], table[:, BLOCK : BLOCK + 1]
    sent = jnp.broadcast_to(rows[0], (table.shape[0], rows[0].shape[1]))
    for d in range(1, len(rows)):
        sent = jnp.where(away == float(d), rows[d], sent)
    lane = lax.broadcasted_iota(jnp.int32, sent.shape, 1).astype(jnp.float32)
    return jnp.where(jnp.logical_or(away == lane, block == sent), 1.0, 0.0)


def second_kernel(*refs):
    jac_hbm, iface_hbm, *small, table_ref, marks_ref, state_ref = refs[:11]
    n = lax.axis_size("net")
    me = lax.axis_index("net")
    outgoing, refs = refs[11 : 10 + n], refs[10 + n :]
    jac_ref, iface_ref, *loaded, first_ref, sems = refs
    cols_ref, send_ref, recv_ref, live_ref, node_ref, gain_ref = loaded
    blocks, cols, width = state_ref.shape
    sources = [jac_hbm.at[1], iface_hbm.at[1, 0], *small]
    loads = [
        pltpu.make_async_copy(source, target, sems.at[i])
        for i, (source, target) in enumerate(zip(sources, [jac_ref, iface_ref, *loaded]))
    ]
    here = lax.axis_index("tm") == 0
    for load in loads[6:]:
        load.start()

    @pl.when(here)
    def _():
        for load in loads[:2]:
            load.start()

    for load in loads[2:6]:
        load.start()
    for load in loads[6:]:
        load.wait()
    node = node_ref[...]
    block_of = node // width
    rows = [
        node,
        node - block_of * width,
        block_of % blocks,
        (block_of // blocks) ^ me,
    ]
    steps = gain_ref.shape[0]
    fill = -(GAIN + steps) % 8
    rows = [row.astype(jnp.float32) for row in rows] + [gain_ref[...], jnp.zeros((fill, cols), jnp.float32)]
    table_ref[...] = jnp.concatenate(rows, axis=0).T

    @pl.when(here)
    def _():
        table = table_ref[...]

        def spread(column):
            return jnp.broadcast_to(column, (cols, width))

        lane = lax.broadcasted_iota(jnp.int32, (cols, width), 1).astype(jnp.float32)
        place = spread(table[:, STATE : STATE + 1] - (me * blocks * width).astype(jnp.float32)) - lane
        gain = spread(table[:, GAIN : GAIN + 1])
        later_gain = spread(table[:, GAIN + 1 : GAIN + 2])
        hit = [place == float(i * width) for i in range(blocks)]
        for i in range(blocks):
            first_ref[i] = jnp.where(hit[i], gain, 0.0).astype(first_ref.dtype)
        away, block = table[:, AWAY : AWAY + 1], table[:, BLOCK : BLOCK + 1]
        for load in loads[2:6]:
            load.wait()
        mine = jnp.logical_or(away != 0.0, block == send_ref[0, me].astype(jnp.float32))
        shot_lane = spread(jnp.where(mine, table[:, LANE : LANE + 1], -1.0))
        shot = jnp.where(lane == shot_lane, gain, 0.0)
        live = recv = jnp.zeros_like(away)
        for d in range(n):
            live = jnp.where(away == float(d), live_ref[0, me ^ d].astype(jnp.float32), live)
            recv = jnp.where(away == float(d), recv_ref[0, me ^ d].astype(jnp.float32), recv)
        away, live, recv = spread(away), spread(live), spread(recv)
        sent = [jnp.where(away == float(d), shot, 0.0).astype(first_ref.dtype) for d in range(n)]
        loads[1].wait()
        ifaces = jnp.concatenate([iface_ref[me ^ d] for d in range(n)], axis=1)
        coupled = times_transposed(jnp.concatenate(sent, axis=1), ifaces)
        coupled = jnp.where(lane < live, coupled, 0.0)
        loads[0].wait()
        for i in range(blocks):
            own = products(i, first_ref, jac_ref, near_by(first_ref, cols_ref))
            own += jnp.where(hit[i], later_gain, 0.0)
            state_ref[i] = (own + jnp.where(recv == float(i), coupled, 0.0)).astype(state_ref.dtype)
        for d in range(1, n):
            outgoing[d - 1][pl.ds(0, cols)] = state_ref[send_ref[0, me ^ d]]

    @pl.when(jnp.logical_not(here))
    def _():
        for load in loads[2:6]:
            load.wait()
        make_marks(marks_ref, blocks, jac_ref.shape[1], cols_ref, send_ref, recv_ref, live_ref)

    for d in range(1, n):
        row = table_row(send_ref, me ^ d, width).astype(state_ref.dtype)
        outgoing[d - 1][pl.ds(cols, ROWS)] = jnp.broadcast_to(row, (ROWS, width))


def write_copies(states, first, out_ref, sems):
    copies = []
    for s, state_ref in enumerate(states, first):
        width = state_ref.shape[2]
        for i in range(state_ref.shape[0]):
            copies.append(
                pltpu.make_async_copy(state_ref.at[i], out_ref.at[s, :, pl.ds(i * width, width)], sems.at[s, i])
            )
    return copies


def write(states, first, out_ref, sems):
    copies = write_copies(states, first, out_ref, sems)
    for copy in copies:
        copy.start()
    for copy in copies:
        copy.wait()


def own_kernel(step, state_ref, jac_ref, iface_ref, table_ref, marks_ref, z_ref):
    table = table_ref[...]
    n = lax.axis_size("net")
    blocks = state_ref.shape[0]
    kinds = jac_ref.shape[2]
    sent, near, _, _ = marks_layout(n, blocks, kinds)
    state = [state_ref[j] for j in range(blocks)]

    def pick(row):
        return picked(state, [marks_ref[pl.ds(row + j, 1)].astype(state_ref.dtype) for j in range(blocks)])

    def near_block(i, k):
        return pick(near + (i * (kinds - 1) + k) * blocks)

    @pl.when(lax.axis_index("tm") > 0)
    def _():
        term = times_transposed(pick(sent), iface_ref[step, 0, lax.axis_index("net")])
        for i in range(blocks):
            own = own_sum(i, state_ref, jac_ref.at[step], near_block, table, step)
            z_ref[i] = own + term * marks_ref[pl.ds(i, 1)]


def first_states(opening, handed, jac_ref, iface_ref, ints, table_ref, made_ref, z_ref):
    cols_ref, send_ref, recv_ref, live_ref = ints
    n = lax.axis_size("net")
    blocks, cols, width = z_ref.shape
    table = table_ref[...]
    made_ref[0] = jnp.zeros_like(made_ref[0])
    for i in range(blocks):
        z_ref[i] = own_sum(i, made_ref.at[0], jac_ref.at[0], near_by(made_ref.at[0], cols_ref), table, 0)
    for q in range(n):
        add_coupled(made_ref[0, 0], iface_ref[0, 0, q], live_ref[0, q], recv_ref[0, q], z_ref)
    made_ref[0] = z_ref[...].astype(made_ref.dtype)
    rows = [table_row(send_ref, lax.axis_index("net"), width)]
    rows += [block[cols : cols + 1].astype(jnp.float32) for block in handed]
    keep = kept(table, rows)[:, 0:1]
    for i in range(blocks):
        made_ref[1, i] = jnp.where(keep > 0.0, opening[i], jnp.zeros_like(opening[i]))
    return [made_ref.at[0], made_ref.at[1]]


def joined(sums, step, iface_ref, marks_ref, arrived, keep=None):
    me = lax.axis_index("net")
    blocks, cols = len(sums), sums[0].shape[0]
    if keep is not None:
        sums = [total * keep[:, 0:1] for total in sums]
    for d, block in enumerate(arrived, 1):
        term = times_transposed(block[pl.ds(0, cols)], iface_ref[step, 0, me ^ d])
        if keep is not None:
            term *= keep[:, d : d + 1]
        sums = [total + term * marks_ref[pl.ds(d * blocks + i, 1)] for i, total in enumerate(sums)]
    return [total.astype(jnp.bfloat16) for total in sums]


def give(made, marks_ref, state_ref, outgoing):
    blocks = len(made)
    n = lax.axis_size("net")
    sent = marks_layout(n, blocks, 1)[0]
    for i in range(blocks):
        state_ref[i] = made[i]
    for d in range(1, n) if outgoing else ():
        marks = [marks_ref[pl.ds(sent + d * blocks + j, 1)].astype(made[j].dtype) for j in range(blocks)]
        outgoing[d - 1][...] = picked(made, marks)


def exchange_order(n, handed):
    return [*range(n // 2, n), *range(n // 2 - 1, 0, -1)] if handed else list(range(n - 1, 0, -1))


def by_distance(refs, handed):
    order = exchange_order(len(refs) + 1, handed)
    return [refs[order.index(d)] for d in range(1, len(refs) + 1)]


def join_kernel(step, fix, section, z_ref, iface_ref, table_ref, marks_ref, *refs):
    n = lax.axis_size("net")
    arrived, state_ref, outgoing = by_distance(refs[: n - 1], step == 0), refs[n - 1], refs[n:]
    blocks, cols, _ = z_ref.shape

    @pl.when(lax.axis_index("tm") == section)
    def _():
        keep = None
        if fix:
            rows = [marks_ref[pl.ds(marks_layout(n, blocks, fix)[2], 1)]]
            rows += [block[cols : cols + 1].astype(jnp.float32) for block in arrived]
            keep = kept(table_ref[...], rows)
        made = joined([z_ref[i] for i in range(blocks)], step, iface_ref, marks_ref, arrived, keep)
        give(made, marks_ref, state_ref, outgoing)


def write_kernel(step, section, firsts, before, state_ref, jac_ref, iface_ref, table_ref, marks_ref, *refs):
    n = lax.axis_size("net")
    *refs, sems = refs
    before, refs = refs[:before], refs[before:]
    if firsts:
        *refs, made_ref, acc_ref, cols_ref, send_ref, recv_ref, live_ref, load_sems = refs
        ints = [cols_ref, send_ref, recv_ref, live_ref]
        opening_ref, handed, sources, (z_ref, out_ref) = refs[0], refs[1:n], refs[n : n + 4], refs[n + 4 :]
    else:
        _, z_ref, out_ref = refs
    here = lax.axis_index("tm") == section

    @pl.when(here)
    def _():
        for copy in write_copies(before, 0, out_ref, sems):
            copy.start()

    own_kernel(step, state_ref, jac_ref, iface_ref, table_ref, marks_ref, z_ref)

    @pl.when(here)
    def _():
        for copy in write_copies(before, 0, out_ref, sems):
            copy.wait()

    if firsts:

        @pl.when(lax.axis_index("tm") == 0)
        def _():
            loads = [
                pltpu.make_async_copy(source, target, load_sems.at[i])
                for i, (source, target) in enumerate(zip(sources, ints))
            ]
            for load in loads:
                load.start()
            for load in loads:
                load.wait()
            made = first_states(opening_ref, handed, jac_ref, iface_ref, ints, table_ref, made_ref, acc_ref)
            write(made, 0, out_ref, sems)


def close_kernel(step, section, place, z_ref, iface_ref, marks_ref, *refs):
    n = lax.axis_size("net")
    arrived, (_, out_ref, state_ref, *outgoing, sems) = by_distance(refs[: n - 1], False), refs[n - 1 :]

    @pl.when(lax.axis_index("tm") == section)
    def _():
        sums = [z_ref[i] for i in range(z_ref.shape[0])]
        give(joined(sums, step, iface_ref, marks_ref, arrived), marks_ref, state_ref, outgoing)
        write([state_ref], place, out_ref, sems)


def local(jac, block_cols, iface_jac, iface_send, iface_recv, iface_live, ctrl_node, ctrl_gain):
    steps, blocks, kinds, width, _ = jac.shape
    cols = ctrl_node.shape[0]
    tm = lax.axis_size("tm")
    n = lax.axis_size("net")
    col_parts = lax.axis_size("cols")
    node = ctrl_node[None]
    near = block_cols.T
    bf16 = functools.partial(jax.ShapeDtypeStruct, dtype=jnp.bfloat16)
    f32 = functools.partial(jax.ShapeDtypeStruct, dtype=jnp.float32)
    whole, one = bf16((blocks, cols, width)), bf16((cols, width))
    table_rows = GAIN + steps + -(GAIN + steps) % 8
    written = bf16((steps, cols, blocks * width))

    pinned = [
        pltpu.with_memory_space_constraint(x, pltpu.HBM)
        for x in (jac, iface_jac, near, iface_send, iface_recv, iface_live, node, ctrl_gain)
    ]
    marks_rows = marks_layout(n, blocks, kinds)[-1]
    table, marks, state, *outgoing = pl.pallas_call(
        second_kernel,
        out_shape=[f32((cols, table_rows)), f32((marks_rows, width)), whole]
        + [bf16((cols + ROWS, width))] * (n - 1),
        in_specs=[HBM] * len(pinned),
        out_specs=[VMEM] * (n + 2),
        scratch_shapes=[
            pltpu.VMEM((blocks, kinds, width, width), jnp.bfloat16),
            pltpu.VMEM((n, width, width), jnp.bfloat16),
            *[pltpu.SMEM(x.shape, x.dtype) for x in (near, iface_send, iface_recv, iface_live)],
            *[pltpu.VMEM(x.shape, x.dtype) for x in (node, ctrl_gain)],
            pltpu.VMEM(whole.shape, jnp.bfloat16),
            DMA((len(pinned),)),
        ],
        compiler_params=LIMIT,
    )(*pinned)

    def own(state, step):
        return pl.pallas_call(
            functools.partial(own_kernel, step),
            out_shape=f32(whole.shape),
            in_specs=[VMEM] * 5,
            out_specs=VMEM,
            compiler_params=LIMIT,
        )(state, jac, iface_jac, table, marks)

    def join(z, step, fix, arrived, section):
        return pl.pallas_call(
            functools.partial(join_kernel, step, kinds if fix else 0, section),
            out_shape=[whole] + [one] * (n - 1),
            in_specs=[VMEM] * (n + 3),
            out_specs=[VMEM] * n,
            compiler_params=LIMIT,
        )(z, iface_jac, table, marks, *[arrived[d - 1] for d in exchange_order(n, step == 0)])

    def own_and_write(state, step, section, before, out):
        firsts = out is None
        arrays = [state, jac, iface_jac, table, marks, *before]
        specs = [VMEM] * len(arrays)
        scratch = [DMA((steps, blocks))]
        aliases = {}
        if firsts:
            arrays += [opening, *handed, *pinned[2:6]]
            specs += [VMEM] * n + [HBM] * 4
            scratch = [
                pltpu.VMEM((2, *whole.shape), jnp.bfloat16),
                pltpu.VMEM(whole.shape, jnp.float32),
                *[pltpu.SMEM(x.shape, x.dtype) for x in pinned[2:6]],
                DMA((4,)),
            ] + scratch
        else:
            aliases = {len(arrays): 1}
            arrays.append(out)
            specs.append(ANY)
        return pl.pallas_call(
            functools.partial(write_kernel, step, section, firsts, len(before)),
            out_shape=[f32(whole.shape), written],
            in_specs=specs,
            out_specs=[VMEM, ANY],
            input_output_aliases=aliases,
            scratch_shapes=scratch,
            compiler_params=LIMIT,
        )(*arrays)

    def close(z, step, arrived, section, out, send):
        ordered = [arrived[d - 1] for d in exchange_order(n, False)]
        return pl.pallas_call(
            functools.partial(close_kernel, step, section, steps - 1),
            out_shape=[written] + ([whole] + [one] * (n - 1) if send else []),
            in_specs=[VMEM] * (n + 2) + [ANY],
            out_specs=[ANY] + [VMEM] * (n if send else 0),
            input_output_aliases={n + 2: 0},
            scratch_shapes=([] if send else [pltpu.VMEM(whole.shape, jnp.bfloat16)]) + [DMA((steps, blocks))],
            compiler_params=LIMIT,
        )(z, iface_jac, marks, *ordered, out)

    def swap(block, first, second, d):
        other = {first: second, second: first}
        pairs = []
        for a in range(tm):
            for q in range(n):
                for c in range(col_parts):
                    to = (other[a] * n + (q ^ d)) * col_parts + c if a in other else (a * n + q) * col_parts + (c ^ 1)
                    pairs.append(((a * n + q) * col_parts + c, to))
        return lax.ppermute(block, ("tm", "net", "cols"), pairs)

    def exchange(outgoing, first, second):
        return [swap(outgoing[d - 1], first, second, d) for d in range(1, n)]

    opening = state
    out = None
    for r in range(1, tm):
        arrived = exchange(outgoing, r - 1, r)
        state = swap(state, r - 1, r, 0)
        if r == 1:
            handed = arrived
        before = []
        for s in range(steps):
            fix = r == 1 and s == 0
            if s > 0:
                arrived = exchange(outgoing, r, r)
            if s < steps - 1:
                state, *outgoing = join(own(state, s), s, fix, arrived, r)
                before.append(state)
            else:
                z, out = own_and_write(state, s, r, before, out)
                out, *rest = close(z, s, arrived, r, out, r < tm - 1)
                state, *outgoing = rest or [None]
    return out


def solution(mesh):
    return jax.shard_map(
        local,
        mesh=mesh,
        in_specs=(
            P("tm", "net", None, None, None),
            P("net", None),
            P("tm", "net", None, None, None),
            P("net", None),
            P("net", None),
            P("net", None),
            P("cols"),
            P("tm", "cols"),
        ),
        out_specs=P("tm", "cols", "net"),
        check_vma=False,
    )
```
